32 devices in a mesh: groups: 2 (over y), row: 8 (over z, x), col: 2 (over core).
Axes of the slice: x: 2, y: 2, z: 4, core: 2. Of those that a mesh axis runs over, the one named last changes fastest.
Arguments:
- pair_in: bfloat16 [32, 16, 128], P(('groups', 'row'), 'col'), parts along dimension 0, may hold values from -6 to 6
- token_mask: int32 [32], P('groups'), parts along dimension 0, may hold values 0 or 1
- positions: int32 [32], P('groups'), parts along dimension 0, may hold values from 0 to 127
- relpos_table: bfloat16 [128, 128], replicated, may hold values from -6 to 6
- tri_norm_in: float32 [128], replicated, may hold values from 0.5 to 1.5
- tri_in_weight: bfloat16 [128, 256], replicated, may hold values from -0.5 to 0.5
- tri_in_gate: bfloat16 [128, 256], replicated, may hold values from -0.5 to 0.5
- tri_out_gate: bfloat16 [128, 128], replicated, may hold values from -0.5 to 0.5
- tri_norm_out: float32 [128], replicated, may hold values from 0.5 to 1.5
- tri_out_weight: bfloat16 [128, 128], replicated, may hold values from -0.5 to 0.5
- att_norm: float32 [128], replicated, may hold values from 0.5 to 1.5
- att_qkv: bfloat16 [128, 384], replicated, may hold values from -0.5 to 0.5
- att_gate: bfloat16 [128, 128], replicated, may hold values from -0.5 to 0.5
- att_bias: bfloat16 [128, 4], replicated, may hold values from -12 to 12
- att_out: bfloat16 [128, 128], replicated, may hold values from -0.5 to 0.5
Outputs:
- pair_out: bfloat16 [32, 16, 128], P(('groups', 'row'), 'col'), parts along dimension 0
The draws below stay inside these ranges and needn't reach their ends.
There are 2 independent parts, one for each index of `groups`. The reference program is written for one: setup_inputs(seed, part) draws one part's arguments, and reference() takes and returns one part's arrays. A program takes and returns all parts, laid end to end along the dimension named above; an argument that names none is the same for every part. Nothing has to cross between parts.
All inputs are finite; a program needn't handle non-finite values.
Results may differ from the reference program's by a relative error of at most 0.012.
The reference program's roundings to bfloat16 on the way count: a program that leaves them out, or rounds other values in their place, can miss the bound.
Values may be sent and summed in bfloat16 or wider, within the bound.
No kernel may reach another device: no remote copies, remote signals or barrier semaphores. Data moves between devices by JAX's collectives and lax.ppermute only.
A program may use at most 64 MiB of HBM per device.

```python
import math
import jax
import jax.numpy as jnp
from jax import lax

PAIR_WIDTH = 128
HEADS = 4
HEAD_DIM = 32
RELPOS_BINS = 128
TOKENS = 16


def draw_att_bias(key, part):
    key = jax.random.fold_in(key, 7)
    values = jax.random.normal(key, (PAIR_WIDTH, HEADS), jnp.float32) * 0.15
    return values.astype(jnp.bfloat16)


def place_ends(drawn, stream_key, low, largest):
    dims = drawn.shape
    index_at = [jax.random.randint(jax.random.fold_in(stream_key, axis), (), 0, dims[axis]) for axis in range(len(dims))]
    drawn = drawn.at[tuple(index_at)].set(low)
    longest = dims.index(max(dims))
    index_at[longest] = (index_at[longest] + 1) % dims[longest]
    return drawn.at[tuple(index_at)].set(largest)


def level_of(own_key, dims, split, least, high):
    level, own = 1.0, jax.random.fold_in(own_key, 6)
    for dim, blocks in split:
        steps = jnp.exp(jax.random.uniform(jax.random.fold_in(own, dim), (blocks,), jnp.float32, least / len(split), high / len(split)))
        level = level * jnp.repeat(steps, dims[dim] // blocks).reshape([-1 if axis == dim else 1 for axis in range(len(dims))])
    return level


def gaussian(own_key, shape, scale, bound, shards=(), kind=jnp.bfloat16):
    level = level_of(own_key, shape, shards, -0.22, 0.18) if shards else 1.0
    entries = jax.random.normal(own_key, shape, jnp.float32) * scale * level
    return jnp.minimum(jnp.maximum(entries, -bound), bound).astype(kind)


def setup_inputs(seed: int = 0, part: int = 0) -> dict:
    key_list = jax.random.split(jax.random.key(seed), 16)
    part_keys = jax.random.split(jax.random.fold_in(key_list[15], part), 16)
    return {
        "pair_in": gaussian(part_keys[0], (TOKENS, TOKENS, PAIR_WIDTH), 1.0, 6.0, ((0, 8), (1, 2))),
        "token_mask": place_ends((jax.random.randint(part_keys[1], (TOKENS,), 0, 8) < 7).astype(jnp.int32), jax.random.fold_in(part_keys[1], 1), 0, 1),
        "positions": place_ends(jax.random.randint(part_keys[2], (TOKENS,), 0, RELPOS_BINS), jax.random.fold_in(part_keys[2], 1), 0, RELPOS_BINS - 1).astype(jnp.int32),
        "relpos_table": gaussian(key_list[3], (RELPOS_BINS, PAIR_WIDTH), 1.0, 6.0),
        "tri_norm_in": jnp.clip(1.0 + 0.1 * jax.random.normal(key_list[4], (PAIR_WIDTH,), jnp.float32), 0.5, 1.5),
        "tri_in_weight": gaussian(key_list[5], (PAIR_WIDTH, 2 * PAIR_WIDTH), PAIR_WIDTH ** -0.5, 0.5),
        "tri_in_gate": gaussian(key_list[6], (PAIR_WIDTH, 2 * PAIR_WIDTH), PAIR_WIDTH ** -0.5, 0.5),
        "tri_out_gate": gaussian(key_list[7], (PAIR_WIDTH, PAIR_WIDTH), PAIR_WIDTH ** -0.5, 0.5),
        "tri_norm_out": jnp.clip(1.0 + 0.1 * jax.random.normal(key_list[8], (PAIR_WIDTH,), jnp.float32), 0.5, 1.5),
        "tri_out_weight": gaussian(key_list[9], (PAIR_WIDTH, PAIR_WIDTH), PAIR_WIDTH ** -0.5, 0.5),
        "att_norm": jnp.clip(1.0 + 0.1 * jax.random.normal(key_list[10], (PAIR_WIDTH,), jnp.float32), 0.5, 1.5),
        "att_qkv": gaussian(key_list[11], (PAIR_WIDTH, 3 * PAIR_WIDTH), PAIR_WIDTH ** -0.5, 0.5),
        "att_gate": gaussian(key_list[12], (PAIR_WIDTH, PAIR_WIDTH), PAIR_WIDTH ** -0.5, 0.5),
        "att_bias": draw_att_bias(jax.random.fold_in(key_list[15], 71), part),
        "att_out": gaussian(key_list[14], (PAIR_WIDTH, PAIR_WIDTH), PAIR_WIDTH ** -0.5, 0.5),
    }


epsilon = 1e-05

def layer_norm(values, gain):
    mean_val = lax.optimization_barrier(jnp.mean(values, axis=-1, keepdims=True))
    centred = values - mean_val
    var_val = lax.optimization_barrier(jnp.mean(centred * centred, axis=-1, keepdims=True))
    return centred * lax.rsqrt(var_val + epsilon) * gain

def flat_dot(values, weight):
    lead = values.shape[:-1]
    flat = values.reshape(-1, values.shape[-1])
    return jnp.dot(flat, weight, preferred_element_type=jnp.float32).reshape(lead + (weight.shape[1],))

def attend_column(query_col, key_col, value_col, bias_all, key_bias):
    tok_total = query_col.shape[0]
    block_rows = min(1024, tok_total)
    scale = 1.0 / math.sqrt(query_col.shape[2])
    key_f = key_col.astype(jnp.float32)
    value_f = value_col.astype(jnp.float32)

    def one_block(block_idx):
        first_row = block_idx * block_rows
        query_blk = lax.dynamic_slice_in_dim(query_col, first_row, block_rows, 0).astype(jnp.float32)
        bias_blk = lax.dynamic_slice_in_dim(bias_all, first_row, block_rows, 1)
        scores = jnp.einsum('ihe,khe->hik', query_blk, key_f) * scale
        scores = scores + bias_blk.astype(jnp.float32) + key_bias[None, None, :]
        row_max = lax.optimization_barrier(jnp.max(scores, axis=-1, keepdims=True))
        expo_f = jnp.exp(scores - row_max)
        totals = lax.optimization_barrier(jnp.sum(expo_f, axis=-1))
        weights = expo_f.astype(jnp.bfloat16).astype(jnp.float32)
        result = jnp.einsum('hik,khe->ihe', weights, value_f)
        return result / jnp.transpose(totals)[:, :, None]
    blocks = lax.map(one_block, jnp.arange(tok_total // block_rows))
    return blocks.reshape(tok_total, query_col.shape[1], query_col.shape[2])

def reference(pair_in, token_mask, positions, relpos_table, tri_norm_in, tri_in_weight, tri_in_gate, tri_out_gate, tri_norm_out, tri_out_weight, att_norm, att_qkv, att_gate, att_bias, att_out):
    channels = PAIR_WIDTH
    mask_float = token_mask.astype(jnp.float32)
    bin_centre = RELPOS_BINS // 2
    bucket = jnp.clip(positions[:, None] - positions[None, :], -bin_centre, bin_centre - 1) + bin_centre
    bucket = bucket.astype(jnp.int32)
    residual = pair_in.astype(jnp.float32) + jnp.take(relpos_table, bucket, axis=0).astype(jnp.float32)
    normed = layer_norm(residual, tri_norm_in).astype(jnp.bfloat16)
    pair_mask = mask_float[:, None] * mask_float[None, :]
    projected = jax.nn.sigmoid(flat_dot(normed, tri_in_gate)) * flat_dot(normed, tri_in_weight) * pair_mask[:, :, None]
    projected = projected.astype(jnp.bfloat16)
    left_ch = jnp.moveaxis(projected[:, :, :channels], 2, 0)
    right_ch = jnp.moveaxis(projected[:, :, channels:], 2, 0)

    def one_channel(operands):
        return jnp.dot(operands[0], jnp.transpose(operands[1]), preferred_element_type=jnp.float32).astype(jnp.bfloat16)
    products = lax.map(one_channel, (left_ch, right_ch))
    tri_x = jnp.moveaxis(products, 0, 2).astype(jnp.float32)
    normed_out = layer_norm(tri_x, tri_norm_out).astype(jnp.bfloat16)
    residual = residual + jax.nn.sigmoid(flat_dot(normed, tri_out_gate)) * flat_dot(normed_out, tri_out_weight)
    normed_att = layer_norm(residual, att_norm).astype(jnp.bfloat16)
    qkv_all = flat_dot(normed_att, att_qkv).astype(jnp.bfloat16)
    qkv_all = qkv_all.reshape(TOKENS, TOKENS, 3, HEADS, HEAD_DIM)
    gate_val = jax.nn.sigmoid(flat_dot(normed_att, att_gate))
    pair_bias = flat_dot(normed_att, att_bias).astype(jnp.bfloat16)
    pair_bias = jnp.transpose(pair_bias, (2, 1, 0))
    key_bias = (mask_float - 1.0) * 1000000000.0
    queries = jnp.moveaxis(qkv_all[:, :, 0], 1, 0)
    keys_all = jnp.moveaxis(qkv_all[:, :, 1], 1, 0)
    values_all = jnp.moveaxis(qkv_all[:, :, 2], 1, 0)

    def one_column(triple):
        return attend_column(triple[0], triple[1], triple[2], pair_bias, key_bias)
    attended = lax.map(one_column, (queries, keys_all, values_all))
    attended = jnp.moveaxis(attended, 0, 1).reshape(TOKENS, TOKENS, channels)
    gated = (gate_val * attended).astype(jnp.bfloat16)
    return (residual + flat_dot(gated, att_out)).astype(jnp.bfloat16)
```

```python
import functools
import math

import jax
import jax.numpy as jnp
from jax import lax
from jax.experimental import pallas as pl
from jax.experimental.pallas import tpu as pltpu
from jax.sharding import PartitionSpec as P

epsilon = 1e-05

WHOLE_PAIR_BYTES = 256 * 1024


def layer_norm(values, gain):
    mean_val = jnp.mean(values, axis=-1, keepdims=True)
    centred = values - mean_val
    var_val = jnp.mean(centred * centred, axis=-1, keepdims=True)
    return centred * lax.rsqrt(var_val + epsilon) * gain


def sigmoid(values):
    return 0.5 * jnp.tanh(0.5 * values) + 0.5


def dot(left, right):
    return jnp.dot(left, right, preferred_element_type=jnp.float32)


def dot_t(left, right):
    return lax.dot_general(
        left, right, (((1,), (1,)), ((), ())), preferred_element_type=jnp.float32
    )


def round_bf16(values):
    return values.astype(jnp.bfloat16).astype(jnp.float32)


def whole_pair_kernel(
    row_dim,
    heads,
    mask_ref,
    pos_ref,
    pair_ref,
    table_ref,
    norm_in_ref,
    in_weight_ref,
    in_gate_ref,
    out_gate_ref,
    norm_out_ref,
    out_weight_ref,
    att_norm_ref,
    qkv_ref,
    att_gate_ref,
    att_bias_ref,
    att_out_ref,
    out_ref,
    base_ref,
    normed_ref,
    left_ref,
    right_ref,
    att_ref,
    upd_ref,
):
    blocks, rows, cols, width = pair_ref.shape
    col_dim = blocks // row_dim
    tokens = row_dim * rows
    bins = table_ref.shape[0]
    head_dim = width // heads
    row_first = lax.axis_index("row") * rows
    col_first = pl.multiple_of(lax.axis_index("col") * cols, cols)
    f32, bf16 = jnp.float32, jnp.bfloat16

    sub = lax.broadcasted_iota(jnp.int32, (cols, bins), 0)
    lane = lax.broadcasted_iota(jnp.int32, (cols, bins), 1)
    col_pos, col_mask = [], []
    for half in range(col_dim):
        pos_vec = jnp.zeros((cols, bins), jnp.int32)
        mask_vec = jnp.zeros((cols, bins), jnp.int32)
        for c in range(cols):
            pos_vec = jnp.where(sub == c, pos_ref[half * cols + c], pos_vec)
            mask_vec = jnp.where(sub == c, mask_ref[half * cols + c], mask_vec)
        col_pos.append(pos_vec)
        col_mask.append(mask_vec)
    hot, pair, masks = [], [], []
    for i in range(tokens):
        for half in range(col_dim):
            bucket = jnp.clip(pos_ref[i] - col_pos[half], -(bins // 2), bins // 2 - 1) + bins // 2
            hot.append((bucket == lane).astype(f32))
            masks.append((col_mask[half] * mask_ref[i]).astype(f32)[:, :1])
            pair.append(pair_ref[(i // rows) * col_dim + half].astype(f32)[i % rows])
    hot = jnp.concatenate(hot, axis=0).astype(bf16)
    masks = jnp.concatenate(masks, axis=0)
    base = jnp.concatenate(pair, axis=0) + dot(hot, table_ref[...])
    base_ref[...] = base

    normed = layer_norm(base, norm_in_ref[...]).astype(bf16)
    normed_ref[...] = normed.astype(f32)
    projected = sigmoid(dot(normed, in_gate_ref[...])) * dot(normed, in_weight_ref[...]) * masks
    projected = round_bf16(projected)
    left_ref[...] = projected[:, :width]
    right_ref[...] = projected[:, width:]

    right_at = [right_ref[pl.ds(col_first * tokens + m, cols, stride=tokens), :] for m in range(tokens)]
    products = []
    for i in range(tokens):
        total = left_ref[pl.ds(i * tokens, 1), :] * right_at[0]
        for m in range(1, tokens):
            total = total + left_ref[pl.ds(i * tokens + m, 1), :] * right_at[m]
        products.append(total)
    extra = [None] * rows
    for m in range(tokens):
        left_at = left_ref[pl.ds(m, tokens, stride=tokens), :]
        for r in range(rows):
            term = left_at * right_ref[pl.ds((row_first + r) * tokens + m, 1), :]
            extra[r] = term if m == 0 else extra[r] + term
    products = round_bf16(jnp.concatenate(products + extra, axis=0))

    def chosen(ref):
        own = [ref[pl.ds(i * tokens + col_first, cols), :] for i in range(tokens)]
        own += [ref[pl.ds(row_first + r, tokens, stride=tokens), :] for r in range(rows)]
        return jnp.concatenate(own, axis=0)

    normed_out = layer_norm(products, norm_out_ref[...]).astype(bf16)
    out_gate = sigmoid(dot(chosen(normed_ref).astype(bf16), out_gate_ref[...]))
    updated = chosen(base_ref) + out_gate * dot(normed_out, out_weight_ref[...])
    normed_att = layer_norm(updated, att_norm_ref[...]).astype(bf16)
    own_pairs = rows * cols
    column_pairs = tokens * cols
    upd_ref[...] = updated[:column_pairs]
    att_f = normed_att.astype(f32)
    att_ref[...] = att_f[:column_pairs]

    own_at = pl.ds(pl.multiple_of(row_first * cols, own_pairs), own_pairs)
    own = att_ref[own_at, :].astype(bf16)
    column = normed_att[:column_pairs]
    queries = dot(own, qkv_ref[:, :width])
    keys = dot(column, qkv_ref[:, width : 2 * width]).astype(bf16)
    values = dot(column, qkv_ref[:, 2 * width :]).astype(bf16)
    own_gate = sigmoid(dot(own, att_gate_ref[...]))

    bias = []
    for r in range(rows):
        part = att_f[column_pairs + r * tokens : column_pairs + (r + 1) * tokens]
        spread = jnp.concatenate(
            [jnp.broadcast_to(part[k : k + 1], (cols, width)) for k in range(tokens)], axis=0
        )
        bias.append(round_bf16(dot_t(att_bias_ref[...], spread.astype(bf16))))

    head_of = lax.broadcasted_iota(jnp.int32, (own_pairs, width), 1) // head_dim
    queries = round_bf16(queries)
    by_head = jnp.concatenate(
        [jnp.where(head_of == h, queries, 0.0) for h in range(heads)], axis=0
    ).astype(bf16)
    scores = dot_t(by_head, keys) * (1.0 / math.sqrt(head_dim))
    biases = jnp.concatenate(
        [jnp.broadcast_to(bias[r][h : h + 1], (cols, column_pairs)) for h in range(heads) for r in range(rows)],
        axis=0,
    )
    lane_row = lax.broadcasted_iota(jnp.int32, (1, column_pairs), 1)
    key_mask = jnp.zeros((1, column_pairs), jnp.int32)
    for k in range(tokens):
        key_mask = jnp.where(lane_row // cols == k, mask_ref[k], key_mask)
    key_bias = (key_mask.astype(f32) - 1.0) * 1000000000.0
    scores = scores + biases + key_bias
    same = (
        lax.broadcasted_iota(jnp.int32, scores.shape, 1) % cols
        == lax.broadcasted_iota(jnp.int32, scores.shape, 0) % cols
    )
    scores = jnp.where(same, scores, -jnp.inf)
    expo = jnp.exp(scores - jnp.max(scores, axis=-1, keepdims=True))
    totals = jnp.sum(expo, axis=-1, keepdims=True)
    mixed = dot(expo.astype(bf16), values) / totals
    attended = jnp.zeros((own_pairs, width), f32)
    for h in range(heads):
        attended = jnp.where(head_of == h, mixed[h * own_pairs : (h + 1) * own_pairs], attended)

    gated = (own_gate * attended).astype(bf16)
    result = upd_ref[own_at, :] + dot(gated, att_out_ref[...])
    out_ref[...] = result.reshape(rows, cols, width).astype(bf16)


def whole_pair_on_device(
    row_dim,
    pair_in,
    token_mask,
    positions,
    relpos_table,
    tri_norm_in,
    tri_in_weight,
    tri_in_gate,
    tri_out_gate,
    tri_norm_out,
    tri_out_weight,
    att_norm,
    att_qkv,
    att_gate,
    att_bias,
    att_out,
):
    rows, cols, width = pair_in.shape
    tokens = row_dim * rows
    heads = att_bias.shape[1]
    pair = lax.all_gather(pair_in, ("row", "col"), axis=0, tiled=False)
    in_vmem = pl.BlockSpec(memory_space=pltpu.VMEM)
    in_smem = pl.BlockSpec(memory_space=pltpu.SMEM)
    wide = pltpu.VMEM((tokens * tokens, width), jnp.float32)
    column = pltpu.VMEM((tokens * cols, width), jnp.float32)
    return pl.pallas_call(
        functools.partial(whole_pair_kernel, row_dim, heads),
        out_shape=jax.ShapeDtypeStruct(pair_in.shape, pair_in.dtype),
        in_specs=[in_smem] * 2 + [in_vmem] * 13,
        out_specs=in_vmem,
        scratch_shapes=[wide] * 4 + [column] * 2,
        compiler_params=pltpu.CompilerParams(vmem_limit_bytes=16 * 1024 * 1024),
    )(
        token_mask,
        positions,
        pair,
        relpos_table,
        tri_norm_in.reshape(1, width),
        tri_in_weight,
        tri_in_gate,
        tri_out_gate,
        tri_norm_out.reshape(1, width),
        tri_out_weight,
        att_norm.reshape(1, width),
        att_qkv,
        att_gate,
        att_bias.T,
        att_out,
    )


def attend_column(query_col, key_col, value_col, bias_all, key_bias, block_rows):
    tok_total = query_col.shape[0]
    scale = 1.0 / math.sqrt(query_col.shape[2])

    def one_block(block_idx):
        scores = (
            jnp.einsum("ihe,khe->hik", query_col, key_col, preferred_element_type=jnp.float32)
            * scale
        )
        scores = scores + bias_all.astype(jnp.float32) + key_bias[None, None, :]
        row_max = jnp.max(scores, axis=-1, keepdims=True)
        expo_f = jnp.exp(scores - row_max)
        totals = jnp.sum(expo_f, axis=-1)
        weights = expo_f.astype(jnp.bfloat16)
        result = jnp.einsum("hik,khe->ihe", weights, value_col, preferred_element_type=jnp.float32)
        return result / jnp.transpose(totals)[:, :, None]

    blocks = lax.map(one_block, jnp.arange(tok_total // block_rows))
    return blocks.reshape(tok_total, query_col.shape[1], query_col.shape[2])


def column_attention(columns, att_qkv, att_gate, bias_all, key_bias, head_local, head_dim):
    tok_total, col_count, channels = columns.shape
    local_width = head_local * head_dim
    weight_three = att_qkv.reshape(channels, 3, channels)
    qkv_all = jnp.einsum(
        "kmc,ctd->tmkd", columns, weight_three, preferred_element_type=jnp.float32
    ).astype(jnp.bfloat16)
    qkv_all = qkv_all.reshape(3, col_count, tok_total, head_local, head_dim)
    gate_val = jax.nn.sigmoid(
        jnp.einsum("kmc,cd->kmd", columns, att_gate, preferred_element_type=jnp.float32)
    )
    block_rows = min(1024, tok_total)

    def one_column(triple):
        return attend_column(triple[0], triple[1], triple[2], bias_all, key_bias, block_rows)

    attended = lax.map(one_column, (qkv_all[0], qkv_all[1], qkv_all[2]))
    attended = jnp.transpose(attended, (1, 0, 2, 3)).reshape(tok_total, col_count, local_width)
    return (gate_val * attended).astype(jnp.bfloat16)


def split_pair_on_device(
    pair_in,
    token_mask,
    positions,
    relpos_table,
    tri_norm_in,
    tri_in_weight,
    tri_in_gate,
    tri_out_gate,
    tri_norm_out,
    tri_out_weight,
    att_norm,
    att_qkv,
    att_gate,
    att_bias,
    att_out,
):
    row_count, col_count, channels = pair_in.shape
    row_first = lax.axis_index("row") * row_count
    col_first = lax.axis_index("col") * col_count
    mask_float = token_mask.astype(jnp.float32)
    row_mask = lax.dynamic_slice_in_dim(mask_float, row_first, row_count)
    col_mask = lax.dynamic_slice_in_dim(mask_float, col_first, col_count)
    row_pos = lax.dynamic_slice_in_dim(positions, row_first, row_count)
    col_pos = lax.dynamic_slice_in_dim(positions, col_first, col_count)
    bin_count = relpos_table.shape[0]
    bin_centre = bin_count // 2
    bucket = jnp.clip(row_pos[:, None] - col_pos[None, :], -bin_centre, bin_centre - 1) + bin_centre
    onehot = (bucket[:, :, None] == jnp.arange(bin_count, dtype=jnp.int32)[None, None, :]).astype(
        jnp.bfloat16
    )
    residual = pair_in.astype(jnp.float32) + jnp.einsum(
        "rjb,bc->rjc", onehot, relpos_table, preferred_element_type=jnp.float32
    )
    normed = layer_norm(residual, tri_norm_in).astype(jnp.bfloat16)
    pair_mask = row_mask[:, None] * col_mask[None, :]
    gate_in = jnp.einsum("rjc,cd->drj", normed, tri_in_gate, preferred_element_type=jnp.float32)
    proj_in = jnp.einsum("rjc,cd->drj", normed, tri_in_weight, preferred_element_type=jnp.float32)
    projected = (jax.nn.sigmoid(gate_in) * proj_in * pair_mask[None, :, :]).astype(jnp.bfloat16)
    left_ch, right_ch = (
        lax.all_to_all(projected[:channels], "row", split_axis=0, concat_axis=1, tiled=True),
        lax.all_to_all(projected[channels:], "row", split_axis=0, concat_axis=1, tiled=True),
    )
    right_rows = lax.all_to_all(right_ch, "col", split_axis=1, concat_axis=2, tiled=True)
    product_sum = jnp.einsum(
        "cik,cjk->cij",
        lax.all_gather(left_ch, "col", axis=2, tiled=True),
        right_rows,
        preferred_element_type=jnp.float32,
    )
    products = product_sum.astype(jnp.bfloat16)
    product_tile = lax.all_to_all(products, "row", split_axis=1, concat_axis=0, tiled=True)
    tri_x = jnp.transpose(product_tile, (1, 2, 0)).astype(jnp.float32)
    normed_out = layer_norm(tri_x, tri_norm_out).astype(jnp.bfloat16)
    out_gate = jax.nn.sigmoid(
        jnp.einsum("rjc,cd->rjd", normed, tri_out_gate, preferred_element_type=jnp.float32)
    )
    residual = residual + out_gate * jnp.einsum(
        "rjc,cd->rjd", normed_out, tri_out_weight, preferred_element_type=jnp.float32
    )
    normed_att = layer_norm(residual, att_norm).astype(jnp.bfloat16)
    bias_piece = jnp.einsum(
        "kic,ch->hik", normed_att, att_bias, preferred_element_type=jnp.float32
    ).astype(jnp.bfloat16)
    key_bias = (mask_float - 1.0) * 1000000000.0
    head_count = att_bias.shape[1]
    head_dim = channels // head_count
    columns = lax.all_to_all(normed_att, "row", split_axis=1, concat_axis=0, tiled=True)
    bias_half = lax.all_gather(bias_piece, "col", axis=1, tiled=True)
    bias_all = lax.all_gather(bias_half, "row", axis=2, tiled=True)
    gated = column_attention(columns, att_qkv, att_gate, bias_all, key_bias, head_count, head_dim)
    gated_tile = lax.all_to_all(gated, "row", split_axis=0, concat_axis=1, tiled=True)
    update = jnp.einsum("rjc,cd->rjd", gated_tile, att_out, preferred_element_type=jnp.float32)
    return (residual + update).astype(jnp.bfloat16)


def on_device(row_dim, pair_in, *others):
    rows, cols, width = pair_in.shape
    tokens = row_dim * rows
    whole_bytes = tokens * tokens * width * pair_in.dtype.itemsize
    if whole_bytes <= WHOLE_PAIR_BYTES and cols % 8 == 0 and width % 128 == 0:
        return whole_pair_on_device(row_dim, pair_in, *others)
    return split_pair_on_device(pair_in, *others)


def solution(mesh):
    return jax.shard_map(
        functools.partial(on_device, mesh.shape["row"]),
        mesh=mesh,
        in_specs=(P(("groups", "row"), "col", None), P("groups"), P("groups")) + (P(),) * 12,
        out_specs=P(("groups", "row"), "col", None),
        check_vma=False,
    )
```

```python
import functools
import math

import jax
import jax.numpy as jnp
from jax import lax
from jax.experimental import pallas as pl
from jax.experimental.pallas import tpu as pltpu
from jax.sharding import PartitionSpec as P

epsilon = 1e-05

WHOLE_PAIR_BYTES = 256 * 1024


def layer_norm(values, gain):
    mean_val = jnp.mean(values, axis=-1, keepdims=True)
    centred = values - mean_val
    var_val = jnp.mean(centred * centred, axis=-1, keepdims=True)
    return centred * lax.rsqrt(var_val + epsilon) * gain


def sigmoid(values):
    return 0.5 * jnp.tanh(0.5 * values) + 0.5


def dot(left, right):
    return jnp.dot(left, right, preferred_element_type=jnp.float32)


def dot_t(left, right):
    return lax.dot_general(
        left, right, (((1,), (1,)), ((), ())), preferred_element_type=jnp.float32
    )


def round_bf16(values):
    return values.astype(jnp.bfloat16).astype(jnp.float32)


def whole_pair_kernel(row_dim, blocks, heads, mask_ref, pos_ref, *refs):
    whole_pair_steps(row_dim, heads, mask_ref, pos_ref, refs[:blocks], *refs[blocks:])


def whole_pair_steps(
    row_dim,
    heads,
    mask_ref,
    pos_ref,
    block_refs,
    table_ref,
    norm_in_ref,
    in_weight_ref,
    in_gate_ref,
    out_gate_ref,
    norm_out_ref,
    out_weight_ref,
    att_norm_ref,
    qkv_ref,
    att_gate_ref,
    att_bias_ref,
    att_out_ref,
    out_ref,
    base_ref,
    normed_ref,
    left_ref,
    right_ref,
    att_ref,
    upd_ref,
):
    rows, cols, width = block_refs[0].shape
    col_dim = len(block_refs) // row_dim
    tokens = row_dim * rows
    bins = table_ref.shape[0]
    head_dim = width // heads
    row_first = lax.axis_index("row") * rows
    col_first = pl.multiple_of(lax.axis_index("col") * cols, cols)
    f32, bf16 = jnp.float32, jnp.bfloat16

    me = lax.axis_index("row") * col_dim + lax.axis_index("col")
    for m, block_ref in enumerate(block_refs):
        owner = me ^ m
        block = block_ref[...].astype(f32)
        for r in range(rows):
            first = (owner // col_dim * rows + r) * tokens + owner % col_dim * cols
            base_ref[pl.ds(pl.multiple_of(first, cols), cols), :] = block[r]

    sub = lax.broadcasted_iota(jnp.int32, (cols, bins), 0)
    lane = lax.broadcasted_iota(jnp.int32, (cols, bins), 1)
    col_pos, col_mask = [], []
    for half in range(col_dim):
        pos_vec = jnp.zeros((cols, bins), jnp.int32)
        mask_vec = jnp.zeros((cols, bins), jnp.int32)
        for c in range(cols):
            pos_vec = jnp.where(sub == c, pos_ref[half * cols + c], pos_vec)
            mask_vec = jnp.where(sub == c, mask_ref[half * cols + c], mask_vec)
        col_pos.append(pos_vec)
        col_mask.append(mask_vec)
    hot, masks = [], []
    for i in range(tokens):
        for half in range(col_dim):
            bucket = jnp.clip(pos_ref[i] - col_pos[half], -(bins // 2), bins // 2 - 1) + bins // 2
            hot.append((bucket == lane).astype(f32))
            masks.append((col_mask[half] * mask_ref[i]).astype(f32)[:, :1])
    hot = jnp.concatenate(hot, axis=0).astype(bf16)
    masks = jnp.concatenate(masks, axis=0)
    base = base_ref[...] + dot(hot, table_ref[...])
    base_ref[...] = base

    normed = layer_norm(base, norm_in_ref[...]).astype(bf16)
    normed_ref[...] = normed.astype(f32)
    projected = sigmoid(dot(normed, in_gate_ref[...])) * dot(normed, in_weight_ref[...]) * masks
    projected = round_bf16(projected)
    left_ref[...] = projected[:, :width]
    right_ref[...] = projected[:, width:]

    right_at = [right_ref[pl.ds(col_first * tokens + m, cols, stride=tokens), :] for m in range(tokens)]
    products = []
    for i in range(tokens):
        total = left_ref[pl.ds(i * tokens, 1), :] * right_at[0]
        for m in range(1, tokens):
            total = total + left_ref[pl.ds(i * tokens + m, 1), :] * right_at[m]
        products.append(total)
    extra = [None] * rows
    for m in range(tokens):
        left_at = left_ref[pl.ds(m, tokens, stride=tokens), :]
        for r in range(rows):
            term = left_at * right_ref[pl.ds((row_first + r) * tokens + m, 1), :]
            extra[r] = term if m == 0 else extra[r] + term
    products = round_bf16(jnp.concatenate(products + extra, axis=0))

    def chosen(ref):
        own = [ref[pl.ds(i * tokens + col_first, cols), :] for i in range(tokens)]
        own += [ref[pl.ds(row_first + r, tokens, stride=tokens), :] for r in range(rows)]
        return jnp.concatenate(own, axis=0)

    normed_out = layer_norm(products, norm_out_ref[...]).astype(bf16)
    out_gate = sigmoid(dot(chosen(normed_ref).astype(bf16), out_gate_ref[...]))
    updated = chosen(base_ref) + out_gate * dot(normed_out, out_weight_ref[...])
    normed_att = layer_norm(updated, att_norm_ref[...]).astype(bf16)
    own_pairs = rows * cols
    column_pairs = tokens * cols
    upd_ref[...] = updated[:column_pairs]
    att_f = normed_att.astype(f32)
    att_ref[...] = att_f[:column_pairs]

    own_at = pl.ds(pl.multiple_of(row_first * cols, own_pairs), own_pairs)
    own = att_ref[own_at, :].astype(bf16)
    column = normed_att[:column_pairs]
    queries = dot(own, qkv_ref[:, :width])
    keys = dot(column, qkv_ref[:, width : 2 * width]).astype(bf16)
    values = dot(column, qkv_ref[:, 2 * width :]).astype(bf16)
    own_gate = sigmoid(dot(own, att_gate_ref[...]))

    bias = []
    for r in range(rows):
        part = att_f[column_pairs + r * tokens : column_pairs + (r + 1) * tokens]
        spread = jnp.concatenate(
            [jnp.broadcast_to(part[k : k + 1], (cols, width)) for k in range(tokens)], axis=0
        )
        bias.append(round_bf16(dot_t(att_bias_ref[...], spread.astype(bf16))))

    head_of = lax.broadcasted_iota(jnp.int32, (own_pairs, width), 1) // head_dim
    queries = round_bf16(queries)
    by_head = jnp.concatenate(
        [jnp.where(head_of == h, queries, 0.0) for h in range(heads)], axis=0
    ).astype(bf16)
    scores = dot_t(by_head, keys) * (1.0 / math.sqrt(head_dim))
    biases = jnp.concatenate(
        [jnp.broadcast_to(bias[r][h : h + 1], (cols, column_pairs)) for h in range(heads) for r in range(rows)],
        axis=0,
    )
    lane_row = lax.broadcasted_iota(jnp.int32, (1, column_pairs), 1)
    key_mask = jnp.zeros((1, column_pairs), jnp.int32)
    for k in range(tokens):
        key_mask = jnp.where(lane_row // cols == k, mask_ref[k], key_mask)
    key_bias = (key_mask.astype(f32) - 1.0) * 1000000000.0
    scores = scores + biases + key_bias
    same = (
        lax.broadcasted_iota(jnp.int32, scores.shape, 1) % cols
        == lax.broadcasted_iota(jnp.int32, scores.shape, 0) % cols
    )
    scores = jnp.where(same, scores, -jnp.inf)
    expo = jnp.exp(scores - jnp.max(scores, axis=-1, keepdims=True))
    totals = jnp.sum(expo, axis=-1, keepdims=True)
    mixed = dot(expo.astype(bf16), values) / totals
    attended = jnp.zeros((own_pairs, width), f32)
    for h in range(heads):
        attended = jnp.where(head_of == h, mixed[h * own_pairs : (h + 1) * own_pairs], attended)

    gated = (own_gate * attended).astype(bf16)
    result = upd_ref[own_at, :] + dot(gated, att_out_ref[...])
    out_ref[...] = result.reshape(rows, cols, width).astype(bf16)


def whole_pair_on_device(
    row_dim,
    col_dim,
    pair_in,
    token_mask,
    positions,
    relpos_table,
    tri_norm_in,
    tri_in_weight,
    tri_in_gate,
    tri_out_gate,
    tri_norm_out,
    tri_out_weight,
    att_norm,
    att_qkv,
    att_gate,
    att_bias,
    att_out,
):
    rows, cols, width = pair_in.shape
    tokens = row_dim * rows
    heads = att_bias.shape[1]
    blocks = row_dim * col_dim
    pair = [pair_in]
    for m in range(1, blocks):
        partners = [(device, device ^ m) for device in range(blocks)]
        pair.append(lax.ppermute(pair_in, ("row", "col"), partners))
    in_vmem = pl.BlockSpec(memory_space=pltpu.VMEM)
    in_smem = pl.BlockSpec(memory_space=pltpu.SMEM)
    wide = pltpu.VMEM((tokens * tokens, width), jnp.float32)
    column = pltpu.VMEM((tokens * cols, width), jnp.float32)
    return pl.pallas_call(
        functools.partial(whole_pair_kernel, row_dim, blocks, heads),
        out_shape=jax.ShapeDtypeStruct(pair_in.shape, pair_in.dtype),
        in_specs=[in_smem] * 2 + [in_vmem] * (blocks + 12),
        out_specs=in_vmem,
        scratch_shapes=[wide] * 4 + [column] * 2,
        compiler_params=pltpu.CompilerParams(vmem_limit_bytes=16 * 1024 * 1024),
    )(
        token_mask,
        positions,
        *pair,
        relpos_table,
        tri_norm_in.reshape(1, width),
        tri_in_weight,
        tri_in_gate,
        tri_out_gate,
        tri_norm_out.reshape(1, width),
        tri_out_weight,
        att_norm.reshape(1, width),
        att_qkv,
        att_gate,
        att_bias.T,
        att_out,
    )


def attend_column(query_col, key_col, value_col, bias_all, key_bias, block_rows):
    tok_total = query_col.shape[0]
    scale = 1.0 / math.sqrt(query_col.shape[2])

    def one_block(block_idx):
        scores = (
            jnp.einsum("ihe,khe->hik", query_col, key_col, preferred_element_type=jnp.float32)
            * scale
        )
        scores = scores + bias_all.astype(jnp.float32) + key_bias[None, None, :]
        row_max = jnp.max(scores, axis=-1, keepdims=True)
        expo_f = jnp.exp(scores - row_max)
        totals = jnp.sum(expo_f, axis=-1)
        weights = expo_f.astype(jnp.bfloat16)
        result = jnp.einsum("hik,khe->ihe", weights, value_col, preferred_element_type=jnp.float32)
        return result / jnp.transpose(totals)[:, :, None]

    blocks = lax.map(one_block, jnp.arange(tok_total // block_rows))
    return blocks.reshape(tok_total, query_col.shape[1], query_col.shape[2])


def column_attention(columns, att_qkv, att_gate, bias_all, key_bias, head_local, head_dim):
    tok_total, col_count, channels = columns.shape
    local_width = head_local * head_dim
    weight_three = att_qkv.reshape(channels, 3, channels)
    qkv_all = jnp.einsum(
        "kmc,ctd->tmkd", columns, weight_three, preferred_element_type=jnp.float32
    ).astype(jnp.bfloat16)
    qkv_all = qkv_all.reshape(3, col_count, tok_total, head_local, head_dim)
    gate_val = jax.nn.sigmoid(
        jnp.einsum("kmc,cd->kmd", columns, att_gate, preferred_element_type=jnp.float32)
    )
    block_rows = min(1024, tok_total)

    def one_column(triple):
        return attend_column(triple[0], triple[1], triple[2], bias_all, key_bias, block_rows)

    attended = lax.map(one_column, (qkv_all[0], qkv_all[1], qkv_all[2]))
    attended = jnp.transpose(attended, (1, 0, 2, 3)).reshape(tok_total, col_count, local_width)
    return (gate_val * attended).astype(jnp.bfloat16)


def split_pair_on_device(
    pair_in,
    token_mask,
    positions,
    relpos_table,
    tri_norm_in,
    tri_in_weight,
    tri_in_gate,
    tri_out_gate,
    tri_norm_out,
    tri_out_weight,
    att_norm,
    att_qkv,
    att_gate,
    att_bias,
    att_out,
):
    row_count, col_count, channels = pair_in.shape
    row_first = lax.axis_index("row") * row_count
    col_first = lax.axis_index("col") * col_count
    mask_float = token_mask.astype(jnp.float32)
    row_mask = lax.dynamic_slice_in_dim(mask_float, row_first, row_count)
    col_mask = lax.dynamic_slice_in_dim(mask_float, col_first, col_count)
    row_pos = lax.dynamic_slice_in_dim(positions, row_first, row_count)
    col_pos = lax.dynamic_slice_in_dim(positions, col_first, col_count)
    bin_count = relpos_table.shape[0]
    bin_centre = bin_count // 2
    bucket = jnp.clip(row_pos[:, None] - col_pos[None, :], -bin_centre, bin_centre - 1) + bin_centre
    onehot = (bucket[:, :, None] == jnp.arange(bin_count, dtype=jnp.int32)[None, None, :]).astype(
        jnp.bfloat16
    )
    residual = pair_in.astype(jnp.float32) + jnp.einsum(
        "rjb,bc->rjc", onehot, relpos_table, preferred_element_type=jnp.float32
    )
    normed = layer_norm(residual, tri_norm_in).astype(jnp.bfloat16)
    pair_mask = row_mask[:, None] * col_mask[None, :]
    gate_in = jnp.einsum("rjc,cd->drj", normed, tri_in_gate, preferred_element_type=jnp.float32)
    proj_in = jnp.einsum("rjc,cd->drj", normed, tri_in_weight, preferred_element_type=jnp.float32)
    projected = (jax.nn.sigmoid(gate_in) * proj_in * pair_mask[None, :, :]).astype(jnp.bfloat16)
    left_ch, right_ch = (
        lax.all_to_all(projected[:channels], "row", split_axis=0, concat_axis=1, tiled=True),
        lax.all_to_all(projected[channels:], "row", split_axis=0, concat_axis=1, tiled=True),
    )
    right_rows = lax.all_to_all(right_ch, "col", split_axis=1, concat_axis=2, tiled=True)
    product_sum = jnp.einsum(
        "cik,cjk->cij",
        lax.all_gather(left_ch, "col", axis=2, tiled=True),
        right_rows,
        preferred_element_type=jnp.float32,
    )
    products = product_sum.astype(jnp.bfloat16)
    product_tile = lax.all_to_all(products, "row", split_axis=1, concat_axis=0, tiled=True)
    tri_x = jnp.transpose(product_tile, (1, 2, 0)).astype(jnp.float32)
    normed_out = layer_norm(tri_x, tri_norm_out).astype(jnp.bfloat16)
    out_gate = jax.nn.sigmoid(
        jnp.einsum("rjc,cd->rjd", normed, tri_out_gate, preferred_element_type=jnp.float32)
    )
    residual = residual + out_gate * jnp.einsum(
        "rjc,cd->rjd", normed_out, tri_out_weight, preferred_element_type=jnp.float32
    )
    normed_att = layer_norm(residual, att_norm).astype(jnp.bfloat16)
    bias_piece = jnp.einsum(
        "kic,ch->hik", normed_att, att_bias, preferred_element_type=jnp.float32
    ).astype(jnp.bfloat16)
    key_bias = (mask_float - 1.0) * 1000000000.0
    head_count = att_bias.shape[1]
    head_dim = channels // head_count
    columns = lax.all_to_all(normed_att, "row", split_axis=1, concat_axis=0, tiled=True)
    bias_half = lax.all_gather(bias_piece, "col", axis=1, tiled=True)
    bias_all = lax.all_gather(bias_half, "row", axis=2, tiled=True)
    gated = column_attention(columns, att_qkv, att_gate, bias_all, key_bias, head_count, head_dim)
    gated_tile = lax.all_to_all(gated, "row", split_axis=0, concat_axis=1, tiled=True)
    update = jnp.einsum("rjc,cd->rjd", gated_tile, att_out, preferred_element_type=jnp.float32)
    return (residual + update).astype(jnp.bfloat16)


def on_device(row_dim, col_dim, pair_in, *others):
    rows, cols, width = pair_in.shape
    tokens = row_dim * rows
    whole_bytes = tokens * tokens * width * pair_in.dtype.itemsize
    blocks = row_dim * col_dim
    tiled = cols % 8 == 0 and width % 128 == 0 and blocks & (blocks - 1) == 0
    if whole_bytes <= WHOLE_PAIR_BYTES and tiled:
        return whole_pair_on_device(row_dim, col_dim, pair_in, *others)
    return split_pair_on_device(pair_in, *others)


def solution(mesh):
    return jax.shard_map(
        functools.partial(on_device, mesh.shape["row"], mesh.shape["col"]),
        mesh=mesh,
        in_specs=(P(("groups", "row"), "col", None), P("groups"), P("groups")) + (P(),) * 12,
        out_specs=P(("groups", "row"), "col", None),
        check_vma=False,
    )
```

```python
import functools
import math

import jax
import jax.numpy as jnp
from jax import lax
from jax.experimental import pallas as pl
from jax.experimental.pallas import tpu as pltpu
from jax.sharding import PartitionSpec as P

epsilon = 1e-05

WHOLE_PAIR_BYTES = 256 * 1024
STAGE_FLOPS = 10**9


def layer_norm(values, gain):
    mean_val = jnp.mean(values, axis=-1, keepdims=True)
    centred = values - mean_val
    var_val = jnp.mean(centred * centred, axis=-1, keepdims=True)
    return centred * lax.rsqrt(var_val + epsilon) * gain


def sigmoid(values):
    return 0.5 * jnp.tanh(0.5 * values) + 0.5


def dot(left, right):
    return jnp.dot(left, right, preferred_element_type=jnp.float32)


def dot_t(left, right):
    return lax.dot_general(
        left, right, (((1,), (1,)), ((), ())), preferred_element_type=jnp.float32
    )


def round_bf16(values):
    return values.astype(jnp.bfloat16).astype(jnp.float32)


def stage_kernel(cols, mask_ref, pos_ref, table_ref, rel_ref, pair_mask_ref):
    tokens = pos_ref.shape[0]
    bins = table_ref.shape[0]
    sub = lax.broadcasted_iota(jnp.int32, (cols, bins), 0)
    lane = lax.broadcasted_iota(jnp.int32, (cols, bins), 1)
    hot = [None] * (tokens * tokens // cols)
    for half in range(tokens // cols):
        pos_vec = jnp.zeros((cols, bins), jnp.int32)
        mask_vec = jnp.zeros((cols, bins), jnp.int32)
        for c in range(cols):
            pos_vec = jnp.where(sub == c, pos_ref[half * cols + c], pos_vec)
            mask_vec = jnp.where(sub == c, mask_ref[half * cols + c], mask_vec)
        for i in range(tokens):
            at = i * (tokens // cols) + half
            bucket = jnp.clip(pos_ref[i] - pos_vec, -(bins // 2), bins // 2 - 1) + bins // 2
            hot[at] = (bucket == lane).astype(jnp.float32)
            pair_mask_ref[at * cols : (at + 1) * cols, :] = (mask_vec * mask_ref[i]).astype(jnp.float32)
    hot = jnp.concatenate(hot, axis=0).astype(jnp.bfloat16)
    rel_ref[...] = dot(hot, table_ref[...])


def whole_pair_kernel(row_dim, col_dim, heads, pieces, *refs):
    whole_pair_steps(row_dim, col_dim, heads, refs[:pieces], *refs[pieces:])


def whole_pair_steps(
    row_dim,
    col_dim,
    heads,
    piece_refs,
    mask_ref,
    rel_ref,
    pair_mask_ref,
    norm_in_ref,
    in_weight_ref,
    in_gate_ref,
    out_gate_ref,
    norm_out_ref,
    out_weight_ref,
    att_norm_ref,
    qkv_ref,
    att_gate_ref,
    att_bias_ref,
    att_out_ref,
    out_ref,
    base_ref,
    normed_ref,
    left_ref,
    right_ref,
    att_ref,
    upd_ref,
):
    rows, cols, width = piece_refs[0].shape[1:]
    tokens = row_dim * rows
    head_dim = width // heads
    row_first = lax.axis_index("row") * rows
    col_first = pl.multiple_of(lax.axis_index("col") * cols, cols)
    f32, bf16 = jnp.float32, jnp.bfloat16

    me = lax.axis_index("row") * col_dim + lax.axis_index("col")
    blocks = [piece_ref[at].astype(f32) for piece_ref in piece_refs for at in range(piece_ref.shape[0])]
    for m, block in enumerate(blocks):
        owner = me ^ m
        for r in range(rows):
            first = (owner // col_dim * rows + r) * tokens + owner % col_dim * cols
            base_ref[pl.ds(pl.multiple_of(first, cols), cols), :] = block[r]

    base = base_ref[...] + rel_ref[...]
    base_ref[...] = base

    normed = layer_norm(base, norm_in_ref[...]).astype(bf16)
    normed_ref[...] = normed.astype(f32)
    projected = sigmoid(dot(normed, in_gate_ref[...])) * dot(normed, in_weight_ref[...])
    pair_mask = pair_mask_ref[...]
    left_ref[...] = round_bf16(projected[:, :width] * pair_mask)
    right_ref[...] = round_bf16(projected[:, width:] * pair_mask)

    right_at = [right_ref[pl.ds(col_first * tokens + m, cols, stride=tokens), :] for m in range(tokens)]
    products = []
    for i in range(tokens):
        total = left_ref[pl.ds(i * tokens, 1), :] * right_at[0]
        for m in range(1, tokens):
            total = total + left_ref[pl.ds(i * tokens + m, 1), :] * right_at[m]
        products.append(total)
    extra = [None] * rows
    for m in range(tokens):
        left_at = left_ref[pl.ds(m, tokens, stride=tokens), :]
        for r in range(rows):
            term = left_at * right_ref[pl.ds((row_first + r) * tokens + m, 1), :]
            extra[r] = term if m == 0 else extra[r] + term
    products = round_bf16(jnp.concatenate(products + extra, axis=0))

    def chosen(ref):
        own = [ref[pl.ds(i * tokens + col_first, cols), :] for i in range(tokens)]
        own += [ref[pl.ds(row_first + r, tokens, stride=tokens), :] for r in range(rows)]
        return jnp.concatenate(own, axis=0)

    normed_out = layer_norm(products, norm_out_ref[...]).astype(bf16)
    out_gate = sigmoid(dot(chosen(normed_ref).astype(bf16), out_gate_ref[...]))
    updated = chosen(base_ref) + out_gate * dot(normed_out, out_weight_ref[...])
    normed_att = layer_norm(updated, att_norm_ref[...]).astype(bf16)
    own_pairs = rows * cols
    column_pairs = tokens * cols
    upd_ref[...] = updated[:column_pairs]
    att_f = normed_att.astype(f32)
    att_ref[...] = att_f[:column_pairs]

    own_at = pl.ds(pl.multiple_of(row_first * cols, own_pairs), own_pairs)
    own = att_ref[own_at, :].astype(bf16)
    column = normed_att[:column_pairs]
    queries = dot(own, qkv_ref[:, :width])
    keys = dot(column, qkv_ref[:, width : 2 * width]).astype(bf16)
    values = dot(column, qkv_ref[:, 2 * width :]).astype(bf16)
    own_gate = sigmoid(dot(own, att_gate_ref[...]))

    bias = []
    for r in range(rows):
        part = att_f[column_pairs + r * tokens : column_pairs + (r + 1) * tokens]
        spread = jnp.concatenate(
            [jnp.broadcast_to(part[k : k + 1], (cols, width)) for k in range(tokens)], axis=0
        )
        bias.append(round_bf16(dot_t(att_bias_ref[...], spread.astype(bf16))))

    head_of = lax.broadcasted_iota(jnp.int32, (own_pairs, width), 1) // head_dim
    queries = round_bf16(queries)
    by_head = jnp.concatenate(
        [jnp.where(head_of == h, queries, 0.0) for h in range(heads)], axis=0
    ).astype(bf16)
    scores = dot_t(by_head, keys) * (1.0 / math.sqrt(head_dim))
    biases = jnp.concatenate(
        [jnp.broadcast_to(bias[r][h : h + 1], (cols, column_pairs)) for h in range(heads) for r in range(rows)],
        axis=0,
    )
    lane_row = lax.broadcasted_iota(jnp.int32, (1, column_pairs), 1)
    key_mask = jnp.zeros((1, column_pairs), jnp.int32)
    for k in range(tokens):
        key_mask = jnp.where(lane_row // cols == k, mask_ref[k], key_mask)
    key_bias = (key_mask.astype(f32) - 1.0) * 1000000000.0
    scores = scores + biases + key_bias
    same = (
        lax.broadcasted_iota(jnp.int32, scores.shape, 1) % cols
        == lax.broadcasted_iota(jnp.int32, scores.shape, 0) % cols
    )
    scores = jnp.where(same, scores, -jnp.inf)
    expo = jnp.exp(scores - jnp.max(scores, axis=-1, keepdims=True))
    totals = jnp.sum(expo, axis=-1, keepdims=True)
    mixed = dot(expo.astype(bf16), values) / totals
    attended = jnp.zeros((own_pairs, width), f32)
    for h in range(heads):
        attended = jnp.where(head_of == h, mixed[h * own_pairs : (h + 1) * own_pairs], attended)

    gated = (own_gate * attended).astype(bf16)
    result = upd_ref[own_at, :] + dot(gated, att_out_ref[...])
    out_ref[...] = result.reshape(rows, cols, width).astype(bf16)


def whole_pair_on_device(
    row_dim,
    col_dim,
    pair_in,
    token_mask,
    positions,
    relpos_table,
    tri_norm_in,
    tri_in_weight,
    tri_in_gate,
    tri_out_gate,
    tri_norm_out,
    tri_out_weight,
    att_norm,
    att_qkv,
    att_gate,
    att_bias,
    att_out,
):
    rows, cols, width = pair_in.shape
    tokens = row_dim * rows
    heads = att_bias.shape[1]
    blocks = row_dim * col_dim
    pair = [pair_in[None]]
    step = 1
    while step < blocks:
        partners = [(device, device ^ step) for device in range(blocks)]
        held = jnp.concatenate(pair, axis=0)
        pair.append(lax.ppermute(held, ("row", "col"), partners))
        step *= 2

    vmem = pl.BlockSpec(memory_space=pltpu.VMEM)
    smem = pl.BlockSpec(memory_space=pltpu.SMEM)
    weights = (
        tri_norm_in.reshape(1, width),
        tri_in_weight,
        tri_in_gate,
        tri_out_gate,
        tri_norm_out.reshape(1, width),
        tri_out_weight,
        att_norm.reshape(1, width),
        att_qkv,
        att_gate,
        att_bias.T,
        att_out,
    )
    wide = pltpu.VMEM((tokens * tokens, width), jnp.float32)
    column = pltpu.VMEM((tokens * cols, width), jnp.float32)
    params = pltpu.CompilerParams(vmem_limit_bytes=16 * 1024 * 1024)
    wide_out = jax.ShapeDtypeStruct((tokens * tokens, width), jnp.float32)
    rel, pair_mask = pl.pallas_call(
        functools.partial(stage_kernel, cols),
        out_shape=[wide_out] * 2,
        in_specs=[smem] * 2 + [vmem],
        out_specs=[vmem] * 2,
        compiler_params=params,
        cost_estimate=pl.CostEstimate(flops=STAGE_FLOPS, bytes_accessed=2**20, transcendentals=0),
    )(token_mask, positions, relpos_table)
    return pl.pallas_call(
        functools.partial(whole_pair_kernel, row_dim, col_dim, heads, len(pair)),
        out_shape=jax.ShapeDtypeStruct(pair_in.shape, pair_in.dtype),
        in_specs=[vmem] * len(pair) + [smem] + [vmem] * (2 + len(weights)),
        out_specs=vmem,
        scratch_shapes=[wide] * 4 + [column] * 2,
        compiler_params=params,
    )(*pair, token_mask, rel, pair_mask, *weights)


def attend_column(query_col, key_col, value_col, bias_all, key_bias, block_rows):
    tok_total = query_col.shape[0]
    scale = 1.0 / math.sqrt(query_col.shape[2])

    def one_block(block_idx):
        scores = (
            jnp.einsum("ihe,khe->hik", query_col, key_col, preferred_element_type=jnp.float32)
            * scale
        )
        scores = scores + bias_all.astype(jnp.float32) + key_bias[None, None, :]
        row_max = jnp.max(scores, axis=-1, keepdims=True)
        expo_f = jnp.exp(scores - row_max)
        totals = jnp.sum(expo_f, axis=-1)
        weights = expo_f.astype(jnp.bfloat16)
        result = jnp.einsum("hik,khe->ihe", weights, value_col, preferred_element_type=jnp.float32)
        return result / jnp.transpose(totals)[:, :, None]

    blocks = lax.map(one_block, jnp.arange(tok_total // block_rows))
    return blocks.reshape(tok_total, query_col.shape[1], query_col.shape[2])


def column_attention(columns, att_qkv, att_gate, bias_all, key_bias, head_local, head_dim):
    tok_total, col_count, channels = columns.shape
    local_width = head_local * head_dim
    weight_three = att_qkv.reshape(channels, 3, channels)
    qkv_all = jnp.einsum(
        "kmc,ctd->tmkd", columns, weight_three, preferred_element_type=jnp.float32
    ).astype(jnp.bfloat16)
    qkv_all = qkv_all.reshape(3, col_count, tok_total, head_local, head_dim)
    gate_val = jax.nn.sigmoid(
        jnp.einsum("kmc,cd->kmd", columns, att_gate, preferred_element_type=jnp.float32)
    )
    block_rows = min(1024, tok_total)

    def one_column(triple):
        return attend_column(triple[0], triple[1], triple[2], bias_all, key_bias, block_rows)

    attended = lax.map(one_column, (qkv_all[0], qkv_all[1], qkv_all[2]))
    attended = jnp.transpose(attended, (1, 0, 2, 3)).reshape(tok_total, col_count, local_width)
    return (gate_val * attended).astype(jnp.bfloat16)


def split_pair_on_device(
    pair_in,
    token_mask,
    positions,
    relpos_table,
    tri_norm_in,
    tri_in_weight,
    tri_in_gate,
    tri_out_gate,
    tri_norm_out,
    tri_out_weight,
    att_norm,
    att_qkv,
    att_gate,
    att_bias,
    att_out,
):
    row_count, col_count, channels = pair_in.shape
    row_first = lax.axis_index("row") * row_count
    col_first = lax.axis_index("col") * col_count
    mask_float = token_mask.astype(jnp.float32)
    row_mask = lax.dynamic_slice_in_dim(mask_float, row_first, row_count)
    col_mask = lax.dynamic_slice_in_dim(mask_float, col_first, col_count)
    row_pos = lax.dynamic_slice_in_dim(positions, row_first, row_count)
    col_pos = lax.dynamic_slice_in_dim(positions, col_first, col_count)
    bin_count = relpos_table.shape[0]
    bin_centre = bin_count // 2
    bucket = jnp.clip(row_pos[:, None] - col_pos[None, :], -bin_centre, bin_centre - 1) + bin_centre
    onehot = (bucket[:, :, None] == jnp.arange(bin_count, dtype=jnp.int32)[None, None, :]).astype(
        jnp.bfloat16
    )
    residual = pair_in.astype(jnp.float32) + jnp.einsum(
        "rjb,bc->rjc", onehot, relpos_table, preferred_element_type=jnp.float32
    )
    normed = layer_norm(residual, tri_norm_in).astype(jnp.bfloat16)
    pair_mask = row_mask[:, None] * col_mask[None, :]
    gate_in = jnp.einsum("rjc,cd->drj", normed, tri_in_gate, preferred_element_type=jnp.float32)
    proj_in = jnp.einsum("rjc,cd->drj", normed, tri_in_weight, preferred_element_type=jnp.float32)
    projected = (jax.nn.sigmoid(gate_in) * proj_in * pair_mask[None, :, :]).astype(jnp.bfloat16)
    left_ch, right_ch = (
        lax.all_to_all(projected[:channels], "row", split_axis=0, concat_axis=1, tiled=True),
        lax.all_to_all(projected[channels:], "row", split_axis=0, concat_axis=1, tiled=True),
    )
    right_rows = lax.all_to_all(right_ch, "col", split_axis=1, concat_axis=2, tiled=True)
    product_sum = jnp.einsum(
        "cik,cjk->cij",
        lax.all_gather(left_ch, "col", axis=2, tiled=True),
        right_rows,
        preferred_element_type=jnp.float32,
    )
    products = product_sum.astype(jnp.bfloat16)
    product_tile = lax.all_to_all(products, "row", split_axis=1, concat_axis=0, tiled=True)
    tri_x = jnp.transpose(product_tile, (1, 2, 0)).astype(jnp.float32)
    normed_out = layer_norm(tri_x, tri_norm_out).astype(jnp.bfloat16)
    out_gate = jax.nn.sigmoid(
        jnp.einsum("rjc,cd->rjd", normed, tri_out_gate, preferred_element_type=jnp.float32)
    )
    residual = residual + out_gate * jnp.einsum(
        "rjc,cd->rjd", normed_out, tri_out_weight, preferred_element_type=jnp.float32
    )
    normed_att = layer_norm(residual, att_norm).astype(jnp.bfloat16)
    bias_piece = jnp.einsum(
        "kic,ch->hik", normed_att, att_bias, preferred_element_type=jnp.float32
    ).astype(jnp.bfloat16)
    key_bias = (mask_float - 1.0) * 1000000000.0
    head_count = att_bias.shape[1]
    head_dim = channels // head_count
    columns = lax.all_to_all(normed_att, "row", split_axis=1, concat_axis=0, tiled=True)
    bias_half = lax.all_gather(bias_piece, "col", axis=1, tiled=True)
    bias_all = lax.all_gather(bias_half, "row", axis=2, tiled=True)
    gated = column_attention(columns, att_qkv, att_gate, bias_all, key_bias, head_count, head_dim)
    gated_tile = lax.all_to_all(gated, "row", split_axis=0, concat_axis=1, tiled=True)
    update = jnp.einsum("rjc,cd->rjd", gated_tile, att_out, preferred_element_type=jnp.float32)
    return (residual + update).astype(jnp.bfloat16)


def on_device(row_dim, col_dim, pair_in, *others):
    rows, cols, width = pair_in.shape
    tokens = row_dim * rows
    whole_bytes = tokens * tokens * width * pair_in.dtype.itemsize
    blocks = row_dim * col_dim
    tiled = cols % 8 == 0 and width % 128 == 0 and blocks & (blocks - 1) == 0
    if whole_bytes <= WHOLE_PAIR_BYTES and tiled:
        return whole_pair_on_device(row_dim, col_dim, pair_in, *others)
    return split_pair_on_device(pair_in, *others)


def solution(mesh):
    return jax.shard_map(
        functools.partial(on_device, mesh.shape["row"], mesh.shape["col"]),
        mesh=mesh,
        in_specs=(P(("groups", "row"), "col", None), P("groups"), P("groups")) + (P(),) * 12,
        out_specs=P(("groups", "row"), "col", None),
        check_vma=False,
    )
```

```python
import functools
import math

import jax
import jax.numpy as jnp
from jax import lax
from jax.experimental import pallas as pl
from jax.experimental.pallas import tpu as pltpu
from jax.sharding import PartitionSpec as P

epsilon = 1e-05

WHOLE_PAIR_BYTES = 256 * 1024
STAGE_FLOPS = 10**9


def layer_norm(values, gain):
    mean_val = jnp.mean(values, axis=-1, keepdims=True)
    centred = values - mean_val
    var_val = jnp.mean(centred * centred, axis=-1, keepdims=True)
    return centred * lax.rsqrt(var_val + epsilon) * gain


def sigmoid(values):
    return 0.5 * jnp.tanh(0.5 * values) + 0.5


def dot(left, right):
    return jnp.dot(left, right, preferred_element_type=jnp.float32)


def dot_t(left, right):
    return lax.dot_general(
        left, right, (((1,), (1,)), ((), ())), preferred_element_type=jnp.float32
    )


def round_bf16(values):
    return values.astype(jnp.bfloat16).astype(jnp.float32)


def stage_kernel(hubs, mask_ref, pos_ref, chip_ref, table_ref, held_ref, rel_ref, pair_mask_ref):
    cols = chip_ref.shape[2]
    row, col = lax.axis_index("row"), lax.axis_index("col")
    is_hub = (col == 1) & ((row == hubs[0]) | (row == hubs[1]))
    held_ref[...] = jnp.where(is_hub, chip_ref[...].astype(jnp.float32), 0.0).astype(held_ref.dtype)
    tokens = pos_ref.shape[0]
    bins = table_ref.shape[0]
    sub = lax.broadcasted_iota(jnp.int32, (cols, bins), 0)
    lane = lax.broadcasted_iota(jnp.int32, (cols, bins), 1)
    hot = [None] * (tokens * tokens // cols)
    for half in range(tokens // cols):
        pos_vec = jnp.zeros((cols, bins), jnp.int32)
        mask_vec = jnp.zeros((cols, bins), jnp.int32)
        for c in range(cols):
            pos_vec = jnp.where(sub == c, pos_ref[half * cols + c], pos_vec)
            mask_vec = jnp.where(sub == c, mask_ref[half * cols + c], mask_vec)
        for i in range(tokens):
            at = i * (tokens // cols) + half
            bucket = jnp.clip(pos_ref[i] - pos_vec, -(bins // 2), bins // 2 - 1) + bins // 2
            hot[at] = (bucket == lane).astype(jnp.float32)
            pair_mask_ref[at * cols : (at + 1) * cols, :] = (mask_vec * mask_ref[i]).astype(jnp.float32)
    hot = jnp.concatenate(hot, axis=0).astype(jnp.bfloat16)
    rel_ref[...] = dot(hot, table_ref[...])


def whole_pair_kernel(
    row_dim,
    heads,
    near_ref,
    far_ref,
    near_sent_ref,
    far_sent_ref,
    mask_ref,
    rel_ref,
    pair_mask_ref,
    norm_in_ref,
    in_weight_ref,
    in_gate_ref,
    out_gate_ref,
    norm_out_ref,
    out_weight_ref,
    att_norm_ref,
    qkv_ref,
    att_gate_ref,
    att_bias_ref,
    att_out_ref,
    out_ref,
    base_ref,
    normed_ref,
    left_ref,
    right_ref,
    att_ref,
    upd_ref,
):
    rows, cols, width = near_ref.shape[1:]
    tokens = row_dim * rows
    head_dim = width // heads
    row_first = lax.axis_index("row") * rows
    col_first = pl.multiple_of(lax.axis_index("col") * cols, cols)
    f32, bf16 = jnp.float32, jnp.bfloat16

    odd = lax.axis_index("col") == 1
    first_half = lax.axis_index("row") < row_dim // 2
    col_dim = 2
    for here, sent, counts_up in (
        (near_ref, near_sent_ref, first_half),
        (far_ref, far_sent_ref, jnp.logical_not(first_half)),
    ):
        for at in range(near_ref.shape[0]):
            q, half = at // col_dim, at % col_dim
            owner = jnp.where(counts_up, q, row_dim - 1 - q)
            block = jnp.where(odd, here[at].astype(f32), sent[at].astype(f32))
            for r in range(rows):
                first = (owner * rows + r) * tokens + half * cols
                base_ref[pl.ds(pl.multiple_of(first, cols), cols), :] = block[r]

    base = base_ref[...] + rel_ref[...]
    base_ref[...] = base

    normed = layer_norm(base, norm_in_ref[...]).astype(bf16)
    normed_ref[...] = normed.astype(f32)
    projected = sigmoid(dot(normed, in_gate_ref[...])) * dot(normed, in_weight_ref[...])
    pair_mask = pair_mask_ref[...]
    left_ref[...] = round_bf16(projected[:, :width] * pair_mask)
    right_ref[...] = round_bf16(projected[:, width:] * pair_mask)

    right_at = [right_ref[pl.ds(col_first * tokens + m, cols, stride=tokens), :] for m in range(tokens)]
    products = []
    for i in range(tokens):
        total = left_ref[pl.ds(i * tokens, 1), :] * right_at[0]
        for m in range(1, tokens):
            total = total + left_ref[pl.ds(i * tokens + m, 1), :] * right_at[m]
        products.append(total)
    extra = [None] * rows
    for m in range(tokens):
        left_at = left_ref[pl.ds(m, tokens, stride=tokens), :]
        for r in range(rows):
            term = left_at * right_ref[pl.ds((row_first + r) * tokens + m, 1), :]
            extra[r] = term if m == 0 else extra[r] + term
    products = round_bf16(jnp.concatenate(products + extra, axis=0))

    def chosen(ref):
        own = [ref[pl.ds(i * tokens + col_first, cols), :] for i in range(tokens)]
        own += [ref[pl.ds(row_first + r, tokens, stride=tokens), :] for r in range(rows)]
        return jnp.concatenate(own, axis=0)

    normed_out = layer_norm(products, norm_out_ref[...]).astype(bf16)
    out_gate = sigmoid(dot(chosen(normed_ref).astype(bf16), out_gate_ref[...]))
    updated = chosen(base_ref) + out_gate * dot(normed_out, out_weight_ref[...])
    normed_att = layer_norm(updated, att_norm_ref[...]).astype(bf16)
    own_pairs = rows * cols
    column_pairs = tokens * cols
    upd_ref[...] = updated[:column_pairs]
    att_f = normed_att.astype(f32)
    att_ref[...] = att_f[:column_pairs]

    own_at = pl.ds(pl.multiple_of(row_first * cols, own_pairs), own_pairs)
    own = att_ref[own_at, :].astype(bf16)
    column = normed_att[:column_pairs]
    queries = dot(own, qkv_ref[:, :width])
    keys = dot(column, qkv_ref[:, width : 2 * width]).astype(bf16)
    values = dot(column, qkv_ref[:, 2 * width :]).astype(bf16)
    own_gate = sigmoid(dot(own, att_gate_ref[...]))

    bias = []
    for r in range(rows):
        part = att_f[column_pairs + r * tokens : column_pairs + (r + 1) * tokens]
        spread = jnp.concatenate(
            [jnp.broadcast_to(part[k : k + 1], (cols, width)) for k in range(tokens)], axis=0
        )
        bias.append(round_bf16(dot_t(att_bias_ref[...], spread.astype(bf16))))

    head_of = lax.broadcasted_iota(jnp.int32, (own_pairs, width), 1) // head_dim
    queries = round_bf16(queries)
    by_head = jnp.concatenate(
        [jnp.where(head_of == h, queries, 0.0) for h in range(heads)], axis=0
    ).astype(bf16)
    scores = dot_t(by_head, keys) * (1.0 / math.sqrt(head_dim))
    biases = jnp.concatenate(
        [jnp.broadcast_to(bias[r][h : h + 1], (cols, column_pairs)) for h in range(heads) for r in range(rows)],
        axis=0,
    )
    lane_row = lax.broadcasted_iota(jnp.int32, (1, column_pairs), 1)
    key_mask = jnp.zeros((1, column_pairs), jnp.int32)
    for k in range(tokens):
        key_mask = jnp.where(lane_row // cols == k, mask_ref[k], key_mask)
    key_bias = (key_mask.astype(f32) - 1.0) * 1000000000.0
    scores = scores + biases + key_bias
    same = (
        lax.broadcasted_iota(jnp.int32, scores.shape, 1) % cols
        == lax.broadcasted_iota(jnp.int32, scores.shape, 0) % cols
    )
    scores = jnp.where(same, scores, -jnp.inf)
    expo = jnp.exp(scores - jnp.max(scores, axis=-1, keepdims=True))
    totals = jnp.sum(expo, axis=-1, keepdims=True)
    mixed = dot(expo.astype(bf16), values) / totals
    attended = jnp.zeros((own_pairs, width), f32)
    for h in range(heads):
        attended = jnp.where(head_of == h, mixed[h * own_pairs : (h + 1) * own_pairs], attended)

    gated = (own_gate * attended).astype(bf16)
    result = upd_ref[own_at, :] + dot(gated, att_out_ref[...])
    out_ref[...] = result.reshape(rows, cols, width).astype(bf16)


def whole_pair_on_device(
    row_dim,
    pair_in,
    token_mask,
    positions,
    relpos_table,
    tri_norm_in,
    tri_in_weight,
    tri_in_gate,
    tri_out_gate,
    tri_norm_out,
    tri_out_weight,
    att_norm,
    att_qkv,
    att_gate,
    att_bias,
    att_out,
):
    rows, cols, width = pair_in.shape
    tokens = row_dim * rows
    heads = att_bias.shape[1]
    def move(values, pairs):
        ids = [(src[0] * 2 + src[1], dst[0] * 2 + dst[1]) for src, dst in pairs]
        return lax.ppermute(values, ("row", "col"), ids)

    last, count = row_dim - 1, row_dim // 2
    hub = count // 2
    hubs = (hub, last - hub)
    hub_devices = [(row, 1) for row in hubs]
    everywhere = range(row_dim)
    even = move(pair_in[None], [((row, 0), (row, 1)) for row in everywhere])
    chip = jnp.concatenate([even, pair_in[None]], axis=0)
    at_hub = {
        q: move(chip, [((q, 1), hub_devices[0]), ((last - q, 1), hub_devices[1])])
        for q in range(count)
        if q != hub
    }

    vmem = pl.BlockSpec(memory_space=pltpu.VMEM)
    smem = pl.BlockSpec(memory_space=pltpu.SMEM)
    weights = (
        tri_norm_in.reshape(1, width),
        tri_in_weight,
        tri_in_gate,
        tri_out_gate,
        tri_norm_out.reshape(1, width),
        tri_out_weight,
        att_norm.reshape(1, width),
        att_qkv,
        att_gate,
        att_bias.T,
        att_out,
    )
    wide = pltpu.VMEM((tokens * tokens, width), jnp.float32)
    column = pltpu.VMEM((tokens * cols, width), jnp.float32)
    params = pltpu.CompilerParams(vmem_limit_bytes=16 * 1024 * 1024)
    wide_out = jax.ShapeDtypeStruct((tokens * tokens, width), jnp.float32)
    held, rel, pair_mask = pl.pallas_call(
        functools.partial(stage_kernel, hubs),
        out_shape=[jax.ShapeDtypeStruct(chip.shape, chip.dtype)] + [wide_out] * 2,
        in_specs=[smem] * 2 + [vmem] * 2,
        out_specs=[vmem] * 3,
        compiler_params=params,
        cost_estimate=pl.CostEstimate(flops=STAGE_FLOPS, bytes_accessed=2**20, transcendentals=0),
    )(token_mask, positions, chip, relpos_table)

    side = jnp.concatenate([held if q == hub else at_hub[q] for q in range(count)], axis=0)
    others = [q for q in range(count) if q != hub]
    near, far = side, None
    for q in others:
        near = near + move(side, [(hub_devices[0], (q, 1)), (hub_devices[1], (last - q, 1))])
    for q in others + [hub]:
        part = move(side, [(hub_devices[0], (last - q, 1)), (hub_devices[1], (q, 1))])
        far = part if far is None else far + part
    to_even = [((row, 1), (row, 0)) for row in everywhere]
    pair = (near, far, move(near, to_even), move(far, to_even))
    return pl.pallas_call(
        functools.partial(whole_pair_kernel, row_dim, heads),
        out_shape=jax.ShapeDtypeStruct(pair_in.shape, pair_in.dtype),
        in_specs=[vmem] * len(pair) + [smem] + [vmem] * (2 + len(weights)),
        out_specs=vmem,
        scratch_shapes=[wide] * 4 + [column] * 2,
        compiler_params=params,
    )(*pair, token_mask, rel, pair_mask, *weights)


def attend_column(query_col, key_col, value_col, bias_all, key_bias, block_rows):
    tok_total = query_col.shape[0]
    scale = 1.0 / math.sqrt(query_col.shape[2])

    def one_block(block_idx):
        scores = (
            jnp.einsum("ihe,khe->hik", query_col, key_col, preferred_element_type=jnp.float32)
            * scale
        )
        scores = scores + bias_all.astype(jnp.float32) + key_bias[None, None, :]
        row_max = jnp.max(scores, axis=-1, keepdims=True)
        expo_f = jnp.exp(scores - row_max)
        totals = jnp.sum(expo_f, axis=-1)
        weights = expo_f.astype(jnp.bfloat16)
        result = jnp.einsum("hik,khe->ihe", weights, value_col, preferred_element_type=jnp.float32)
        return result / jnp.transpose(totals)[:, :, None]

    blocks = lax.map(one_block, jnp.arange(tok_total // block_rows))
    return blocks.reshape(tok_total, query_col.shape[1], query_col.shape[2])


def column_attention(columns, att_qkv, att_gate, bias_all, key_bias, head_local, head_dim):
    tok_total, col_count, channels = columns.shape
    local_width = head_local * head_dim
    weight_three = att_qkv.reshape(channels, 3, channels)
    qkv_all = jnp.einsum(
        "kmc,ctd->tmkd", columns, weight_three, preferred_element_type=jnp.float32
    ).astype(jnp.bfloat16)
    qkv_all = qkv_all.reshape(3, col_count, tok_total, head_local, head_dim)
    gate_val = jax.nn.sigmoid(
        jnp.einsum("kmc,cd->kmd", columns, att_gate, preferred_element_type=jnp.float32)
    )
    block_rows = min(1024, tok_total)

    def one_column(triple):
        return attend_column(triple[0], triple[1], triple[2], bias_all, key_bias, block_rows)

    attended = lax.map(one_column, (qkv_all[0], qkv_all[1], qkv_all[2]))
    attended = jnp.transpose(attended, (1, 0, 2, 3)).reshape(tok_total, col_count, local_width)
    return (gate_val * attended).astype(jnp.bfloat16)


def split_pair_on_device(
    pair_in,
    token_mask,
    positions,
    relpos_table,
    tri_norm_in,
    tri_in_weight,
    tri_in_gate,
    tri_out_gate,
    tri_norm_out,
    tri_out_weight,
    att_norm,
    att_qkv,
    att_gate,
    att_bias,
    att_out,
):
    row_count, col_count, channels = pair_in.shape
    row_first = lax.axis_index("row") * row_count
    col_first = lax.axis_index("col") * col_count
    mask_float = token_mask.astype(jnp.float32)
    row_mask = lax.dynamic_slice_in_dim(mask_float, row_first, row_count)
    col_mask = lax.dynamic_slice_in_dim(mask_float, col_first, col_count)
    row_pos = lax.dynamic_slice_in_dim(positions, row_first, row_count)
    col_pos = lax.dynamic_slice_in_dim(positions, col_first, col_count)
    bin_count = relpos_table.shape[0]
    bin_centre = bin_count // 2
    bucket = jnp.clip(row_pos[:, None] - col_pos[None, :], -bin_centre, bin_centre - 1) + bin_centre
    onehot = (bucket[:, :, None] == jnp.arange(bin_count, dtype=jnp.int32)[None, None, :]).astype(
        jnp.bfloat16
    )
    residual = pair_in.astype(jnp.float32) + jnp.einsum(
        "rjb,bc->rjc", onehot, relpos_table, preferred_element_type=jnp.float32
    )
    normed = layer_norm(residual, tri_norm_in).astype(jnp.bfloat16)
    pair_mask = row_mask[:, None] * col_mask[None, :]
    gate_in = jnp.einsum("rjc,cd->drj", normed, tri_in_gate, preferred_element_type=jnp.float32)
    proj_in = jnp.einsum("rjc,cd->drj", normed, tri_in_weight, preferred_element_type=jnp.float32)
    projected = (jax.nn.sigmoid(gate_in) * proj_in * pair_mask[None, :, :]).astype(jnp.bfloat16)
    left_ch, right_ch = (
        lax.all_to_all(projected[:channels], "row", split_axis=0, concat_axis=1, tiled=True),
        lax.all_to_all(projected[channels:], "row", split_axis=0, concat_axis=1, tiled=True),
    )
    right_rows = lax.all_to_all(right_ch, "col", split_axis=1, concat_axis=2, tiled=True)
    product_sum = jnp.einsum(
        "cik,cjk->cij",
        lax.all_gather(left_ch, "col", axis=2, tiled=True),
        right_rows,
        preferred_element_type=jnp.float32,
    )
    products = product_sum.astype(jnp.bfloat16)
    product_tile = lax.all_to_all(products, "row", split_axis=1, concat_axis=0, tiled=True)
    tri_x = jnp.transpose(product_tile, (1, 2, 0)).astype(jnp.float32)
    normed_out = layer_norm(tri_x, tri_norm_out).astype(jnp.bfloat16)
    out_gate = jax.nn.sigmoid(
        jnp.einsum("rjc,cd->rjd", normed, tri_out_gate, preferred_element_type=jnp.float32)
    )
    residual = residual + out_gate * jnp.einsum(
        "rjc,cd->rjd", normed_out, tri_out_weight, preferred_element_type=jnp.float32
    )
    normed_att = layer_norm(residual, att_norm).astype(jnp.bfloat16)
    bias_piece = jnp.einsum(
        "kic,ch->hik", normed_att, att_bias, preferred_element_type=jnp.float32
    ).astype(jnp.bfloat16)
    key_bias = (mask_float - 1.0) * 1000000000.0
    head_count = att_bias.shape[1]
    head_dim = channels // head_count
    columns = lax.all_to_all(normed_att, "row", split_axis=1, concat_axis=0, tiled=True)
    bias_half = lax.all_gather(bias_piece, "col", axis=1, tiled=True)
    bias_all = lax.all_gather(bias_half, "row", axis=2, tiled=True)
    gated = column_attention(columns, att_qkv, att_gate, bias_all, key_bias, head_count, head_dim)
    gated_tile = lax.all_to_all(gated, "row", split_axis=0, concat_axis=1, tiled=True)
    update = jnp.einsum("rjc,cd->rjd", gated_tile, att_out, preferred_element_type=jnp.float32)
    return (residual + update).astype(jnp.bfloat16)


def on_device(row_dim, col_dim, pair_in, *others):
    rows, cols, width = pair_in.shape
    tokens = row_dim * rows
    whole_bytes = tokens * tokens * width * pair_in.dtype.itemsize
    tiled = cols % 8 == 0 and width % 128 == 0 and row_dim % 4 == 0 and col_dim == 2
    if whole_bytes <= WHOLE_PAIR_BYTES and tiled:
        return whole_pair_on_device(row_dim, pair_in, *others)
    return split_pair_on_device(pair_in, *others)


def solution(mesh):
    return jax.shard_map(
        functools.partial(on_device, mesh.shape["row"], mesh.shape["col"]),
        mesh=mesh,
        in_specs=(P(("groups", "row"), "col", None), P("groups"), P("groups")) + (P(),) * 12,
        out_specs=P(("groups", "row"), "col", None),
        check_vma=False,
    )
```

```python
import functools
import math

import jax
import jax.numpy as jnp
from jax import lax
from jax.experimental import pallas as pl
from jax.experimental.pallas import tpu as pltpu
from jax.sharding import PartitionSpec as P

epsilon = 1e-05

WHOLE_PAIR_BYTES = 256 * 1024
STAGE_FLOPS = 10**9


def layer_norm(values, gain):
    mean_val = jnp.mean(values, axis=-1, keepdims=True)
    centred = values - mean_val
    var_val = jnp.mean(centred * centred, axis=-1, keepdims=True)
    return centred * lax.rsqrt(var_val + epsilon) * gain


def sigmoid(values):
    return 0.5 * jnp.tanh(0.5 * values) + 0.5


def dot(left, right):
    return jnp.dot(left, right, preferred_element_type=jnp.float32)


def dot_t(left, right):
    return lax.dot_general(
        left, right, (((1,), (1,)), ((), ())), preferred_element_type=jnp.float32
    )


def round_bf16(values):
    return values.astype(jnp.bfloat16).astype(jnp.float32)


def own_kernel(pair_ref, chip_ref):
    chip_ref[0] = pair_ref[...]


def stage_kernel(
    cols,
    mask_ref,
    pos_ref,
    table_ref,
    norm_in_ref,
    norm_out_ref,
    att_norm_ref,
    att_bias_ref,
    rel_ref,
    pair_mask_ref,
    gains_ref,
    bias_ref,
):
    gains_ref[0:1] = norm_in_ref[...]
    gains_ref[1:2] = norm_out_ref[...]
    gains_ref[2:3] = att_norm_ref[...]
    bias_ref[...] = att_bias_ref[...]
    tokens = pos_ref.shape[0]
    bins = table_ref.shape[0]
    sub = lax.broadcasted_iota(jnp.int32, (cols, bins), 0)
    lane = lax.broadcasted_iota(jnp.int32, (cols, bins), 1)
    hot = [None] * (tokens * tokens // cols)
    for half in range(tokens // cols):
        pos_vec = jnp.zeros((cols, bins), jnp.int32)
        mask_vec = jnp.zeros((cols, bins), jnp.int32)
        for c in range(cols):
            pos_vec = jnp.where(sub == c, pos_ref[half * cols + c], pos_vec)
            mask_vec = jnp.where(sub == c, mask_ref[half * cols + c], mask_vec)
        for i in range(tokens):
            at = i * (tokens // cols) + half
            bucket = jnp.clip(pos_ref[i] - pos_vec, -(bins // 2), bins // 2 - 1) + bins // 2
            hot[at] = (bucket == lane).astype(jnp.float32)
            pair_mask_ref[at * cols : (at + 1) * cols, :] = (mask_vec * mask_ref[i]).astype(jnp.float32)
    hot = jnp.concatenate(hot, axis=0).astype(jnp.bfloat16)
    rel_ref[...] = dot(hot, table_ref[...])


def whole_pair_kernel(
    row_dim,
    heads,
    held_ref,
    last_ref,
    held_sent_ref,
    last_sent_ref,
    mask_ref,
    rel_ref,
    pair_mask_ref,
    gains_ref,
    att_bias_ref,
    in_weight_ref,
    in_gate_ref,
    out_gate_ref,
    out_weight_ref,
    qkv_ref,
    att_gate_ref,
    att_out_ref,
    out_ref,
    base_ref,
    normed_ref,
    left_ref,
    right_ref,
    att_ref,
    upd_ref,
):
    rows, cols, width = held_ref.shape[1:]
    tokens = row_dim * rows
    head_dim = width // heads
    row_first = lax.axis_index("row") * rows
    col_first = pl.multiple_of(lax.axis_index("col") * cols, cols)
    f32, bf16 = jnp.float32, jnp.bfloat16

    is_odd = lax.axis_index("col") == 1
    odd = lax.axis_index("row") * 2 + 1
    for m in range(2 * row_dim):
        here, sent = ((held_ref, held_sent_ref), (last_ref, last_sent_ref))[m // row_dim]
        owner = odd ^ m
        block = jnp.where(is_odd, here[m % row_dim].astype(f32), sent[m % row_dim].astype(f32))
        for r in range(rows):
            first = (owner // 2 * rows + r) * tokens + owner % 2 * cols
            base_ref[pl.ds(pl.multiple_of(first, cols), cols), :] = block[r]

    base = base_ref[...] + rel_ref[...]
    base_ref[...] = base

    normed = layer_norm(base, gains_ref[0:1]).astype(bf16)
    normed_ref[...] = normed.astype(f32)
    projected = sigmoid(dot(normed, in_gate_ref[...])) * dot(normed, in_weight_ref[...])
    pair_mask = pair_mask_ref[...]
    left_ref[...] = round_bf16(projected[:, :width] * pair_mask)
    right_ref[...] = round_bf16(projected[:, width:] * pair_mask)

    right_at = [right_ref[pl.ds(col_first * tokens + m, cols, stride=tokens), :] for m in range(tokens)]
    products = []
    for i in range(tokens):
        total = left_ref[pl.ds(i * tokens, 1), :] * right_at[0]
        for m in range(1, tokens):
            total = total + left_ref[pl.ds(i * tokens + m, 1), :] * right_at[m]
        products.append(total)
    extra = [None] * rows
    for m in range(tokens):
        left_at = left_ref[pl.ds(m, tokens, stride=tokens), :]
        for r in range(rows):
            term = left_at * right_ref[pl.ds((row_first + r) * tokens + m, 1), :]
            extra[r] = term if m == 0 else extra[r] + term
    products = round_bf16(jnp.concatenate(products + extra, axis=0))

    def chosen(ref):
        own = [ref[pl.ds(i * tokens + col_first, cols), :] for i in range(tokens)]
        own += [ref[pl.ds(row_first + r, tokens, stride=tokens), :] for r in range(rows)]
        return jnp.concatenate(own, axis=0)

    normed_out = layer_norm(products, gains_ref[1:2]).astype(bf16)
    out_gate = sigmoid(dot(chosen(normed_ref).astype(bf16), out_gate_ref[...]))
    updated = chosen(base_ref) + out_gate * dot(normed_out, out_weight_ref[...])
    normed_att = layer_norm(updated, gains_ref[2:3]).astype(bf16)
    own_pairs = rows * cols
    column_pairs = tokens * cols
    upd_ref[...] = updated[:column_pairs]
    att_f = normed_att.astype(f32)
    att_ref[...] = att_f[:column_pairs]

    own_at = pl.ds(pl.multiple_of(row_first * cols, own_pairs), own_pairs)
    own = att_ref[own_at, :].astype(bf16)
    column = normed_att[:column_pairs]
    queries = dot(own, qkv_ref[:, :width])
    keys = dot(column, qkv_ref[:, width : 2 * width]).astype(bf16)
    values = dot(column, qkv_ref[:, 2 * width :]).astype(bf16)
    own_gate = sigmoid(dot(own, att_gate_ref[...]))

    bias = []
    for r in range(rows):
        part = att_f[column_pairs + r * tokens : column_pairs + (r + 1) * tokens]
        spread = jnp.concatenate(
            [jnp.broadcast_to(part[k : k + 1], (cols, width)) for k in range(tokens)], axis=0
        )
        bias.append(round_bf16(dot_t(att_bias_ref[...], spread.astype(bf16))))

    head_of = lax.broadcasted_iota(jnp.int32, (own_pairs, width), 1) // head_dim
    queries = round_bf16(queries)
    by_head = jnp.concatenate(
        [jnp.where(head_of == h, queries, 0.0) for h in range(heads)], axis=0
    ).astype(bf16)
    scores = dot_t(by_head, keys) * (1.0 / math.sqrt(head_dim))
    biases = jnp.concatenate(
        [jnp.broadcast_to(bias[r][h : h + 1], (cols, column_pairs)) for h in range(heads) for r in range(rows)],
        axis=0,
    )
    lane_row = lax.broadcasted_iota(jnp.int32, (1, column_pairs), 1)
    key_mask = jnp.zeros((1, column_pairs), jnp.int32)
    for k in range(tokens):
        key_mask = jnp.where(lane_row // cols == k, mask_ref[k], key_mask)
    key_bias = (key_mask.astype(f32) - 1.0) * 1000000000.0
    scores = scores + biases + key_bias
    same = (
        lax.broadcasted_iota(jnp.int32, scores.shape, 1) % cols
        == lax.broadcasted_iota(jnp.int32, scores.shape, 0) % cols
    )
    scores = jnp.where(same, scores, -jnp.inf)
    expo = jnp.exp(scores - jnp.max(scores, axis=-1, keepdims=True))
    totals = jnp.sum(expo, axis=-1, keepdims=True)
    mixed = dot(expo.astype(bf16), values) / totals
    attended = jnp.zeros((own_pairs, width), f32)
    for h in range(heads):
        attended = jnp.where(head_of == h, mixed[h * own_pairs : (h + 1) * own_pairs], attended)

    gated = (own_gate * attended).astype(bf16)
    result = upd_ref[own_at, :] + dot(gated, att_out_ref[...])
    out_ref[...] = result.reshape(rows, cols, width).astype(bf16)


def whole_pair_on_device(
    row_dim,
    pair_in,
    token_mask,
    positions,
    relpos_table,
    tri_norm_in,
    tri_in_weight,
    tri_in_gate,
    tri_out_gate,
    tri_norm_out,
    tri_out_weight,
    att_norm,
    att_qkv,
    att_gate,
    att_bias,
    att_out,
):
    rows, cols, width = pair_in.shape
    vmem = pl.BlockSpec(memory_space=pltpu.VMEM)
    smem = pl.BlockSpec(memory_space=pltpu.SMEM)
    params = pltpu.CompilerParams(vmem_limit_bytes=16 * 1024 * 1024)

    tokens, heads = row_dim * rows, att_bias.shape[1]

    def move(values, step, devices):
        return lax.ppermute(values, ("row", "col"), [(device, device ^ step) for device in devices])

    blocks = 2 * row_dim
    chip = pl.pallas_call(
        own_kernel,
        out_shape=jax.ShapeDtypeStruct((2,) + pair_in.shape, pair_in.dtype),
        in_specs=[vmem],
        out_specs=vmem,
        compiler_params=params,
    )(pair_in)
    held = chip.at[1].set(move(pair_in, 1, range(blocks)))
    step = 2
    while True:
        last = move(held, step, range(1, blocks, 2))
        step *= 2
        if step == blocks:
            break
        held = jnp.concatenate([held, last], axis=0)
    held_sent = move(held, 1, range(blocks))

    wide_out = jax.ShapeDtypeStruct((tokens * tokens, width), jnp.float32)
    staged = pl.pallas_call(
        functools.partial(stage_kernel, cols),
        out_shape=[
            wide_out,
            wide_out,
            jax.ShapeDtypeStruct((3, width), jnp.float32),
            jax.ShapeDtypeStruct((heads, width), att_bias.dtype),
        ],
        in_specs=[smem] * 2 + [vmem] * 5,
        out_specs=[vmem] * 4,
        compiler_params=params,
        cost_estimate=pl.CostEstimate(flops=STAGE_FLOPS, bytes_accessed=2**20, transcendentals=0),
    )(
        token_mask,
        positions,
        relpos_table,
        tri_norm_in.reshape(1, width),
        tri_norm_out.reshape(1, width),
        att_norm.reshape(1, width),
        att_bias.T,
    )
    last, *staged = lax.optimization_barrier((last, *staged))
    gathered = (held, last, held_sent, move(last, 1, range(blocks)))

    weights = (tri_in_weight, tri_in_gate, tri_out_gate, tri_out_weight, att_qkv, att_gate, att_out)
    wide = pltpu.VMEM((tokens * tokens, width), jnp.float32)
    column = pltpu.VMEM((tokens * cols, width), jnp.float32)
    return pl.pallas_call(
        functools.partial(whole_pair_kernel, row_dim, heads),
        out_shape=jax.ShapeDtypeStruct(pair_in.shape, pair_in.dtype),
        in_specs=[vmem] * 4 + [smem] + [vmem] * (4 + len(weights)),
        out_specs=vmem,
        scratch_shapes=[wide] * 4 + [column] * 2,
        compiler_params=params,
    )(*gathered, token_mask, *staged, *weights)


def attend_column(query_col, key_col, value_col, bias_all, key_bias, block_rows):
    tok_total = query_col.shape[0]
    scale = 1.0 / math.sqrt(query_col.shape[2])

    def one_block(block_idx):
        scores = (
            jnp.einsum("ihe,khe->hik", query_col, key_col, preferred_element_type=jnp.float32)
            * scale
        )
        scores = scores + bias_all.astype(jnp.float32) + key_bias[None, None, :]
        row_max = jnp.max(scores, axis=-1, keepdims=True)
        expo_f = jnp.exp(scores - row_max)
        totals = jnp.sum(expo_f, axis=-1)
        weights = expo_f.astype(jnp.bfloat16)
        result = jnp.einsum("hik,khe->ihe", weights, value_col, preferred_element_type=jnp.float32)
        return result / jnp.transpose(totals)[:, :, None]

    blocks = lax.map(one_block, jnp.arange(tok_total // block_rows))
    return blocks.reshape(tok_total, query_col.shape[1], query_col.shape[2])


def column_attention(columns, att_qkv, att_gate, bias_all, key_bias, head_local, head_dim):
    tok_total, col_count, channels = columns.shape
    local_width = head_local * head_dim
    weight_three = att_qkv.reshape(channels, 3, channels)
    qkv_all = jnp.einsum(
        "kmc,ctd->tmkd", columns, weight_three, preferred_element_type=jnp.float32
    ).astype(jnp.bfloat16)
    qkv_all = qkv_all.reshape(3, col_count, tok_total, head_local, head_dim)
    gate_val = jax.nn.sigmoid(
        jnp.einsum("kmc,cd->kmd", columns, att_gate, preferred_element_type=jnp.float32)
    )
    block_rows = min(1024, tok_total)

    def one_column(triple):
        return attend_column(triple[0], triple[1], triple[2], bias_all, key_bias, block_rows)

    attended = lax.map(one_column, (qkv_all[0], qkv_all[1], qkv_all[2]))
    attended = jnp.transpose(attended, (1, 0, 2, 3)).reshape(tok_total, col_count, local_width)
    return (gate_val * attended).astype(jnp.bfloat16)


def split_pair_on_device(
    pair_in,
    token_mask,
    positions,
    relpos_table,
    tri_norm_in,
    tri_in_weight,
    tri_in_gate,
    tri_out_gate,
    tri_norm_out,
    tri_out_weight,
    att_norm,
    att_qkv,
    att_gate,
    att_bias,
    att_out,
):
    row_count, col_count, channels = pair_in.shape
    row_first = lax.axis_index("row") * row_count
    col_first = lax.axis_index("col") * col_count
    mask_float = token_mask.astype(jnp.float32)
    row_mask = lax.dynamic_slice_in_dim(mask_float, row_first, row_count)
    col_mask = lax.dynamic_slice_in_dim(mask_float, col_first, col_count)
    row_pos = lax.dynamic_slice_in_dim(positions, row_first, row_count)
    col_pos = lax.dynamic_slice_in_dim(positions, col_first, col_count)
    bin_count = relpos_table.shape[0]
    bin_centre = bin_count // 2
    bucket = jnp.clip(row_pos[:, None] - col_pos[None, :], -bin_centre, bin_centre - 1) + bin_centre
    onehot = (bucket[:, :, None] == jnp.arange(bin_count, dtype=jnp.int32)[None, None, :]).astype(
        jnp.bfloat16
    )
    residual = pair_in.astype(jnp.float32) + jnp.einsum(
        "rjb,bc->rjc", onehot, relpos_table, preferred_element_type=jnp.float32
    )
    normed = layer_norm(residual, tri_norm_in).astype(jnp.bfloat16)
    pair_mask = row_mask[:, None] * col_mask[None, :]
    gate_in = jnp.einsum("rjc,cd->drj", normed, tri_in_gate, preferred_element_type=jnp.float32)
    proj_in = jnp.einsum("rjc,cd->drj", normed, tri_in_weight, preferred_element_type=jnp.float32)
    projected = (jax.nn.sigmoid(gate_in) * proj_in * pair_mask[None, :, :]).astype(jnp.bfloat16)
    left_ch, right_ch = (
        lax.all_to_all(projected[:channels], "row", split_axis=0, concat_axis=1, tiled=True),
        lax.all_to_all(projected[channels:], "row", split_axis=0, concat_axis=1, tiled=True),
    )
    right_rows = lax.all_to_all(right_ch, "col", split_axis=1, concat_axis=2, tiled=True)
    product_sum = jnp.einsum(
        "cik,cjk->cij",
        lax.all_gather(left_ch, "col", axis=2, tiled=True),
        right_rows,
        preferred_element_type=jnp.float32,
    )
    products = product_sum.astype(jnp.bfloat16)
    product_tile = lax.all_to_all(products, "row", split_axis=1, concat_axis=0, tiled=True)
    tri_x = jnp.transpose(product_tile, (1, 2, 0)).astype(jnp.float32)
    normed_out = layer_norm(tri_x, tri_norm_out).astype(jnp.bfloat16)
    out_gate = jax.nn.sigmoid(
        jnp.einsum("rjc,cd->rjd", normed, tri_out_gate, preferred_element_type=jnp.float32)
    )
    residual = residual + out_gate * jnp.einsum(
        "rjc,cd->rjd", normed_out, tri_out_weight, preferred_element_type=jnp.float32
    )
    normed_att = layer_norm(residual, att_norm).astype(jnp.bfloat16)
    bias_piece = jnp.einsum(
        "kic,ch->hik", normed_att, att_bias, preferred_element_type=jnp.float32
    ).astype(jnp.bfloat16)
    key_bias = (mask_float - 1.0) * 1000000000.0
    head_count = att_bias.shape[1]
    head_dim = channels // head_count
    columns = lax.all_to_all(normed_att, "row", split_axis=1, concat_axis=0, tiled=True)
    bias_half = lax.all_gather(bias_piece, "col", axis=1, tiled=True)
    bias_all = lax.all_gather(bias_half, "row", axis=2, tiled=True)
    gated = column_attention(columns, att_qkv, att_gate, bias_all, key_bias, head_count, head_dim)
    gated_tile = lax.all_to_all(gated, "row", split_axis=0, concat_axis=1, tiled=True)
    update = jnp.einsum("rjc,cd->rjd", gated_tile, att_out, preferred_element_type=jnp.float32)
    return (residual + update).astype(jnp.bfloat16)


def on_device(row_dim, col_dim, pair_in, *others):
    rows, cols, width = pair_in.shape
    tokens = row_dim * rows
    whole_bytes = tokens * tokens * width * pair_in.dtype.itemsize
    blocks = row_dim * col_dim
    tiled = cols % 8 == 0 and width % 128 == 0 and blocks & (blocks - 1) == 0 and blocks >= 4 and col_dim == 2
    if whole_bytes <= WHOLE_PAIR_BYTES and tiled:
        return whole_pair_on_device(row_dim, pair_in, *others)
    return split_pair_on_device(pair_in, *others)


def solution(mesh):
    return jax.shard_map(
        functools.partial(on_device, mesh.shape["row"], mesh.shape["col"]),
        mesh=mesh,
        in_specs=(P(("groups", "row"), "col", None), P("groups"), P("groups")) + (P(),) * 12,
        out_specs=P(("groups", "row"), "col", None),
        check_vma=False,
    )
```

```python
import functools
import math

import jax
import jax.numpy as jnp
from jax import lax
from jax.experimental import pallas as pl
from jax.experimental.pallas import tpu as pltpu
from jax.sharding import PartitionSpec as P

epsilon = 1e-05

WHOLE_PAIR_BYTES = 256 * 1024
STAGE_FLOPS = 10**9


def layer_norm(values, gain):
    mean_val = jnp.mean(values, axis=-1, keepdims=True)
    centred = values - mean_val
    var_val = jnp.mean(centred * centred, axis=-1, keepdims=True)
    return centred * lax.rsqrt(var_val + epsilon) * gain


def sigmoid(values):
    return 0.5 * jnp.tanh(0.5 * values) + 0.5


def dot(left, right):
    return jnp.dot(left, right, preferred_element_type=jnp.float32)


def dot_t(left, right):
    return lax.dot_general(
        left, right, (((1,), (1,)), ((), ())), preferred_element_type=jnp.float32
    )


def round_bf16(values):
    return values.astype(jnp.bfloat16).astype(jnp.float32)


def own_kernel(pair_ref, chip_ref):
    chip_ref[0] = pair_ref[...]


def stage_kernel(
    cols,
    mask_ref,
    pos_ref,
    table_ref,
    norm_in_ref,
    norm_out_ref,
    att_norm_ref,
    att_bias_ref,
    rel_ref,
    pair_mask_ref,
    gains_ref,
    bias_ref,
):
    gains_ref[0:1] = norm_in_ref[...]
    gains_ref[1:2] = norm_out_ref[...]
    gains_ref[2:3] = att_norm_ref[...]
    bias_ref[...] = att_bias_ref[...]
    tokens = pos_ref.shape[0]
    bins = table_ref.shape[0]
    sub = lax.broadcasted_iota(jnp.int32, (cols, bins), 0)
    lane = lax.broadcasted_iota(jnp.int32, (cols, bins), 1)
    hot = [None] * (tokens * tokens // cols)
    for half in range(tokens // cols):
        pos_vec = jnp.zeros((cols, bins), jnp.int32)
        mask_vec = jnp.zeros((cols, bins), jnp.int32)
        for c in range(cols):
            pos_vec = jnp.where(sub == c, pos_ref[half * cols + c], pos_vec)
            mask_vec = jnp.where(sub == c, mask_ref[half * cols + c], mask_vec)
        for i in range(tokens):
            at = i * (tokens // cols) + half
            bucket = jnp.clip(pos_ref[i] - pos_vec, -(bins // 2), bins // 2 - 1) + bins // 2
            hot[at] = (bucket == lane).astype(jnp.float32)
            pair_mask_ref[at * cols : (at + 1) * cols, :] = (mask_vec * mask_ref[i]).astype(jnp.float32)
    hot = jnp.concatenate(hot, axis=0).astype(jnp.bfloat16)
    rel_ref[...] = dot(hot, table_ref[...])


def whole_pair_kernel(
    row_dim,
    heads,
    held_ref,
    last_ref,
    held_sent_ref,
    last_sent_ref,
    mask_ref,
    rel_ref,
    pair_mask_ref,
    gains_ref,
    att_bias_ref,
    in_weight_ref,
    in_gate_ref,
    out_gate_ref,
    out_weight_ref,
    qkv_ref,
    att_gate_ref,
    att_out_ref,
    out_ref,
    base_ref,
    normed_ref,
    left_ref,
    right_ref,
    att_ref,
    upd_ref,
):
    rows, cols, width = held_ref.shape[1:]
    tokens = row_dim * rows
    head_dim = width // heads
    row_first = lax.axis_index("row") * rows
    col_first = pl.multiple_of(lax.axis_index("col") * cols, cols)
    f32, bf16 = jnp.float32, jnp.bfloat16

    is_odd = lax.axis_index("col") == 1
    odd = lax.axis_index("row") * 2 + 1
    for m in range(2 * row_dim):
        here, sent = ((held_ref, held_sent_ref), (last_ref, last_sent_ref))[m // row_dim]
        owner = odd ^ m
        block = jnp.where(is_odd, here[m % row_dim].astype(f32), sent[m % row_dim].astype(f32))
        for r in range(rows):
            first = (owner // 2 * rows + r) * tokens + owner % 2 * cols
            base_ref[pl.ds(pl.multiple_of(first, cols), cols), :] = block[r]

    base = base_ref[...] + rel_ref[...]
    base_ref[...] = base

    normed = layer_norm(base, gains_ref[0:1]).astype(bf16)
    normed_ref[...] = normed.astype(f32)
    projected = sigmoid(dot(normed, in_gate_ref[...])) * dot(normed, in_weight_ref[...])
    pair_mask = pair_mask_ref[...]
    left_ref[...] = round_bf16(projected[:, :width] * pair_mask)
    right_ref[...] = round_bf16(projected[:, width:] * pair_mask)

    right_at = [right_ref[pl.ds(col_first * tokens + m, cols, stride=tokens), :] for m in range(tokens)]
    products = []
    for i in range(tokens):
        total = left_ref[pl.ds(i * tokens, 1), :] * right_at[0]
        for m in range(1, tokens):
            total = total + left_ref[pl.ds(i * tokens + m, 1), :] * right_at[m]
        products.append(total)
    extra = [None] * rows
    for m in range(tokens):
        left_at = left_ref[pl.ds(m, tokens, stride=tokens), :]
        for r in range(rows):
            term = left_at * right_ref[pl.ds((row_first + r) * tokens + m, 1), :]
            extra[r] = term if m == 0 else extra[r] + term
    products = round_bf16(jnp.concatenate(products + extra, axis=0))

    def chosen(ref):
        own = [ref[pl.ds(i * tokens + col_first, cols), :] for i in range(tokens)]
        own += [ref[pl.ds(row_first + r, tokens, stride=tokens), :] for r in range(rows)]
        return jnp.concatenate(own, axis=0)

    normed_out = layer_norm(products, gains_ref[1:2]).astype(bf16)
    out_gate = sigmoid(dot(chosen(normed_ref).astype(bf16), out_gate_ref[...]))
    updated = chosen(base_ref) + out_gate * dot(normed_out, out_weight_ref[...])
    normed_att = layer_norm(updated, gains_ref[2:3]).astype(bf16)
    own_pairs = rows * cols
    column_pairs = tokens * cols
    upd_ref[...] = updated[:column_pairs]
    att_f = normed_att.astype(f32)
    att_ref[...] = att_f[:column_pairs]

    own_at = pl.ds(pl.multiple_of(row_first * cols, own_pairs), own_pairs)
    own = att_ref[own_at, :].astype(bf16)
    column = normed_att[:column_pairs]
    queries = dot(own, qkv_ref[:, :width])
    keys = dot(column, qkv_ref[:, width : 2 * width]).astype(bf16)
    values = dot(column, qkv_ref[:, 2 * width :]).astype(bf16)
    own_gate = sigmoid(dot(own, att_gate_ref[...]))

    bias = []
    for r in range(rows):
        part = att_f[column_pairs + r * tokens : column_pairs + (r + 1) * tokens]
        spread = jnp.concatenate(
            [jnp.broadcast_to(part[k : k + 1], (cols, width)) for k in range(tokens)], axis=0
        )
        bias.append(round_bf16(dot_t(att_bias_ref[...], spread.astype(bf16))))

    head_of = lax.broadcasted_iota(jnp.int32, (own_pairs, width), 1) // head_dim
    queries = round_bf16(queries)
    by_head = jnp.concatenate(
        [jnp.where(head_of == h, queries, 0.0) for h in range(heads)], axis=0
    ).astype(bf16)
    scores = dot_t(by_head, keys) * (1.0 / math.sqrt(head_dim))
    biases = jnp.concatenate(
        [jnp.broadcast_to(bias[r][h : h + 1], (cols, column_pairs)) for h in range(heads) for r in range(rows)],
        axis=0,
    )
    lane_row = lax.broadcasted_iota(jnp.int32, (1, column_pairs), 1)
    key_mask = jnp.zeros((1, column_pairs), jnp.int32)
    for k in range(tokens):
        key_mask = jnp.where(lane_row // cols == k, mask_ref[k], key_mask)
    key_bias = (key_mask.astype(f32) - 1.0) * 1000000000.0
    scores = scores + biases + key_bias
    same = (
        lax.broadcasted_iota(jnp.int32, scores.shape, 1) % cols
        == lax.broadcasted_iota(jnp.int32, scores.shape, 0) % cols
    )
    scores = jnp.where(same, scores, -jnp.inf)
    expo = jnp.exp(scores - jnp.max(scores, axis=-1, keepdims=True))
    totals = jnp.sum(expo, axis=-1, keepdims=True)
    mixed = dot(expo.astype(bf16), values) / totals
    attended = jnp.zeros((own_pairs, width), f32)
    for h in range(heads):
        attended = jnp.where(head_of == h, mixed[h * own_pairs : (h + 1) * own_pairs], attended)

    gated = (own_gate * attended).astype(bf16)
    result = upd_ref[own_at, :] + dot(gated, att_out_ref[...])
    out_ref[...] = result.reshape(rows, cols, width).astype(bf16)


def whole_pair_on_device(
    row_dim,
    pair_in,
    token_mask,
    positions,
    relpos_table,
    tri_norm_in,
    tri_in_weight,
    tri_in_gate,
    tri_out_gate,
    tri_norm_out,
    tri_out_weight,
    att_norm,
    att_qkv,
    att_gate,
    att_bias,
    att_out,
):
    rows, cols, width = pair_in.shape
    vmem = pl.BlockSpec(memory_space=pltpu.VMEM)
    smem = pl.BlockSpec(memory_space=pltpu.SMEM)
    params = pltpu.CompilerParams(vmem_limit_bytes=16 * 1024 * 1024)

    tokens, heads = row_dim * rows, att_bias.shape[1]

    def move(values, step):
        pairs = [(device, device ^ step if step == 1 or device % 2 else device) for device in range(blocks)]
        return lax.ppermute(values, ("row", "col"), pairs)

    blocks = 2 * row_dim
    chip = pl.pallas_call(
        own_kernel,
        out_shape=jax.ShapeDtypeStruct((2,) + pair_in.shape, pair_in.dtype),
        in_specs=[vmem],
        out_specs=vmem,
        compiler_params=params,
    )(pair_in)
    held = chip.at[1].set(move(pair_in, 1))
    step = 2
    while True:
        last = move(held, step)
        step *= 2
        if step == blocks:
            break
        held = jnp.concatenate([held, last], axis=0)
    held_sent = move(held, 1)

    wide_out = jax.ShapeDtypeStruct((tokens * tokens, width), jnp.float32)
    staged = pl.pallas_call(
        functools.partial(stage_kernel, cols),
        out_shape=[
            wide_out,
            wide_out,
            jax.ShapeDtypeStruct((3, width), jnp.float32),
            jax.ShapeDtypeStruct((heads, width), att_bias.dtype),
        ],
        in_specs=[smem] * 2 + [vmem] * 5,
        out_specs=[vmem] * 4,
        compiler_params=params,
        cost_estimate=pl.CostEstimate(flops=STAGE_FLOPS, bytes_accessed=2**20, transcendentals=0),
    )(
        token_mask,
        positions,
        relpos_table,
        tri_norm_in.reshape(1, width),
        tri_norm_out.reshape(1, width),
        att_norm.reshape(1, width),
        att_bias.T,
    )
    last, *staged = lax.optimization_barrier((last, *staged))
    gathered = (held, last, held_sent, move(last, 1))

    weights = (tri_in_weight, tri_in_gate, tri_out_gate, tri_out_weight, att_qkv, att_gate, att_out)
    wide = pltpu.VMEM((tokens * tokens, width), jnp.float32)
    column = pltpu.VMEM((tokens * cols, width), jnp.float32)
    return pl.pallas_call(
        functools.partial(whole_pair_kernel, row_dim, heads),
        out_shape=jax.ShapeDtypeStruct(pair_in.shape, pair_in.dtype),
        in_specs=[vmem] * 4 + [smem] + [vmem] * (4 + len(weights)),
        out_specs=vmem,
        scratch_shapes=[wide] * 4 + [column] * 2,
        compiler_params=params,
    )(*gathered, token_mask, *staged, *weights)


def attend_column(query_col, key_col, value_col, bias_all, key_bias, block_rows):
    tok_total = query_col.shape[0]
    scale = 1.0 / math.sqrt(query_col.shape[2])

    def one_block(block_idx):
        scores = (
            jnp.einsum("ihe,khe->hik", query_col, key_col, preferred_element_type=jnp.float32)
            * scale
        )
        scores = scores + bias_all.astype(jnp.float32) + key_bias[None, None, :]
        row_max = jnp.max(scores, axis=-1, keepdims=True)
        expo_f = jnp.exp(scores - row_max)
        totals = jnp.sum(expo_f, axis=-1)
        weights = expo_f.astype(jnp.bfloat16)
        result = jnp.einsum("hik,khe->ihe", weights, value_col, preferred_element_type=jnp.float32)
        return result / jnp.transpose(totals)[:, :, None]

    blocks = lax.map(one_block, jnp.arange(tok_total // block_rows))
    return blocks.reshape(tok_total, query_col.shape[1], query_col.shape[2])


def column_attention(columns, att_qkv, att_gate, bias_all, key_bias, head_local, head_dim):
    tok_total, col_count, channels = columns.shape
    local_width = head_local * head_dim
    weight_three = att_qkv.reshape(channels, 3, channels)
    qkv_all = jnp.einsum(
        "kmc,ctd->tmkd", columns, weight_three, preferred_element_type=jnp.float32
    ).astype(jnp.bfloat16)
    qkv_all = qkv_all.reshape(3, col_count, tok_total, head_local, head_dim)
    gate_val = jax.nn.sigmoid(
        jnp.einsum("kmc,cd->kmd", columns, att_gate, preferred_element_type=jnp.float32)
    )
    block_rows = min(1024, tok_total)

    def one_column(triple):
        return attend_column(triple[0], triple[1], triple[2], bias_all, key_bias, block_rows)

    attended = lax.map(one_column, (qkv_all[0], qkv_all[1], qkv_all[2]))
    attended = jnp.transpose(attended, (1, 0, 2, 3)).reshape(tok_total, col_count, local_width)
    return (gate_val * attended).astype(jnp.bfloat16)


def split_pair_on_device(
    pair_in,
    token_mask,
    positions,
    relpos_table,
    tri_norm_in,
    tri_in_weight,
    tri_in_gate,
    tri_out_gate,
    tri_norm_out,
    tri_out_weight,
    att_norm,
    att_qkv,
    att_gate,
    att_bias,
    att_out,
):
    row_count, col_count, channels = pair_in.shape
    row_first = lax.axis_index("row") * row_count
    col_first = lax.axis_index("col") * col_count
    mask_float = token_mask.astype(jnp.float32)
    row_mask = lax.dynamic_slice_in_dim(mask_float, row_first, row_count)
    col_mask = lax.dynamic_slice_in_dim(mask_float, col_first, col_count)
    row_pos = lax.dynamic_slice_in_dim(positions, row_first, row_count)
    col_pos = lax.dynamic_slice_in_dim(positions, col_first, col_count)
    bin_count = relpos_table.shape[0]
    bin_centre = bin_count // 2
    bucket = jnp.clip(row_pos[:, None] - col_pos[None, :], -bin_centre, bin_centre - 1) + bin_centre
    onehot = (bucket[:, :, None] == jnp.arange(bin_count, dtype=jnp.int32)[None, None, :]).astype(
        jnp.bfloat16
    )
    residual = pair_in.astype(jnp.float32) + jnp.einsum(
        "rjb,bc->rjc", onehot, relpos_table, preferred_element_type=jnp.float32
    )
    normed = layer_norm(residual, tri_norm_in).astype(jnp.bfloat16)
    pair_mask = row_mask[:, None] * col_mask[None, :]
    gate_in = jnp.einsum("rjc,cd->drj", normed, tri_in_gate, preferred_element_type=jnp.float32)
    proj_in = jnp.einsum("rjc,cd->drj", normed, tri_in_weight, preferred_element_type=jnp.float32)
    projected = (jax.nn.sigmoid(gate_in) * proj_in * pair_mask[None, :, :]).astype(jnp.bfloat16)
    left_ch, right_ch = (
        lax.all_to_all(projected[:channels], "row", split_axis=0, concat_axis=1, tiled=True),
        lax.all_to_all(projected[channels:], "row", split_axis=0, concat_axis=1, tiled=True),
    )
    right_rows = lax.all_to_all(right_ch, "col", split_axis=1, concat_axis=2, tiled=True)
    product_sum = jnp.einsum(
        "cik,cjk->cij",
        lax.all_gather(left_ch, "col", axis=2, tiled=True),
        right_rows,
        preferred_element_type=jnp.float32,
    )
    products = product_sum.astype(jnp.bfloat16)
    product_tile = lax.all_to_all(products, "row", split_axis=1, concat_axis=0, tiled=True)
    tri_x = jnp.transpose(product_tile, (1, 2, 0)).astype(jnp.float32)
    normed_out = layer_norm(tri_x, tri_norm_out).astype(jnp.bfloat16)
    out_gate = jax.nn.sigmoid(
        jnp.einsum("rjc,cd->rjd", normed, tri_out_gate, preferred_element_type=jnp.float32)
    )
    residual = residual + out_gate * jnp.einsum(
        "rjc,cd->rjd", normed_out, tri_out_weight, preferred_element_type=jnp.float32
    )
    normed_att = layer_norm(residual, att_norm).astype(jnp.bfloat16)
    bias_piece = jnp.einsum(
        "kic,ch->hik", normed_att, att_bias, preferred_element_type=jnp.float32
    ).astype(jnp.bfloat16)
    key_bias = (mask_float - 1.0) * 1000000000.0
    head_count = att_bias.shape[1]
    head_dim = channels // head_count
    columns = lax.all_to_all(normed_att, "row", split_axis=1, concat_axis=0, tiled=True)
    bias_half = lax.all_gather(bias_piece, "col", axis=1, tiled=True)
    bias_all = lax.all_gather(bias_half, "row", axis=2, tiled=True)
    gated = column_attention(columns, att_qkv, att_gate, bias_all, key_bias, head_count, head_dim)
    gated_tile = lax.all_to_all(gated, "row", split_axis=0, concat_axis=1, tiled=True)
    update = jnp.einsum("rjc,cd->rjd", gated_tile, att_out, preferred_element_type=jnp.float32)
    return (residual + update).astype(jnp.bfloat16)


def on_device(row_dim, col_dim, pair_in, *others):
    rows, cols, width = pair_in.shape
    tokens = row_dim * rows
    whole_bytes = tokens * tokens * width * pair_in.dtype.itemsize
    blocks = row_dim * col_dim
    tiled = cols % 8 == 0 and width % 128 == 0 and blocks & (blocks - 1) == 0 and blocks >= 4 and col_dim == 2
    if whole_bytes <= WHOLE_PAIR_BYTES and tiled:
        return whole_pair_on_device(row_dim, pair_in, *others)
    return split_pair_on_device(pair_in, *others)


def solution(mesh):
    return jax.shard_map(
        functools.partial(on_device, mesh.shape["row"], mesh.shape["col"]),
        mesh=mesh,
        in_specs=(P(("groups", "row"), "col", None), P("groups"), P("groups")) + (P(),) * 12,
        out_specs=P(("groups", "row"), "col", None),
        check_vma=False,
    )
```

```python
import functools
import math

import jax
import jax.numpy as jnp
from jax import lax
from jax.experimental import pallas as pl
from jax.experimental.pallas import tpu as pltpu
from jax.sharding import PartitionSpec as P

epsilon = 1e-05

WHOLE_PAIR_BYTES = 256 * 1024
STAGE_FLOPS = 10**9


def layer_norm(values, gain):
    mean_val = jnp.mean(values, axis=-1, keepdims=True)
    centred = values - mean_val
    var_val = jnp.mean(centred * centred, axis=-1, keepdims=True)
    return centred * lax.rsqrt(var_val + epsilon) * gain


def sigmoid(values):
    return 0.5 * jnp.tanh(0.5 * values) + 0.5


def dot(left, right):
    return jnp.dot(left, right, preferred_element_type=jnp.float32)


def dot_t(left, right):
    return lax.dot_general(
        left, right, (((1,), (1,)), ((), ())), preferred_element_type=jnp.float32
    )


def round_bf16(values):
    return values.astype(jnp.bfloat16).astype(jnp.float32)


def own_kernel(pair_ref, chip_ref):
    chip_ref[0] = pair_ref[...]


def stage_kernel(
    cols,
    mask_ref,
    pos_ref,
    table_ref,
    norm_in_ref,
    norm_out_ref,
    att_norm_ref,
    att_bias_ref,
    rel_ref,
    pair_mask_ref,
    gains_ref,
    bias_ref,
):
    gains_ref[0:1] = norm_in_ref[...]
    gains_ref[1:2] = norm_out_ref[...]
    gains_ref[2:3] = att_norm_ref[...]
    bias_ref[...] = att_bias_ref[...]
    tokens = pos_ref.shape[0]
    bins = table_ref.shape[0]
    sub = lax.broadcasted_iota(jnp.int32, (cols, bins), 0)
    lane = lax.broadcasted_iota(jnp.int32, (cols, bins), 1)
    hot = [None] * (tokens * tokens // cols)
    for half in range(tokens // cols):
        pos_vec = jnp.zeros((cols, bins), jnp.int32)
        mask_vec = jnp.zeros((cols, bins), jnp.int32)
        for c in range(cols):
            pos_vec = jnp.where(sub == c, pos_ref[half * cols + c], pos_vec)
            mask_vec = jnp.where(sub == c, mask_ref[half * cols + c], mask_vec)
        for i in range(tokens):
            at = i * (tokens // cols) + half
            bucket = jnp.clip(pos_ref[i] - pos_vec, -(bins // 2), bins // 2 - 1) + bins // 2
            hot[at] = (bucket == lane).astype(jnp.float32)
            pair_mask_ref[at * cols : (at + 1) * cols, :] = (mask_vec * mask_ref[i]).astype(jnp.float32)
    hot = jnp.concatenate(hot, axis=0).astype(jnp.bfloat16)
    rel_ref[...] = dot(hot, table_ref[...])


def whole_pair_kernel(
    row_dim,
    heads,
    order,
    held_ref,
    other_ref,
    mask_ref,
    rel_ref,
    pair_mask_ref,
    gains_ref,
    att_bias_ref,
    in_weight_ref,
    in_gate_ref,
    out_gate_ref,
    out_weight_ref,
    qkv_ref,
    att_gate_ref,
    att_out_ref,
    out_ref,
    base_ref,
    normed_ref,
    left_ref,
    right_ref,
    att_ref,
    upd_ref,
):
    rows, cols, width = held_ref.shape[1:]
    tokens = row_dim * rows
    head_dim = width // heads
    row_first = lax.axis_index("row") * rows
    col_first = pl.multiple_of(lax.axis_index("col") * cols, cols)
    f32, bf16 = jnp.float32, jnp.bfloat16

    me = lax.axis_index("row") * 2 + lax.axis_index("col")
    for ref, flip in ((held_ref, 0), (other_ref, 1)):
        for at, place in enumerate(order):
            owner = me ^ (place ^ flip)
            block = ref[at].astype(f32)
            for r in range(rows):
                first = (owner // 2 * rows + r) * tokens + owner % 2 * cols
                base_ref[pl.ds(pl.multiple_of(first, cols), cols), :] = block[r]

    base = base_ref[...] + rel_ref[...]
    base_ref[...] = base

    normed = layer_norm(base, gains_ref[0:1]).astype(bf16)
    normed_ref[...] = normed.astype(f32)
    projected = sigmoid(dot(normed, in_gate_ref[...])) * dot(normed, in_weight_ref[...])
    pair_mask = pair_mask_ref[...]
    left_ref[...] = round_bf16(projected[:, :width] * pair_mask)
    right_ref[...] = round_bf16(projected[:, width:] * pair_mask)

    right_at = [right_ref[pl.ds(col_first * tokens + m, cols, stride=tokens), :] for m in range(tokens)]
    products = []
    for i in range(tokens):
        total = left_ref[pl.ds(i * tokens, 1), :] * right_at[0]
        for m in range(1, tokens):
            total = total + left_ref[pl.ds(i * tokens + m, 1), :] * right_at[m]
        products.append(total)
    extra = [None] * rows
    for m in range(tokens):
        left_at = left_ref[pl.ds(m, tokens, stride=tokens), :]
        for r in range(rows):
            term = left_at * right_ref[pl.ds((row_first + r) * tokens + m, 1), :]
            extra[r] = term if m == 0 else extra[r] + term
    products = round_bf16(jnp.concatenate(products + extra, axis=0))

    def chosen(ref):
        own = [ref[pl.ds(i * tokens + col_first, cols), :] for i in range(tokens)]
        own += [ref[pl.ds(row_first + r, tokens, stride=tokens), :] for r in range(rows)]
        return jnp.concatenate(own, axis=0)

    normed_out = layer_norm(products, gains_ref[1:2]).astype(bf16)
    out_gate = sigmoid(dot(chosen(normed_ref).astype(bf16), out_gate_ref[...]))
    updated = chosen(base_ref) + out_gate * dot(normed_out, out_weight_ref[...])
    normed_att = layer_norm(updated, gains_ref[2:3]).astype(bf16)
    own_pairs = rows * cols
    column_pairs = tokens * cols
    upd_ref[...] = updated[:column_pairs]
    att_f = normed_att.astype(f32)
    att_ref[...] = att_f[:column_pairs]

    own_at = pl.ds(pl.multiple_of(row_first * cols, own_pairs), own_pairs)
    own = att_ref[own_at, :].astype(bf16)
    column = normed_att[:column_pairs]
    queries = dot(own, qkv_ref[:, :width])
    keys = dot(column, qkv_ref[:, width : 2 * width]).astype(bf16)
    values = dot(column, qkv_ref[:, 2 * width :]).astype(bf16)
    own_gate = sigmoid(dot(own, att_gate_ref[...]))

    bias = []
    for r in range(rows):
        part = att_f[column_pairs + r * tokens : column_pairs + (r + 1) * tokens]
        spread = jnp.concatenate(
            [jnp.broadcast_to(part[k : k + 1], (cols, width)) for k in range(tokens)], axis=0
        )
        bias.append(round_bf16(dot_t(att_bias_ref[...], spread.astype(bf16))))

    head_of = lax.broadcasted_iota(jnp.int32, (own_pairs, width), 1) // head_dim
    queries = round_bf16(queries)
    by_head = jnp.concatenate(
        [jnp.where(head_of == h, queries, 0.0) for h in range(heads)], axis=0
    ).astype(bf16)
    scores = dot_t(by_head, keys) * (1.0 / math.sqrt(head_dim))
    biases = jnp.concatenate(
        [jnp.broadcast_to(bias[r][h : h + 1], (cols, column_pairs)) for h in range(heads) for r in range(rows)],
        axis=0,
    )
    lane_row = lax.broadcasted_iota(jnp.int32, (1, column_pairs), 1)
    key_mask = jnp.zeros((1, column_pairs), jnp.int32)
    for k in range(tokens):
        key_mask = jnp.where(lane_row // cols == k, mask_ref[k], key_mask)
    key_bias = (key_mask.astype(f32) - 1.0) * 1000000000.0
    scores = scores + biases + key_bias
    same = (
        lax.broadcasted_iota(jnp.int32, scores.shape, 1) % cols
        == lax.broadcasted_iota(jnp.int32, scores.shape, 0) % cols
    )
    scores = jnp.where(same, scores, -jnp.inf)
    expo = jnp.exp(scores - jnp.max(scores, axis=-1, keepdims=True))
    totals = jnp.sum(expo, axis=-1, keepdims=True)
    mixed = dot(expo.astype(bf16), values) / totals
    attended = jnp.zeros((own_pairs, width), f32)
    for h in range(heads):
        attended = jnp.where(head_of == h, mixed[h * own_pairs : (h + 1) * own_pairs], attended)

    gated = (own_gate * attended).astype(bf16)
    result = upd_ref[own_at, :] + dot(gated, att_out_ref[...])
    out_ref[...] = result.reshape(rows, cols, width).astype(bf16)


def whole_pair_on_device(
    row_dim,
    pair_in,
    token_mask,
    positions,
    relpos_table,
    tri_norm_in,
    tri_in_weight,
    tri_in_gate,
    tri_out_gate,
    tri_norm_out,
    tri_out_weight,
    att_norm,
    att_qkv,
    att_gate,
    att_bias,
    att_out,
):
    rows, cols, width = pair_in.shape
    vmem = pl.BlockSpec(memory_space=pltpu.VMEM)
    smem = pl.BlockSpec(memory_space=pltpu.SMEM)
    params = pltpu.CompilerParams(vmem_limit_bytes=16 * 1024 * 1024)
    tokens, heads = row_dim * rows, att_bias.shape[1]

    blocks = 2 * row_dim

    def move(values, step):
        return lax.ppermute(values, ("row", "col"), [(device, device ^ step) for device in range(blocks)])

    held = pl.pallas_call(
        own_kernel,
        out_shape=jax.ShapeDtypeStruct((2,) + pair_in.shape, pair_in.dtype),
        in_specs=[vmem],
        out_specs=vmem,
        compiler_params=params,
    )(pair_in)
    held, order = held.at[1].set(move(pair_in, 3)), (0, 3)
    while len(order) < row_dim:
        step = 2 * len(order) + 1
        held = jnp.concatenate([held, move(held, step)], axis=0)
        order += tuple(place ^ step for place in order)

    wide_out = jax.ShapeDtypeStruct((tokens * tokens, width), jnp.float32)
    staged = pl.pallas_call(
        functools.partial(stage_kernel, cols),
        out_shape=[
            wide_out,
            wide_out,
            jax.ShapeDtypeStruct((3, width), jnp.float32),
            jax.ShapeDtypeStruct((heads, width), att_bias.dtype),
        ],
        in_specs=[smem] * 2 + [vmem] * 5,
        out_specs=[vmem] * 4,
        compiler_params=params,
        cost_estimate=pl.CostEstimate(flops=STAGE_FLOPS, bytes_accessed=2**20, transcendentals=0),
    )(
        token_mask,
        positions,
        relpos_table,
        tri_norm_in.reshape(1, width),
        tri_norm_out.reshape(1, width),
        att_norm.reshape(1, width),
        att_bias.T,
    )
    held, *staged = lax.optimization_barrier((held, *staged))
    gathered = (held, move(held, 1))

    weights = (tri_in_weight, tri_in_gate, tri_out_gate, tri_out_weight, att_qkv, att_gate, att_out)
    wide = pltpu.VMEM((tokens * tokens, width), jnp.float32)
    column = pltpu.VMEM((tokens * cols, width), jnp.float32)
    return pl.pallas_call(
        functools.partial(whole_pair_kernel, row_dim, heads, order),
        out_shape=jax.ShapeDtypeStruct(pair_in.shape, pair_in.dtype),
        in_specs=[vmem] * 2 + [smem] + [vmem] * (4 + len(weights)),
        out_specs=vmem,
        scratch_shapes=[wide] * 4 + [column] * 2,
        compiler_params=params,
    )(*gathered, token_mask, *staged, *weights)


def attend_column(query_col, key_col, value_col, bias_all, key_bias, block_rows):
    tok_total = query_col.shape[0]
    scale = 1.0 / math.sqrt(query_col.shape[2])

    def one_block(block_idx):
        scores = (
            jnp.einsum("ihe,khe->hik", query_col, key_col, preferred_element_type=jnp.float32)
            * scale
        )
        scores = scores + bias_all.astype(jnp.float32) + key_bias[None, None, :]
        row_max = jnp.max(scores, axis=-1, keepdims=True)
        expo_f = jnp.exp(scores - row_max)
        totals = jnp.sum(expo_f, axis=-1)
        weights = expo_f.astype(jnp.bfloat16)
        result = jnp.einsum("hik,khe->ihe", weights, value_col, preferred_element_type=jnp.float32)
        return result / jnp.transpose(totals)[:, :, None]

    blocks = lax.map(one_block, jnp.arange(tok_total // block_rows))
    return blocks.reshape(tok_total, query_col.shape[1], query_col.shape[2])


def column_attention(columns, att_qkv, att_gate, bias_all, key_bias, head_local, head_dim):
    tok_total, col_count, channels = columns.shape
    local_width = head_local * head_dim
    weight_three = att_qkv.reshape(channels, 3, channels)
    qkv_all = jnp.einsum(
        "kmc,ctd->tmkd", columns, weight_three, preferred_element_type=jnp.float32
    ).astype(jnp.bfloat16)
    qkv_all = qkv_all.reshape(3, col_count, tok_total, head_local, head_dim)
    gate_val = jax.nn.sigmoid(
        jnp.einsum("kmc,cd->kmd", columns, att_gate, preferred_element_type=jnp.float32)
    )
    block_rows = min(1024, tok_total)

    def one_column(triple):
        return attend_column(triple[0], triple[1], triple[2], bias_all, key_bias, block_rows)

    attended = lax.map(one_column, (qkv_all[0], qkv_all[1], qkv_all[2]))
    attended = jnp.transpose(attended, (1, 0, 2, 3)).reshape(tok_total, col_count, local_width)
    return (gate_val * attended).astype(jnp.bfloat16)


def split_pair_on_device(
    pair_in,
    token_mask,
    positions,
    relpos_table,
    tri_norm_in,
    tri_in_weight,
    tri_in_gate,
    tri_out_gate,
    tri_norm_out,
    tri_out_weight,
    att_norm,
    att_qkv,
    att_gate,
    att_bias,
    att_out,
):
    row_count, col_count, channels = pair_in.shape
    row_first = lax.axis_index("row") * row_count
    col_first = lax.axis_index("col") * col_count
    mask_float = token_mask.astype(jnp.float32)
    row_mask = lax.dynamic_slice_in_dim(mask_float, row_first, row_count)
    col_mask = lax.dynamic_slice_in_dim(mask_float, col_first, col_count)
    row_pos = lax.dynamic_slice_in_dim(positions, row_first, row_count)
    col_pos = lax.dynamic_slice_in_dim(positions, col_first, col_count)
    bin_count = relpos_table.shape[0]
    bin_centre = bin_count // 2
    bucket = jnp.clip(row_pos[:, None] - col_pos[None, :], -bin_centre, bin_centre - 1) + bin_centre
    onehot = (bucket[:, :, None] == jnp.arange(bin_count, dtype=jnp.int32)[None, None, :]).astype(
        jnp.bfloat16
    )
    residual = pair_in.astype(jnp.float32) + jnp.einsum(
        "rjb,bc->rjc", onehot, relpos_table, preferred_element_type=jnp.float32
    )
    normed = layer_norm(residual, tri_norm_in).astype(jnp.bfloat16)
    pair_mask = row_mask[:, None] * col_mask[None, :]
    gate_in = jnp.einsum("rjc,cd->drj", normed, tri_in_gate, preferred_element_type=jnp.float32)
    proj_in = jnp.einsum("rjc,cd->drj", normed, tri_in_weight, preferred_element_type=jnp.float32)
    projected = (jax.nn.sigmoid(gate_in) * proj_in * pair_mask[None, :, :]).astype(jnp.bfloat16)
    left_ch, right_ch = (
        lax.all_to_all(projected[:channels], "row", split_axis=0, concat_axis=1, tiled=True),
        lax.all_to_all(projected[channels:], "row", split_axis=0, concat_axis=1, tiled=True),
    )
    right_rows = lax.all_to_all(right_ch, "col", split_axis=1, concat_axis=2, tiled=True)
    product_sum = jnp.einsum(
        "cik,cjk->cij",
        lax.all_gather(left_ch, "col", axis=2, tiled=True),
        right_rows,
        preferred_element_type=jnp.float32,
    )
    products = product_sum.astype(jnp.bfloat16)
    product_tile = lax.all_to_all(products, "row", split_axis=1, concat_axis=0, tiled=True)
    tri_x = jnp.transpose(product_tile, (1, 2, 0)).astype(jnp.float32)
    normed_out = layer_norm(tri_x, tri_norm_out).astype(jnp.bfloat16)
    out_gate = jax.nn.sigmoid(
        jnp.einsum("rjc,cd->rjd", normed, tri_out_gate, preferred_element_type=jnp.float32)
    )
    residual = residual + out_gate * jnp.einsum(
        "rjc,cd->rjd", normed_out, tri_out_weight, preferred_element_type=jnp.float32
    )
    normed_att = layer_norm(residual, att_norm).astype(jnp.bfloat16)
    bias_piece = jnp.einsum(
        "kic,ch->hik", normed_att, att_bias, preferred_element_type=jnp.float32
    ).astype(jnp.bfloat16)
    key_bias = (mask_float - 1.0) * 1000000000.0
    head_count = att_bias.shape[1]
    head_dim = channels // head_count
    columns = lax.all_to_all(normed_att, "row", split_axis=1, concat_axis=0, tiled=True)
    bias_half = lax.all_gather(bias_piece, "col", axis=1, tiled=True)
    bias_all = lax.all_gather(bias_half, "row", axis=2, tiled=True)
    gated = column_attention(columns, att_qkv, att_gate, bias_all, key_bias, head_count, head_dim)
    gated_tile = lax.all_to_all(gated, "row", split_axis=0, concat_axis=1, tiled=True)
    update = jnp.einsum("rjc,cd->rjd", gated_tile, att_out, preferred_element_type=jnp.float32)
    return (residual + update).astype(jnp.bfloat16)


def on_device(row_dim, col_dim, pair_in, *others):
    rows, cols, width = pair_in.shape
    tokens = row_dim * rows
    whole_bytes = tokens * tokens * width * pair_in.dtype.itemsize
    blocks = row_dim * col_dim
    tiled = cols % 8 == 0 and width % 128 == 0 and blocks & (blocks - 1) == 0 and blocks >= 4 and col_dim == 2
    if whole_bytes <= WHOLE_PAIR_BYTES and tiled:
        return whole_pair_on_device(row_dim, pair_in, *others)
    return split_pair_on_device(pair_in, *others)


def solution(mesh):
    return jax.shard_map(
        functools.partial(on_device, mesh.shape["row"], mesh.shape["col"]),
        mesh=mesh,
        in_specs=(P(("groups", "row"), "col", None), P("groups"), P("groups")) + (P(),) * 12,
        out_specs=P(("groups", "row"), "col", None),
        check_vma=False,
    )
```

```python
import functools
import math

import jax
import jax.numpy as jnp
from jax import lax
from jax.experimental import pallas as pl
from jax.experimental.pallas import tpu as pltpu
from jax.sharding import PartitionSpec as P

epsilon = 1e-05

WHOLE_PAIR_BYTES = 256 * 1024
STAGE_FLOPS = 10**9


def layer_norm(values, gain):
    mean_val = jnp.mean(values, axis=-1, keepdims=True)
    centred = values - mean_val
    var_val = jnp.mean(centred * centred, axis=-1, keepdims=True)
    return centred * lax.rsqrt(var_val + epsilon) * gain


def sigmoid(values):
    return 0.5 * jnp.tanh(0.5 * values) + 0.5


def dot(left, right):
    return jnp.dot(left, right, preferred_element_type=jnp.float32)


def dot_t(left, right):
    return lax.dot_general(
        left, right, (((1,), (1,)), ((), ())), preferred_element_type=jnp.float32
    )


def round_bf16(values):
    return values.astype(jnp.bfloat16).astype(jnp.float32)


def stage_kernel(
    cols,
    mask_ref,
    pos_ref,
    table_ref,
    norm_in_ref,
    norm_out_ref,
    att_norm_ref,
    att_bias_ref,
    rel_ref,
    pair_mask_ref,
    gains_ref,
    bias_ref,
):
    gains_ref[0:1] = norm_in_ref[...]
    gains_ref[1:2] = norm_out_ref[...]
    gains_ref[2:3] = att_norm_ref[...]
    bias_ref[...] = att_bias_ref[...]
    tokens = pos_ref.shape[0]
    bins = table_ref.shape[0]
    sub = lax.broadcasted_iota(jnp.int32, (cols, bins), 0)
    lane = lax.broadcasted_iota(jnp.int32, (cols, bins), 1)
    hot = [None] * (tokens * tokens // cols)
    for half in range(tokens // cols):
        pos_vec = jnp.zeros((cols, bins), jnp.int32)
        mask_vec = jnp.zeros((cols, bins), jnp.int32)
        for c in range(cols):
            pos_vec = jnp.where(sub == c, pos_ref[half * cols + c], pos_vec)
            mask_vec = jnp.where(sub == c, mask_ref[half * cols + c], mask_vec)
        for i in range(tokens):
            at = i * (tokens // cols) + half
            bucket = jnp.clip(pos_ref[i] - pos_vec, -(bins // 2), bins // 2 - 1) + bins // 2
            hot[at] = (bucket == lane).astype(jnp.float32)
            pair_mask_ref[at * cols : (at + 1) * cols, :] = (mask_vec * mask_ref[i]).astype(jnp.float32)
    hot = jnp.concatenate(hot, axis=0).astype(jnp.bfloat16)
    rel_ref[...] = dot(hot, table_ref[...])


def whole_pair_kernel(
    row_dim,
    heads,
    order,
    held_ref,
    other_ref,
    mask_ref,
    rel_ref,
    pair_mask_ref,
    gains_ref,
    att_bias_ref,
    in_weight_ref,
    in_gate_ref,
    out_gate_ref,
    out_weight_ref,
    qkv_ref,
    att_gate_ref,
    att_out_ref,
    out_ref,
    base_ref,
    normed_ref,
    left_ref,
    right_ref,
    att_ref,
    upd_ref,
):
    rows, cols, width = held_ref.shape[1:]
    tokens = row_dim * rows
    head_dim = width // heads
    row_first = lax.axis_index("row") * rows
    col_first = pl.multiple_of(lax.axis_index("col") * cols, cols)
    f32, bf16 = jnp.float32, jnp.bfloat16

    row, col = lax.axis_index("row"), lax.axis_index("col")
    for ref, other in ((held_ref, 0), (other_ref, 1)):
        for at, (back, flip) in enumerate(order):
            owner = lax.rem(row + row_dim - back, row_dim)
            block = ref[at].astype(f32)
            for r in range(rows):
                first = (owner * rows + r) * tokens + (col ^ flip ^ other) * cols
                base_ref[pl.ds(pl.multiple_of(first, cols), cols), :] = block[r]

    base = base_ref[...] + rel_ref[...]
    base_ref[...] = base

    normed = layer_norm(base, gains_ref[0:1]).astype(bf16)
    normed_ref[...] = normed.astype(f32)
    projected = sigmoid(dot(normed, in_gate_ref[...])) * dot(normed, in_weight_ref[...])
    pair_mask = pair_mask_ref[...]
    left_ref[...] = round_bf16(projected[:, :width] * pair_mask)
    right_ref[...] = round_bf16(projected[:, width:] * pair_mask)

    right_at = [right_ref[pl.ds(col_first * tokens + m, cols, stride=tokens), :] for m in range(tokens)]
    products = []
    for i in range(tokens):
        total = left_ref[pl.ds(i * tokens, 1), :] * right_at[0]
        for m in range(1, tokens):
            total = total + left_ref[pl.ds(i * tokens + m, 1), :] * right_at[m]
        products.append(total)
    extra = [None] * rows
    for m in range(tokens):
        left_at = left_ref[pl.ds(m, tokens, stride=tokens), :]
        for r in range(rows):
            term = left_at * right_ref[pl.ds((row_first + r) * tokens + m, 1), :]
            extra[r] = term if m == 0 else extra[r] + term
    products = round_bf16(jnp.concatenate(products + extra, axis=0))

    def chosen(ref):
        own = [ref[pl.ds(i * tokens + col_first, cols), :] for i in range(tokens)]
        own += [ref[pl.ds(row_first + r, tokens, stride=tokens), :] for r in range(rows)]
        return jnp.concatenate(own, axis=0)

    normed_out = layer_norm(products, gains_ref[1:2]).astype(bf16)
    out_gate = sigmoid(dot(chosen(normed_ref).astype(bf16), out_gate_ref[...]))
    updated = chosen(base_ref) + out_gate * dot(normed_out, out_weight_ref[...])
    normed_att = layer_norm(updated, gains_ref[2:3]).astype(bf16)
    own_pairs = rows * cols
    column_pairs = tokens * cols
    upd_ref[...] = updated[:column_pairs]
    att_f = normed_att.astype(f32)
    att_ref[...] = att_f[:column_pairs]

    own_at = pl.ds(pl.multiple_of(row_first * cols, own_pairs), own_pairs)
    own = att_ref[own_at, :].astype(bf16)
    column = normed_att[:column_pairs]
    queries = dot(own, qkv_ref[:, :width])
    keys = dot(column, qkv_ref[:, width : 2 * width]).astype(bf16)
    values = dot(column, qkv_ref[:, 2 * width :]).astype(bf16)
    own_gate = sigmoid(dot(own, att_gate_ref[...]))

    bias = []
    for r in range(rows):
        part = att_f[column_pairs + r * tokens : column_pairs + (r + 1) * tokens]
        spread = jnp.concatenate(
            [jnp.broadcast_to(part[k : k + 1], (cols, width)) for k in range(tokens)], axis=0
        )
        bias.append(round_bf16(dot_t(att_bias_ref[...], spread.astype(bf16))))

    head_of = lax.broadcasted_iota(jnp.int32, (own_pairs, width), 1) // head_dim
    queries = round_bf16(queries)
    by_head = jnp.concatenate(
        [jnp.where(head_of == h, queries, 0.0) for h in range(heads)], axis=0
    ).astype(bf16)
    scores = dot_t(by_head, keys) * (1.0 / math.sqrt(head_dim))
    biases = jnp.concatenate(
        [jnp.broadcast_to(bias[r][h : h + 1], (cols, column_pairs)) for h in range(heads) for r in range(rows)],
        axis=0,
    )
    lane_row = lax.broadcasted_iota(jnp.int32, (1, column_pairs), 1)
    key_mask = jnp.zeros((1, column_pairs), jnp.int32)
    for k in range(tokens):
        key_mask = jnp.where(lane_row // cols == k, mask_ref[k], key_mask)
    key_bias = (key_mask.astype(f32) - 1.0) * 1000000000.0
    scores = scores + biases + key_bias
    same = (
        lax.broadcasted_iota(jnp.int32, scores.shape, 1) % cols
        == lax.broadcasted_iota(jnp.int32, scores.shape, 0) % cols
    )
    scores = jnp.where(same, scores, -jnp.inf)
    expo = jnp.exp(scores - jnp.max(scores, axis=-1, keepdims=True))
    totals = jnp.sum(expo, axis=-1, keepdims=True)
    mixed = dot(expo.astype(bf16), values) / totals
    attended = jnp.zeros((own_pairs, width), f32)
    for h in range(heads):
        attended = jnp.where(head_of == h, mixed[h * own_pairs : (h + 1) * own_pairs], attended)

    gated = (own_gate * attended).astype(bf16)
    result = upd_ref[own_at, :] + dot(gated, att_out_ref[...])
    out_ref[...] = result.reshape(rows, cols, width).astype(bf16)


def whole_pair_on_device(
    row_dim,
    pair_in,
    token_mask,
    positions,
    relpos_table,
    tri_norm_in,
    tri_in_weight,
    tri_in_gate,
    tri_out_gate,
    tri_norm_out,
    tri_out_weight,
    att_norm,
    att_qkv,
    att_gate,
    att_bias,
    att_out,
):
    rows, cols, width = pair_in.shape
    vmem = pl.BlockSpec(memory_space=pltpu.VMEM)
    smem = pl.BlockSpec(memory_space=pltpu.SMEM)
    params = pltpu.CompilerParams(vmem_limit_bytes=16 * 1024 * 1024)
    tokens, heads = row_dim * rows, att_bias.shape[1]

    def shift(values, back):
        pairs = [
            (row * 2 + core, (row + back) % row_dim * 2 + 1 - core) for row in range(row_dim) for core in range(2)
        ]
        return lax.ppermute(values, ("row", "col"), pairs)

    pieces = [pair_in[None]]
    places = [((0, 0),)]
    while sum(len(piece) for piece in places) < row_dim:
        ready = max(1, len(pieces) - 1)
        known = tuple(place for piece in places for place in piece)
        back = len(known)
        wanted = min(sum(len(piece) for piece in places[:ready]), row_dim - back)
        sent = jnp.concatenate(pieces[:ready], axis=0)[:wanted]
        pieces.append(shift(sent, back))
        places.append(tuple((back + rows_back, 1 - flip) for rows_back, flip in known[:wanted]))
    pieces[-2], positions = lax.optimization_barrier((pieces[-2], positions))
    held = jnp.concatenate(pieces, axis=0)
    order = tuple(place for piece in places for place in piece)

    wide_out = jax.ShapeDtypeStruct((tokens * tokens, width), jnp.float32)
    staged = pl.pallas_call(
        functools.partial(stage_kernel, cols),
        out_shape=[
            wide_out,
            wide_out,
            jax.ShapeDtypeStruct((3, width), jnp.float32),
            jax.ShapeDtypeStruct((heads, width), att_bias.dtype),
        ],
        in_specs=[smem] * 2 + [vmem] * 5,
        out_specs=[vmem] * 4,
        compiler_params=params,
        cost_estimate=pl.CostEstimate(flops=STAGE_FLOPS, bytes_accessed=2**20, transcendentals=0),
    )(
        token_mask,
        positions,
        relpos_table,
        tri_norm_in.reshape(1, width),
        tri_norm_out.reshape(1, width),
        att_norm.reshape(1, width),
        att_bias.T,
    )
    held, *staged = lax.optimization_barrier((held, *staged))
    swap = [(device, device ^ 1) for device in range(2 * row_dim)]
    gathered = (held, lax.ppermute(held, ("row", "col"), swap))

    weights = (tri_in_weight, tri_in_gate, tri_out_gate, tri_out_weight, att_qkv, att_gate, att_out)
    wide = pltpu.VMEM((tokens * tokens, width), jnp.float32)
    column = pltpu.VMEM((tokens * cols, width), jnp.float32)
    return pl.pallas_call(
        functools.partial(whole_pair_kernel, row_dim, heads, order),
        out_shape=jax.ShapeDtypeStruct(pair_in.shape, pair_in.dtype),
        in_specs=[vmem] * 2 + [smem] + [vmem] * (4 + len(weights)),
        out_specs=vmem,
        scratch_shapes=[wide] * 4 + [column] * 2,
        compiler_params=params,
    )(*gathered, token_mask, *staged, *weights)


def attend_column(query_col, key_col, value_col, bias_all, key_bias, block_rows):
    tok_total = query_col.shape[0]
    scale = 1.0 / math.sqrt(query_col.shape[2])

    def one_block(block_idx):
        scores = (
            jnp.einsum("ihe,khe->hik", query_col, key_col, preferred_element_type=jnp.float32)
            * scale
        )
        scores = scores + bias_all.astype(jnp.float32) + key_bias[None, None, :]
        row_max = jnp.max(scores, axis=-1, keepdims=True)
        expo_f = jnp.exp(scores - row_max)
        totals = jnp.sum(expo_f, axis=-1)
        weights = expo_f.astype(jnp.bfloat16)
        result = jnp.einsum("hik,khe->ihe", weights, value_col, preferred_element_type=jnp.float32)
        return result / jnp.transpose(totals)[:, :, None]

    blocks = lax.map(one_block, jnp.arange(tok_total // block_rows))
    return blocks.reshape(tok_total, query_col.shape[1], query_col.shape[2])


def column_attention(columns, att_qkv, att_gate, bias_all, key_bias, head_local, head_dim):
    tok_total, col_count, channels = columns.shape
    local_width = head_local * head_dim
    weight_three = att_qkv.reshape(channels, 3, channels)
    qkv_all = jnp.einsum(
        "kmc,ctd->tmkd", columns, weight_three, preferred_element_type=jnp.float32
    ).astype(jnp.bfloat16)
    qkv_all = qkv_all.reshape(3, col_count, tok_total, head_local, head_dim)
    gate_val = jax.nn.sigmoid(
        jnp.einsum("kmc,cd->kmd", columns, att_gate, preferred_element_type=jnp.float32)
    )
    block_rows = min(1024, tok_total)

    def one_column(triple):
        return attend_column(triple[0], triple[1], triple[2], bias_all, key_bias, block_rows)

    attended = lax.map(one_column, (qkv_all[0], qkv_all[1], qkv_all[2]))
    attended = jnp.transpose(attended, (1, 0, 2, 3)).reshape(tok_total, col_count, local_width)
    return (gate_val * attended).astype(jnp.bfloat16)


def split_pair_on_device(
    pair_in,
    token_mask,
    positions,
    relpos_table,
    tri_norm_in,
    tri_in_weight,
    tri_in_gate,
    tri_out_gate,
    tri_norm_out,
    tri_out_weight,
    att_norm,
    att_qkv,
    att_gate,
    att_bias,
    att_out,
):
    row_count, col_count, channels = pair_in.shape
    row_first = lax.axis_index("row") * row_count
    col_first = lax.axis_index("col") * col_count
    mask_float = token_mask.astype(jnp.float32)
    row_mask = lax.dynamic_slice_in_dim(mask_float, row_first, row_count)
    col_mask = lax.dynamic_slice_in_dim(mask_float, col_first, col_count)
    row_pos = lax.dynamic_slice_in_dim(positions, row_first, row_count)
    col_pos = lax.dynamic_slice_in_dim(positions, col_first, col_count)
    bin_count = relpos_table.shape[0]
    bin_centre = bin_count // 2
    bucket = jnp.clip(row_pos[:, None] - col_pos[None, :], -bin_centre, bin_centre - 1) + bin_centre
    onehot = (bucket[:, :, None] == jnp.arange(bin_count, dtype=jnp.int32)[None, None, :]).astype(
        jnp.bfloat16
    )
    residual = pair_in.astype(jnp.float32) + jnp.einsum(
        "rjb,bc->rjc", onehot, relpos_table, preferred_element_type=jnp.float32
    )
    normed = layer_norm(residual, tri_norm_in).astype(jnp.bfloat16)
    pair_mask = row_mask[:, None] * col_mask[None, :]
    gate_in = jnp.einsum("rjc,cd->drj", normed, tri_in_gate, preferred_element_type=jnp.float32)
    proj_in = jnp.einsum("rjc,cd->drj", normed, tri_in_weight, preferred_element_type=jnp.float32)
    projected = (jax.nn.sigmoid(gate_in) * proj_in * pair_mask[None, :, :]).astype(jnp.bfloat16)
    left_ch, right_ch = (
        lax.all_to_all(projected[:channels], "row", split_axis=0, concat_axis=1, tiled=True),
        lax.all_to_all(projected[channels:], "row", split_axis=0, concat_axis=1, tiled=True),
    )
    right_rows = lax.all_to_all(right_ch, "col", split_axis=1, concat_axis=2, tiled=True)
    product_sum = jnp.einsum(
        "cik,cjk->cij",
        lax.all_gather(left_ch, "col", axis=2, tiled=True),
        right_rows,
        preferred_element_type=jnp.float32,
    )
    products = product_sum.astype(jnp.bfloat16)
    product_tile = lax.all_to_all(products, "row", split_axis=1, concat_axis=0, tiled=True)
    tri_x = jnp.transpose(product_tile, (1, 2, 0)).astype(jnp.float32)
    normed_out = layer_norm(tri_x, tri_norm_out).astype(jnp.bfloat16)
    out_gate = jax.nn.sigmoid(
        jnp.einsum("rjc,cd->rjd", normed, tri_out_gate, preferred_element_type=jnp.float32)
    )
    residual = residual + out_gate * jnp.einsum(
        "rjc,cd->rjd", normed_out, tri_out_weight, preferred_element_type=jnp.float32
    )
    normed_att = layer_norm(residual, att_norm).astype(jnp.bfloat16)
    bias_piece = jnp.einsum(
        "kic,ch->hik", normed_att, att_bias, preferred_element_type=jnp.float32
    ).astype(jnp.bfloat16)
    key_bias = (mask_float - 1.0) * 1000000000.0
    head_count = att_bias.shape[1]
    head_dim = channels // head_count
    columns = lax.all_to_all(normed_att, "row", split_axis=1, concat_axis=0, tiled=True)
    bias_half = lax.all_gather(bias_piece, "col", axis=1, tiled=True)
    bias_all = lax.all_gather(bias_half, "row", axis=2, tiled=True)
    gated = column_attention(columns, att_qkv, att_gate, bias_all, key_bias, head_count, head_dim)
    gated_tile = lax.all_to_all(gated, "row", split_axis=0, concat_axis=1, tiled=True)
    update = jnp.einsum("rjc,cd->rjd", gated_tile, att_out, preferred_element_type=jnp.float32)
    return (residual + update).astype(jnp.bfloat16)


def on_device(row_dim, col_dim, pair_in, *others):
    rows, cols, width = pair_in.shape
    tokens = row_dim * rows
    whole_bytes = tokens * tokens * width * pair_in.dtype.itemsize
    blocks = row_dim * col_dim
    tiled = cols % 8 == 0 and width % 128 == 0 and blocks & (blocks - 1) == 0 and blocks >= 4 and col_dim == 2
    if whole_bytes <= WHOLE_PAIR_BYTES and tiled:
        return whole_pair_on_device(row_dim, pair_in, *others)
    return split_pair_on_device(pair_in, *others)


def solution(mesh):
    return jax.shard_map(
        functools.partial(on_device, mesh.shape["row"], mesh.shape["col"]),
        mesh=mesh,
        in_specs=(P(("groups", "row"), "col", None), P("groups"), P("groups")) + (P(),) * 12,
        out_specs=P(("groups", "row"), "col", None),
        check_vma=False,
    )
```

```python
import functools
import math

import jax
import jax.numpy as jnp
from jax import lax
from jax.experimental import pallas as pl
from jax.experimental.pallas import tpu as pltpu
from jax.sharding import PartitionSpec as P

epsilon = 1e-05

WHOLE_PAIR_BYTES = 256 * 1024
STAGE_FLOPS = 10**9


def layer_norm(values, gain):
    mean_val = jnp.mean(values, axis=-1, keepdims=True)
    centred = values - mean_val
    var_val = jnp.mean(centred * centred, axis=-1, keepdims=True)
    return centred * lax.rsqrt(var_val + epsilon) * gain


def sigmoid(values):
    return 0.5 * jnp.tanh(0.5 * values) + 0.5


def dot(left, right):
    return jnp.dot(left, right, preferred_element_type=jnp.float32)


def dot_t(left, right):
    return lax.dot_general(
        left, right, (((1,), (1,)), ((), ())), preferred_element_type=jnp.float32
    )


def round_bf16(values):
    return values.astype(jnp.bfloat16).astype(jnp.float32)


def own_kernel(pair_ref, chip_ref):
    chip_ref[0] = pair_ref[...]


def stage_kernel(
    cols,
    mask_ref,
    pos_ref,
    table_ref,
    norm_in_ref,
    norm_out_ref,
    att_norm_ref,
    att_bias_ref,
    rel_ref,
    pair_mask_ref,
    gains_ref,
    bias_ref,
    key_bias_ref,
):
    gains_ref[0:1] = norm_in_ref[...]
    gains_ref[1:2] = norm_out_ref[...]
    gains_ref[2:3] = att_norm_ref[...]
    bias_ref[...] = att_bias_ref[...]
    tokens = pos_ref.shape[0]
    bins = table_ref.shape[0]
    sub = lax.broadcasted_iota(jnp.int32, (cols, bins), 0)
    lane = lax.broadcasted_iota(jnp.int32, (cols, bins), 1)
    hot = [None] * (tokens * tokens // cols)
    for half in range(tokens // cols):
        pos_vec = jnp.zeros((cols, bins), jnp.int32)
        mask_vec = jnp.zeros((cols, bins), jnp.int32)
        for c in range(cols):
            pos_vec = jnp.where(sub == c, pos_ref[half * cols + c], pos_vec)
            mask_vec = jnp.where(sub == c, mask_ref[half * cols + c], mask_vec)
        for i in range(tokens):
            at = i * (tokens // cols) + half
            bucket = jnp.clip(pos_ref[i] - pos_vec, -(bins // 2), bins // 2 - 1) + bins // 2
            hot[at] = (bucket == lane).astype(jnp.float32)
            pair_mask_ref[at * cols : (at + 1) * cols, :] = (mask_vec * mask_ref[i]).astype(jnp.float32)
    key_sub = lax.broadcasted_iota(jnp.int32, key_bias_ref.shape, 0)
    key_lane = lax.broadcasted_iota(jnp.int32, key_bias_ref.shape, 1)
    key_mask = jnp.zeros(key_bias_ref.shape, jnp.int32)
    for k in range(tokens):
        key_mask = jnp.where(key_lane // cols == k, mask_ref[k], key_mask)
    key_bias = (key_mask.astype(jnp.float32) - 1.0) * 1000000000.0
    key_bias_ref[...] = jnp.where(key_lane % cols == key_sub, key_bias, -jnp.inf)
    hot = jnp.concatenate(hot, axis=0).astype(jnp.bfloat16)
    rel_ref[...] = dot(hot, table_ref[...])


def whole_pair_kernel(
    row_dim,
    heads,
    order,
    held_ref,
    other_ref,
    rel_ref,
    pair_mask_ref,
    gains_ref,
    att_bias_ref,
    key_bias_ref,
    in_weight_ref,
    in_gate_ref,
    out_gate_ref,
    out_weight_ref,
    qkv_ref,
    att_gate_ref,
    att_out_ref,
    out_ref,
    base_ref,
    normed_ref,
    left_ref,
    right_ref,
    att_ref,
    upd_ref,
):
    rows, cols, width = held_ref.shape[1:]
    tokens = row_dim * rows
    head_dim = width // heads
    row_first = lax.axis_index("row") * rows
    col_first = pl.multiple_of(lax.axis_index("col") * cols, cols)
    f32, bf16 = jnp.float32, jnp.bfloat16

    me = lax.axis_index("row") * 2 + lax.axis_index("col")
    for ref, flip in ((held_ref, 0), (other_ref, 1)):
        for at, place in enumerate(order):
            owner = me ^ (place ^ flip)
            block = ref[at].astype(f32)
            for r in range(rows):
                first = (owner // 2 * rows + r) * tokens + owner % 2 * cols
                base_ref[pl.ds(pl.multiple_of(first, cols), cols), :] = block[r]

    base = base_ref[...] + rel_ref[...]
    base_ref[...] = base

    normed = layer_norm(base, gains_ref[0:1]).astype(bf16)
    normed_ref[...] = normed.astype(f32)
    projected = sigmoid(dot(normed, in_gate_ref[...])) * dot(normed, in_weight_ref[...])
    pair_mask = pair_mask_ref[...]
    left_ref[...] = round_bf16(projected[:, :width] * pair_mask)
    right_ref[...] = round_bf16(projected[:, width:] * pair_mask)

    right_at = [right_ref[pl.ds(col_first * tokens + m, cols, stride=tokens), :] for m in range(tokens)]
    products = []
    for i in range(tokens):
        total = left_ref[pl.ds(i * tokens, 1), :] * right_at[0]
        for m in range(1, tokens):
            total = total + left_ref[pl.ds(i * tokens + m, 1), :] * right_at[m]
        products.append(total)
    extra = [None] * rows
    for m in range(tokens):
        left_at = left_ref[pl.ds(m, tokens, stride=tokens), :]
        for r in range(rows):
            term = left_at * right_ref[pl.ds((row_first + r) * tokens + m, 1), :]
            extra[r] = term if m == 0 else extra[r] + term
    products = round_bf16(jnp.concatenate(products + extra, axis=0))

    def chosen(ref):
        own = [ref[pl.ds(i * tokens + col_first, cols), :] for i in range(tokens)]
        own += [ref[pl.ds(row_first + r, tokens, stride=tokens), :] for r in range(rows)]
        return jnp.concatenate(own, axis=0)

    normed_out = layer_norm(products, gains_ref[1:2]).astype(bf16)
    out_gate = sigmoid(dot(chosen(normed_ref).astype(bf16), out_gate_ref[...]))
    updated = chosen(base_ref) + out_gate * dot(normed_out, out_weight_ref[...])
    normed_att = layer_norm(updated, gains_ref[2:3]).astype(bf16)
    own_pairs = rows * cols
    column_pairs = tokens * cols
    upd_ref[...] = updated[:column_pairs]
    att_f = normed_att.astype(f32)
    att_ref[...] = att_f[:column_pairs]

    own_at = pl.ds(pl.multiple_of(row_first * cols, own_pairs), own_pairs)
    own = att_ref[own_at, :].astype(bf16)
    column = normed_att[:column_pairs]
    queries = dot(own, qkv_ref[:, :width])
    keys = dot(column, qkv_ref[:, width : 2 * width]).astype(bf16)
    values = dot(column, qkv_ref[:, 2 * width :]).astype(bf16)
    own_gate = sigmoid(dot(own, att_gate_ref[...]))

    bias = []
    for r in range(rows):
        part = att_f[column_pairs + r * tokens : column_pairs + (r + 1) * tokens]
        spread = jnp.concatenate(
            [jnp.broadcast_to(part[k : k + 1], (cols, width)) for k in range(tokens)], axis=0
        )
        bias.append(round_bf16(dot_t(att_bias_ref[...], spread.astype(bf16))))

    head_of = lax.broadcasted_iota(jnp.int32, (own_pairs, width), 1) // head_dim
    queries = round_bf16(queries)
    by_head = jnp.concatenate(
        [jnp.where(head_of == h, queries, 0.0) for h in range(heads)], axis=0
    ).astype(bf16)
    scores = dot_t(by_head, keys) * (1.0 / math.sqrt(head_dim))
    biases = jnp.concatenate(
        [jnp.broadcast_to(bias[r][h : h + 1], (cols, column_pairs)) for h in range(heads) for r in range(rows)],
        axis=0,
    )
    key_bias = jnp.concatenate([key_bias_ref[...]] * (heads * rows), axis=0)
    scores = scores + biases + key_bias
    expo = jnp.exp(scores - jnp.max(scores, axis=-1, keepdims=True))
    totals = jnp.sum(expo, axis=-1, keepdims=True)
    mixed = dot(expo.astype(bf16), values) / totals
    attended = jnp.zeros((own_pairs, width), f32)
    for h in range(heads):
        attended = jnp.where(head_of == h, mixed[h * own_pairs : (h + 1) * own_pairs], attended)

    gated = (own_gate * attended).astype(bf16)
    result = upd_ref[own_at, :] + dot(gated, att_out_ref[...])
    out_ref[...] = result.reshape(rows, cols, width).astype(bf16)


def whole_pair_on_device(
    row_dim,
    pair_in,
    token_mask,
    positions,
    relpos_table,
    tri_norm_in,
    tri_in_weight,
    tri_in_gate,
    tri_out_gate,
    tri_norm_out,
    tri_out_weight,
    att_norm,
    att_qkv,
    att_gate,
    att_bias,
    att_out,
):
    rows, cols, width = pair_in.shape
    vmem = pl.BlockSpec(memory_space=pltpu.VMEM)
    smem = pl.BlockSpec(memory_space=pltpu.SMEM)
    params = pltpu.CompilerParams(vmem_limit_bytes=16 * 1024 * 1024)
    tokens, heads = row_dim * rows, att_bias.shape[1]

    blocks = 2 * row_dim

    def move(values, step):
        return lax.ppermute(values, ("row", "col"), [(device, device ^ step) for device in range(blocks)])

    held = pl.pallas_call(
        own_kernel,
        out_shape=jax.ShapeDtypeStruct((2,) + pair_in.shape, pair_in.dtype),
        in_specs=[vmem],
        out_specs=vmem,
        compiler_params=params,
    )(pair_in)
    held, order = held.at[1].set(move(pair_in, 3)), (0, 3)
    while len(order) < row_dim:
        step = 2 * len(order) + 1
        held = jnp.concatenate([held, move(held, step)], axis=0)
        order += tuple(place ^ step for place in order)

    wide_out = jax.ShapeDtypeStruct((tokens * tokens, width), jnp.float32)
    staged = pl.pallas_call(
        functools.partial(stage_kernel, cols),
        out_shape=[
            wide_out,
            wide_out,
            jax.ShapeDtypeStruct((3, width), jnp.float32),
            jax.ShapeDtypeStruct((heads, width), att_bias.dtype),
            jax.ShapeDtypeStruct((cols, tokens * cols), jnp.float32),
        ],
        in_specs=[smem] * 2 + [vmem] * 5,
        out_specs=[vmem] * 5,
        compiler_params=params,
        cost_estimate=pl.CostEstimate(flops=STAGE_FLOPS, bytes_accessed=2**20, transcendentals=0),
    )(
        token_mask,
        positions,
        relpos_table,
        tri_norm_in.reshape(1, width),
        tri_norm_out.reshape(1, width),
        att_norm.reshape(1, width),
        att_bias.T,
    )
    held, *staged = lax.optimization_barrier((held, *staged))
    gathered = (held, move(held, 1))

    weights = (tri_in_weight, tri_in_gate, tri_out_gate, tri_out_weight, att_qkv, att_gate, att_out)
    wide = pltpu.VMEM((tokens * tokens, width), jnp.float32)
    column = pltpu.VMEM((tokens * cols, width), jnp.float32)
    return pl.pallas_call(
        functools.partial(whole_pair_kernel, row_dim, heads, order),
        out_shape=jax.ShapeDtypeStruct(pair_in.shape, pair_in.dtype),
        in_specs=[vmem] * (7 + len(weights)),
        out_specs=vmem,
        scratch_shapes=[wide] * 4 + [column] * 2,
        compiler_params=params,
    )(*gathered, *staged, *weights)


def attend_column(query_col, key_col, value_col, bias_all, key_bias, block_rows):
    tok_total = query_col.shape[0]
    scale = 1.0 / math.sqrt(query_col.shape[2])

    def one_block(block_idx):
        scores = (
            jnp.einsum("ihe,khe->hik", query_col, key_col, preferred_element_type=jnp.float32)
            * scale
        )
        scores = scores + bias_all.astype(jnp.float32) + key_bias[None, None, :]
        row_max = jnp.max(scores, axis=-1, keepdims=True)
        expo_f = jnp.exp(scores - row_max)
        totals = jnp.sum(expo_f, axis=-1)
        weights = expo_f.astype(jnp.bfloat16)
        result = jnp.einsum("hik,khe->ihe", weights, value_col, preferred_element_type=jnp.float32)
        return result / jnp.transpose(totals)[:, :, None]

    blocks = lax.map(one_block, jnp.arange(tok_total // block_rows))
    return blocks.reshape(tok_total, query_col.shape[1], query_col.shape[2])


def column_attention(columns, att_qkv, att_gate, bias_all, key_bias, head_local, head_dim):
    tok_total, col_count, channels = columns.shape
    local_width = head_local * head_dim
    weight_three = att_qkv.reshape(channels, 3, channels)
    qkv_all = jnp.einsum(
        "kmc,ctd->tmkd", columns, weight_three, preferred_element_type=jnp.float32
    ).astype(jnp.bfloat16)
    qkv_all = qkv_all.reshape(3, col_count, tok_total, head_local, head_dim)
    gate_val = jax.nn.sigmoid(
        jnp.einsum("kmc,cd->kmd", columns, att_gate, preferred_element_type=jnp.float32)
    )
    block_rows = min(1024, tok_total)

    def one_column(triple):
        return attend_column(triple[0], triple[1], triple[2], bias_all, key_bias, block_rows)

    attended = lax.map(one_column, (qkv_all[0], qkv_all[1], qkv_all[2]))
    attended = jnp.transpose(attended, (1, 0, 2, 3)).reshape(tok_total, col_count, local_width)
    return (gate_val * attended).astype(jnp.bfloat16)


def split_pair_on_device(
    pair_in,
    token_mask,
    positions,
    relpos_table,
    tri_norm_in,
    tri_in_weight,
    tri_in_gate,
    tri_out_gate,
    tri_norm_out,
    tri_out_weight,
    att_norm,
    att_qkv,
    att_gate,
    att_bias,
    att_out,
):
    row_count, col_count, channels = pair_in.shape
    row_first = lax.axis_index("row") * row_count
    col_first = lax.axis_index("col") * col_count
    mask_float = token_mask.astype(jnp.float32)
    row_mask = lax.dynamic_slice_in_dim(mask_float, row_first, row_count)
    col_mask = lax.dynamic_slice_in_dim(mask_float, col_first, col_count)
    row_pos = lax.dynamic_slice_in_dim(positions, row_first, row_count)
    col_pos = lax.dynamic_slice_in_dim(positions, col_first, col_count)
    bin_count = relpos_table.shape[0]
    bin_centre = bin_count // 2
    bucket = jnp.clip(row_pos[:, None] - col_pos[None, :], -bin_centre, bin_centre - 1) + bin_centre
    onehot = (bucket[:, :, None] == jnp.arange(bin_count, dtype=jnp.int32)[None, None, :]).astype(
        jnp.bfloat16
    )
    residual = pair_in.astype(jnp.float32) + jnp.einsum(
        "rjb,bc->rjc", onehot, relpos_table, preferred_element_type=jnp.float32
    )
    normed = layer_norm(residual, tri_norm_in).astype(jnp.bfloat16)
    pair_mask = row_mask[:, None] * col_mask[None, :]
    gate_in = jnp.einsum("rjc,cd->drj", normed, tri_in_gate, preferred_element_type=jnp.float32)
    proj_in = jnp.einsum("rjc,cd->drj", normed, tri_in_weight, preferred_element_type=jnp.float32)
    projected = (jax.nn.sigmoid(gate_in) * proj_in * pair_mask[None, :, :]).astype(jnp.bfloat16)
    left_ch, right_ch = (
        lax.all_to_all(projected[:channels], "row", split_axis=0, concat_axis=1, tiled=True),
        lax.all_to_all(projected[channels:], "row", split_axis=0, concat_axis=1, tiled=True),
    )
    right_rows = lax.all_to_all(right_ch, "col", split_axis=1, concat_axis=2, tiled=True)
    product_sum = jnp.einsum(
        "cik,cjk->cij",
        lax.all_gather(left_ch, "col", axis=2, tiled=True),
        right_rows,
        preferred_element_type=jnp.float32,
    )
    products = product_sum.astype(jnp.bfloat16)
    product_tile = lax.all_to_all(products, "row", split_axis=1, concat_axis=0, tiled=True)
    tri_x = jnp.transpose(product_tile, (1, 2, 0)).astype(jnp.float32)
    normed_out = layer_norm(tri_x, tri_norm_out).astype(jnp.bfloat16)
    out_gate = jax.nn.sigmoid(
        jnp.einsum("rjc,cd->rjd", normed, tri_out_gate, preferred_element_type=jnp.float32)
    )
    residual = residual + out_gate * jnp.einsum(
        "rjc,cd->rjd", normed_out, tri_out_weight, preferred_element_type=jnp.float32
    )
    normed_att = layer_norm(residual, att_norm).astype(jnp.bfloat16)
    bias_piece = jnp.einsum(
        "kic,ch->hik", normed_att, att_bias, preferred_element_type=jnp.float32
    ).astype(jnp.bfloat16)
    key_bias = (mask_float - 1.0) * 1000000000.0
    head_count = att_bias.shape[1]
    head_dim = channels // head_count
    columns = lax.all_to_all(normed_att, "row", split_axis=1, concat_axis=0, tiled=True)
    bias_half = lax.all_gather(bias_piece, "col", axis=1, tiled=True)
    bias_all = lax.all_gather(bias_half, "row", axis=2, tiled=True)
    gated = column_attention(columns, att_qkv, att_gate, bias_all, key_bias, head_count, head_dim)
    gated_tile = lax.all_to_all(gated, "row", split_axis=0, concat_axis=1, tiled=True)
    update = jnp.einsum("rjc,cd->rjd", gated_tile, att_out, preferred_element_type=jnp.float32)
    return (residual + update).astype(jnp.bfloat16)


def on_device(row_dim, col_dim, pair_in, *others):
    rows, cols, width = pair_in.shape
    tokens = row_dim * rows
    whole_bytes = tokens * tokens * width * pair_in.dtype.itemsize
    blocks = row_dim * col_dim
    tiled = cols % 8 == 0 and width % 128 == 0 and blocks & (blocks - 1) == 0 and blocks >= 4 and col_dim == 2
    if whole_bytes <= WHOLE_PAIR_BYTES and tiled:
        return whole_pair_on_device(row_dim, pair_in, *others)
    return split_pair_on_device(pair_in, *others)


def solution(mesh):
    return jax.shard_map(
        functools.partial(on_device, mesh.shape["row"], mesh.shape["col"]),
        mesh=mesh,
        in_specs=(P(("groups", "row"), "col", None), P("groups"), P("groups")) + (P(),) * 12,
        out_specs=P(("groups", "row"), "col", None),
        check_vma=False,
    )
```

```python
import functools
import math

import jax
import jax.numpy as jnp
from jax import lax
from jax.experimental import pallas as pl
from jax.experimental.pallas import tpu as pltpu
from jax.sharding import PartitionSpec as P

epsilon = 1e-05

WHOLE_PAIR_BYTES = 256 * 1024
STAGE_FLOPS = 10**9


def layer_norm(values, gain):
    mean_val = jnp.mean(values, axis=-1, keepdims=True)
    centred = values - mean_val
    var_val = jnp.mean(centred * centred, axis=-1, keepdims=True)
    return centred * lax.rsqrt(var_val + epsilon) * gain


def sigmoid(values):
    return 0.5 * jnp.tanh(0.5 * values) + 0.5


def dot(left, right):
    return jnp.dot(left, right, preferred_element_type=jnp.float32)


def dot_t(left, right):
    return lax.dot_general(
        left, right, (((1,), (1,)), ((), ())), preferred_element_type=jnp.float32
    )


def round_bf16(values):
    return values.astype(jnp.bfloat16).astype(jnp.float32)


def token_column(ref, first, shape):
    sub = lax.broadcasted_iota(jnp.int32, shape, 0)
    column = jnp.zeros(shape, jnp.int32)
    for s in range(shape[0]):
        column = jnp.where(sub == s, ref[first + s], column)
    return column


def own_kernel(mask_ref, pair_ref, att_bias_ref, chip_ref, bias_ref, pair_mask_ref, key_bias_ref):
    chip_ref[0] = pair_ref[...]
    bias_ref[...] = att_bias_ref[...]
    tokens = mask_ref.shape[0]
    cols, width = key_bias_ref.shape[0], pair_mask_ref.shape[1]
    for half in range(tokens // cols):
        column = token_column(mask_ref, half * cols, (cols, width))
        for i in range(tokens):
            first = i * tokens + half * cols
            pair_mask_ref[first : first + cols, :] = (column * mask_ref[i]).astype(jnp.float32)
    sub = lax.broadcasted_iota(jnp.int32, key_bias_ref.shape, 0)
    lane = lax.broadcasted_iota(jnp.int32, key_bias_ref.shape, 1)
    key_mask = jnp.zeros(key_bias_ref.shape, jnp.int32)
    for k in range(tokens):
        key_mask = jnp.where(lane // cols == k, mask_ref[k], key_mask)
    key_bias = (key_mask.astype(jnp.float32) - 1.0) * 1000000000.0
    key_bias_ref[...] = jnp.where(lane % cols == sub, key_bias, -jnp.inf)


def stage_kernel(cols, pos_ref, table_ref, norm_in_ref, norm_out_ref, att_norm_ref, rel_ref, gains_ref):
    gains_ref[0:1] = norm_in_ref[...]
    gains_ref[1:2] = norm_out_ref[...]
    gains_ref[2:3] = att_norm_ref[...]
    tokens = pos_ref.shape[0]
    bins = table_ref.shape[0]
    lane = lax.broadcasted_iota(jnp.int32, (cols, bins), 1)
    hot = [None] * (tokens * tokens // cols)
    for half in range(tokens // cols):
        column = token_column(pos_ref, half * cols, (cols, bins))
        for i in range(tokens):
            bucket = jnp.clip(pos_ref[i] - column, -(bins // 2), bins // 2 - 1) + bins // 2
            hot[i * (tokens // cols) + half] = (bucket == lane).astype(jnp.float32)
    hot = jnp.concatenate(hot, axis=0).astype(jnp.bfloat16)
    rel_ref[...] = dot(hot, table_ref[...])


def whole_pair_kernel(
    row_dim,
    heads,
    order,
    held_ref,
    other_ref,
    rel_ref,
    pair_mask_ref,
    gains_ref,
    att_bias_ref,
    key_bias_ref,
    in_weight_ref,
    in_gate_ref,
    out_gate_ref,
    out_weight_ref,
    qkv_ref,
    att_gate_ref,
    att_out_ref,
    out_ref,
    base_ref,
    normed_ref,
    left_ref,
    right_ref,
    att_ref,
    upd_ref,
):
    rows, cols, width = held_ref.shape[1:]
    tokens = row_dim * rows
    head_dim = width // heads
    row_first = lax.axis_index("row") * rows
    col_first = pl.multiple_of(lax.axis_index("col") * cols, cols)
    f32, bf16 = jnp.float32, jnp.bfloat16

    me = lax.axis_index("row") * 2 + lax.axis_index("col")
    for ref, flip in ((held_ref, 0), (other_ref, 1)):
        for at, place in enumerate(order):
            owner = me ^ (place ^ flip)
            block = ref[at].astype(f32)
            for r in range(rows):
                first = (owner // 2 * rows + r) * tokens + owner % 2 * cols
                base_ref[pl.ds(pl.multiple_of(first, cols), cols), :] = block[r]

    base = base_ref[...] + rel_ref[...]
    base_ref[...] = base

    normed = layer_norm(base, gains_ref[0:1]).astype(bf16)
    normed_ref[...] = normed.astype(f32)
    projected = sigmoid(dot(normed, in_gate_ref[...])) * dot(normed, in_weight_ref[...])
    pair_mask = pair_mask_ref[...]
    left_ref[...] = round_bf16(projected[:, :width] * pair_mask)
    right_ref[...] = round_bf16(projected[:, width:] * pair_mask)

    right_at = [right_ref[pl.ds(col_first * tokens + m, cols, stride=tokens), :] for m in range(tokens)]
    products = []
    for i in range(tokens):
        total = left_ref[pl.ds(i * tokens, 1), :] * right_at[0]
        for m in range(1, tokens):
            total = total + left_ref[pl.ds(i * tokens + m, 1), :] * right_at[m]
        products.append(total)
    extra = [None] * rows
    for m in range(tokens):
        left_at = left_ref[pl.ds(m, tokens, stride=tokens), :]
        for r in range(rows):
            term = left_at * right_ref[pl.ds((row_first + r) * tokens + m, 1), :]
            extra[r] = term if m == 0 else extra[r] + term
    products = round_bf16(jnp.concatenate(products + extra, axis=0))

    def chosen(ref):
        own = [ref[pl.ds(i * tokens + col_first, cols), :] for i in range(tokens)]
        own += [ref[pl.ds(row_first + r, tokens, stride=tokens), :] for r in range(rows)]
        return jnp.concatenate(own, axis=0)

    normed_out = layer_norm(products, gains_ref[1:2]).astype(bf16)
    out_gate = sigmoid(dot(chosen(normed_ref).astype(bf16), out_gate_ref[...]))
    updated = chosen(base_ref) + out_gate * dot(normed_out, out_weight_ref[...])
    normed_att = layer_norm(updated, gains_ref[2:3]).astype(bf16)
    own_pairs = rows * cols
    column_pairs = tokens * cols
    upd_ref[...] = updated[:column_pairs]
    att_f = normed_att.astype(f32)
    att_ref[...] = att_f[:column_pairs]

    own_at = pl.ds(pl.multiple_of(row_first * cols, own_pairs), own_pairs)
    own = att_ref[own_at, :].astype(bf16)
    column = normed_att[:column_pairs]
    queries = dot(own, qkv_ref[:, :width])
    keys = dot(column, qkv_ref[:, width : 2 * width]).astype(bf16)
    values = dot(column, qkv_ref[:, 2 * width :]).astype(bf16)
    own_gate = sigmoid(dot(own, att_gate_ref[...]))

    bias = []
    for r in range(rows):
        part = att_f[column_pairs + r * tokens : column_pairs + (r + 1) * tokens]
        spread = jnp.concatenate(
            [jnp.broadcast_to(part[k : k + 1], (cols, width)) for k in range(tokens)], axis=0
        )
        bias.append(round_bf16(dot_t(att_bias_ref[...], spread.astype(bf16))))

    head_of = lax.broadcasted_iota(jnp.int32, (own_pairs, width), 1) // head_dim
    queries = round_bf16(queries)
    by_head = jnp.concatenate(
        [jnp.where(head_of == h, queries, 0.0) for h in range(heads)], axis=0
    ).astype(bf16)
    scores = dot_t(by_head, keys) * (1.0 / math.sqrt(head_dim))
    biases = jnp.concatenate(
        [jnp.broadcast_to(bias[r][h : h + 1], (cols, column_pairs)) for h in range(heads) for r in range(rows)],
        axis=0,
    )
    key_bias = jnp.concatenate([key_bias_ref[...]] * (heads * rows), axis=0)
    scores = scores + biases + key_bias
    expo = jnp.exp(scores - jnp.max(scores, axis=-1, keepdims=True))
    totals = jnp.sum(expo, axis=-1, keepdims=True)
    mixed = dot(expo.astype(bf16), values) / totals
    attended = jnp.zeros((own_pairs, width), f32)
    for h in range(heads):
        attended = jnp.where(head_of == h, mixed[h * own_pairs : (h + 1) * own_pairs], attended)

    gated = (own_gate * attended).astype(bf16)
    result = upd_ref[own_at, :] + dot(gated, att_out_ref[...])
    out_ref[...] = result.reshape(rows, cols, width).astype(bf16)


def whole_pair_on_device(
    row_dim,
    pair_in,
    token_mask,
    positions,
    relpos_table,
    tri_norm_in,
    tri_in_weight,
    tri_in_gate,
    tri_out_gate,
    tri_norm_out,
    tri_out_weight,
    att_norm,
    att_qkv,
    att_gate,
    att_bias,
    att_out,
):
    rows, cols, width = pair_in.shape
    vmem = pl.BlockSpec(memory_space=pltpu.VMEM)
    smem = pl.BlockSpec(memory_space=pltpu.SMEM)
    params = pltpu.CompilerParams(vmem_limit_bytes=16 * 1024 * 1024)
    tokens, heads = row_dim * rows, att_bias.shape[1]

    beside = pl.CostEstimate(flops=STAGE_FLOPS, bytes_accessed=2**20, transcendentals=0)
    wide_out = jax.ShapeDtypeStruct((tokens * tokens, width), jnp.float32)
    rel, gains = pl.pallas_call(
        functools.partial(stage_kernel, cols),
        out_shape=[wide_out, jax.ShapeDtypeStruct((3, width), jnp.float32)],
        in_specs=[smem] + [vmem] * 4,
        out_specs=[vmem] * 2,
        compiler_params=params,
        cost_estimate=beside,
    )(
        positions,
        relpos_table,
        tri_norm_in.reshape(1, width),
        tri_norm_out.reshape(1, width),
        att_norm.reshape(1, width),
    )

    blocks = 2 * row_dim

    def move(values, step):
        return lax.ppermute(values, ("row", "col"), [(device, device ^ step) for device in range(blocks)])

    line = tuple(range(blocks - 3, 1, -4))
    held, bias, pair_mask, key_bias = pl.pallas_call(
        own_kernel,
        out_shape=[
            jax.ShapeDtypeStruct((1 + len(line),) + pair_in.shape, pair_in.dtype),
            jax.ShapeDtypeStruct((heads, width), att_bias.dtype),
            wide_out,
            jax.ShapeDtypeStruct((cols, tokens * cols), jnp.float32),
        ],
        in_specs=[smem] + [vmem] * 2,
        out_specs=[vmem] * 4,
        compiler_params=params,
        cost_estimate=beside,
    )(token_mask, pair_in, att_bias.T)
    for at, step in enumerate(line):
        held = held.at[1 + at].set(move(pair_in, step))
    order = (0,) + line
    held = jnp.concatenate([held, move(held, 3)], axis=0)
    order += tuple(place ^ 3 for place in order)
    held, rel, gains = lax.optimization_barrier((held, rel, gains))
    gathered = (held, move(held, 1))

    weights = (tri_in_weight, tri_in_gate, tri_out_gate, tri_out_weight, att_qkv, att_gate, att_out)
    wide = pltpu.VMEM((tokens * tokens, width), jnp.float32)
    column = pltpu.VMEM((tokens * cols, width), jnp.float32)
    return pl.pallas_call(
        functools.partial(whole_pair_kernel, row_dim, heads, order),
        out_shape=jax.ShapeDtypeStruct(pair_in.shape, pair_in.dtype),
        in_specs=[vmem] * (7 + len(weights)),
        out_specs=vmem,
        scratch_shapes=[wide] * 4 + [column] * 2,
        compiler_params=params,
    )(*gathered, rel, pair_mask, gains, bias, key_bias, *weights)


def attend_column(query_col, key_col, value_col, bias_all, key_bias, block_rows):
    tok_total = query_col.shape[0]
    scale = 1.0 / math.sqrt(query_col.shape[2])

    def one_block(block_idx):
        scores = (
            jnp.einsum("ihe,khe->hik", query_col, key_col, preferred_element_type=jnp.float32)
            * scale
        )
        scores = scores + bias_all.astype(jnp.float32) + key_bias[None, None, :]
        row_max = jnp.max(scores, axis=-1, keepdims=True)
        expo_f = jnp.exp(scores - row_max)
        totals = jnp.sum(expo_f, axis=-1)
        weights = expo_f.astype(jnp.bfloat16)
        result = jnp.einsum("hik,khe->ihe", weights, value_col, preferred_element_type=jnp.float32)
        return result / jnp.transpose(totals)[:, :, None]

    blocks = lax.map(one_block, jnp.arange(tok_total // block_rows))
    return blocks.reshape(tok_total, query_col.shape[1], query_col.shape[2])


def column_attention(columns, att_qkv, att_gate, bias_all, key_bias, head_local, head_dim):
    tok_total, col_count, channels = columns.shape
    local_width = head_local * head_dim
    weight_three = att_qkv.reshape(channels, 3, channels)
    qkv_all = jnp.einsum(
        "kmc,ctd->tmkd", columns, weight_three, preferred_element_type=jnp.float32
    ).astype(jnp.bfloat16)
    qkv_all = qkv_all.reshape(3, col_count, tok_total, head_local, head_dim)
    gate_val = jax.nn.sigmoid(
        jnp.einsum("kmc,cd->kmd", columns, att_gate, preferred_element_type=jnp.float32)
    )
    block_rows = min(1024, tok_total)

    def one_column(triple):
        return attend_column(triple[0], triple[1], triple[2], bias_all, key_bias, block_rows)

    attended = lax.map(one_column, (qkv_all[0], qkv_all[1], qkv_all[2]))
    attended = jnp.transpose(attended, (1, 0, 2, 3)).reshape(tok_total, col_count, local_width)
    return (gate_val * attended).astype(jnp.bfloat16)


def split_pair_on_device(
    pair_in,
    token_mask,
    positions,
    relpos_table,
    tri_norm_in,
    tri_in_weight,
    tri_in_gate,
    tri_out_gate,
    tri_norm_out,
    tri_out_weight,
    att_norm,
    att_qkv,
    att_gate,
    att_bias,
    att_out,
):
    row_count, col_count, channels = pair_in.shape
    row_first = lax.axis_index("row") * row_count
    col_first = lax.axis_index("col") * col_count
    mask_float = token_mask.astype(jnp.float32)
    row_mask = lax.dynamic_slice_in_dim(mask_float, row_first, row_count)
    col_mask = lax.dynamic_slice_in_dim(mask_float, col_first, col_count)
    row_pos = lax.dynamic_slice_in_dim(positions, row_first, row_count)
    col_pos = lax.dynamic_slice_in_dim(positions, col_first, col_count)
    bin_count = relpos_table.shape[0]
    bin_centre = bin_count // 2
    bucket = jnp.clip(row_pos[:, None] - col_pos[None, :], -bin_centre, bin_centre - 1) + bin_centre
    onehot = (bucket[:, :, None] == jnp.arange(bin_count, dtype=jnp.int32)[None, None, :]).astype(
        jnp.bfloat16
    )
    residual = pair_in.astype(jnp.float32) + jnp.einsum(
        "rjb,bc->rjc", onehot, relpos_table, preferred_element_type=jnp.float32
    )
    normed = layer_norm(residual, tri_norm_in).astype(jnp.bfloat16)
    pair_mask = row_mask[:, None] * col_mask[None, :]
    gate_in = jnp.einsum("rjc,cd->drj", normed, tri_in_gate, preferred_element_type=jnp.float32)
    proj_in = jnp.einsum("rjc,cd->drj", normed, tri_in_weight, preferred_element_type=jnp.float32)
    projected = (jax.nn.sigmoid(gate_in) * proj_in * pair_mask[None, :, :]).astype(jnp.bfloat16)
    left_ch, right_ch = (
        lax.all_to_all(projected[:channels], "row", split_axis=0, concat_axis=1, tiled=True),
        lax.all_to_all(projected[channels:], "row", split_axis=0, concat_axis=1, tiled=True),
    )
    right_rows = lax.all_to_all(right_ch, "col", split_axis=1, concat_axis=2, tiled=True)
    product_sum = jnp.einsum(
        "cik,cjk->cij",
        lax.all_gather(left_ch, "col", axis=2, tiled=True),
        right_rows,
        preferred_element_type=jnp.float32,
    )
    products = product_sum.astype(jnp.bfloat16)
    product_tile = lax.all_to_all(products, "row", split_axis=1, concat_axis=0, tiled=True)
    tri_x = jnp.transpose(product_tile, (1, 2, 0)).astype(jnp.float32)
    normed_out = layer_norm(tri_x, tri_norm_out).astype(jnp.bfloat16)
    out_gate = jax.nn.sigmoid(
        jnp.einsum("rjc,cd->rjd", normed, tri_out_gate, preferred_element_type=jnp.float32)
    )
    residual = residual + out_gate * jnp.einsum(
        "rjc,cd->rjd", normed_out, tri_out_weight, preferred_element_type=jnp.float32
    )
    normed_att = layer_norm(residual, att_norm).astype(jnp.bfloat16)
    bias_piece = jnp.einsum(
        "kic,ch->hik", normed_att, att_bias, preferred_element_type=jnp.float32
    ).astype(jnp.bfloat16)
    key_bias = (mask_float - 1.0) * 1000000000.0
    head_count = att_bias.shape[1]
    head_dim = channels // head_count
    columns = lax.all_to_all(normed_att, "row", split_axis=1, concat_axis=0, tiled=True)
    bias_half = lax.all_gather(bias_piece, "col", axis=1, tiled=True)
    bias_all = lax.all_gather(bias_half, "row", axis=2, tiled=True)
    gated = column_attention(columns, att_qkv, att_gate, bias_all, key_bias, head_count, head_dim)
    gated_tile = lax.all_to_all(gated, "row", split_axis=0, concat_axis=1, tiled=True)
    update = jnp.einsum("rjc,cd->rjd", gated_tile, att_out, preferred_element_type=jnp.float32)
    return (residual + update).astype(jnp.bfloat16)


def on_device(row_dim, col_dim, pair_in, *others):
    rows, cols, width = pair_in.shape
    tokens = row_dim * rows
    whole_bytes = tokens * tokens * width * pair_in.dtype.itemsize
    blocks = row_dim * col_dim
    tiled = cols % 8 == 0 and width % 128 == 0 and blocks & (blocks - 1) == 0 and blocks >= 4 and col_dim == 2
    if whole_bytes <= WHOLE_PAIR_BYTES and tiled:
        return whole_pair_on_device(row_dim, pair_in, *others)
    return split_pair_on_device(pair_in, *others)


def solution(mesh):
    return jax.shard_map(
        functools.partial(on_device, mesh.shape["row"], mesh.shape["col"]),
        mesh=mesh,
        in_specs=(P(("groups", "row"), "col", None), P("groups"), P("groups")) + (P(),) * 12,
        out_specs=P(("groups", "row"), "col", None),
        check_vma=False,
    )
```

```python
import functools
import math

import jax
import jax.numpy as jnp
from jax import lax
from jax.experimental import pallas as pl
from jax.experimental.pallas import tpu as pltpu
from jax.sharding import PartitionSpec as P

epsilon = 1e-05

WHOLE_PAIR_BYTES = 256 * 1024
STAGE_FLOPS = 10**9


def layer_norm(values, gain):
    mean_val = jnp.mean(values, axis=-1, keepdims=True)
    centred = values - mean_val
    var_val = jnp.mean(centred * centred, axis=-1, keepdims=True)
    return centred * lax.rsqrt(var_val + epsilon) * gain


def sigmoid(values):
    return 0.5 * jnp.tanh(0.5 * values) + 0.5


def dot(left, right):
    return jnp.dot(left, right, preferred_element_type=jnp.float32)


def dot_t(left, right):
    return lax.dot_general(
        left, right, (((1,), (1,)), ((), ())), preferred_element_type=jnp.float32
    )


def round_bf16(values):
    return values.astype(jnp.bfloat16).astype(jnp.float32)


def token_column(ref, first, shape):
    sub = lax.broadcasted_iota(jnp.int32, shape, 0)
    column = jnp.zeros(shape, jnp.int32)
    for s in range(shape[0]):
        column = jnp.where(sub == s, ref[first + s], column)
    return column


def own_kernel(mask_ref, pair_ref, att_bias_ref, chip_ref, bias_ref, pair_mask_ref, key_bias_ref):
    chip_ref[0] = pair_ref[...]
    bias_ref[...] = att_bias_ref[...]
    tokens = mask_ref.shape[0]
    cols, width = key_bias_ref.shape[0], pair_mask_ref.shape[1]
    for half in range(tokens // cols):
        column = token_column(mask_ref, half * cols, (cols, width))
        for i in range(tokens):
            first = i * tokens + half * cols
            pair_mask_ref[first : first + cols, :] = (column * mask_ref[i]).astype(jnp.float32)
    sub = lax.broadcasted_iota(jnp.int32, key_bias_ref.shape, 0)
    lane = lax.broadcasted_iota(jnp.int32, key_bias_ref.shape, 1)
    key_mask = jnp.zeros(key_bias_ref.shape, jnp.int32)
    for k in range(tokens):
        key_mask = jnp.where(lane // cols == k, mask_ref[k], key_mask)
    key_bias = (key_mask.astype(jnp.float32) - 1.0) * 1000000000.0
    key_bias_ref[...] = jnp.where(lane % cols == sub, key_bias, -jnp.inf)


def stage_kernel(cols, pos_ref, table_ref, norm_in_ref, norm_out_ref, att_norm_ref, rel_ref, gains_ref):
    gains_ref[0:1] = norm_in_ref[...]
    gains_ref[1:2] = norm_out_ref[...]
    gains_ref[2:3] = att_norm_ref[...]
    tokens = pos_ref.shape[0]
    bins = table_ref.shape[0]
    lane = lax.broadcasted_iota(jnp.int32, (cols, bins), 1)
    hot = [None] * (tokens * tokens // cols)
    for half in range(tokens // cols):
        column = token_column(pos_ref, half * cols, (cols, bins))
        for i in range(tokens):
            bucket = jnp.clip(pos_ref[i] - column, -(bins // 2), bins // 2 - 1) + bins // 2
            hot[i * (tokens // cols) + half] = (bucket == lane).astype(jnp.float32)
    hot = jnp.concatenate(hot, axis=0).astype(jnp.bfloat16)
    rel_ref[...] = dot(hot, table_ref[...])


def whole_pair_kernel(
    row_dim,
    heads,
    order,
    held_ref,
    other_ref,
    rel_ref,
    pair_mask_ref,
    gains_ref,
    att_bias_ref,
    key_bias_ref,
    in_weight_ref,
    in_gate_ref,
    out_gate_ref,
    out_weight_ref,
    qkv_ref,
    att_gate_ref,
    att_out_ref,
    out_ref,
    base_ref,
    normed_ref,
    left_ref,
    right_ref,
    att_ref,
    upd_ref,
):
    rows, cols, width = held_ref.shape[1:]
    tokens = row_dim * rows
    head_dim = width // heads
    row_first = lax.axis_index("row") * rows
    col_first = pl.multiple_of(lax.axis_index("col") * cols, cols)
    f32, bf16 = jnp.float32, jnp.bfloat16

    me = lax.axis_index("row") * 2 + lax.axis_index("col")
    for ref, flip in ((held_ref, 0), (other_ref, 1)):
        for at, place in enumerate(order):
            owner = me ^ (place ^ flip)
            block = ref[at].astype(f32)
            for r in range(rows):
                first = (owner // 2 * rows + r) * tokens + owner % 2 * cols
                base_ref[pl.ds(pl.multiple_of(first, cols), cols), :] = block[r]

    base = base_ref[...] + rel_ref[...]
    base_ref[...] = base

    normed = layer_norm(base, gains_ref[0:1]).astype(bf16)
    normed_ref[...] = normed.astype(f32)
    projected = sigmoid(dot(normed, in_gate_ref[...])) * dot(normed, in_weight_ref[...])
    pair_mask = pair_mask_ref[...]
    left_ref[...] = round_bf16(projected[:, :width] * pair_mask)
    right_ref[...] = round_bf16(projected[:, width:] * pair_mask)

    right_at = [right_ref[pl.ds(col_first * tokens + m, cols, stride=tokens), :] for m in range(tokens)]
    products = []
    for i in range(tokens):
        total = left_ref[pl.ds(i * tokens, 1), :] * right_at[0]
        for m in range(1, tokens):
            total = total + left_ref[pl.ds(i * tokens + m, 1), :] * right_at[m]
        products.append(total)
    extra = [None] * rows
    for m in range(tokens):
        left_at = left_ref[pl.ds(m, tokens, stride=tokens), :]
        for r in range(rows):
            term = left_at * right_ref[pl.ds((row_first + r) * tokens + m, 1), :]
            extra[r] = term if m == 0 else extra[r] + term
    products = round_bf16(jnp.concatenate(products + extra, axis=0))

    def chosen(ref):
        own = [ref[pl.ds(i * tokens + col_first, cols), :] for i in range(tokens)]
        own += [ref[pl.ds(row_first + r, tokens, stride=tokens), :] for r in range(rows)]
        return jnp.concatenate(own, axis=0)

    normed_out = layer_norm(products, gains_ref[1:2]).astype(bf16)
    out_gate = sigmoid(dot(chosen(normed_ref).astype(bf16), out_gate_ref[...]))
    updated = chosen(base_ref) + out_gate * dot(normed_out, out_weight_ref[...])
    normed_att = layer_norm(updated, gains_ref[2:3]).astype(bf16)
    own_pairs = rows * cols
    column_pairs = tokens * cols
    upd_ref[...] = updated[:column_pairs]
    att_f = normed_att.astype(f32)
    att_ref[...] = att_f[:column_pairs]

    own_at = pl.ds(pl.multiple_of(row_first * cols, own_pairs), own_pairs)
    own = att_ref[own_at, :].astype(bf16)
    column = normed_att[:column_pairs]
    queries = dot(own, qkv_ref[:, :width])
    keys = dot(column, qkv_ref[:, width : 2 * width]).astype(bf16)
    values = dot(column, qkv_ref[:, 2 * width :]).astype(bf16)
    own_gate = sigmoid(dot(own, att_gate_ref[...]))

    bias = []
    for r in range(rows):
        part = att_f[column_pairs + r * tokens : column_pairs + (r + 1) * tokens]
        spread = jnp.concatenate(
            [jnp.broadcast_to(part[k : k + 1], (cols, width)) for k in range(tokens)], axis=0
        )
        bias.append(round_bf16(dot_t(att_bias_ref[...], spread.astype(bf16))))

    head_of = lax.broadcasted_iota(jnp.int32, (own_pairs, width), 1) // head_dim
    queries = round_bf16(queries)
    by_head = jnp.concatenate(
        [jnp.where(head_of == h, queries, 0.0) for h in range(heads)], axis=0
    ).astype(bf16)
    scores = dot_t(by_head, keys) * (1.0 / math.sqrt(head_dim))
    biases = jnp.concatenate(
        [jnp.broadcast_to(bias[r][h : h + 1], (cols, column_pairs)) for h in range(heads) for r in range(rows)],
        axis=0,
    )
    key_bias = jnp.concatenate([key_bias_ref[...]] * (heads * rows), axis=0)
    scores = scores + biases + key_bias
    expo = jnp.exp(scores - jnp.max(scores, axis=-1, keepdims=True))
    totals = jnp.sum(expo, axis=-1, keepdims=True)
    mixed = dot(expo.astype(bf16), values) / totals
    attended = jnp.zeros((own_pairs, width), f32)
    for h in range(heads):
        attended = jnp.where(head_of == h, mixed[h * own_pairs : (h + 1) * own_pairs], attended)

    gated = (own_gate * attended).astype(bf16)
    result = upd_ref[own_at, :] + dot(gated, att_out_ref[...])
    out_ref[...] = result.reshape(rows, cols, width).astype(bf16)


def whole_pair_on_device(
    row_dim,
    pair_in,
    token_mask,
    positions,
    relpos_table,
    tri_norm_in,
    tri_in_weight,
    tri_in_gate,
    tri_out_gate,
    tri_norm_out,
    tri_out_weight,
    att_norm,
    att_qkv,
    att_gate,
    att_bias,
    att_out,
):
    rows, cols, width = pair_in.shape
    vmem = pl.BlockSpec(memory_space=pltpu.VMEM)
    smem = pl.BlockSpec(memory_space=pltpu.SMEM)
    params = pltpu.CompilerParams(vmem_limit_bytes=16 * 1024 * 1024)
    tokens, heads = row_dim * rows, att_bias.shape[1]

    beside = pl.CostEstimate(flops=STAGE_FLOPS, bytes_accessed=2**20, transcendentals=0)
    wide_out = jax.ShapeDtypeStruct((tokens * tokens, width), jnp.float32)
    rel, gains = pl.pallas_call(
        functools.partial(stage_kernel, cols),
        out_shape=[wide_out, jax.ShapeDtypeStruct((3, width), jnp.float32)],
        in_specs=[smem] + [vmem] * 4,
        out_specs=[vmem] * 2,
        compiler_params=params,
        cost_estimate=beside,
    )(
        positions,
        relpos_table,
        tri_norm_in.reshape(1, width),
        tri_norm_out.reshape(1, width),
        att_norm.reshape(1, width),
    )

    blocks = 2 * row_dim

    def move(values, step):
        return lax.ppermute(values, ("row", "col"), [(device, device ^ step) for device in range(blocks)])

    square = (7, 4, 3)
    held, bias, pair_mask, key_bias = pl.pallas_call(
        own_kernel,
        out_shape=[
            jax.ShapeDtypeStruct((1 + len(square),) + pair_in.shape, pair_in.dtype),
            jax.ShapeDtypeStruct((heads, width), att_bias.dtype),
            wide_out,
            jax.ShapeDtypeStruct((cols, tokens * cols), jnp.float32),
        ],
        in_specs=[smem] + [vmem] * 2,
        out_specs=[vmem] * 4,
        compiler_params=params,
        cost_estimate=beside,
    )(token_mask, pair_in, att_bias.T)
    for at, step in enumerate(square):
        held = held.at[1 + at].set(move(pair_in, step))
    order = (0,) + square
    while len(order) < row_dim:
        step = 2 * len(order) + 1
        held = jnp.concatenate([held, move(held, step)], axis=0)
        order += tuple(place ^ step for place in order)
    held, rel, gains = lax.optimization_barrier((held, rel, gains))
    gathered = (held, move(held, 1))

    weights = (tri_in_weight, tri_in_gate, tri_out_gate, tri_out_weight, att_qkv, att_gate, att_out)
    wide = pltpu.VMEM((tokens * tokens, width), jnp.float32)
    column = pltpu.VMEM((tokens * cols, width), jnp.float32)
    return pl.pallas_call(
        functools.partial(whole_pair_kernel, row_dim, heads, order),
        out_shape=jax.ShapeDtypeStruct(pair_in.shape, pair_in.dtype),
        in_specs=[vmem] * (7 + len(weights)),
        out_specs=vmem,
        scratch_shapes=[wide] * 4 + [column] * 2,
        compiler_params=params,
    )(*gathered, rel, pair_mask, gains, bias, key_bias, *weights)


def attend_column(query_col, key_col, value_col, bias_all, key_bias, block_rows):
    tok_total = query_col.shape[0]
    scale = 1.0 / math.sqrt(query_col.shape[2])

    def one_block(block_idx):
        scores = (
            jnp.einsum("ihe,khe->hik", query_col, key_col, preferred_element_type=jnp.float32)
            * scale
        )
        scores = scores + bias_all.astype(jnp.float32) + key_bias[None, None, :]
        row_max = jnp.max(scores, axis=-1, keepdims=True)
        expo_f = jnp.exp(scores - row_max)
        totals = jnp.sum(expo_f, axis=-1)
        weights = expo_f.astype(jnp.bfloat16)
        result = jnp.einsum("hik,khe->ihe", weights, value_col, preferred_element_type=jnp.float32)
        return result / jnp.transpose(totals)[:, :, None]

    blocks = lax.map(one_block, jnp.arange(tok_total // block_rows))
    return blocks.reshape(tok_total, query_col.shape[1], query_col.shape[2])


def column_attention(columns, att_qkv, att_gate, bias_all, key_bias, head_local, head_dim):
    tok_total, col_count, channels = columns.shape
    local_width = head_local * head_dim
    weight_three = att_qkv.reshape(channels, 3, channels)
    qkv_all = jnp.einsum(
        "kmc,ctd->tmkd", columns, weight_three, preferred_element_type=jnp.float32
    ).astype(jnp.bfloat16)
    qkv_all = qkv_all.reshape(3, col_count, tok_total, head_local, head_dim)
    gate_val = jax.nn.sigmoid(
        jnp.einsum("kmc,cd->kmd", columns, att_gate, preferred_element_type=jnp.float32)
    )
    block_rows = min(1024, tok_total)

    def one_column(triple):
        return attend_column(triple[0], triple[1], triple[2], bias_all, key_bias, block_rows)

    attended = lax.map(one_column, (qkv_all[0], qkv_all[1], qkv_all[2]))
    attended = jnp.transpose(attended, (1, 0, 2, 3)).reshape(tok_total, col_count, local_width)
    return (gate_val * attended).astype(jnp.bfloat16)


def split_pair_on_device(
    pair_in,
    token_mask,
    positions,
    relpos_table,
    tri_norm_in,
    tri_in_weight,
    tri_in_gate,
    tri_out_gate,
    tri_norm_out,
    tri_out_weight,
    att_norm,
    att_qkv,
    att_gate,
    att_bias,
    att_out,
):
    row_count, col_count, channels = pair_in.shape
    row_first = lax.axis_index("row") * row_count
    col_first = lax.axis_index("col") * col_count
    mask_float = token_mask.astype(jnp.float32)
    row_mask = lax.dynamic_slice_in_dim(mask_float, row_first, row_count)
    col_mask = lax.dynamic_slice_in_dim(mask_float, col_first, col_count)
    row_pos = lax.dynamic_slice_in_dim(positions, row_first, row_count)
    col_pos = lax.dynamic_slice_in_dim(positions, col_first, col_count)
    bin_count = relpos_table.shape[0]
    bin_centre = bin_count // 2
    bucket = jnp.clip(row_pos[:, None] - col_pos[None, :], -bin_centre, bin_centre - 1) + bin_centre
    onehot = (bucket[:, :, None] == jnp.arange(bin_count, dtype=jnp.int32)[None, None, :]).astype(
        jnp.bfloat16
    )
    residual = pair_in.astype(jnp.float32) + jnp.einsum(
        "rjb,bc->rjc", onehot, relpos_table, preferred_element_type=jnp.float32
    )
    normed = layer_norm(residual, tri_norm_in).astype(jnp.bfloat16)
    pair_mask = row_mask[:, None] * col_mask[None, :]
    gate_in = jnp.einsum("rjc,cd->drj", normed, tri_in_gate, preferred_element_type=jnp.float32)
    proj_in = jnp.einsum("rjc,cd->drj", normed, tri_in_weight, preferred_element_type=jnp.float32)
    projected = (jax.nn.sigmoid(gate_in) * proj_in * pair_mask[None, :, :]).astype(jnp.bfloat16)
    left_ch, right_ch = (
        lax.all_to_all(projected[:channels], "row", split_axis=0, concat_axis=1, tiled=True),
        lax.all_to_all(projected[channels:], "row", split_axis=0, concat_axis=1, tiled=True),
    )
    right_rows = lax.all_to_all(right_ch, "col", split_axis=1, concat_axis=2, tiled=True)
    product_sum = jnp.einsum(
        "cik,cjk->cij",
        lax.all_gather(left_ch, "col", axis=2, tiled=True),
        right_rows,
        preferred_element_type=jnp.float32,
    )
    products = product_sum.astype(jnp.bfloat16)
    product_tile = lax.all_to_all(products, "row", split_axis=1, concat_axis=0, tiled=True)
    tri_x = jnp.transpose(product_tile, (1, 2, 0)).astype(jnp.float32)
    normed_out = layer_norm(tri_x, tri_norm_out).astype(jnp.bfloat16)
    out_gate = jax.nn.sigmoid(
        jnp.einsum("rjc,cd->rjd", normed, tri_out_gate, preferred_element_type=jnp.float32)
    )
    residual = residual + out_gate * jnp.einsum(
        "rjc,cd->rjd", normed_out, tri_out_weight, preferred_element_type=jnp.float32
    )
    normed_att = layer_norm(residual, att_norm).astype(jnp.bfloat16)
    bias_piece = jnp.einsum(
        "kic,ch->hik", normed_att, att_bias, preferred_element_type=jnp.float32
    ).astype(jnp.bfloat16)
    key_bias = (mask_float - 1.0) * 1000000000.0
    head_count = att_bias.shape[1]
    head_dim = channels // head_count
    columns = lax.all_to_all(normed_att, "row", split_axis=1, concat_axis=0, tiled=True)
    bias_half = lax.all_gather(bias_piece, "col", axis=1, tiled=True)
    bias_all = lax.all_gather(bias_half, "row", axis=2, tiled=True)
    gated = column_attention(columns, att_qkv, att_gate, bias_all, key_bias, head_count, head_dim)
    gated_tile = lax.all_to_all(gated, "row", split_axis=0, concat_axis=1, tiled=True)
    update = jnp.einsum("rjc,cd->rjd", gated_tile, att_out, preferred_element_type=jnp.float32)
    return (residual + update).astype(jnp.bfloat16)


def on_device(row_dim, col_dim, pair_in, *others):
    rows, cols, width = pair_in.shape
    tokens = row_dim * rows
    whole_bytes = tokens * tokens * width * pair_in.dtype.itemsize
    blocks = row_dim * col_dim
    tiled = cols % 8 == 0 and width % 128 == 0 and blocks & (blocks - 1) == 0 and blocks >= 8 and col_dim == 2
    if whole_bytes <= WHOLE_PAIR_BYTES and tiled:
        return whole_pair_on_device(row_dim, pair_in, *others)
    return split_pair_on_device(pair_in, *others)


def solution(mesh):
    return jax.shard_map(
        functools.partial(on_device, mesh.shape["row"], mesh.shape["col"]),
        mesh=mesh,
        in_specs=(P(("groups", "row"), "col", None), P("groups"), P("groups")) + (P(),) * 12,
        out_specs=P(("groups", "row"), "col", None),
        check_vma=False,
    )
```

```python
import functools
import math

import jax
import jax.numpy as jnp
from jax import lax
from jax.experimental import pallas as pl
from jax.experimental.pallas import tpu as pltpu
from jax.sharding import PartitionSpec as P

epsilon = 1e-05

WHOLE_PAIR_BYTES = 256 * 1024
STAGE_FLOPS = 10**9


def layer_norm(values, gain):
    mean_val = jnp.mean(values, axis=-1, keepdims=True)
    centred = values - mean_val
    var_val = jnp.mean(centred * centred, axis=-1, keepdims=True)
    return centred * lax.rsqrt(var_val + epsilon) * gain


def sigmoid(values):
    return 0.5 * jnp.tanh(0.5 * values) + 0.5


def dot(left, right):
    return jnp.dot(left, right, preferred_element_type=jnp.float32)


def dot_t(left, right):
    return lax.dot_general(
        left, right, (((1,), (1,)), ((), ())), preferred_element_type=jnp.float32
    )


def round_bf16(values):
    return values.astype(jnp.bfloat16).astype(jnp.float32)


def token_column(ref, first, shape):
    sub = lax.broadcasted_iota(jnp.int32, shape, 0)
    column = jnp.zeros(shape, jnp.int32)
    for s in range(shape[0]):
        column = jnp.where(sub == s, ref[first + s], column)
    return column


def own_kernel(pair_ref, chip_ref):
    chip_ref[0] = pair_ref[...]


def stage_kernel(
    cols,
    mask_ref,
    pos_ref,
    table_ref,
    norm_in_ref,
    norm_out_ref,
    att_norm_ref,
    att_bias_ref,
    rel_ref,
    pair_mask_ref,
    gains_ref,
    bias_ref,
    key_bias_ref,
):
    gains_ref[0:1] = norm_in_ref[...]
    gains_ref[1:2] = norm_out_ref[...]
    gains_ref[2:3] = att_norm_ref[...]
    bias_ref[...] = att_bias_ref[...]
    tokens = pos_ref.shape[0]
    bins = table_ref.shape[0]
    lane = lax.broadcasted_iota(jnp.int32, (cols, bins), 1)
    hot = [None] * (tokens * tokens // cols)
    for half in range(tokens // cols):
        column = token_column(pos_ref, half * cols, (cols, bins))
        column_mask = token_column(mask_ref, half * cols, (cols, bins))
        for i in range(tokens):
            first = i * tokens + half * cols
            pair_mask_ref[first : first + cols, :] = (column_mask * mask_ref[i]).astype(jnp.float32)
            bucket = jnp.clip(pos_ref[i] - column, -(bins // 2), bins // 2 - 1) + bins // 2
            hot[i * (tokens // cols) + half] = (bucket == lane).astype(jnp.float32)
    sub = lax.broadcasted_iota(jnp.int32, key_bias_ref.shape, 0)
    lane = lax.broadcasted_iota(jnp.int32, key_bias_ref.shape, 1)
    key_mask = jnp.zeros(key_bias_ref.shape, jnp.int32)
    for k in range(tokens):
        key_mask = jnp.where(lane // cols == k, mask_ref[k], key_mask)
    key_bias = (key_mask.astype(jnp.float32) - 1.0) * 1000000000.0
    key_bias_ref[...] = jnp.where(lane % cols == sub, key_bias, -jnp.inf)
    hot = jnp.concatenate(hot, axis=0).astype(jnp.bfloat16)
    rel_ref[...] = dot(hot, table_ref[...])


def whole_pair_kernel(row_dim, heads, orders, *refs):
    whole_pair_steps(row_dim, heads, orders, refs[: len(orders)], *refs[len(orders) :])


def whole_pair_steps(
    row_dim,
    heads,
    orders,
    piece_refs,
    rel_ref,
    pair_mask_ref,
    gains_ref,
    att_bias_ref,
    key_bias_ref,
    in_weight_ref,
    in_gate_ref,
    out_gate_ref,
    out_weight_ref,
    qkv_ref,
    att_gate_ref,
    att_out_ref,
    out_ref,
    base_ref,
    normed_ref,
    left_ref,
    right_ref,
    att_ref,
    upd_ref,
):
    rows, cols, width = piece_refs[0].shape[1:]
    tokens = row_dim * rows
    head_dim = width // heads
    row_first = lax.axis_index("row") * rows
    col_first = pl.multiple_of(lax.axis_index("col") * cols, cols)
    f32, bf16 = jnp.float32, jnp.bfloat16

    me = lax.axis_index("row") * 2 + lax.axis_index("col")
    for ref, order in zip(piece_refs, orders):
        for at, place in enumerate(order):
            owner = me ^ place
            block = ref[at].astype(f32)
            for r in range(rows):
                first = (owner // 2 * rows + r) * tokens + owner % 2 * cols
                base_ref[pl.ds(pl.multiple_of(first, cols), cols), :] = block[r]

    base = base_ref[...] + rel_ref[...]
    base_ref[...] = base

    normed = layer_norm(base, gains_ref[0:1]).astype(bf16)
    normed_ref[...] = normed.astype(f32)
    projected = sigmoid(dot(normed, in_gate_ref[...])) * dot(normed, in_weight_ref[...])
    pair_mask = pair_mask_ref[...]
    left_ref[...] = round_bf16(projected[:, :width] * pair_mask)
    right_ref[...] = round_bf16(projected[:, width:] * pair_mask)

    right_at = [right_ref[pl.ds(col_first * tokens + m, cols, stride=tokens), :] for m in range(tokens)]
    products = []
    for i in range(tokens):
        total = left_ref[pl.ds(i * tokens, 1), :] * right_at[0]
        for m in range(1, tokens):
            total = total + left_ref[pl.ds(i * tokens + m, 1), :] * right_at[m]
        products.append(total)
    extra = [None] * rows
    for m in range(tokens):
        left_at = left_ref[pl.ds(m, tokens, stride=tokens), :]
        for r in range(rows):
            term = left_at * right_ref[pl.ds((row_first + r) * tokens + m, 1), :]
            extra[r] = term if m == 0 else extra[r] + term
    products = round_bf16(jnp.concatenate(products + extra, axis=0))

    def chosen(ref):
        own = [ref[pl.ds(i * tokens + col_first, cols), :] for i in range(tokens)]
        own += [ref[pl.ds(row_first + r, tokens, stride=tokens), :] for r in range(rows)]
        return jnp.concatenate(own, axis=0)

    normed_out = layer_norm(products, gains_ref[1:2]).astype(bf16)
    out_gate = sigmoid(dot(chosen(normed_ref).astype(bf16), out_gate_ref[...]))
    updated = chosen(base_ref) + out_gate * dot(normed_out, out_weight_ref[...])
    normed_att = layer_norm(updated, gains_ref[2:3]).astype(bf16)
    own_pairs = rows * cols
    column_pairs = tokens * cols
    upd_ref[...] = updated[:column_pairs]
    att_f = normed_att.astype(f32)
    att_ref[...] = att_f[:column_pairs]

    own_at = pl.ds(pl.multiple_of(row_first * cols, own_pairs), own_pairs)
    own = att_ref[own_at, :].astype(bf16)
    column = normed_att[:column_pairs]
    queries = dot(own, qkv_ref[:, :width])
    keys = dot(column, qkv_ref[:, width : 2 * width]).astype(bf16)
    values = dot(column, qkv_ref[:, 2 * width :]).astype(bf16)
    own_gate = sigmoid(dot(own, att_gate_ref[...]))

    bias = []
    for r in range(rows):
        part = att_f[column_pairs + r * tokens : column_pairs + (r + 1) * tokens]
        spread = jnp.concatenate(
            [jnp.broadcast_to(part[k : k + 1], (cols, width)) for k in range(tokens)], axis=0
        )
        bias.append(round_bf16(dot_t(att_bias_ref[...], spread.astype(bf16))))

    head_of = lax.broadcasted_iota(jnp.int32, (own_pairs, width), 1) // head_dim
    queries = round_bf16(queries)
    by_head = jnp.concatenate(
        [jnp.where(head_of == h, queries, 0.0) for h in range(heads)], axis=0
    ).astype(bf16)
    scores = dot_t(by_head, keys) * (1.0 / math.sqrt(head_dim))
    biases = jnp.concatenate(
        [jnp.broadcast_to(bias[r][h : h + 1], (cols, column_pairs)) for h in range(heads) for r in range(rows)],
        axis=0,
    )
    key_bias = jnp.concatenate([key_bias_ref[...]] * (heads * rows), axis=0)
    scores = scores + biases + key_bias
    expo = jnp.exp(scores - jnp.max(scores, axis=-1, keepdims=True))
    totals = jnp.sum(expo, axis=-1, keepdims=True)
    mixed = dot(expo.astype(bf16), values) / totals
    attended = jnp.zeros((own_pairs, width), f32)
    for h in range(heads):
        attended = jnp.where(head_of == h, mixed[h * own_pairs : (h + 1) * own_pairs], attended)

    gated = (own_gate * attended).astype(bf16)
    result = upd_ref[own_at, :] + dot(gated, att_out_ref[...])
    out_ref[...] = result.reshape(rows, cols, width).astype(bf16)


def whole_pair_on_device(
    row_dim,
    pair_in,
    token_mask,
    positions,
    relpos_table,
    tri_norm_in,
    tri_in_weight,
    tri_in_gate,
    tri_out_gate,
    tri_norm_out,
    tri_out_weight,
    att_norm,
    att_qkv,
    att_gate,
    att_bias,
    att_out,
):
    rows, cols, width = pair_in.shape
    vmem = pl.BlockSpec(memory_space=pltpu.VMEM)
    smem = pl.BlockSpec(memory_space=pltpu.SMEM)
    params = pltpu.CompilerParams(vmem_limit_bytes=16 * 1024 * 1024)
    tokens, heads = row_dim * rows, att_bias.shape[1]

    beside = pl.CostEstimate(flops=STAGE_FLOPS, bytes_accessed=2**20, transcendentals=0)
    wide_out = jax.ShapeDtypeStruct((tokens * tokens, width), jnp.float32)
    staged = pl.pallas_call(
        functools.partial(stage_kernel, cols),
        out_shape=[
            wide_out,
            wide_out,
            jax.ShapeDtypeStruct((3, width), jnp.float32),
            jax.ShapeDtypeStruct((heads, width), att_bias.dtype),
            jax.ShapeDtypeStruct((cols, tokens * cols), jnp.float32),
        ],
        in_specs=[smem] * 2 + [vmem] * 5,
        out_specs=[vmem] * 5,
        compiler_params=params,
        cost_estimate=beside,
    )(
        token_mask,
        positions,
        relpos_table,
        tri_norm_in.reshape(1, width),
        tri_norm_out.reshape(1, width),
        att_norm.reshape(1, width),
        att_bias.T,
    )

    blocks = 2 * row_dim

    def move(piece, step):
        values, order = piece
        values = lax.ppermute(values, ("row", "col"), [(device, device ^ step) for device in range(blocks)])
        return values, tuple(place ^ step for place in order)

    chip = pl.pallas_call(
        own_kernel,
        out_shape=jax.ShapeDtypeStruct((2,) + pair_in.shape, pair_in.dtype),
        in_specs=[vmem],
        out_specs=vmem,
        compiler_params=params,
        cost_estimate=beside,
    )(pair_in)
    other, _ = move((pair_in, (0,)), 1)
    pieces = [(chip.at[1].set(other), (0, 1))]
    first = move(pieces[0], 9)
    pieces += [first, move(pieces[0], 7), move(pieces[0], 15)]
    both = jnp.concatenate([pieces[0][0], first[0]], axis=0), pieces[0][1] + first[1]
    pieces += [move(both, 5), move(both, 3)]
    gathered = [values for values, _ in pieces]
    orders = [order for _, order in pieces]

    weights = (tri_in_weight, tri_in_gate, tri_out_gate, tri_out_weight, att_qkv, att_gate, att_out)
    wide = pltpu.VMEM((tokens * tokens, width), jnp.float32)
    column = pltpu.VMEM((tokens * cols, width), jnp.float32)
    return pl.pallas_call(
        functools.partial(whole_pair_kernel, row_dim, heads, orders),
        out_shape=jax.ShapeDtypeStruct(pair_in.shape, pair_in.dtype),
        in_specs=[vmem] * (len(gathered) + 5 + len(weights)),
        out_specs=vmem,
        scratch_shapes=[wide] * 4 + [column] * 2,
        compiler_params=params,
    )(*gathered, *staged, *weights)


def attend_column(query_col, key_col, value_col, bias_all, key_bias, block_rows):
    tok_total = query_col.shape[0]
    scale = 1.0 / math.sqrt(query_col.shape[2])

    def one_block(block_idx):
        scores = (
            jnp.einsum("ihe,khe->hik", query_col, key_col, preferred_element_type=jnp.float32)
            * scale
        )
        scores = scores + bias_all.astype(jnp.float32) + key_bias[None, None, :]
        row_max = jnp.max(scores, axis=-1, keepdims=True)
        expo_f = jnp.exp(scores - row_max)
        totals = jnp.sum(expo_f, axis=-1)
        weights = expo_f.astype(jnp.bfloat16)
        result = jnp.einsum("hik,khe->ihe", weights, value_col, preferred_element_type=jnp.float32)
        return result / jnp.transpose(totals)[:, :, None]

    blocks = lax.map(one_block, jnp.arange(tok_total // block_rows))
    return blocks.reshape(tok_total, query_col.shape[1], query_col.shape[2])


def column_attention(columns, att_qkv, att_gate, bias_all, key_bias, head_local, head_dim):
    tok_total, col_count, channels = columns.shape
    local_width = head_local * head_dim
    weight_three = att_qkv.reshape(channels, 3, channels)
    qkv_all = jnp.einsum(
        "kmc,ctd->tmkd", columns, weight_three, preferred_element_type=jnp.float32
    ).astype(jnp.bfloat16)
    qkv_all = qkv_all.reshape(3, col_count, tok_total, head_local, head_dim)
    gate_val = jax.nn.sigmoid(
        jnp.einsum("kmc,cd->kmd", columns, att_gate, preferred_element_type=jnp.float32)
    )
    block_rows = min(1024, tok_total)

    def one_column(triple):
        return attend_column(triple[0], triple[1], triple[2], bias_all, key_bias, block_rows)

    attended = lax.map(one_column, (qkv_all[0], qkv_all[1], qkv_all[2]))
    attended = jnp.transpose(attended, (1, 0, 2, 3)).reshape(tok_total, col_count, local_width)
    return (gate_val * attended).astype(jnp.bfloat16)


def split_pair_on_device(
    pair_in,
    token_mask,
    positions,
    relpos_table,
    tri_norm_in,
    tri_in_weight,
    tri_in_gate,
    tri_out_gate,
    tri_norm_out,
    tri_out_weight,
    att_norm,
    att_qkv,
    att_gate,
    att_bias,
    att_out,
):
    row_count, col_count, channels = pair_in.shape
    row_first = lax.axis_index("row") * row_count
    col_first = lax.axis_index("col") * col_count
    mask_float = token_mask.astype(jnp.float32)
    row_mask = lax.dynamic_slice_in_dim(mask_float, row_first, row_count)
    col_mask = lax.dynamic_slice_in_dim(mask_float, col_first, col_count)
    row_pos = lax.dynamic_slice_in_dim(positions, row_first, row_count)
    col_pos = lax.dynamic_slice_in_dim(positions, col_first, col_count)
    bin_count = relpos_table.shape[0]
    bin_centre = bin_count // 2
    bucket = jnp.clip(row_pos[:, None] - col_pos[None, :], -bin_centre, bin_centre - 1) + bin_centre
    onehot = (bucket[:, :, None] == jnp.arange(bin_count, dtype=jnp.int32)[None, None, :]).astype(
        jnp.bfloat16
    )
    residual = pair_in.astype(jnp.float32) + jnp.einsum(
        "rjb,bc->rjc", onehot, relpos_table, preferred_element_type=jnp.float32
    )
    normed = layer_norm(residual, tri_norm_in).astype(jnp.bfloat16)
    pair_mask = row_mask[:, None] * col_mask[None, :]
    gate_in = jnp.einsum("rjc,cd->drj", normed, tri_in_gate, preferred_element_type=jnp.float32)
    proj_in = jnp.einsum("rjc,cd->drj", normed, tri_in_weight, preferred_element_type=jnp.float32)
    projected = (jax.nn.sigmoid(gate_in) * proj_in * pair_mask[None, :, :]).astype(jnp.bfloat16)
    left_ch, right_ch = (
        lax.all_to_all(projected[:channels], "row", split_axis=0, concat_axis=1, tiled=True),
        lax.all_to_all(projected[channels:], "row", split_axis=0, concat_axis=1, tiled=True),
    )
    right_rows = lax.all_to_all(right_ch, "col", split_axis=1, concat_axis=2, tiled=True)
    product_sum = jnp.einsum(
        "cik,cjk->cij",
        lax.all_gather(left_ch, "col", axis=2, tiled=True),
        right_rows,
        preferred_element_type=jnp.float32,
    )
    products = product_sum.astype(jnp.bfloat16)
    product_tile = lax.all_to_all(products, "row", split_axis=1, concat_axis=0, tiled=True)
    tri_x = jnp.transpose(product_tile, (1, 2, 0)).astype(jnp.float32)
    normed_out = layer_norm(tri_x, tri_norm_out).astype(jnp.bfloat16)
    out_gate = jax.nn.sigmoid(
        jnp.einsum("rjc,cd->rjd", normed, tri_out_gate, preferred_element_type=jnp.float32)
    )
    residual = residual + out_gate * jnp.einsum(
        "rjc,cd->rjd", normed_out, tri_out_weight, preferred_element_type=jnp.float32
    )
    normed_att = layer_norm(residual, att_norm).astype(jnp.bfloat16)
    bias_piece = jnp.einsum(
        "kic,ch->hik", normed_att, att_bias, preferred_element_type=jnp.float32
    ).astype(jnp.bfloat16)
    key_bias = (mask_float - 1.0) * 1000000000.0
    head_count = att_bias.shape[1]
    head_dim = channels // head_count
    columns = lax.all_to_all(normed_att, "row", split_axis=1, concat_axis=0, tiled=True)
    bias_half = lax.all_gather(bias_piece, "col", axis=1, tiled=True)
    bias_all = lax.all_gather(bias_half, "row", axis=2, tiled=True)
    gated = column_attention(columns, att_qkv, att_gate, bias_all, key_bias, head_count, head_dim)
    gated_tile = lax.all_to_all(gated, "row", split_axis=0, concat_axis=1, tiled=True)
    update = jnp.einsum("rjc,cd->rjd", gated_tile, att_out, preferred_element_type=jnp.float32)
    return (residual + update).astype(jnp.bfloat16)


def on_device(row_dim, col_dim, pair_in, *others):
    rows, cols, width = pair_in.shape
    tokens = row_dim * rows
    whole_bytes = tokens * tokens * width * pair_in.dtype.itemsize
    blocks = row_dim * col_dim
    tiled = cols % 8 == 0 and width % 128 == 0 and blocks == 16 and col_dim == 2
    if whole_bytes <= WHOLE_PAIR_BYTES and tiled:
        return whole_pair_on_device(row_dim, pair_in, *others)
    return split_pair_on_device(pair_in, *others)


def solution(mesh):
    return jax.shard_map(
        functools.partial(on_device, mesh.shape["row"], mesh.shape["col"]),
        mesh=mesh,
        in_specs=(P(("groups", "row"), "col", None), P("groups"), P("groups")) + (P(),) * 12,
        out_specs=P(("groups", "row"), "col", None),
        check_vma=False,
    )
```

```python
import functools
import math

import jax
import jax.numpy as jnp
from jax import lax
from jax.experimental import pallas as pl
from jax.experimental.pallas import tpu as pltpu
from jax.sharding import PartitionSpec as P

epsilon = 1e-05

WHOLE_PAIR_BYTES = 256 * 1024
STAGE_FLOPS = 10**9


def layer_norm(values, gain):
    mean_val = jnp.mean(values, axis=-1, keepdims=True)
    centred = values - mean_val
    var_val = jnp.mean(centred * centred, axis=-1, keepdims=True)
    return centred * lax.rsqrt(var_val + epsilon) * gain


def lane_mean(values, terms):
    parts = []
    for _ in range(terms):
        parts.append(values.astype(jnp.bfloat16))
        values = values - parts[-1].astype(jnp.float32)
    width = values.shape[1]
    share = jnp.full((terms * width, width), 1.0 / width, jnp.bfloat16)
    return dot(jnp.concatenate(parts, axis=1), share)


def lane_norm(values, gain):
    centred = values - lane_mean(values, 3)
    return centred * lax.rsqrt(lane_mean(centred * centred, 2) + epsilon) * gain


def sigmoid(values):
    return 0.5 * jnp.tanh(0.5 * values) + 0.5


def dot(left, right):
    return jnp.dot(left, right, preferred_element_type=jnp.float32)


def dot_t(left, right):
    return lax.dot_general(
        left, right, (((1,), (1,)), ((), ())), preferred_element_type=jnp.float32
    )


def round_bf16(values):
    return values.astype(jnp.bfloat16).astype(jnp.float32)


def token_column(ref, first, shape):
    sub = lax.broadcasted_iota(jnp.int32, shape, 0)
    column = jnp.zeros(shape, jnp.int32)
    for s in range(shape[0]):
        column = jnp.where(sub == s, ref[first + s], column)
    return column


def own_kernel(pair_ref, chip_ref):
    chip_ref[0] = pair_ref[...]


def stage_kernel(
    cols,
    mask_ref,
    pos_ref,
    table_ref,
    norm_in_ref,
    norm_out_ref,
    att_norm_ref,
    att_bias_ref,
    rel_ref,
    pair_mask_ref,
    gains_ref,
    bias_ref,
    key_bias_ref,
):
    gains_ref[0:1] = norm_in_ref[...]
    gains_ref[1:2] = norm_out_ref[...]
    gains_ref[2:3] = att_norm_ref[...]
    bias_ref[...] = att_bias_ref[...]
    tokens = pos_ref.shape[0]
    bins = table_ref.shape[0]
    lane = lax.broadcasted_iota(jnp.int32, (cols, bins), 1)
    hot = [None] * (tokens * tokens // cols)
    for half in range(tokens // cols):
        column = token_column(pos_ref, half * cols, (cols, bins))
        column_mask = token_column(mask_ref, half * cols, (cols, bins))
        for i in range(tokens):
            first = i * tokens + half * cols
            pair_mask_ref[first : first + cols, :] = (column_mask * mask_ref[i]).astype(jnp.float32)
            bucket = jnp.clip(pos_ref[i] - column, -(bins // 2), bins // 2 - 1) + bins // 2
            hot[i * (tokens // cols) + half] = (bucket == lane).astype(jnp.float32)
    sub = lax.broadcasted_iota(jnp.int32, key_bias_ref.shape, 0)
    lane = lax.broadcasted_iota(jnp.int32, key_bias_ref.shape, 1)
    key_mask = jnp.zeros(key_bias_ref.shape, jnp.int32)
    for k in range(tokens):
        key_mask = jnp.where(lane // cols == k, mask_ref[k], key_mask)
    key_bias = (key_mask.astype(jnp.float32) - 1.0) * 1000000000.0
    key_bias_ref[...] = jnp.where(lane % cols == sub, key_bias, -jnp.inf)
    hot = jnp.concatenate(hot, axis=0).astype(jnp.bfloat16)
    rel_ref[...] = dot(hot, table_ref[...])


def whole_pair_kernel(row_dim, heads, orders, *refs):
    whole_pair_steps(row_dim, heads, orders, refs[: len(orders)], *refs[len(orders) :])


def whole_pair_steps(
    row_dim,
    heads,
    orders,
    piece_refs,
    rel_ref,
    pair_mask_ref,
    gains_ref,
    att_bias_ref,
    key_bias_ref,
    in_weight_ref,
    in_gate_ref,
    out_gate_ref,
    out_weight_ref,
    qkv_ref,
    att_gate_ref,
    att_out_ref,
    out_ref,
    base_ref,
    normed_ref,
    left_ref,
    right_ref,
    att_ref,
    upd_ref,
):
    rows, cols, width = piece_refs[0].shape[1:]
    tokens = row_dim * rows
    head_dim = width // heads
    row_first = lax.axis_index("row") * rows
    col_first = pl.multiple_of(lax.axis_index("col") * cols, cols)
    f32, bf16 = jnp.float32, jnp.bfloat16

    me = lax.axis_index("row") * 2 + lax.axis_index("col")
    for ref, order in zip(piece_refs, orders):
        for at, place in enumerate(order):
            owner = me ^ place
            block = ref[at].astype(f32)
            for r in range(rows):
                first = (owner // 2 * rows + r) * tokens + owner % 2 * cols
                base_ref[pl.ds(pl.multiple_of(first, cols), cols), :] = block[r]

    base = base_ref[...] + rel_ref[...]
    base_ref[...] = base

    normed = lane_norm(base, gains_ref[0:1]).astype(bf16)
    normed_ref[...] = normed.astype(f32)
    projected = sigmoid(dot(normed, in_gate_ref[...])) * dot(normed, in_weight_ref[...])
    pair_mask = pair_mask_ref[...]
    left_ref[...] = round_bf16(projected[:, :width] * pair_mask)
    right_ref[...] = round_bf16(projected[:, width:] * pair_mask)

    right_at = [right_ref[pl.ds(col_first * tokens + m, cols, stride=tokens), :] for m in range(tokens)]
    products = []
    for i in range(tokens):
        total = left_ref[pl.ds(i * tokens, 1), :] * right_at[0]
        for m in range(1, tokens):
            total = total + left_ref[pl.ds(i * tokens + m, 1), :] * right_at[m]
        products.append(total)
    extra = [None] * rows
    for m in range(tokens):
        left_at = left_ref[pl.ds(m, tokens, stride=tokens), :]
        for r in range(rows):
            term = left_at * right_ref[pl.ds((row_first + r) * tokens + m, 1), :]
            extra[r] = term if m == 0 else extra[r] + term
    products = round_bf16(jnp.concatenate(products + extra, axis=0))

    def chosen(ref):
        own = [ref[pl.ds(i * tokens + col_first, cols), :] for i in range(tokens)]
        own += [ref[pl.ds(row_first + r, tokens, stride=tokens), :] for r in range(rows)]
        return jnp.concatenate(own, axis=0)

    normed_out = lane_norm(products, gains_ref[1:2]).astype(bf16)
    out_gate = sigmoid(dot(chosen(normed_ref).astype(bf16), out_gate_ref[...]))
    updated = chosen(base_ref) + out_gate * dot(normed_out, out_weight_ref[...])
    normed_att = lane_norm(updated, gains_ref[2:3]).astype(bf16)
    own_pairs = rows * cols
    column_pairs = tokens * cols
    upd_ref[...] = updated[:column_pairs]
    att_f = normed_att.astype(f32)
    att_ref[...] = att_f[:column_pairs]

    own_at = pl.ds(pl.multiple_of(row_first * cols, own_pairs), own_pairs)
    own = att_ref[own_at, :].astype(bf16)
    column = normed_att[:column_pairs]
    queries = dot(own, qkv_ref[:, :width])
    keys = dot(column, qkv_ref[:, width : 2 * width]).astype(bf16)
    values = dot(column, qkv_ref[:, 2 * width :]).astype(bf16)
    own_gate = sigmoid(dot(own, att_gate_ref[...]))

    bias = []
    for r in range(rows):
        part = att_f[column_pairs + r * tokens : column_pairs + (r + 1) * tokens]
        spread = jnp.concatenate(
            [jnp.broadcast_to(part[k : k + 1], (cols, width)) for k in range(tokens)], axis=0
        )
        bias.append(round_bf16(dot_t(att_bias_ref[...], spread.astype(bf16))))

    head_of = lax.broadcasted_iota(jnp.int32, (own_pairs, width), 1) // head_dim
    queries = round_bf16(queries)
    by_head = jnp.concatenate(
        [jnp.where(head_of == h, queries, 0.0) for h in range(heads)], axis=0
    ).astype(bf16)
    scores = dot_t(by_head, keys) * (1.0 / math.sqrt(head_dim))
    biases = jnp.concatenate(
        [jnp.broadcast_to(bias[r][h : h + 1], (cols, column_pairs)) for h in range(heads) for r in range(rows)],
        axis=0,
    )
    key_bias = jnp.concatenate([key_bias_ref[...]] * (heads * rows), axis=0)
    scores = scores + biases + key_bias
    expo = jnp.exp(scores - jnp.max(scores, axis=-1, keepdims=True))
    shares = 1.0 / jnp.sum(expo, axis=-1, keepdims=True)
    mixed = dot(expo.astype(bf16), values) * shares
    attended = jnp.zeros((own_pairs, width), f32)
    for h in range(heads):
        attended = jnp.where(head_of == h, mixed[h * own_pairs : (h + 1) * own_pairs], attended)

    gated = (own_gate * attended).astype(bf16)
    result = upd_ref[own_at, :] + dot(gated, att_out_ref[...])
    out_ref[...] = result.reshape(rows, cols, width).astype(bf16)


def whole_pair_on_device(
    row_dim,
    pair_in,
    token_mask,
    positions,
    relpos_table,
    tri_norm_in,
    tri_in_weight,
    tri_in_gate,
    tri_out_gate,
    tri_norm_out,
    tri_out_weight,
    att_norm,
    att_qkv,
    att_gate,
    att_bias,
    att_out,
):
    rows, cols, width = pair_in.shape
    vmem = pl.BlockSpec(memory_space=pltpu.VMEM)
    smem = pl.BlockSpec(memory_space=pltpu.SMEM)
    params = pltpu.CompilerParams(vmem_limit_bytes=16 * 1024 * 1024)
    tokens, heads = row_dim * rows, att_bias.shape[1]

    beside = pl.CostEstimate(flops=STAGE_FLOPS, bytes_accessed=2**20, transcendentals=0)
    wide_out = jax.ShapeDtypeStruct((tokens * tokens, width), jnp.float32)
    staged = pl.pallas_call(
        functools.partial(stage_kernel, cols),
        out_shape=[
            wide_out,
            wide_out,
            jax.ShapeDtypeStruct((3, width), jnp.float32),
            jax.ShapeDtypeStruct((heads, width), att_bias.dtype),
            jax.ShapeDtypeStruct((cols, tokens * cols), jnp.float32),
        ],
        in_specs=[smem] * 2 + [vmem] * 5,
        out_specs=[vmem] * 5,
        compiler_params=params,
        cost_estimate=beside,
    )(
        token_mask,
        positions,
        relpos_table,
        tri_norm_in.reshape(1, width),
        tri_norm_out.reshape(1, width),
        att_norm.reshape(1, width),
        att_bias.T,
    )

    blocks = 2 * row_dim

    def move(piece, step):
        values, order = piece
        values = lax.ppermute(values, ("row", "col"), [(device, device ^ step) for device in range(blocks)])
        return values, tuple(place ^ step for place in order)

    chip = pl.pallas_call(
        own_kernel,
        out_shape=jax.ShapeDtypeStruct((2,) + pair_in.shape, pair_in.dtype),
        in_specs=[vmem],
        out_specs=vmem,
        compiler_params=params,
        cost_estimate=beside,
    )(pair_in)
    other, _ = move((pair_in, (0,)), 1)
    pieces = [(chip.at[1].set(other), (0, 1))]
    first = move(pieces[0], 9)
    pieces += [first, move(pieces[0], 7), move(pieces[0], 15)]
    both = jnp.concatenate([pieces[0][0], first[0]], axis=0), pieces[0][1] + first[1]
    pieces += [move(both, 5), move(both, 3)]
    gathered = [values for values, _ in pieces]
    orders = [order for _, order in pieces]

    weights = (tri_in_weight, tri_in_gate, tri_out_gate, tri_out_weight, att_qkv, att_gate, att_out)
    wide = pltpu.VMEM((tokens * tokens, width), jnp.float32)
    column = pltpu.VMEM((tokens * cols, width), jnp.float32)
    return pl.pallas_call(
        functools.partial(whole_pair_kernel, row_dim, heads, orders),
        out_shape=jax.ShapeDtypeStruct(pair_in.shape, pair_in.dtype),
        in_specs=[vmem] * (len(gathered) + 5 + len(weights)),
        out_specs=vmem,
        scratch_shapes=[wide] * 4 + [column] * 2,
        compiler_params=params,
    )(*gathered, *staged, *weights)


def attend_column(query_col, key_col, value_col, bias_all, key_bias, block_rows):
    tok_total = query_col.shape[0]
    scale = 1.0 / math.sqrt(query_col.shape[2])

    def one_block(block_idx):
        scores = (
            jnp.einsum("ihe,khe->hik", query_col, key_col, preferred_element_type=jnp.float32)
            * scale
        )
        scores = scores + bias_all.astype(jnp.float32) + key_bias[None, None, :]
        row_max = jnp.max(scores, axis=-1, keepdims=True)
        expo_f = jnp.exp(scores - row_max)
        totals = jnp.sum(expo_f, axis=-1)
        weights = expo_f.astype(jnp.bfloat16)
        result = jnp.einsum("hik,khe->ihe", weights, value_col, preferred_element_type=jnp.float32)
        return result / jnp.transpose(totals)[:, :, None]

    blocks = lax.map(one_block, jnp.arange(tok_total // block_rows))
    return blocks.reshape(tok_total, query_col.shape[1], query_col.shape[2])


def column_attention(columns, att_qkv, att_gate, bias_all, key_bias, head_local, head_dim):
    tok_total, col_count, channels = columns.shape
    local_width = head_local * head_dim
    weight_three = att_qkv.reshape(channels, 3, channels)
    qkv_all = jnp.einsum(
        "kmc,ctd->tmkd", columns, weight_three, preferred_element_type=jnp.float32
    ).astype(jnp.bfloat16)
    qkv_all = qkv_all.reshape(3, col_count, tok_total, head_local, head_dim)
    gate_val = jax.nn.sigmoid(
        jnp.einsum("kmc,cd->kmd", columns, att_gate, preferred_element_type=jnp.float32)
    )
    block_rows = min(1024, tok_total)

    def one_column(triple):
        return attend_column(triple[0], triple[1], triple[2], bias_all, key_bias, block_rows)

    attended = lax.map(one_column, (qkv_all[0], qkv_all[1], qkv_all[2]))
    attended = jnp.transpose(attended, (1, 0, 2, 3)).reshape(tok_total, col_count, local_width)
    return (gate_val * attended).astype(jnp.bfloat16)


def split_pair_on_device(
    pair_in,
    token_mask,
    positions,
    relpos_table,
    tri_norm_in,
    tri_in_weight,
    tri_in_gate,
    tri_out_gate,
    tri_norm_out,
    tri_out_weight,
    att_norm,
    att_qkv,
    att_gate,
    att_bias,
    att_out,
):
    row_count, col_count, channels = pair_in.shape
    row_first = lax.axis_index("row") * row_count
    col_first = lax.axis_index("col") * col_count
    mask_float = token_mask.astype(jnp.float32)
    row_mask = lax.dynamic_slice_in_dim(mask_float, row_first, row_count)
    col_mask = lax.dynamic_slice_in_dim(mask_float, col_first, col_count)
    row_pos = lax.dynamic_slice_in_dim(positions, row_first, row_count)
    col_pos = lax.dynamic_slice_in_dim(positions, col_first, col_count)
    bin_count = relpos_table.shape[0]
    bin_centre = bin_count // 2
    bucket = jnp.clip(row_pos[:, None] - col_pos[None, :], -bin_centre, bin_centre - 1) + bin_centre
    onehot = (bucket[:, :, None] == jnp.arange(bin_count, dtype=jnp.int32)[None, None, :]).astype(
        jnp.bfloat16
    )
    residual = pair_in.astype(jnp.float32) + jnp.einsum(
        "rjb,bc->rjc", onehot, relpos_table, preferred_element_type=jnp.float32
    )
    normed = layer_norm(residual, tri_norm_in).astype(jnp.bfloat16)
    pair_mask = row_mask[:, None] * col_mask[None, :]
    gate_in = jnp.einsum("rjc,cd->drj", normed, tri_in_gate, preferred_element_type=jnp.float32)
    proj_in = jnp.einsum("rjc,cd->drj", normed, tri_in_weight, preferred_element_type=jnp.float32)
    projected = (jax.nn.sigmoid(gate_in) * proj_in * pair_mask[None, :, :]).astype(jnp.bfloat16)
    left_ch, right_ch = (
        lax.all_to_all(projected[:channels], "row", split_axis=0, concat_axis=1, tiled=True),
        lax.all_to_all(projected[channels:], "row", split_axis=0, concat_axis=1, tiled=True),
    )
    right_rows = lax.all_to_all(right_ch, "col", split_axis=1, concat_axis=2, tiled=True)
    product_sum = jnp.einsum(
        "cik,cjk->cij",
        lax.all_gather(left_ch, "col", axis=2, tiled=True),
        right_rows,
        preferred_element_type=jnp.float32,
    )
    products = product_sum.astype(jnp.bfloat16)
    product_tile = lax.all_to_all(products, "row", split_axis=1, concat_axis=0, tiled=True)
    tri_x = jnp.transpose(product_tile, (1, 2, 0)).astype(jnp.float32)
    normed_out = layer_norm(tri_x, tri_norm_out).astype(jnp.bfloat16)
    out_gate = jax.nn.sigmoid(
        jnp.einsum("rjc,cd->rjd", normed, tri_out_gate, preferred_element_type=jnp.float32)
    )
    residual = residual + out_gate * jnp.einsum(
        "rjc,cd->rjd", normed_out, tri_out_weight, preferred_element_type=jnp.float32
    )
    normed_att = layer_norm(residual, att_norm).astype(jnp.bfloat16)
    bias_piece = jnp.einsum(
        "kic,ch->hik", normed_att, att_bias, preferred_element_type=jnp.float32
    ).astype(jnp.bfloat16)
    key_bias = (mask_float - 1.0) * 1000000000.0
    head_count = att_bias.shape[1]
    head_dim = channels // head_count
    columns = lax.all_to_all(normed_att, "row", split_axis=1, concat_axis=0, tiled=True)
    bias_half = lax.all_gather(bias_piece, "col", axis=1, tiled=True)
    bias_all = lax.all_gather(bias_half, "row", axis=2, tiled=True)
    gated = column_attention(columns, att_qkv, att_gate, bias_all, key_bias, head_count, head_dim)
    gated_tile = lax.all_to_all(gated, "row", split_axis=0, concat_axis=1, tiled=True)
    update = jnp.einsum("rjc,cd->rjd", gated_tile, att_out, preferred_element_type=jnp.float32)
    return (residual + update).astype(jnp.bfloat16)


def on_device(row_dim, col_dim, pair_in, *others):
    rows, cols, width = pair_in.shape
    tokens = row_dim * rows
    whole_bytes = tokens * tokens * width * pair_in.dtype.itemsize
    blocks = row_dim * col_dim
    tiled = cols % 8 == 0 and width == 128 and blocks == 16 and col_dim == 2
    if whole_bytes <= WHOLE_PAIR_BYTES and tiled:
        return whole_pair_on_device(row_dim, pair_in, *others)
    return split_pair_on_device(pair_in, *others)


def solution(mesh):
    return jax.shard_map(
        functools.partial(on_device, mesh.shape["row"], mesh.shape["col"]),
        mesh=mesh,
        in_specs=(P(("groups", "row"), "col", None), P("groups"), P("groups")) + (P(),) * 12,
        out_specs=P(("groups", "row"), "col", None),
        check_vma=False,
    )
```

```python
import functools
import math

import jax
import jax.numpy as jnp
from jax import lax
from jax.experimental import pallas as pl
from jax.experimental.pallas import tpu as pltpu
from jax.sharding import PartitionSpec as P

epsilon = 1e-05

WHOLE_PAIR_BYTES = 256 * 1024
STAGE_FLOPS = 10**9


def layer_norm(values, gain):
    mean_val = jnp.mean(values, axis=-1, keepdims=True)
    centred = values - mean_val
    var_val = jnp.mean(centred * centred, axis=-1, keepdims=True)
    return centred * lax.rsqrt(var_val + epsilon) * gain


def sigmoid(values):
    return 0.5 * jnp.tanh(0.5 * values) + 0.5


def dot(left, right):
    return jnp.dot(left, right, preferred_element_type=jnp.float32)


def dot_t(left, right):
    return lax.dot_general(
        left, right, (((1,), (1,)), ((), ())), preferred_element_type=jnp.float32
    )


def round_bf16(values):
    return values.astype(jnp.bfloat16).astype(jnp.float32)


def column_kernel(other_columns_ref):
    sub = lax.broadcasted_iota(jnp.int32, other_columns_ref.shape, 0)
    lane = lax.broadcasted_iota(jnp.int32, other_columns_ref.shape, 1)
    other_columns_ref[...] = jnp.where(lane % other_columns_ref.shape[0] == sub, 0.0, -jnp.inf)


def stage_kernel(
    pair_ref,
    mask_ref,
    pos_ref,
    table_ref,
    norm_in_ref,
    norm_out_ref,
    att_norm_ref,
    att_bias_ref,
    other_columns_ref,
    chip_ref,
    rel_ref,
    pair_mask_ref,
    gains_ref,
    bias_ref,
    key_bias_ref,
):
    chip_ref[0] = pair_ref[...]
    gains_ref[0:1] = norm_in_ref[...]
    gains_ref[1:2] = norm_out_ref[...]
    gains_ref[2:3] = att_norm_ref[...]
    bias_ref[...] = att_bias_ref[...]
    tokens, (cols, lanes) = pos_ref.shape[1], key_bias_ref.shape
    bins, width = table_ref.shape
    f32 = jnp.float32

    def by_row(ref):
        sub = lax.broadcasted_iota(jnp.int32, (tokens, tokens), 0)
        lane = lax.broadcasted_iota(jnp.int32, (tokens, tokens), 1)
        spread = jnp.where(sub == lane, jnp.broadcast_to(ref[...].astype(f32), (tokens, tokens)), 0.0)
        return jnp.broadcast_to(jnp.sum(spread, axis=1, keepdims=True), (tokens, bins))

    pos, mask = by_row(pos_ref), by_row(mask_ref)
    lane = lax.broadcasted_iota(jnp.int32, (cols, bins), 1).astype(f32)
    centre = float(bins // 2)
    hot = []
    for i in range(tokens):
        for first in range(0, tokens, cols):
            bucket = jnp.clip(pos[i : i + 1] - pos[first : first + cols], -centre, centre - 1.0) + centre
            hot.append((bucket == lane).astype(f32))
            at = i * tokens + first
            pair_mask_ref[at : at + cols, :] = mask[first : first + cols, :width] * mask[i : i + 1, :width]
    rel_ref[...] = dot(jnp.concatenate(hot, axis=0).astype(jnp.bfloat16), table_ref[...])
    key_of = lax.broadcasted_iota(jnp.int32, (tokens, lanes), 1) // cols
    own_key = key_of == lax.broadcasted_iota(jnp.int32, (tokens, lanes), 0)
    key_mask = jnp.sum(jnp.where(own_key, mask[:, :1], 0.0), axis=0, keepdims=True)
    key_bias_ref[...] = (key_mask - 1.0) * 1000000000.0 + other_columns_ref[...]


def tile_places(row_dim, rows, cols, order):
    me = lax.axis_index("row") * 2 + lax.axis_index("col")
    places = []
    for place in order:
        owner = me ^ place
        for r in range(rows):
            first = (owner // 2 * rows + r) * row_dim * rows + owner % 2 * cols
            places.append(pl.ds(pl.multiple_of(first, cols), cols))
    return places


def edge_operands(pieces, places, rel_ref, pair_mask_ref, gain, in_gate, in_weight):
    width = rel_ref.shape[1]
    blocks = [piece[at].astype(jnp.float32) for piece in pieces for at in range(piece.shape[0])]
    rows = len(places) // len(blocks)
    tiles = [block[r] for block in blocks for r in range(rows)]
    base = jnp.concatenate([tile + rel_ref[place, :] for tile, place in zip(tiles, places)], axis=0)
    pair_mask = jnp.concatenate([pair_mask_ref[place, :] for place in places], axis=0)
    normed = layer_norm(base, gain).astype(jnp.bfloat16)
    projected = sigmoid(dot(normed, in_gate)) * dot(normed, in_weight)
    left = round_bf16(projected[:, :width] * pair_mask)
    right = round_bf16(projected[:, width:] * pair_mask)
    return left, right, base, normed.astype(jnp.float32)


def early_kernel(row_dim, orders, *refs):
    piece_refs, (rel_ref, pair_mask_ref, gains_ref, in_weight_ref, in_gate_ref) = refs[:-9], refs[-9:-4]
    rows, cols = piece_refs[0].shape[1:3]
    places = tile_places(row_dim, rows, cols, sum(orders, ()))
    found = edge_operands(
        piece_refs, places, rel_ref, pair_mask_ref, gains_ref[0:1], in_gate_ref[...], in_weight_ref[...]
    )
    for ref, values in zip(refs[-4:], found):
        ref[...] = values


def whole_pair_kernel(row_dim, heads, early, orders, *refs):
    whole_pair_steps(row_dim, heads, early, orders, refs[: len(orders)], *refs[len(orders) :])


def whole_pair_steps(
    row_dim,
    heads,
    early,
    orders,
    piece_refs,
    early_left_ref,
    early_right_ref,
    early_base_ref,
    early_normed_ref,
    rel_ref,
    pair_mask_ref,
    gains_ref,
    att_bias_ref,
    key_bias_ref,
    in_weight_ref,
    in_gate_ref,
    out_gate_ref,
    out_weight_ref,
    qkv_ref,
    att_gate_ref,
    att_out_ref,
    out_ref,
    base_ref,
    normed_ref,
    left_ref,
    right_ref,
    att_ref,
    upd_ref,
):
    rows, cols, width = piece_refs[0].shape[1:]
    tokens = row_dim * rows
    head_dim = width // heads
    row_first = lax.axis_index("row") * rows
    col_first = pl.multiple_of(lax.axis_index("col") * cols, cols)
    f32, bf16 = jnp.float32, jnp.bfloat16

    def stored(places, found):
        for ref, values in zip((left_ref, right_ref, base_ref, normed_ref), found):
            for at, place in enumerate(places):
                ref[place, :] = values[at * cols : (at + 1) * cols]

    places = tile_places(row_dim, rows, cols, sum(orders, ()))
    found = edge_operands(
        piece_refs, places, rel_ref, pair_mask_ref, gains_ref[0:1], in_gate_ref[...], in_weight_ref[...]
    )
    stored(
        tile_places(row_dim, rows, cols, sum(early, ())),
        [ref[...] for ref in (early_left_ref, early_right_ref, early_base_ref, early_normed_ref)],
    )
    stored(places, found)

    right_at = [right_ref[pl.ds(col_first * tokens + m, cols, stride=tokens), :] for m in range(tokens)]
    products = []
    for i in range(tokens):
        total = left_ref[pl.ds(i * tokens, 1), :] * right_at[0]
        for m in range(1, tokens):
            total = total + left_ref[pl.ds(i * tokens + m, 1), :] * right_at[m]
        products.append(total)
    extra = [None] * rows
    for m in range(tokens):
        left_at = left_ref[pl.ds(m, tokens, stride=tokens), :]
        for r in range(rows):
            term = left_at * right_ref[pl.ds((row_first + r) * tokens + m, 1), :]
            extra[r] = term if m == 0 else extra[r] + term
    products = round_bf16(jnp.concatenate(products + extra, axis=0))

    def chosen(ref):
        own = [ref[pl.ds(i * tokens + col_first, cols), :] for i in range(tokens)]
        own += [ref[pl.ds(row_first + r, tokens, stride=tokens), :] for r in range(rows)]
        return jnp.concatenate(own, axis=0)

    normed_out = layer_norm(products, gains_ref[1:2]).astype(bf16)
    out_gate = sigmoid(dot(chosen(normed_ref).astype(bf16), out_gate_ref[...]))
    updated = chosen(base_ref) + out_gate * dot(normed_out, out_weight_ref[...])
    normed_att = layer_norm(updated, gains_ref[2:3]).astype(bf16)
    own_pairs = rows * cols
    column_pairs = tokens * cols
    upd_ref[...] = updated[:column_pairs]
    att_f = normed_att.astype(f32)
    att_ref[...] = att_f[:column_pairs]

    own_at = pl.ds(pl.multiple_of(row_first * cols, own_pairs), own_pairs)
    own = att_ref[own_at, :].astype(bf16)
    column = normed_att[:column_pairs]
    queries = dot(own, qkv_ref[:, :width])
    keys = dot(column, qkv_ref[:, width : 2 * width]).astype(bf16)
    values = dot(column, qkv_ref[:, 2 * width :]).astype(bf16)
    own_gate = sigmoid(dot(own, att_gate_ref[...]))

    bias = []
    for r in range(rows):
        part = att_f[column_pairs + r * tokens : column_pairs + (r + 1) * tokens]
        spread = jnp.concatenate(
            [jnp.broadcast_to(part[k : k + 1], (cols, width)) for k in range(tokens)], axis=0
        )
        bias.append(round_bf16(dot_t(att_bias_ref[...], spread.astype(bf16))))

    head_of = lax.broadcasted_iota(jnp.int32, (own_pairs, width), 1) // head_dim
    queries = round_bf16(queries)
    by_head = jnp.concatenate(
        [jnp.where(head_of == h, queries, 0.0) for h in range(heads)], axis=0
    ).astype(bf16)
    scores = dot_t(by_head, keys) * (1.0 / math.sqrt(head_dim))
    biases = jnp.concatenate(
        [jnp.broadcast_to(bias[r][h : h + 1], (cols, column_pairs)) for h in range(heads) for r in range(rows)],
        axis=0,
    )
    key_bias = jnp.concatenate([key_bias_ref[...]] * (heads * rows), axis=0)
    scores = scores + biases + key_bias
    expo = jnp.exp(scores - jnp.max(scores, axis=-1, keepdims=True))
    shares = 1.0 / jnp.sum(expo, axis=-1, keepdims=True)
    mixed = dot(expo.astype(bf16), values) * shares
    attended = jnp.zeros((own_pairs, width), f32)
    for h in range(heads):
        attended = jnp.where(head_of == h, mixed[h * own_pairs : (h + 1) * own_pairs], attended)

    gated = (own_gate * attended).astype(bf16)
    result = upd_ref[own_at, :] + dot(gated, att_out_ref[...])
    out_ref[...] = result.reshape(rows, cols, width).astype(bf16)


def whole_pair_on_device(
    row_dim,
    pair_in,
    token_mask,
    positions,
    relpos_table,
    tri_norm_in,
    tri_in_weight,
    tri_in_gate,
    tri_out_gate,
    tri_norm_out,
    tri_out_weight,
    att_norm,
    att_qkv,
    att_gate,
    att_bias,
    att_out,
):
    rows, cols, width = pair_in.shape
    vmem = pl.BlockSpec(memory_space=pltpu.VMEM)
    params = pltpu.CompilerParams(vmem_limit_bytes=16 * 1024 * 1024)
    tokens, heads = row_dim * rows, att_bias.shape[1]

    beside = pl.CostEstimate(flops=STAGE_FLOPS, bytes_accessed=2**20, transcendentals=0)
    wide_out = jax.ShapeDtypeStruct((tokens * tokens, width), jnp.float32)
    key_shape = jax.ShapeDtypeStruct((cols, tokens * cols), jnp.float32)
    other_columns = pl.pallas_call(
        column_kernel,
        out_shape=key_shape,
        out_specs=vmem,
        compiler_params=params,
        cost_estimate=beside,
    )()
    chip, *staged = pl.pallas_call(
        stage_kernel,
        out_shape=[
            jax.ShapeDtypeStruct((2,) + pair_in.shape, pair_in.dtype),
            wide_out,
            wide_out,
            jax.ShapeDtypeStruct((3, width), jnp.float32),
            jax.ShapeDtypeStruct((heads, width), att_bias.dtype),
            key_shape,
        ],
        in_specs=[vmem] * 9,
        out_specs=[vmem] * 6,
        compiler_params=params,
        cost_estimate=beside,
    )(
        pair_in,
        token_mask.reshape(1, tokens),
        positions.reshape(1, tokens),
        relpos_table,
        tri_norm_in.reshape(1, width),
        tri_norm_out.reshape(1, width),
        att_norm.reshape(1, width),
        att_bias.T,
        other_columns,
    )

    blocks = 2 * row_dim

    def move(piece, step):
        values, order = piece
        values = lax.ppermute(values, ("row", "col"), [(device, device ^ step) for device in range(blocks)])
        return values, tuple(place ^ step for place in order)

    other, _ = move((pair_in, (0,)), 1)
    pieces = [(chip.at[1].set(other), (0, 1))]
    first = move(pieces[0], 9)
    pieces += [first, move(pieces[0], 15), move(pieces[0], 7)]
    both = jnp.concatenate([pieces[0][0], first[0]], axis=0), pieces[0][1] + first[1]
    pieces += [move(both, 3), move(both, 5)]
    rel, pair_mask, gains, *_ = staged
    early = [order for _, order in pieces[:4]]
    half = jax.ShapeDtypeStruct((tokens * tokens // 2, width), jnp.float32)
    halves = pl.pallas_call(
        functools.partial(early_kernel, row_dim, early),
        out_shape=[half] * 4,
        in_specs=[vmem] * 9,
        out_specs=[vmem] * 4,
        compiler_params=params,
        cost_estimate=beside,
    )(*[values for values, _ in pieces[:4]], rel, pair_mask, gains, tri_in_weight, tri_in_gate)
    late = [order for _, order in pieces[4:]]
    gathered = [values for values, _ in pieces[4:]]
    weights = (tri_in_weight, tri_in_gate, tri_out_gate, tri_out_weight, att_qkv, att_gate, att_out)
    wide = pltpu.VMEM((tokens * tokens, width), jnp.float32)
    column = pltpu.VMEM((tokens * cols, width), jnp.float32)
    return pl.pallas_call(
        functools.partial(whole_pair_kernel, row_dim, heads, early, late),
        out_shape=jax.ShapeDtypeStruct(pair_in.shape, pair_in.dtype),
        in_specs=[vmem] * (len(gathered) + 9 + len(weights)),
        out_specs=vmem,
        scratch_shapes=[wide] * 4 + [column] * 2,
        compiler_params=params,
    )(*gathered, *halves, *staged, *weights)


def attend_column(query_col, key_col, value_col, bias_all, key_bias, block_rows):
    tok_total = query_col.shape[0]
    scale = 1.0 / math.sqrt(query_col.shape[2])

    def one_block(block_idx):
        scores = (
            jnp.einsum("ihe,khe->hik", query_col, key_col, preferred_element_type=jnp.float32)
            * scale
        )
        scores = scores + bias_all.astype(jnp.float32) + key_bias[None, None, :]
        row_max = jnp.max(scores, axis=-1, keepdims=True)
        expo_f = jnp.exp(scores - row_max)
        totals = jnp.sum(expo_f, axis=-1)
        weights = expo_f.astype(jnp.bfloat16)
        result = jnp.einsum("hik,khe->ihe", weights, value_col, preferred_element_type=jnp.float32)
        return result / jnp.transpose(totals)[:, :, None]

    blocks = lax.map(one_block, jnp.arange(tok_total // block_rows))
    return blocks.reshape(tok_total, query_col.shape[1], query_col.shape[2])


def column_attention(columns, att_qkv, att_gate, bias_all, key_bias, head_local, head_dim):
    tok_total, col_count, channels = columns.shape
    local_width = head_local * head_dim
    weight_three = att_qkv.reshape(channels, 3, channels)
    qkv_all = jnp.einsum(
        "kmc,ctd->tmkd", columns, weight_three, preferred_element_type=jnp.float32
    ).astype(jnp.bfloat16)
    qkv_all = qkv_all.reshape(3, col_count, tok_total, head_local, head_dim)
    gate_val = jax.nn.sigmoid(
        jnp.einsum("kmc,cd->kmd", columns, att_gate, preferred_element_type=jnp.float32)
    )
    block_rows = min(1024, tok_total)

    def one_column(triple):
        return attend_column(triple[0], triple[1], triple[2], bias_all, key_bias, block_rows)

    attended = lax.map(one_column, (qkv_all[0], qkv_all[1], qkv_all[2]))
    attended = jnp.transpose(attended, (1, 0, 2, 3)).reshape(tok_total, col_count, local_width)
    return (gate_val * attended).astype(jnp.bfloat16)


def split_pair_on_device(
    pair_in,
    token_mask,
    positions,
    relpos_table,
    tri_norm_in,
    tri_in_weight,
    tri_in_gate,
    tri_out_gate,
    tri_norm_out,
    tri_out_weight,
    att_norm,
    att_qkv,
    att_gate,
    att_bias,
    att_out,
):
    row_count, col_count, channels = pair_in.shape
    row_first = lax.axis_index("row") * row_count
    col_first = lax.axis_index("col") * col_count
    mask_float = token_mask.astype(jnp.float32)
    row_mask = lax.dynamic_slice_in_dim(mask_float, row_first, row_count)
    col_mask = lax.dynamic_slice_in_dim(mask_float, col_first, col_count)
    row_pos = lax.dynamic_slice_in_dim(positions, row_first, row_count)
    col_pos = lax.dynamic_slice_in_dim(positions, col_first, col_count)
    bin_count = relpos_table.shape[0]
    bin_centre = bin_count // 2
    bucket = jnp.clip(row_pos[:, None] - col_pos[None, :], -bin_centre, bin_centre - 1) + bin_centre
    onehot = (bucket[:, :, None] == jnp.arange(bin_count, dtype=jnp.int32)[None, None, :]).astype(
        jnp.bfloat16
    )
    residual = pair_in.astype(jnp.float32) + jnp.einsum(
        "rjb,bc->rjc", onehot, relpos_table, preferred_element_type=jnp.float32
    )
    normed = layer_norm(residual, tri_norm_in).astype(jnp.bfloat16)
    pair_mask = row_mask[:, None] * col_mask[None, :]
    gate_in = jnp.einsum("rjc,cd->drj", normed, tri_in_gate, preferred_element_type=jnp.float32)
    proj_in = jnp.einsum("rjc,cd->drj", normed, tri_in_weight, preferred_element_type=jnp.float32)
    projected = (jax.nn.sigmoid(gate_in) * proj_in * pair_mask[None, :, :]).astype(jnp.bfloat16)
    left_ch, right_ch = (
        lax.all_to_all(projected[:channels], "row", split_axis=0, concat_axis=1, tiled=True),
        lax.all_to_all(projected[channels:], "row", split_axis=0, concat_axis=1, tiled=True),
    )
    right_rows = lax.all_to_all(right_ch, "col", split_axis=1, concat_axis=2, tiled=True)
    product_sum = jnp.einsum(
        "cik,cjk->cij",
        lax.all_gather(left_ch, "col", axis=2, tiled=True),
        right_rows,
        preferred_element_type=jnp.float32,
    )
    products = product_sum.astype(jnp.bfloat16)
    product_tile = lax.all_to_all(products, "row", split_axis=1, concat_axis=0, tiled=True)
    tri_x = jnp.transpose(product_tile, (1, 2, 0)).astype(jnp.float32)
    normed_out = layer_norm(tri_x, tri_norm_out).astype(jnp.bfloat16)
    out_gate = jax.nn.sigmoid(
        jnp.einsum("rjc,cd->rjd", normed, tri_out_gate, preferred_element_type=jnp.float32)
    )
    residual = residual + out_gate * jnp.einsum(
        "rjc,cd->rjd", normed_out, tri_out_weight, preferred_element_type=jnp.float32
    )
    normed_att = layer_norm(residual, att_norm).astype(jnp.bfloat16)
    bias_piece = jnp.einsum(
        "kic,ch->hik", normed_att, att_bias, preferred_element_type=jnp.float32
    ).astype(jnp.bfloat16)
    key_bias = (mask_float - 1.0) * 1000000000.0
    head_count = att_bias.shape[1]
    head_dim = channels // head_count
    columns = lax.all_to_all(normed_att, "row", split_axis=1, concat_axis=0, tiled=True)
    bias_half = lax.all_gather(bias_piece, "col", axis=1, tiled=True)
    bias_all = lax.all_gather(bias_half, "row", axis=2, tiled=True)
    gated = column_attention(columns, att_qkv, att_gate, bias_all, key_bias, head_count, head_dim)
    gated_tile = lax.all_to_all(gated, "row", split_axis=0, concat_axis=1, tiled=True)
    update = jnp.einsum("rjc,cd->rjd", gated_tile, att_out, preferred_element_type=jnp.float32)
    return (residual + update).astype(jnp.bfloat16)


def on_device(row_dim, col_dim, pair_in, *others):
    rows, cols, width = pair_in.shape
    tokens = row_dim * rows
    whole_bytes = tokens * tokens * width * pair_in.dtype.itemsize
    blocks = row_dim * col_dim
    tiled = cols % 8 == 0 and width == 128 and blocks == 16 and col_dim == 2
    if whole_bytes <= WHOLE_PAIR_BYTES and tiled:
        return whole_pair_on_device(row_dim, pair_in, *others)
    return split_pair_on_device(pair_in, *others)


def solution(mesh):
    return jax.shard_map(
        functools.partial(on_device, mesh.shape["row"], mesh.shape["col"]),
        mesh=mesh,
        in_specs=(P(("groups", "row"), "col", None), P("groups"), P("groups")) + (P(),) * 12,
        out_specs=P(("groups", "row"), "col", None),
        check_vma=False,
    )
```

```python
import functools
import math

import jax
import jax.numpy as jnp
from jax import lax
from jax.experimental import pallas as pl
from jax.experimental.pallas import tpu as pltpu
from jax.sharding import PartitionSpec as P

epsilon = 1e-05

WHOLE_PAIR_BYTES = 256 * 1024
STAGE_FLOPS = 10**9


def layer_norm(values, gain):
    mean_val = jnp.mean(values, axis=-1, keepdims=True)
    centred = values - mean_val
    var_val = jnp.mean(centred * centred, axis=-1, keepdims=True)
    return centred * lax.rsqrt(var_val + epsilon) * gain


def sigmoid(values):
    return 0.5 * jnp.tanh(0.5 * values) + 0.5


def dot(left, right):
    return jnp.dot(left, right, preferred_element_type=jnp.float32)


def dot_t(left, right):
    return lax.dot_general(
        left, right, (((1,), (1,)), ((), ())), preferred_element_type=jnp.float32
    )


def round_bf16(values):
    return values.astype(jnp.bfloat16).astype(jnp.float32)


def column_kernel(other_columns_ref):
    sub = lax.broadcasted_iota(jnp.int32, other_columns_ref.shape, 0)
    lane = lax.broadcasted_iota(jnp.int32, other_columns_ref.shape, 1)
    other_columns_ref[...] = jnp.where(lane % other_columns_ref.shape[0] == sub, 0.0, -jnp.inf)


def stage_kernel(
    pair_ref,
    mask_ref,
    pos_ref,
    table_ref,
    norm_in_ref,
    norm_out_ref,
    att_norm_ref,
    att_bias_ref,
    other_columns_ref,
    chip_ref,
    rel_ref,
    pair_mask_ref,
    gains_ref,
    bias_ref,
    key_bias_ref,
):
    chip_ref[0] = pair_ref[...]
    gains_ref[0:1] = norm_in_ref[...]
    gains_ref[1:2] = norm_out_ref[...]
    gains_ref[2:3] = att_norm_ref[...]
    bias_ref[...] = att_bias_ref[...]
    tokens, (cols, lanes) = pos_ref.shape[1], key_bias_ref.shape
    bins, width = table_ref.shape
    f32 = jnp.float32

    def by_row(ref):
        sub = lax.broadcasted_iota(jnp.int32, (tokens, tokens), 0)
        lane = lax.broadcasted_iota(jnp.int32, (tokens, tokens), 1)
        spread = jnp.where(sub == lane, jnp.broadcast_to(ref[...].astype(f32), (tokens, tokens)), 0.0)
        return jnp.broadcast_to(jnp.sum(spread, axis=1, keepdims=True), (tokens, bins))

    pos, mask = by_row(pos_ref), by_row(mask_ref)
    lane = lax.broadcasted_iota(jnp.int32, (cols, bins), 1).astype(f32)
    centre = float(bins // 2)
    hot = []
    for i in range(tokens):
        for first in range(0, tokens, cols):
            bucket = jnp.clip(pos[i : i + 1] - pos[first : first + cols], -centre, centre - 1.0) + centre
            hot.append((bucket == lane).astype(f32))
            at = i * tokens + first
            pair_mask_ref[at : at + cols, :] = mask[first : first + cols, :width] * mask[i : i + 1, :width]
    rel_ref[...] = dot(jnp.concatenate(hot, axis=0).astype(jnp.bfloat16), table_ref[...])
    key_of = lax.broadcasted_iota(jnp.int32, (tokens, lanes), 1) // cols
    own_key = key_of == lax.broadcasted_iota(jnp.int32, (tokens, lanes), 0)
    key_mask = jnp.sum(jnp.where(own_key, mask[:, :1], 0.0), axis=0, keepdims=True)
    key_bias_ref[...] = (key_mask - 1.0) * 1000000000.0 + other_columns_ref[...]


def tile_places(row_dim, rows, cols, order):
    me = lax.axis_index("row") * 2 + lax.axis_index("col")
    places = []
    for place in order:
        owner = me ^ place
        for r in range(rows):
            first = (owner // 2 * rows + r) * row_dim * rows + owner % 2 * cols
            places.append(pl.ds(pl.multiple_of(first, cols), cols))
    return places


def edge_operands(pieces, places, rel_ref, pair_mask_ref, gain, in_gate, in_weight):
    width = rel_ref.shape[1]
    blocks = [piece[at].astype(jnp.float32) for piece in pieces for at in range(piece.shape[0])]
    rows = len(places) // len(blocks)
    tiles = [block[r] for block in blocks for r in range(rows)]
    base = jnp.concatenate([tile + rel_ref[place, :] for tile, place in zip(tiles, places)], axis=0)
    pair_mask = jnp.concatenate([pair_mask_ref[place, :] for place in places], axis=0)
    normed = layer_norm(base, gain).astype(jnp.bfloat16)
    projected = sigmoid(dot(normed, in_gate)) * dot(normed, in_weight)
    left = round_bf16(projected[:, :width] * pair_mask)
    right = round_bf16(projected[:, width:] * pair_mask)
    return left, right, base, normed.astype(jnp.float32)


def early_kernel(row_dim, orders, *refs):
    piece_refs = refs[: len(orders)]
    rel_ref, pair_mask_ref, gains_ref, in_weight_ref, in_gate_ref = refs[len(orders) : len(orders) + 5]
    rows, cols = piece_refs[0].shape[1:3]
    places = tile_places(row_dim, rows, cols, sum(orders, ()))
    found = edge_operands(
        piece_refs, places, rel_ref, pair_mask_ref, gains_ref[0:1], in_gate_ref[...], in_weight_ref[...]
    )
    for ref, values in zip(refs[-4:], found):
        ref[...] = values


def whole_pair_kernel(row_dim, heads, early, orders, *refs):
    whole_pair_steps(row_dim, heads, early, orders, refs[: len(orders)], *refs[len(orders) :])


def whole_pair_steps(
    row_dim,
    heads,
    early,
    orders,
    piece_refs,
    early_left_ref,
    early_right_ref,
    early_base_ref,
    early_normed_ref,
    rel_ref,
    pair_mask_ref,
    gains_ref,
    att_bias_ref,
    key_bias_ref,
    in_weight_ref,
    in_gate_ref,
    out_gate_ref,
    out_weight_ref,
    qkv_ref,
    att_gate_ref,
    att_out_ref,
    out_ref,
    base_ref,
    normed_ref,
    left_ref,
    right_ref,
    att_ref,
    upd_ref,
):
    rows, cols, width = piece_refs[0].shape[1:]
    tokens = row_dim * rows
    head_dim = width // heads
    row_first = lax.axis_index("row") * rows
    col_first = pl.multiple_of(lax.axis_index("col") * cols, cols)
    f32, bf16 = jnp.float32, jnp.bfloat16

    def stored(places, found):
        for ref, values in zip((left_ref, right_ref, base_ref, normed_ref), found):
            for at, place in enumerate(places):
                ref[place, :] = values[at * cols : (at + 1) * cols]

    places = tile_places(row_dim, rows, cols, sum(orders, ()))
    found = edge_operands(
        piece_refs, places, rel_ref, pair_mask_ref, gains_ref[0:1], in_gate_ref[...], in_weight_ref[...]
    )
    stored(
        tile_places(row_dim, rows, cols, sum(early, ())),
        [ref[...] for ref in (early_left_ref, early_right_ref, early_base_ref, early_normed_ref)],
    )
    stored(places, found)

    right_at = [right_ref[pl.ds(col_first * tokens + m, cols, stride=tokens), :] for m in range(tokens)]
    products = []
    for i in range(tokens):
        total = left_ref[pl.ds(i * tokens, 1), :] * right_at[0]
        for m in range(1, tokens):
            total = total + left_ref[pl.ds(i * tokens + m, 1), :] * right_at[m]
        products.append(total)
    extra = [None] * rows
    for m in range(tokens):
        left_at = left_ref[pl.ds(m, tokens, stride=tokens), :]
        for r in range(rows):
            term = left_at * right_ref[pl.ds((row_first + r) * tokens + m, 1), :]
            extra[r] = term if m == 0 else extra[r] + term
    products = round_bf16(jnp.concatenate(products + extra, axis=0))

    def chosen(ref):
        own = [ref[pl.ds(i * tokens + col_first, cols), :] for i in range(tokens)]
        own += [ref[pl.ds(row_first + r, tokens, stride=tokens), :] for r in range(rows)]
        return jnp.concatenate(own, axis=0)

    normed_out = layer_norm(products, gains_ref[1:2]).astype(bf16)
    out_gate = sigmoid(dot(chosen(normed_ref).astype(bf16), out_gate_ref[...]))
    updated = chosen(base_ref) + out_gate * dot(normed_out, out_weight_ref[...])
    normed_att = layer_norm(updated, gains_ref[2:3]).astype(bf16)
    own_pairs = rows * cols
    column_pairs = tokens * cols
    upd_ref[...] = updated[:column_pairs]
    att_f = normed_att.astype(f32)
    att_ref[...] = att_f[:column_pairs]

    own_at = pl.ds(pl.multiple_of(row_first * cols, own_pairs), own_pairs)
    own = att_ref[own_at, :].astype(bf16)
    column = normed_att[:column_pairs]
    queries = dot(own, qkv_ref[:, :width])
    keys = dot(column, qkv_ref[:, width : 2 * width]).astype(bf16)
    values = dot(column, qkv_ref[:, 2 * width :]).astype(bf16)
    own_gate = sigmoid(dot(own, att_gate_ref[...]))

    bias = []
    for r in range(rows):
        part = att_f[column_pairs + r * tokens : column_pairs + (r + 1) * tokens]
        spread = jnp.concatenate(
            [jnp.broadcast_to(part[k : k + 1], (cols, width)) for k in range(tokens)], axis=0
        )
        bias.append(round_bf16(dot_t(att_bias_ref[...], spread.astype(bf16))))

    head_of = lax.broadcasted_iota(jnp.int32, (own_pairs, width), 1) // head_dim
    queries = round_bf16(queries)
    by_head = jnp.concatenate(
        [jnp.where(head_of == h, queries, 0.0) for h in range(heads)], axis=0
    ).astype(bf16)
    scores = dot_t(by_head, keys) * (1.0 / math.sqrt(head_dim))
    biases = jnp.concatenate(
        [jnp.broadcast_to(bias[r][h : h + 1], (cols, column_pairs)) for h in range(heads) for r in range(rows)],
        axis=0,
    )
    key_bias = jnp.concatenate([key_bias_ref[...]] * (heads * rows), axis=0)
    scores = scores + biases + key_bias
    expo = jnp.exp(scores - jnp.max(scores, axis=-1, keepdims=True))
    shares = 1.0 / jnp.sum(expo, axis=-1, keepdims=True)
    mixed = dot(expo.astype(bf16), values) * shares
    attended = jnp.zeros((own_pairs, width), f32)
    for h in range(heads):
        attended = jnp.where(head_of == h, mixed[h * own_pairs : (h + 1) * own_pairs], attended)

    gated = (own_gate * attended).astype(bf16)
    result = upd_ref[own_at, :] + dot(gated, att_out_ref[...])
    out_ref[...] = result.reshape(rows, cols, width).astype(bf16)


def whole_pair_on_device(
    row_dim,
    pair_in,
    token_mask,
    positions,
    relpos_table,
    tri_norm_in,
    tri_in_weight,
    tri_in_gate,
    tri_out_gate,
    tri_norm_out,
    tri_out_weight,
    att_norm,
    att_qkv,
    att_gate,
    att_bias,
    att_out,
):
    rows, cols, width = pair_in.shape
    vmem = pl.BlockSpec(memory_space=pltpu.VMEM)
    params = pltpu.CompilerParams(vmem_limit_bytes=16 * 1024 * 1024)
    tokens, heads = row_dim * rows, att_bias.shape[1]

    beside = pl.CostEstimate(flops=STAGE_FLOPS, bytes_accessed=2**20, transcendentals=0)
    wide_out = jax.ShapeDtypeStruct((tokens * tokens, width), jnp.float32)
    key_shape = jax.ShapeDtypeStruct((cols, tokens * cols), jnp.float32)
    other_columns = pl.pallas_call(
        column_kernel,
        out_shape=key_shape,
        out_specs=vmem,
        compiler_params=params,
        cost_estimate=beside,
    )()
    chip, *staged = pl.pallas_call(
        stage_kernel,
        out_shape=[
            jax.ShapeDtypeStruct((2,) + pair_in.shape, pair_in.dtype),
            wide_out,
            wide_out,
            jax.ShapeDtypeStruct((3, width), jnp.float32),
            jax.ShapeDtypeStruct((heads, width), att_bias.dtype),
            key_shape,
        ],
        in_specs=[vmem] * 9,
        out_specs=[vmem] * 6,
        compiler_params=params,
        cost_estimate=beside,
    )(
        pair_in,
        token_mask.reshape(1, tokens),
        positions.reshape(1, tokens),
        relpos_table,
        tri_norm_in.reshape(1, width),
        tri_norm_out.reshape(1, width),
        att_norm.reshape(1, width),
        att_bias.T,
        other_columns,
    )

    blocks = 2 * row_dim

    def move(piece, step):
        values, order = piece
        values = lax.ppermute(values, ("row", "col"), [(device, device ^ step) for device in range(blocks)])
        return values, tuple(place ^ step for place in order)

    other, _ = move((pair_in, (0,)), 1)
    pieces = [(chip.at[1].set(other), (0, 1))]
    first = move(pieces[0], 9)
    pieces += [first, move(pieces[0], 15), move(pieces[0], 7)]
    both = jnp.concatenate([pieces[0][0], first[0]], axis=0), pieces[0][1] + first[1]
    pieces += [move(both, 3), move(both, 5)]
    weights = (tri_in_weight, tri_in_gate, tri_out_gate, tri_out_weight, att_qkv, att_gate, att_out)
    rel, pair_mask, gains, *_ = staged
    early = [order for _, order in pieces[:4]]
    half = jax.ShapeDtypeStruct((tokens * tokens // 2, width), jnp.float32)
    halves = pl.pallas_call(
        functools.partial(early_kernel, row_dim, early),
        out_shape=[half] * 4,
        in_specs=[vmem] * (7 + len(weights)),
        out_specs=[vmem] * 4,
        compiler_params=params,
        cost_estimate=beside,
    )(*[values for values, _ in pieces[:4]], rel, pair_mask, gains, *weights)
    late = [order for _, order in pieces[4:]]
    gathered = [values for values, _ in pieces[4:]]
    wide = pltpu.VMEM((tokens * tokens, width), jnp.float32)
    column = pltpu.VMEM((tokens * cols, width), jnp.float32)
    return pl.pallas_call(
        functools.partial(whole_pair_kernel, row_dim, heads, early, late),
        out_shape=jax.ShapeDtypeStruct(pair_in.shape, pair_in.dtype),
        in_specs=[vmem] * (len(gathered) + 9 + len(weights)),
        out_specs=vmem,
        scratch_shapes=[wide] * 4 + [column] * 2,
        compiler_params=params,
    )(*gathered, *halves, *staged, *weights)


def attend_column(query_col, key_col, value_col, bias_all, key_bias, block_rows):
    tok_total = query_col.shape[0]
    scale = 1.0 / math.sqrt(query_col.shape[2])

    def one_block(block_idx):
        scores = (
            jnp.einsum("ihe,khe->hik", query_col, key_col, preferred_element_type=jnp.float32)
            * scale
        )
        scores = scores + bias_all.astype(jnp.float32) + key_bias[None, None, :]
        row_max = jnp.max(scores, axis=-1, keepdims=True)
        expo_f = jnp.exp(scores - row_max)
        totals = jnp.sum(expo_f, axis=-1)
        weights = expo_f.astype(jnp.bfloat16)
        result = jnp.einsum("hik,khe->ihe", weights, value_col, preferred_element_type=jnp.float32)
        return result / jnp.transpose(totals)[:, :, None]

    blocks = lax.map(one_block, jnp.arange(tok_total // block_rows))
    return blocks.reshape(tok_total, query_col.shape[1], query_col.shape[2])


def column_attention(columns, att_qkv, att_gate, bias_all, key_bias, head_local, head_dim):
    tok_total, col_count, channels = columns.shape
    local_width = head_local * head_dim
    weight_three = att_qkv.reshape(channels, 3, channels)
    qkv_all = jnp.einsum(
        "kmc,ctd->tmkd", columns, weight_three, preferred_element_type=jnp.float32
    ).astype(jnp.bfloat16)
    qkv_all = qkv_all.reshape(3, col_count, tok_total, head_local, head_dim)
    gate_val = jax.nn.sigmoid(
        jnp.einsum("kmc,cd->kmd", columns, att_gate, preferred_element_type=jnp.float32)
    )
    block_rows = min(1024, tok_total)

    def one_column(triple):
        return attend_column(triple[0], triple[1], triple[2], bias_all, key_bias, block_rows)

    attended = lax.map(one_column, (qkv_all[0], qkv_all[1], qkv_all[2]))
    attended = jnp.transpose(attended, (1, 0, 2, 3)).reshape(tok_total, col_count, local_width)
    return (gate_val * attended).astype(jnp.bfloat16)


def split_pair_on_device(
    pair_in,
    token_mask,
    positions,
    relpos_table,
    tri_norm_in,
    tri_in_weight,
    tri_in_gate,
    tri_out_gate,
    tri_norm_out,
    tri_out_weight,
    att_norm,
    att_qkv,
    att_gate,
    att_bias,
    att_out,
):
    row_count, col_count, channels = pair_in.shape
    row_first = lax.axis_index("row") * row_count
    col_first = lax.axis_index("col") * col_count
    mask_float = token_mask.astype(jnp.float32)
    row_mask = lax.dynamic_slice_in_dim(mask_float, row_first, row_count)
    col_mask = lax.dynamic_slice_in_dim(mask_float, col_first, col_count)
    row_pos = lax.dynamic_slice_in_dim(positions, row_first, row_count)
    col_pos = lax.dynamic_slice_in_dim(positions, col_first, col_count)
    bin_count = relpos_table.shape[0]
    bin_centre = bin_count // 2
    bucket = jnp.clip(row_pos[:, None] - col_pos[None, :], -bin_centre, bin_centre - 1) + bin_centre
    onehot = (bucket[:, :, None] == jnp.arange(bin_count, dtype=jnp.int32)[None, None, :]).astype(
        jnp.bfloat16
    )
    residual = pair_in.astype(jnp.float32) + jnp.einsum(
        "rjb,bc->rjc", onehot, relpos_table, preferred_element_type=jnp.float32
    )
    normed = layer_norm(residual, tri_norm_in).astype(jnp.bfloat16)
    pair_mask = row_mask[:, None] * col_mask[None, :]
    gate_in = jnp.einsum("rjc,cd->drj", normed, tri_in_gate, preferred_element_type=jnp.float32)
    proj_in = jnp.einsum("rjc,cd->drj", normed, tri_in_weight, preferred_element_type=jnp.float32)
    projected = (jax.nn.sigmoid(gate_in) * proj_in * pair_mask[None, :, :]).astype(jnp.bfloat16)
    left_ch, right_ch = (
        lax.all_to_all(projected[:channels], "row", split_axis=0, concat_axis=1, tiled=True),
        lax.all_to_all(projected[channels:], "row", split_axis=0, concat_axis=1, tiled=True),
    )
    right_rows = lax.all_to_all(right_ch, "col", split_axis=1, concat_axis=2, tiled=True)
    product_sum = jnp.einsum(
        "cik,cjk->cij",
        lax.all_gather(left_ch, "col", axis=2, tiled=True),
        right_rows,
        preferred_element_type=jnp.float32,
    )
    products = product_sum.astype(jnp.bfloat16)
    product_tile = lax.all_to_all(products, "row", split_axis=1, concat_axis=0, tiled=True)
    tri_x = jnp.transpose(product_tile, (1, 2, 0)).astype(jnp.float32)
    normed_out = layer_norm(tri_x, tri_norm_out).astype(jnp.bfloat16)
    out_gate = jax.nn.sigmoid(
        jnp.einsum("rjc,cd->rjd", normed, tri_out_gate, preferred_element_type=jnp.float32)
    )
    residual = residual + out_gate * jnp.einsum(
        "rjc,cd->rjd", normed_out, tri_out_weight, preferred_element_type=jnp.float32
    )
    normed_att = layer_norm(residual, att_norm).astype(jnp.bfloat16)
    bias_piece = jnp.einsum(
        "kic,ch->hik", normed_att, att_bias, preferred_element_type=jnp.float32
    ).astype(jnp.bfloat16)
    key_bias = (mask_float - 1.0) * 1000000000.0
    head_count = att_bias.shape[1]
    head_dim = channels // head_count
    columns = lax.all_to_all(normed_att, "row", split_axis=1, concat_axis=0, tiled=True)
    bias_half = lax.all_gather(bias_piece, "col", axis=1, tiled=True)
    bias_all = lax.all_gather(bias_half, "row", axis=2, tiled=True)
    gated = column_attention(columns, att_qkv, att_gate, bias_all, key_bias, head_count, head_dim)
    gated_tile = lax.all_to_all(gated, "row", split_axis=0, concat_axis=1, tiled=True)
    update = jnp.einsum("rjc,cd->rjd", gated_tile, att_out, preferred_element_type=jnp.float32)
    return (residual + update).astype(jnp.bfloat16)


def on_device(row_dim, col_dim, pair_in, *others):
    rows, cols, width = pair_in.shape
    tokens = row_dim * rows
    whole_bytes = tokens * tokens * width * pair_in.dtype.itemsize
    blocks = row_dim * col_dim
    tiled = cols % 8 == 0 and width == 128 and blocks == 16 and col_dim == 2
    if whole_bytes <= WHOLE_PAIR_BYTES and tiled:
        return whole_pair_on_device(row_dim, pair_in, *others)
    return split_pair_on_device(pair_in, *others)


def solution(mesh):
    return jax.shard_map(
        functools.partial(on_device, mesh.shape["row"], mesh.shape["col"]),
        mesh=mesh,
        in_specs=(P(("groups", "row"), "col", None), P("groups"), P("groups")) + (P(),) * 12,
        out_specs=P(("groups", "row"), "col", None),
        check_vma=False,
    )
```

```python
import functools
import math

import jax
import jax.numpy as jnp
from jax import lax
from jax.experimental import pallas as pl
from jax.experimental.pallas import tpu as pltpu
from jax.sharding import PartitionSpec as P

epsilon = 1e-05

WHOLE_PAIR_BYTES = 256 * 1024
STAGE_FLOPS = 10**9


def layer_norm(values, gain):
    mean_val = jnp.mean(values, axis=-1, keepdims=True)
    centred = values - mean_val
    var_val = jnp.mean(centred * centred, axis=-1, keepdims=True)
    return centred * lax.rsqrt(var_val + epsilon) * gain


def sigmoid(values):
    return 0.5 * jnp.tanh(0.5 * values) + 0.5


def dot(left, right):
    return jnp.dot(left, right, preferred_element_type=jnp.float32)


def dot_t(left, right):
    return lax.dot_general(
        left, right, (((1,), (1,)), ((), ())), preferred_element_type=jnp.float32
    )


def round_bf16(values):
    return values.astype(jnp.bfloat16).astype(jnp.float32)


def column_kernel(other_columns_ref):
    sub = lax.broadcasted_iota(jnp.int32, other_columns_ref.shape, 0)
    lane = lax.broadcasted_iota(jnp.int32, other_columns_ref.shape, 1)
    cols, lanes = other_columns_ref.shape
    other_columns_ref[...] = jnp.where(lane // (lanes // cols) == sub, 0.0, -jnp.inf)


def stage_kernel(
    pair_ref,
    mask_ref,
    pos_ref,
    table_ref,
    norm_in_ref,
    norm_out_ref,
    att_norm_ref,
    att_bias_ref,
    other_columns_ref,
    chip_ref,
    rel_ref,
    pair_mask_ref,
    gains_ref,
    bias_ref,
    key_bias_ref,
):
    chip_ref[0] = pair_ref[...]
    gains_ref[0:1] = norm_in_ref[...]
    gains_ref[1:2] = norm_out_ref[...]
    gains_ref[2:3] = att_norm_ref[...]
    bias_ref[...] = att_bias_ref[...]
    tokens, (cols, lanes) = pos_ref.shape[1], key_bias_ref.shape
    bins, width = table_ref.shape
    f32 = jnp.float32

    def by_row(ref):
        sub = lax.broadcasted_iota(jnp.int32, (tokens, tokens), 0)
        lane = lax.broadcasted_iota(jnp.int32, (tokens, tokens), 1)
        spread = jnp.where(sub == lane, jnp.broadcast_to(ref[...].astype(f32), (tokens, tokens)), 0.0)
        return jnp.broadcast_to(jnp.sum(spread, axis=1, keepdims=True), (tokens, bins))

    pos, mask = by_row(pos_ref), by_row(mask_ref)
    lane = lax.broadcasted_iota(jnp.int32, (cols, bins), 1).astype(f32)
    centre = float(bins // 2)
    hot = []
    for i in range(tokens):
        for first in range(0, tokens, cols):
            bucket = jnp.clip(pos[i : i + 1] - pos[first : first + cols], -centre, centre - 1.0) + centre
            hot.append((bucket == lane).astype(f32))
            at = i * tokens + first
            pair_mask_ref[at : at + cols, :] = mask[first : first + cols, :width] * mask[i : i + 1, :width]
    rel_ref[...] = dot(jnp.concatenate(hot, axis=0).astype(jnp.bfloat16), table_ref[...])
    key_of = lax.broadcasted_iota(jnp.int32, (tokens, lanes), 1) % tokens
    own_key = key_of == lax.broadcasted_iota(jnp.int32, (tokens, lanes), 0)
    key_mask = jnp.sum(jnp.where(own_key, mask[:, :1], 0.0), axis=0, keepdims=True)
    key_bias_ref[...] = (key_mask - 1.0) * 1000000000.0 + other_columns_ref[...]


def tile_places(row_dim, rows, cols, order):
    me = lax.axis_index("row") * 2 + lax.axis_index("col")
    places = []
    for place in order:
        owner = me ^ place
        for r in range(rows):
            first = (owner // 2 * rows + r) * row_dim * rows + owner % 2 * cols
            places.append(pl.ds(pl.multiple_of(first, cols), cols))
    return places


def edge_operands(pieces, places, rel_ref, pair_mask_ref, gain, in_gate, in_weight):
    width = rel_ref.shape[1]
    blocks = [piece[at].astype(jnp.float32) for piece in pieces for at in range(piece.shape[0])]
    rows = len(places) // len(blocks)
    tiles = [block[r] for block in blocks for r in range(rows)]
    base = jnp.concatenate([tile + rel_ref[place, :] for tile, place in zip(tiles, places)], axis=0)
    pair_mask = jnp.concatenate([pair_mask_ref[place, :] for place in places], axis=0)
    normed = layer_norm(base, gain).astype(jnp.bfloat16)
    projected = sigmoid(dot(normed, in_gate)) * dot(normed, in_weight)
    left = round_bf16(projected[:, :width] * pair_mask)
    right = round_bf16(projected[:, width:] * pair_mask)
    return left, right, base, normed.astype(jnp.float32)


def early_kernel(row_dim, orders, *refs):
    piece_refs = refs[: len(orders)]
    rel_ref, pair_mask_ref, gains_ref, in_weight_ref, in_gate_ref = refs[len(orders) : len(orders) + 5]
    rows, cols = piece_refs[0].shape[1:3]
    places = tile_places(row_dim, rows, cols, sum(orders, ()))
    found = edge_operands(
        piece_refs, places, rel_ref, pair_mask_ref, gains_ref[0:1], in_gate_ref[...], in_weight_ref[...]
    )
    for ref, values in zip(refs[-4:], found):
        ref[...] = values


def whole_pair_kernel(row_dim, heads, early, orders, *refs):
    whole_pair_steps(row_dim, heads, early, orders, refs[: len(orders)], *refs[len(orders) :])


def whole_pair_steps(
    row_dim,
    heads,
    early,
    orders,
    piece_refs,
    early_left_ref,
    early_right_ref,
    early_base_ref,
    early_normed_ref,
    rel_ref,
    pair_mask_ref,
    gains_ref,
    att_bias_ref,
    key_bias_ref,
    in_weight_ref,
    in_gate_ref,
    out_gate_ref,
    out_weight_ref,
    qkv_ref,
    att_gate_ref,
    att_out_ref,
    out_ref,
    base_ref,
    normed_ref,
    left_ref,
    right_ref,
    att_ref,
    upd_ref,
):
    rows, cols, width = piece_refs[0].shape[1:]
    tokens = row_dim * rows
    head_dim = width // heads
    row_first = lax.axis_index("row") * rows
    col_first = pl.multiple_of(lax.axis_index("col") * cols, cols)
    f32, bf16 = jnp.float32, jnp.bfloat16

    def stored(places, found):
        for ref, values in zip((left_ref, right_ref, base_ref, normed_ref), found):
            for at, place in enumerate(places):
                ref[place, :] = values[at * cols : (at + 1) * cols]

    places = tile_places(row_dim, rows, cols, sum(orders, ()))
    found = edge_operands(
        piece_refs, places, rel_ref, pair_mask_ref, gains_ref[0:1], in_gate_ref[...], in_weight_ref[...]
    )
    stored(
        tile_places(row_dim, rows, cols, sum(early, ())),
        [ref[...] for ref in (early_left_ref, early_right_ref, early_base_ref, early_normed_ref)],
    )
    stored(places, found)

    seconds = [col_first + c for c in range(cols)] + [row_first + r for r in range(rows)]
    products = [None] * len(seconds)
    for m in range(tokens):
        left_at = left_ref[pl.ds(m, tokens, stride=tokens), :]
        for at, second in enumerate(seconds):
            term = left_at * right_ref[pl.ds(second * tokens + m, 1), :]
            products[at] = term if m == 0 else products[at] + term
    products = round_bf16(jnp.concatenate(products, axis=0))

    def chosen(ref):
        return jnp.concatenate([ref[pl.ds(second, tokens, stride=tokens), :] for second in seconds], axis=0)

    normed_out = layer_norm(products, gains_ref[1:2]).astype(bf16)
    out_gate = sigmoid(dot(chosen(normed_ref).astype(bf16), out_gate_ref[...]))
    updated = chosen(base_ref) + out_gate * dot(normed_out, out_weight_ref[...])
    normed_att = layer_norm(updated, gains_ref[2:3]).astype(bf16)
    own_pairs = rows * cols
    column_pairs = tokens * cols
    upd_ref[...] = updated[:column_pairs]
    att_ref[...] = normed_att[:column_pairs].astype(f32)

    def own_rows(ref):
        return jnp.concatenate([ref[pl.ds(row_first + r, cols, stride=tokens), :] for r in range(rows)], axis=0)

    own = own_rows(att_ref).astype(bf16)
    column = normed_att[:column_pairs]
    queries = dot(own, qkv_ref[:, :width])
    keys = dot(column, qkv_ref[:, width : 2 * width]).astype(bf16)
    values = dot(column, qkv_ref[:, 2 * width :]).astype(bf16)
    own_gate = sigmoid(dot(own, att_gate_ref[...]))

    bias = []
    for r in range(rows):
        part = normed_att[column_pairs + r * tokens : column_pairs + (r + 1) * tokens]
        bias.append(round_bf16(dot_t(att_bias_ref[...], jnp.concatenate([part] * cols, axis=0))))

    head_of = lax.broadcasted_iota(jnp.int32, (own_pairs, width), 1) // head_dim
    queries = round_bf16(queries)
    by_head = jnp.concatenate(
        [jnp.where(head_of == h, queries, 0.0) for h in range(heads)], axis=0
    ).astype(bf16)
    scores = dot_t(by_head, keys) * (1.0 / math.sqrt(head_dim))
    biases = jnp.concatenate(
        [jnp.broadcast_to(bias[r][h : h + 1], (cols, column_pairs)) for h in range(heads) for r in range(rows)],
        axis=0,
    )
    key_bias = jnp.concatenate([key_bias_ref[...]] * (heads * rows), axis=0)
    scores = scores + biases + key_bias
    expo = jnp.exp(scores - jnp.max(scores, axis=-1, keepdims=True))
    shares = 1.0 / jnp.sum(expo, axis=-1, keepdims=True)
    mixed = dot(expo.astype(bf16), values) * shares
    attended = jnp.zeros((own_pairs, width), f32)
    for h in range(heads):
        attended = jnp.where(head_of == h, mixed[h * own_pairs : (h + 1) * own_pairs], attended)

    gated = (own_gate * attended).astype(bf16)
    result = own_rows(upd_ref) + dot(gated, att_out_ref[...])
    out_ref[...] = result.reshape(rows, cols, width).astype(bf16)


def whole_pair_on_device(
    row_dim,
    pair_in,
    token_mask,
    positions,
    relpos_table,
    tri_norm_in,
    tri_in_weight,
    tri_in_gate,
    tri_out_gate,
    tri_norm_out,
    tri_out_weight,
    att_norm,
    att_qkv,
    att_gate,
    att_bias,
    att_out,
):
    rows, cols, width = pair_in.shape
    vmem = pl.BlockSpec(memory_space=pltpu.VMEM)
    params = pltpu.CompilerParams(vmem_limit_bytes=16 * 1024 * 1024)
    tokens, heads = row_dim * rows, att_bias.shape[1]

    beside = pl.CostEstimate(flops=STAGE_FLOPS, bytes_accessed=2**20, transcendentals=0)
    wide_out = jax.ShapeDtypeStruct((tokens * tokens, width), jnp.float32)
    key_shape = jax.ShapeDtypeStruct((cols, tokens * cols), jnp.float32)
    other_columns = pl.pallas_call(
        column_kernel,
        out_shape=key_shape,
        out_specs=vmem,
        compiler_params=params,
        cost_estimate=beside,
    )()
    chip, *staged = pl.pallas_call(
        stage_kernel,
        out_shape=[
            jax.ShapeDtypeStruct((2,) + pair_in.shape, pair_in.dtype),
            wide_out,
            wide_out,
            jax.ShapeDtypeStruct((3, width), jnp.float32),
            jax.ShapeDtypeStruct((heads, width), att_bias.dtype),
            key_shape,
        ],
        in_specs=[vmem] * 9,
        out_specs=[vmem] * 6,
        compiler_params=params,
        cost_estimate=beside,
    )(
        pair_in,
        token_mask.reshape(1, tokens),
        positions.reshape(1, tokens),
        relpos_table,
        tri_norm_in.reshape(1, width),
        tri_norm_out.reshape(1, width),
        att_norm.reshape(1, width),
        att_bias.T,
        other_columns,
    )

    blocks = 2 * row_dim

    def move(piece, step):
        values, order = piece
        values = lax.ppermute(values, ("row", "col"), [(device, device ^ step) for device in range(blocks)])
        return values, tuple(place ^ step for place in order)

    other, _ = move((pair_in, (0,)), 1)
    pieces = [(chip.at[1].set(other), (0, 1))]
    first = move(pieces[0], 9)
    pieces += [first, move(pieces[0], 15), move(pieces[0], 7)]
    both = jnp.concatenate([pieces[0][0], first[0]], axis=0), pieces[0][1] + first[1]
    pieces += [move(both, 3), move(both, 5)]
    weights = (tri_in_weight, tri_in_gate, tri_out_gate, tri_out_weight, att_qkv, att_gate, att_out)
    rel, pair_mask, gains, *_ = staged
    early = [order for _, order in pieces[:4]]
    half = jax.ShapeDtypeStruct((tokens * tokens // 2, width), jnp.float32)
    halves = pl.pallas_call(
        functools.partial(early_kernel, row_dim, early),
        out_shape=[half] * 4,
        in_specs=[vmem] * (7 + len(weights)),
        out_specs=[vmem] * 4,
        compiler_params=params,
        cost_estimate=beside,
    )(*[values for values, _ in pieces[:4]], rel, pair_mask, gains, *weights)
    late = [order for _, order in pieces[4:]]
    gathered = [values for values, _ in pieces[4:]]
    wide = pltpu.VMEM((tokens * tokens, width), jnp.float32)
    column = pltpu.VMEM((tokens * cols, width), jnp.float32)
    return pl.pallas_call(
        functools.partial(whole_pair_kernel, row_dim, heads, early, late),
        out_shape=jax.ShapeDtypeStruct(pair_in.shape, pair_in.dtype),
        in_specs=[vmem] * (len(gathered) + 9 + len(weights)),
        out_specs=vmem,
        scratch_shapes=[wide] * 4 + [column] * 2,
        compiler_params=params,
    )(*gathered, *halves, *staged, *weights)


def attend_column(query_col, key_col, value_col, bias_all, key_bias, block_rows):
    tok_total = query_col.shape[0]
    scale = 1.0 / math.sqrt(query_col.shape[2])

    def one_block(block_idx):
        scores = (
            jnp.einsum("ihe,khe->hik", query_col, key_col, preferred_element_type=jnp.float32)
            * scale
        )
        scores = scores + bias_all.astype(jnp.float32) + key_bias[None, None, :]
        row_max = jnp.max(scores, axis=-1, keepdims=True)
        expo_f = jnp.exp(scores - row_max)
        totals = jnp.sum(expo_f, axis=-1)
        weights = expo_f.astype(jnp.bfloat16)
        result = jnp.einsum("hik,khe->ihe", weights, value_col, preferred_element_type=jnp.float32)
        return result / jnp.transpose(totals)[:, :, None]

    blocks = lax.map(one_block, jnp.arange(tok_total // block_rows))
    return blocks.reshape(tok_total, query_col.shape[1], query_col.shape[2])


def column_attention(columns, att_qkv, att_gate, bias_all, key_bias, head_local, head_dim):
    tok_total, col_count, channels = columns.shape
    local_width = head_local * head_dim
    weight_three = att_qkv.reshape(channels, 3, channels)
    qkv_all = jnp.einsum(
        "kmc,ctd->tmkd", columns, weight_three, preferred_element_type=jnp.float32
    ).astype(jnp.bfloat16)
    qkv_all = qkv_all.reshape(3, col_count, tok_total, head_local, head_dim)
    gate_val = jax.nn.sigmoid(
        jnp.einsum("kmc,cd->kmd", columns, att_gate, preferred_element_type=jnp.float32)
    )
    block_rows = min(1024, tok_total)

    def one_column(triple):
        return attend_column(triple[0], triple[1], triple[2], bias_all, key_bias, block_rows)

    attended = lax.map(one_column, (qkv_all[0], qkv_all[1], qkv_all[2]))
    attended = jnp.transpose(attended, (1, 0, 2, 3)).reshape(tok_total, col_count, local_width)
    return (gate_val * attended).astype(jnp.bfloat16)


def split_pair_on_device(
    pair_in,
    token_mask,
    positions,
    relpos_table,
    tri_norm_in,
    tri_in_weight,
    tri_in_gate,
    tri_out_gate,
    tri_norm_out,
    tri_out_weight,
    att_norm,
    att_qkv,
    att_gate,
    att_bias,
    att_out,
):
    row_count, col_count, channels = pair_in.shape
    row_first = lax.axis_index("row") * row_count
    col_first = lax.axis_index("col") * col_count
    mask_float = token_mask.astype(jnp.float32)
    row_mask = lax.dynamic_slice_in_dim(mask_float, row_first, row_count)
    col_mask = lax.dynamic_slice_in_dim(mask_float, col_first, col_count)
    row_pos = lax.dynamic_slice_in_dim(positions, row_first, row_count)
    col_pos = lax.dynamic_slice_in_dim(positions, col_first, col_count)
    bin_count = relpos_table.shape[0]
    bin_centre = bin_count // 2
    bucket = jnp.clip(row_pos[:, None] - col_pos[None, :], -bin_centre, bin_centre - 1) + bin_centre
    onehot = (bucket[:, :, None] == jnp.arange(bin_count, dtype=jnp.int32)[None, None, :]).astype(
        jnp.bfloat16
    )
    residual = pair_in.astype(jnp.float32) + jnp.einsum(
        "rjb,bc->rjc", onehot, relpos_table, preferred_element_type=jnp.float32
    )
    normed = layer_norm(residual, tri_norm_in).astype(jnp.bfloat16)
    pair_mask = row_mask[:, None] * col_mask[None, :]
    gate_in = jnp.einsum("rjc,cd->drj", normed, tri_in_gate, preferred_element_type=jnp.float32)
    proj_in = jnp.einsum("rjc,cd->drj", normed, tri_in_weight, preferred_element_type=jnp.float32)
    projected = (jax.nn.sigmoid(gate_in) * proj_in * pair_mask[None, :, :]).astype(jnp.bfloat16)
    left_ch, right_ch = (
        lax.all_to_all(projected[:channels], "row", split_axis=0, concat_axis=1, tiled=True),
        lax.all_to_all(projected[channels:], "row", split_axis=0, concat_axis=1, tiled=True),
    )
    right_rows = lax.all_to_all(right_ch, "col", split_axis=1, concat_axis=2, tiled=True)
    product_sum = jnp.einsum(
        "cik,cjk->cij",
        lax.all_gather(left_ch, "col", axis=2, tiled=True),
        right_rows,
        preferred_element_type=jnp.float32,
    )
    products = product_sum.astype(jnp.bfloat16)
    product_tile = lax.all_to_all(products, "row", split_axis=1, concat_axis=0, tiled=True)
    tri_x = jnp.transpose(product_tile, (1, 2, 0)).astype(jnp.float32)
    normed_out = layer_norm(tri_x, tri_norm_out).astype(jnp.bfloat16)
    out_gate = jax.nn.sigmoid(
        jnp.einsum("rjc,cd->rjd", normed, tri_out_gate, preferred_element_type=jnp.float32)
    )
    residual = residual + out_gate * jnp.einsum(
        "rjc,cd->rjd", normed_out, tri_out_weight, preferred_element_type=jnp.float32
    )
    normed_att = layer_norm(residual, att_norm).astype(jnp.bfloat16)
    bias_piece = jnp.einsum(
        "kic,ch->hik", normed_att, att_bias, preferred_element_type=jnp.float32
    ).astype(jnp.bfloat16)
    key_bias = (mask_float - 1.0) * 1000000000.0
    head_count = att_bias.shape[1]
    head_dim = channels // head_count
    columns = lax.all_to_all(normed_att, "row", split_axis=1, concat_axis=0, tiled=True)
    bias_half = lax.all_gather(bias_piece, "col", axis=1, tiled=True)
    bias_all = lax.all_gather(bias_half, "row", axis=2, tiled=True)
    gated = column_attention(columns, att_qkv, att_gate, bias_all, key_bias, head_count, head_dim)
    gated_tile = lax.all_to_all(gated, "row", split_axis=0, concat_axis=1, tiled=True)
    update = jnp.einsum("rjc,cd->rjd", gated_tile, att_out, preferred_element_type=jnp.float32)
    return (residual + update).astype(jnp.bfloat16)


def on_device(row_dim, col_dim, pair_in, *others):
    rows, cols, width = pair_in.shape
    tokens = row_dim * rows
    whole_bytes = tokens * tokens * width * pair_in.dtype.itemsize
    blocks = row_dim * col_dim
    tiled = cols % 8 == 0 and width == 128 and blocks == 16 and col_dim == 2
    if whole_bytes <= WHOLE_PAIR_BYTES and tiled:
        return whole_pair_on_device(row_dim, pair_in, *others)
    return split_pair_on_device(pair_in, *others)


def solution(mesh):
    return jax.shard_map(
        functools.partial(on_device, mesh.shape["row"], mesh.shape["col"]),
        mesh=mesh,
        in_specs=(P(("groups", "row"), "col", None), P("groups"), P("groups")) + (P(),) * 12,
        out_specs=P(("groups", "row"), "col", None),
        check_vma=False,
    )
```

```python
import functools
import math

import jax
import jax.numpy as jnp
from jax import lax
from jax.experimental import pallas as pl
from jax.experimental.pallas import tpu as pltpu
from jax.sharding import PartitionSpec as P

epsilon = 1e-05

WHOLE_PAIR_BYTES = 256 * 1024
STAGE_FLOPS = 10**9


def layer_norm(values, gain):
    mean_val = jnp.mean(values, axis=-1, keepdims=True)
    centred = values - mean_val
    var_val = jnp.mean(centred * centred, axis=-1, keepdims=True)
    return centred * lax.rsqrt(var_val + epsilon) * gain


def sigmoid(values):
    return 0.5 * jnp.tanh(0.5 * values) + 0.5


def dot(left, right):
    return jnp.dot(left, right, preferred_element_type=jnp.float32)


def dot_t(left, right):
    return lax.dot_general(
        left, right, (((1,), (1,)), ((), ())), preferred_element_type=jnp.float32
    )


def round_bf16(values):
    return values.astype(jnp.bfloat16).astype(jnp.float32)


def column_kernel(other_columns_ref):
    sub = lax.broadcasted_iota(jnp.int32, other_columns_ref.shape, 0)
    lane = lax.broadcasted_iota(jnp.int32, other_columns_ref.shape, 1)
    other_columns_ref[...] = jnp.where(lane % other_columns_ref.shape[0] == sub, 0.0, -jnp.inf)


def token_rows(chips, rows):
    return [(lax.axis_index("row") ^ chip) * rows + r for chip in chips for r in range(rows)]


def stage_kernel(
    chips,
    rows,
    pair_ref,
    mask_ref,
    pos_ref,
    table_ref,
    norm_in_ref,
    norm_out_ref,
    att_norm_ref,
    att_bias_ref,
    other_columns_ref,
    chip_ref,
    rel_ref,
    pair_mask_ref,
    gains_ref,
    bias_ref,
    key_bias_ref,
    pos_rows_ref,
    mask_rows_ref,
):
    chip_ref[0] = pair_ref[...]
    gains_ref[0:1] = norm_in_ref[...]
    gains_ref[1:2] = norm_out_ref[...]
    gains_ref[2:3] = att_norm_ref[...]
    bias_ref[...] = att_bias_ref[...]
    tokens, (cols, lanes) = pos_ref.shape[1], key_bias_ref.shape
    bins, width = table_ref.shape
    f32 = jnp.float32

    def by_row(ref):
        sub = lax.broadcasted_iota(jnp.int32, (tokens, tokens), 0)
        lane = lax.broadcasted_iota(jnp.int32, (tokens, tokens), 1)
        spread = jnp.where(sub == lane, jnp.broadcast_to(ref[...].astype(f32), (tokens, tokens)), 0.0)
        return jnp.broadcast_to(jnp.sum(spread, axis=1, keepdims=True), (tokens, bins))

    pos_rows_ref[...] = by_row(pos_ref)
    mask_rows_ref[...] = by_row(mask_ref)
    own_half = lax.axis_index("col")
    halves = [pl.ds(pl.multiple_of((own_half ^ half) * cols, cols), cols) for half in range(tokens // cols)]
    lane = lax.broadcasted_iota(jnp.int32, (cols, bins), 1).astype(f32)
    key_of = lax.broadcasted_iota(jnp.int32, (1, lanes), 1) // cols
    key_mask = jnp.zeros((1, lanes), f32)
    centre = float(bins // 2)
    hot = []
    for at, token in enumerate(token_rows(chips, rows)):
        pos, mask = pos_rows_ref[pl.ds(token, 1), :], mask_rows_ref[pl.ds(token, 1), :]
        for half in halves:
            bucket = jnp.clip(pos - pos_rows_ref[half, :], -centre, centre - 1.0) + centre
            first = len(hot) * cols
            pair_mask_ref[first : first + cols, :] = mask_rows_ref[half, :] * mask
            hot.append((bucket == lane).astype(f32))
        key_mask = jnp.where(key_of == at, mask, key_mask)
    rel_ref[...] = dot(jnp.concatenate(hot, axis=0).astype(jnp.bfloat16), table_ref[...])
    key_bias_ref[...] = (key_mask - 1.0) * 1000000000.0 + other_columns_ref[...]


def edge_operands(pieces, orders, rows, rel, pair_mask, gain, in_gate, in_weight):
    width = rel.shape[1]
    blocks = {
        place: piece[at].astype(jnp.float32) for piece, order in zip(pieces, orders) for at, place in enumerate(order)
    }
    tiles = [blocks[2 * chip + half][r] for chip in chips_of(orders) for r in range(rows) for half in range(2)]
    base = jnp.concatenate(tiles, axis=0) + rel
    normed = layer_norm(base, gain).astype(jnp.bfloat16)
    projected = sigmoid(dot(normed, in_gate)) * dot(normed, in_weight)
    left = round_bf16(projected[:, :width] * pair_mask)
    right = round_bf16(projected[:, width:] * pair_mask)
    return left, right, base, normed.astype(jnp.float32)


def chips_of(orders):
    return list(dict.fromkeys(place // 2 for order in orders for place in order))


def early_kernel(orders, *refs):
    piece_refs = refs[: len(orders)]
    rel_ref, pair_mask_ref, gains_ref, in_weight_ref, in_gate_ref = refs[len(orders) : len(orders) + 5]
    here = refs[-1].shape[0]
    found = edge_operands(
        piece_refs,
        orders,
        piece_refs[0].shape[1],
        rel_ref[:here],
        pair_mask_ref[:here],
        gains_ref[0:1],
        in_gate_ref[...],
        in_weight_ref[...],
    )
    for ref, values in zip(refs[-4:], found):
        ref[...] = values


def whole_pair_kernel(row_dim, heads, early, late, *refs):
    whole_pair_steps(row_dim, heads, early, late, refs[: len(late)], *refs[len(late) :])


def whole_pair_steps(
    row_dim,
    heads,
    early,
    late,
    piece_refs,
    early_left_ref,
    early_right_ref,
    early_base_ref,
    early_normed_ref,
    rel_ref,
    pair_mask_ref,
    gains_ref,
    att_bias_ref,
    key_bias_ref,
    in_weight_ref,
    in_gate_ref,
    out_gate_ref,
    out_weight_ref,
    qkv_ref,
    att_gate_ref,
    att_out_ref,
    out_ref,
    late_left_ref,
    late_base_ref,
    late_normed_ref,
    right_ref,
):
    rows, cols, width = piece_refs[0].shape[1:]
    tokens = row_dim * rows
    head_dim = width // heads
    row, col = lax.axis_index("row"), lax.axis_index("col")
    f32, bf16 = jnp.float32, jnp.bfloat16

    here = early_left_ref.shape[0]
    left, right, base, normed = edge_operands(
        piece_refs, late, rows, rel_ref[here:], pair_mask_ref[here:], gains_ref[0:1], in_gate_ref[...], in_weight_ref[...]
    )
    late_left_ref[...] = left
    late_base_ref[...] = base
    late_normed_ref[...] = normed
    lefts = (early_left_ref, late_left_ref)

    for at, token in enumerate(token_rows(chips_of(early + late), rows)):
        place = pl.ds(pl.multiple_of(token * tokens, tokens), tokens)
        first = at * tokens
        if first < here:
            right_ref[place, :] = early_right_ref[first : first + tokens]
        else:
            right_ref[place, :] = right[first - here : first - here + tokens]

    right_at = [right_ref[pl.ds(col * cols * tokens + m, cols, stride=tokens), :] for m in range(tokens)]
    products = []
    for i in range(tokens):
        ref, first = lefts[i * tokens // here], i * tokens % here
        total = ref[first : first + 1] * right_at[0]
        for m in range(1, tokens):
            total = total + ref[first + m : first + m + 1] * right_at[m]
        products.append(total)
    extra = [None] * rows
    for m in range(tokens):
        left_at = jnp.concatenate([ref[pl.ds(m, here // tokens, stride=tokens), :] for ref in lefts], axis=0)
        for r in range(rows):
            term = left_at * early_right_ref[r * tokens + m : r * tokens + m + 1]
            extra[r] = term if m == 0 else extra[r] + term
    products = round_bf16(jnp.concatenate(products + extra, axis=0))

    own_token = row * rows
    own_column = ((own_token // cols) ^ col) * cols + own_token % cols

    def chosen(early_ref, late_ref):
        pair = (early_ref, late_ref)
        own = [pair[i * tokens // here][i * tokens % here : i * tokens % here + cols] for i in range(tokens)]
        for r in range(rows):
            own += [ref[pl.ds(own_column + r, here // tokens, stride=tokens), :] for ref in pair]
        return jnp.concatenate(own, axis=0)

    normed_out = layer_norm(products, gains_ref[1:2]).astype(bf16)
    out_gate = sigmoid(dot(chosen(early_normed_ref, late_normed_ref).astype(bf16), out_gate_ref[...]))
    updated = chosen(early_base_ref, late_base_ref) + out_gate * dot(normed_out, out_weight_ref[...])
    normed_att = layer_norm(updated, gains_ref[2:3]).astype(bf16)
    own_pairs = rows * cols
    column_pairs = tokens * cols

    own = normed_att[:own_pairs]
    column = normed_att[:column_pairs]
    queries = dot(own, qkv_ref[:, :width])
    keys = dot(column, qkv_ref[:, width : 2 * width]).astype(bf16)
    values = dot(column, qkv_ref[:, 2 * width :]).astype(bf16)
    own_gate = sigmoid(dot(own, att_gate_ref[...]))

    bias = []
    att_f = normed_att[column_pairs:].astype(f32)
    for r in range(rows):
        part = att_f[r * tokens : (r + 1) * tokens]
        spread = jnp.concatenate(
            [jnp.broadcast_to(part[k : k + 1], (cols, width)) for k in range(tokens)], axis=0
        )
        bias.append(round_bf16(dot_t(att_bias_ref[...], spread.astype(bf16))))

    head_of = lax.broadcasted_iota(jnp.int32, (own_pairs, width), 1) // head_dim
    queries = round_bf16(queries)
    by_head = jnp.concatenate(
        [jnp.where(head_of == h, queries, 0.0) for h in range(heads)], axis=0
    ).astype(bf16)
    scores = dot_t(by_head, keys) * (1.0 / math.sqrt(head_dim))
    biases = jnp.concatenate(
        [jnp.broadcast_to(bias[r][h : h + 1], (cols, column_pairs)) for h in range(heads) for r in range(rows)],
        axis=0,
    )
    key_bias = jnp.concatenate([key_bias_ref[...]] * (heads * rows), axis=0)
    scores = scores + biases + key_bias
    expo = jnp.exp(scores - jnp.max(scores, axis=-1, keepdims=True))
    shares = 1.0 / jnp.sum(expo, axis=-1, keepdims=True)
    mixed = dot(expo.astype(bf16), values) * shares
    attended = jnp.zeros((own_pairs, width), f32)
    for h in range(heads):
        attended = jnp.where(head_of == h, mixed[h * own_pairs : (h + 1) * own_pairs], attended)

    gated = (own_gate * attended).astype(bf16)
    result = updated[:own_pairs] + dot(gated, att_out_ref[...])
    out_ref[...] = result.reshape(rows, cols, width).astype(bf16)


def whole_pair_on_device(
    row_dim,
    pair_in,
    token_mask,
    positions,
    relpos_table,
    tri_norm_in,
    tri_in_weight,
    tri_in_gate,
    tri_out_gate,
    tri_norm_out,
    tri_out_weight,
    att_norm,
    att_qkv,
    att_gate,
    att_bias,
    att_out,
):
    rows, cols, width = pair_in.shape
    vmem = pl.BlockSpec(memory_space=pltpu.VMEM)
    params = pltpu.CompilerParams(vmem_limit_bytes=16 * 1024 * 1024)
    tokens, heads = row_dim * rows, att_bias.shape[1]

    blocks = 2 * row_dim

    def moved(order, step):
        return tuple(place ^ step for place in order)

    def move(values, step):
        return lax.ppermute(values, ("row", "col"), [(device, device ^ step) for device in range(blocks)])

    own_order = (0, 1)
    early = [own_order] + [moved(own_order, step) for step in (9, 15, 7)]
    late = [moved(own_order + early[1], step) for step in (3, 5)]

    beside = pl.CostEstimate(flops=STAGE_FLOPS, bytes_accessed=2**20, transcendentals=0)
    wide_out = jax.ShapeDtypeStruct((tokens * tokens, width), jnp.float32)
    key_shape = jax.ShapeDtypeStruct((cols, tokens * cols), jnp.float32)
    other_columns = pl.pallas_call(
        column_kernel,
        out_shape=key_shape,
        out_specs=vmem,
        compiler_params=params,
        cost_estimate=beside,
    )()
    chip, *staged = pl.pallas_call(
        functools.partial(stage_kernel, chips_of(early + late), rows),
        out_shape=[
            jax.ShapeDtypeStruct((2,) + pair_in.shape, pair_in.dtype),
            wide_out,
            wide_out,
            jax.ShapeDtypeStruct((3, width), jnp.float32),
            jax.ShapeDtypeStruct((heads, width), att_bias.dtype),
            key_shape,
        ],
        in_specs=[vmem] * 9,
        out_specs=[vmem] * 6,
        scratch_shapes=[pltpu.VMEM((tokens, relpos_table.shape[0]), jnp.float32)] * 2,
        compiler_params=params,
        cost_estimate=beside,
    )(
        pair_in,
        token_mask.reshape(1, tokens),
        positions.reshape(1, tokens),
        relpos_table,
        tri_norm_in.reshape(1, width),
        tri_norm_out.reshape(1, width),
        att_norm.reshape(1, width),
        att_bias.T,
        other_columns,
    )

    chip = chip.at[1].set(move(pair_in, 1))
    first = move(chip, 9)
    pieces = [chip, first, move(chip, 15), move(chip, 7)]
    both = jnp.concatenate([chip, first], axis=0)
    last = [move(both, 3), move(both, 5)]
    weights = (tri_in_weight, tri_in_gate, tri_out_gate, tri_out_weight, att_qkv, att_gate, att_out)
    rel, pair_mask, gains, *_ = staged
    half = jax.ShapeDtypeStruct((tokens * tokens // 2, width), jnp.float32)
    halves = pl.pallas_call(
        functools.partial(early_kernel, early),
        out_shape=[half] * 4,
        in_specs=[vmem] * (7 + len(weights)),
        out_specs=[vmem] * 4,
        compiler_params=params,
        cost_estimate=beside,
    )(*pieces, rel, pair_mask, gains, *weights)
    return pl.pallas_call(
        functools.partial(whole_pair_kernel, row_dim, heads, early, late),
        out_shape=jax.ShapeDtypeStruct(pair_in.shape, pair_in.dtype),
        in_specs=[vmem] * (len(last) + 9 + len(weights)),
        out_specs=vmem,
        scratch_shapes=[pltpu.VMEM(half.shape, half.dtype)] * 3 + [pltpu.VMEM(wide_out.shape, wide_out.dtype)],
        compiler_params=params,
    )(*last, *halves, *staged, *weights)


def attend_column(query_col, key_col, value_col, bias_all, key_bias, block_rows):
    tok_total = query_col.shape[0]
    scale = 1.0 / math.sqrt(query_col.shape[2])

    def one_block(block_idx):
        scores = (
            jnp.einsum("ihe,khe->hik", query_col, key_col, preferred_element_type=jnp.float32)
            * scale
        )
        scores = scores + bias_all.astype(jnp.float32) + key_bias[None, None, :]
        row_max = jnp.max(scores, axis=-1, keepdims=True)
        expo_f = jnp.exp(scores - row_max)
        totals = jnp.sum(expo_f, axis=-1)
        weights = expo_f.astype(jnp.bfloat16)
        result = jnp.einsum("hik,khe->ihe", weights, value_col, preferred_element_type=jnp.float32)
        return result / jnp.transpose(totals)[:, :, None]

    blocks = lax.map(one_block, jnp.arange(tok_total // block_rows))
    return blocks.reshape(tok_total, query_col.shape[1], query_col.shape[2])


def column_attention(columns, att_qkv, att_gate, bias_all, key_bias, head_local, head_dim):
    tok_total, col_count, channels = columns.shape
    local_width = head_local * head_dim
    weight_three = att_qkv.reshape(channels, 3, channels)
    qkv_all = jnp.einsum(
        "kmc,ctd->tmkd", columns, weight_three, preferred_element_type=jnp.float32
    ).astype(jnp.bfloat16)
    qkv_all = qkv_all.reshape(3, col_count, tok_total, head_local, head_dim)
    gate_val = jax.nn.sigmoid(
        jnp.einsum("kmc,cd->kmd", columns, att_gate, preferred_element_type=jnp.float32)
    )
    block_rows = min(1024, tok_total)

    def one_column(triple):
        return attend_column(triple[0], triple[1], triple[2], bias_all, key_bias, block_rows)

    attended = lax.map(one_column, (qkv_all[0], qkv_all[1], qkv_all[2]))
    attended = jnp.transpose(attended, (1, 0, 2, 3)).reshape(tok_total, col_count, local_width)
    return (gate_val * attended).astype(jnp.bfloat16)


def split_pair_on_device(
    pair_in,
    token_mask,
    positions,
    relpos_table,
    tri_norm_in,
    tri_in_weight,
    tri_in_gate,
    tri_out_gate,
    tri_norm_out,
    tri_out_weight,
    att_norm,
    att_qkv,
    att_gate,
    att_bias,
    att_out,
):
    row_count, col_count, channels = pair_in.shape
    row_first = lax.axis_index("row") * row_count
    col_first = lax.axis_index("col") * col_count
    mask_float = token_mask.astype(jnp.float32)
    row_mask = lax.dynamic_slice_in_dim(mask_float, row_first, row_count)
    col_mask = lax.dynamic_slice_in_dim(mask_float, col_first, col_count)
    row_pos = lax.dynamic_slice_in_dim(positions, row_first, row_count)
    col_pos = lax.dynamic_slice_in_dim(positions, col_first, col_count)
    bin_count = relpos_table.shape[0]
    bin_centre = bin_count // 2
    bucket = jnp.clip(row_pos[:, None] - col_pos[None, :], -bin_centre, bin_centre - 1) + bin_centre
    onehot = (bucket[:, :, None] == jnp.arange(bin_count, dtype=jnp.int32)[None, None, :]).astype(
        jnp.bfloat16
    )
    residual = pair_in.astype(jnp.float32) + jnp.einsum(
        "rjb,bc->rjc", onehot, relpos_table, preferred_element_type=jnp.float32
    )
    normed = layer_norm(residual, tri_norm_in).astype(jnp.bfloat16)
    pair_mask = row_mask[:, None] * col_mask[None, :]
    gate_in = jnp.einsum("rjc,cd->drj", normed, tri_in_gate, preferred_element_type=jnp.float32)
    proj_in = jnp.einsum("rjc,cd->drj", normed, tri_in_weight, preferred_element_type=jnp.float32)
    projected = (jax.nn.sigmoid(gate_in) * proj_in * pair_mask[None, :, :]).astype(jnp.bfloat16)
    left_ch, right_ch = (
        lax.all_to_all(projected[:channels], "row", split_axis=0, concat_axis=1, tiled=True),
        lax.all_to_all(projected[channels:], "row", split_axis=0, concat_axis=1, tiled=True),
    )
    right_rows = lax.all_to_all(right_ch, "col", split_axis=1, concat_axis=2, tiled=True)
    product_sum = jnp.einsum(
        "cik,cjk->cij",
        lax.all_gather(left_ch, "col", axis=2, tiled=True),
        right_rows,
        preferred_element_type=jnp.float32,
    )
    products = product_sum.astype(jnp.bfloat16)
    product_tile = lax.all_to_all(products, "row", split_axis=1, concat_axis=0, tiled=True)
    tri_x = jnp.transpose(product_tile, (1, 2, 0)).astype(jnp.float32)
    normed_out = layer_norm(tri_x, tri_norm_out).astype(jnp.bfloat16)
    out_gate = jax.nn.sigmoid(
        jnp.einsum("rjc,cd->rjd", normed, tri_out_gate, preferred_element_type=jnp.float32)
    )
    residual = residual + out_gate * jnp.einsum(
        "rjc,cd->rjd", normed_out, tri_out_weight, preferred_element_type=jnp.float32
    )
    normed_att = layer_norm(residual, att_norm).astype(jnp.bfloat16)
    bias_piece = jnp.einsum(
        "kic,ch->hik", normed_att, att_bias, preferred_element_type=jnp.float32
    ).astype(jnp.bfloat16)
    key_bias = (mask_float - 1.0) * 1000000000.0
    head_count = att_bias.shape[1]
    head_dim = channels // head_count
    columns = lax.all_to_all(normed_att, "row", split_axis=1, concat_axis=0, tiled=True)
    bias_half = lax.all_gather(bias_piece, "col", axis=1, tiled=True)
    bias_all = lax.all_gather(bias_half, "row", axis=2, tiled=True)
    gated = column_attention(columns, att_qkv, att_gate, bias_all, key_bias, head_count, head_dim)
    gated_tile = lax.all_to_all(gated, "row", split_axis=0, concat_axis=1, tiled=True)
    update = jnp.einsum("rjc,cd->rjd", gated_tile, att_out, preferred_element_type=jnp.float32)
    return (residual + update).astype(jnp.bfloat16)


def on_device(row_dim, col_dim, pair_in, *others):
    rows, cols, width = pair_in.shape
    tokens = row_dim * rows
    whole_bytes = tokens * tokens * width * pair_in.dtype.itemsize
    bins = others[2].shape[0]
    tiled = cols % 8 == 0 and cols % rows == 0 and width == bins == tokens * cols == 128
    if whole_bytes <= WHOLE_PAIR_BYTES and tiled and (row_dim, col_dim) == (8, 2):
        return whole_pair_on_device(row_dim, pair_in, *others)
    return split_pair_on_device(pair_in, *others)


def solution(mesh):
    return jax.shard_map(
        functools.partial(on_device, mesh.shape["row"], mesh.shape["col"]),
        mesh=mesh,
        in_specs=(P(("groups", "row"), "col", None), P("groups"), P("groups")) + (P(),) * 12,
        out_specs=P(("groups", "row"), "col", None),
        check_vma=False,
    )
```

```python
import functools
import math

import jax
import jax.numpy as jnp
from jax import lax
from jax.experimental import pallas as pl
from jax.experimental.pallas import tpu as pltpu
from jax.sharding import PartitionSpec as P

epsilon = 1e-05

WHOLE_PAIR_BYTES = 256 * 1024
SPARE_ROWS = 16
STAGE_FLOPS = 10**9


def layer_norm(values, gain):
    mean_val = jnp.mean(values, axis=-1, keepdims=True)
    centred = values - mean_val
    var_val = jnp.mean(centred * centred, axis=-1, keepdims=True)
    return centred * lax.rsqrt(var_val + epsilon) * gain


def sigmoid(values):
    return 0.5 * jnp.tanh(0.5 * values) + 0.5


def dot(left, right):
    return jnp.dot(left, right, preferred_element_type=jnp.float32)


def dot_t(left, right):
    return lax.dot_general(
        left, right, (((1,), (1,)), ((), ())), preferred_element_type=jnp.float32
    )


def round_bf16(values):
    return values.astype(jnp.bfloat16).astype(jnp.float32)


def column_kernel(other_columns_ref):
    sub = lax.broadcasted_iota(jnp.int32, other_columns_ref.shape, 0)
    lane = lax.broadcasted_iota(jnp.int32, other_columns_ref.shape, 1)
    other_columns_ref[...] = jnp.where(lane % other_columns_ref.shape[0] == sub, 0.0, -jnp.inf)


def token_rows(chips, rows):
    return [(lax.axis_index("row") ^ chip) * rows + r for chip in chips for r in range(rows)]


def stage_kernel(
    chips,
    rows,
    pair_ref,
    mask_ref,
    pos_ref,
    table_ref,
    norm_in_ref,
    norm_out_ref,
    att_norm_ref,
    att_bias_ref,
    other_columns_ref,
    chip_ref,
    rel_ref,
    pair_mask_ref,
    gains_ref,
    bias_ref,
    key_bias_ref,
    pos_rows_ref,
    mask_rows_ref,
):
    chip_ref[0] = pair_ref[...]
    gains_ref[0:1] = norm_in_ref[...]
    gains_ref[1:2] = norm_out_ref[...]
    gains_ref[2:3] = att_norm_ref[...]
    bias_ref[...] = att_bias_ref[...]
    tokens, (cols, lanes) = pos_ref.shape[1], key_bias_ref.shape
    bins, width = table_ref.shape
    f32 = jnp.float32

    def by_row(ref):
        sub = lax.broadcasted_iota(jnp.int32, (tokens, tokens), 0)
        lane = lax.broadcasted_iota(jnp.int32, (tokens, tokens), 1)
        spread = jnp.where(sub == lane, jnp.broadcast_to(ref[...].astype(f32), (tokens, tokens)), 0.0)
        return jnp.broadcast_to(jnp.sum(spread, axis=1, keepdims=True), (tokens, bins))

    pos_rows_ref[...] = by_row(pos_ref)
    mask_rows_ref[...] = by_row(mask_ref)
    own_half = lax.axis_index("col")
    halves = [pl.ds(pl.multiple_of((own_half ^ half) * cols, cols), cols) for half in range(tokens // cols)]
    lane = lax.broadcasted_iota(jnp.int32, (cols, bins), 1).astype(f32)
    key_of = lax.broadcasted_iota(jnp.int32, (1, lanes), 1) // cols
    key_mask = jnp.zeros((1, lanes), f32)
    centre = float(bins // 2)
    hot = []
    for at, token in enumerate(token_rows(chips, rows)):
        pos, mask = pos_rows_ref[pl.ds(token, 1), :], mask_rows_ref[pl.ds(token, 1), :]
        for half in halves:
            bucket = jnp.clip(pos - pos_rows_ref[half, :], -centre, centre - 1.0) + centre
            first = len(hot) * cols
            pair_mask_ref[first : first + cols, :] = mask_rows_ref[half, :] * mask
            hot.append((bucket == lane).astype(f32))
        key_mask = jnp.where(key_of == at, mask, key_mask)
    rel_ref[...] = dot(jnp.concatenate(hot, axis=0).astype(jnp.bfloat16), table_ref[...])
    key_bias_ref[...] = (key_mask - 1.0) * 1000000000.0 + other_columns_ref[...]


def edge_operands(pieces, orders, rows, rel, pair_mask, gain, in_gate, in_weight):
    width = rel.shape[1]
    blocks = {
        place: piece[at].astype(jnp.float32) for piece, order in zip(pieces, orders) for at, place in enumerate(order)
    }
    tiles = [blocks[2 * chip + half][r] for chip in chips_of(orders) for r in range(rows) for half in range(2)]
    base = jnp.concatenate(tiles, axis=0) + rel
    normed = layer_norm(base, gain).astype(jnp.bfloat16)
    projected = sigmoid(dot(normed, in_gate)) * dot(normed, in_weight)
    left = round_bf16(projected[:, :width] * pair_mask)
    right = round_bf16(projected[:, width:] * pair_mask)
    return left, right, base, normed.astype(jnp.float32)


def chips_of(orders):
    return list(dict.fromkeys(place // 2 for order in orders for place in order))


def early_kernel(orders, *refs):
    piece_refs = refs[: len(orders)]
    rel_ref, pair_mask_ref, gains_ref, in_weight_ref, in_gate_ref = refs[len(orders) : len(orders) + 5]
    here = refs[-1].shape[0] - SPARE_ROWS
    found = edge_operands(
        piece_refs,
        orders,
        piece_refs[0].shape[1],
        rel_ref[:here],
        pair_mask_ref[:here],
        gains_ref[0:1],
        in_gate_ref[...],
        in_weight_ref[...],
    )
    for ref, values in zip(refs[-4:], found):
        ref[:here] = values


def whole_pair_kernel(row_dim, heads, early, late, *refs):
    whole_pair_steps(row_dim, heads, early, late, refs[: len(late)], *refs[len(late) :])


def whole_pair_steps(
    row_dim,
    heads,
    early,
    late,
    piece_refs,
    early_left_ref,
    early_right_ref,
    early_base_ref,
    early_normed_ref,
    rel_ref,
    pair_mask_ref,
    gains_ref,
    att_bias_ref,
    key_bias_ref,
    in_weight_ref,
    in_gate_ref,
    out_gate_ref,
    out_weight_ref,
    qkv_ref,
    att_gate_ref,
    att_out_ref,
    out_ref,
    late_left_ref,
    late_base_ref,
    late_normed_ref,
    right_ref,
):
    rows, cols, width = piece_refs[0].shape[1:]
    tokens = row_dim * rows
    head_dim = width // heads
    row, col = lax.axis_index("row"), lax.axis_index("col")
    f32, bf16 = jnp.float32, jnp.bfloat16

    here = early_left_ref.shape[0] - SPARE_ROWS
    left, right, base, normed = edge_operands(
        piece_refs, late, rows, rel_ref[here:], pair_mask_ref[here:], gains_ref[0:1], in_gate_ref[...], in_weight_ref[...]
    )
    late_left_ref[:here] = left
    late_base_ref[:here] = base
    late_normed_ref[:here] = normed
    lefts = (early_left_ref, late_left_ref)

    for at, token in enumerate(token_rows(chips_of(early + late), rows)):
        place = pl.ds(pl.multiple_of(token * tokens, tokens), tokens)
        first = at * tokens
        if first < here:
            right_ref[place, :] = early_right_ref[first : first + tokens]
        else:
            right_ref[place, :] = right[first - here : first - here + tokens]

    right_at = [right_ref[pl.ds(col * cols * tokens + m, cols, stride=tokens), :] for m in range(tokens)]
    products = []
    for i in range(tokens):
        ref, first = lefts[i * tokens // here], i * tokens % here
        total = ref[first : first + 1] * right_at[0]
        for m in range(1, tokens):
            total = total + ref[first + m : first + m + 1] * right_at[m]
        products.append(total)
    extra = [None] * rows
    for m in range(tokens):
        left_at = jnp.concatenate([ref[pl.ds(m, here // tokens, stride=tokens), :] for ref in lefts], axis=0)
        for r in range(rows):
            term = left_at * early_right_ref[r * tokens + m : r * tokens + m + 1]
            extra[r] = term if m == 0 else extra[r] + term
    products = round_bf16(jnp.concatenate(products + extra, axis=0))

    own_token = row * rows
    own_column = ((own_token // cols) ^ col) * cols + own_token % cols

    def chosen(early_ref, late_ref):
        pair = (early_ref, late_ref)
        own = [pair[i * tokens // here][i * tokens % here : i * tokens % here + cols] for i in range(tokens)]
        for r in range(rows):
            own += [ref[pl.ds(own_column + r, here // tokens, stride=tokens), :] for ref in pair]
        return jnp.concatenate(own, axis=0)

    normed_out = layer_norm(products, gains_ref[1:2]).astype(bf16)
    out_gate = sigmoid(dot(chosen(early_normed_ref, late_normed_ref).astype(bf16), out_gate_ref[...]))
    updated = chosen(early_base_ref, late_base_ref) + out_gate * dot(normed_out, out_weight_ref[...])
    normed_att = layer_norm(updated, gains_ref[2:3]).astype(bf16)
    own_pairs = rows * cols
    column_pairs = tokens * cols

    own = normed_att[:own_pairs]
    column = normed_att[:column_pairs]
    queries = dot(own, qkv_ref[:, :width])
    keys = dot(column, qkv_ref[:, width : 2 * width]).astype(bf16)
    values = dot(column, qkv_ref[:, 2 * width :]).astype(bf16)
    own_gate = sigmoid(dot(own, att_gate_ref[...]))

    bias = dot_t(att_bias_ref[...], normed_att[column_pairs:]).astype(bf16)
    shape = (rows * tokens, rows * column_pairs)
    source = lax.broadcasted_iota(jnp.int32, shape, 0)
    repeated = source == lax.broadcasted_iota(jnp.int32, shape, 1) // cols
    bias = dot(bias, repeated.astype(f32).astype(bf16))

    head_of = lax.broadcasted_iota(jnp.int32, (own_pairs, width), 1) // head_dim
    queries = round_bf16(queries)
    by_head = jnp.concatenate(
        [jnp.where(head_of == h, queries, 0.0) for h in range(heads)], axis=0
    ).astype(bf16)
    scores = dot_t(by_head, keys) * (1.0 / math.sqrt(head_dim))
    biases = jnp.concatenate(
        [
            jnp.broadcast_to(bias[h : h + 1, r * column_pairs : (r + 1) * column_pairs], (cols, column_pairs))
            for h in range(heads)
            for r in range(rows)
        ],
        axis=0,
    )
    key_bias = jnp.concatenate([key_bias_ref[...]] * (heads * rows), axis=0)
    scores = scores + biases + key_bias
    expo = jnp.exp(scores - jnp.max(scores, axis=-1, keepdims=True))
    shares = 1.0 / jnp.sum(expo, axis=-1, keepdims=True)
    mixed = dot(expo.astype(bf16), values) * shares
    attended = jnp.zeros((own_pairs, width), f32)
    for h in range(heads):
        attended = jnp.where(head_of == h, mixed[h * own_pairs : (h + 1) * own_pairs], attended)

    gated = (own_gate * attended).astype(bf16)
    result = updated[:own_pairs] + dot(gated, att_out_ref[...])
    out_ref[...] = result.reshape(rows, cols, width).astype(bf16)


def whole_pair_on_device(
    row_dim,
    pair_in,
    token_mask,
    positions,
    relpos_table,
    tri_norm_in,
    tri_in_weight,
    tri_in_gate,
    tri_out_gate,
    tri_norm_out,
    tri_out_weight,
    att_norm,
    att_qkv,
    att_gate,
    att_bias,
    att_out,
):
    rows, cols, width = pair_in.shape
    vmem = pl.BlockSpec(memory_space=pltpu.VMEM)
    params = pltpu.CompilerParams(vmem_limit_bytes=16 * 1024 * 1024)
    tokens, heads = row_dim * rows, att_bias.shape[1]

    blocks = 2 * row_dim

    def moved(order, step):
        return tuple(place ^ step for place in order)

    def move(values, step):
        return lax.ppermute(values, ("row", "col"), [(device, device ^ step) for device in range(blocks)])

    own_order = (0, 1)
    early = [own_order] + [moved(own_order, step) for step in (9, 15, 7)]
    late = [moved(own_order + early[1], step) for step in (3, 5)]

    beside = pl.CostEstimate(flops=STAGE_FLOPS, bytes_accessed=2**20, transcendentals=0)
    wide_out = jax.ShapeDtypeStruct((tokens * tokens, width), jnp.float32)
    key_shape = jax.ShapeDtypeStruct((cols, tokens * cols), jnp.float32)
    other_columns = pl.pallas_call(
        column_kernel,
        out_shape=key_shape,
        out_specs=vmem,
        compiler_params=params,
        cost_estimate=beside,
    )()
    chip, *staged = pl.pallas_call(
        functools.partial(stage_kernel, chips_of(early + late), rows),
        out_shape=[
            jax.ShapeDtypeStruct((2,) + pair_in.shape, pair_in.dtype),
            wide_out,
            wide_out,
            jax.ShapeDtypeStruct((3, width), jnp.float32),
            jax.ShapeDtypeStruct((heads, width), att_bias.dtype),
            key_shape,
        ],
        in_specs=[vmem] * 9,
        out_specs=[vmem] * 6,
        scratch_shapes=[pltpu.VMEM((tokens, relpos_table.shape[0]), jnp.float32)] * 2,
        compiler_params=params,
        cost_estimate=beside,
    )(
        pair_in,
        token_mask.reshape(1, tokens),
        positions.reshape(1, tokens),
        relpos_table,
        tri_norm_in.reshape(1, width),
        tri_norm_out.reshape(1, width),
        att_norm.reshape(1, width),
        att_bias.T,
        other_columns,
    )

    chip = chip.at[1].set(move(pair_in, 1))
    first = move(chip, 9)
    pieces = [chip, first, move(chip, 15), move(chip, 7)]
    both = jnp.concatenate([chip, first], axis=0)
    last = [move(both, 3), move(both, 5)]
    weights = (tri_in_weight, tri_in_gate, tri_out_gate, tri_out_weight, att_qkv, att_gate, att_out)
    rel, pair_mask, gains, *_ = staged
    half = jax.ShapeDtypeStruct((tokens * tokens // 2 + SPARE_ROWS, width), jnp.float32)
    halves = pl.pallas_call(
        functools.partial(early_kernel, early),
        out_shape=[half] * 4,
        in_specs=[vmem] * (7 + len(weights)),
        out_specs=[vmem] * 4,
        compiler_params=params,
        cost_estimate=beside,
    )(*pieces, rel, pair_mask, gains, *weights)
    return pl.pallas_call(
        functools.partial(whole_pair_kernel, row_dim, heads, early, late),
        out_shape=jax.ShapeDtypeStruct(pair_in.shape, pair_in.dtype),
        in_specs=[vmem] * (len(last) + 9 + len(weights)),
        out_specs=vmem,
        scratch_shapes=[pltpu.VMEM(half.shape, half.dtype)] * 3 + [pltpu.VMEM((tokens * tokens + SPARE_ROWS, width), jnp.float32)],
        compiler_params=params,
    )(*last, *halves, *staged, *weights)


def attend_column(query_col, key_col, value_col, bias_all, key_bias, block_rows):
    tok_total = query_col.shape[0]
    scale = 1.0 / math.sqrt(query_col.shape[2])

    def one_block(block_idx):
        scores = (
            jnp.einsum("ihe,khe->hik", query_col, key_col, preferred_element_type=jnp.float32)
            * scale
        )
        scores = scores + bias_all.astype(jnp.float32) + key_bias[None, None, :]
        row_max = jnp.max(scores, axis=-1, keepdims=True)
        expo_f = jnp.exp(scores - row_max)
        totals = jnp.sum(expo_f, axis=-1)
        weights = expo_f.astype(jnp.bfloat16)
        result = jnp.einsum("hik,khe->ihe", weights, value_col, preferred_element_type=jnp.float32)
        return result / jnp.transpose(totals)[:, :, None]

    blocks = lax.map(one_block, jnp.arange(tok_total // block_rows))
    return blocks.reshape(tok_total, query_col.shape[1], query_col.shape[2])


def column_attention(columns, att_qkv, att_gate, bias_all, key_bias, head_local, head_dim):
    tok_total, col_count, channels = columns.shape
    local_width = head_local * head_dim
    weight_three = att_qkv.reshape(channels, 3, channels)
    qkv_all = jnp.einsum(
        "kmc,ctd->tmkd", columns, weight_three, preferred_element_type=jnp.float32
    ).astype(jnp.bfloat16)
    qkv_all = qkv_all.reshape(3, col_count, tok_total, head_local, head_dim)
    gate_val = jax.nn.sigmoid(
        jnp.einsum("kmc,cd->kmd", columns, att_gate, preferred_element_type=jnp.float32)
    )
    block_rows = min(1024, tok_total)

    def one_column(triple):
        return attend_column(triple[0], triple[1], triple[2], bias_all, key_bias, block_rows)

    attended = lax.map(one_column, (qkv_all[0], qkv_all[1], qkv_all[2]))
    attended = jnp.transpose(attended, (1, 0, 2, 3)).reshape(tok_total, col_count, local_width)
    return (gate_val * attended).astype(jnp.bfloat16)


def split_pair_on_device(
    pair_in,
    token_mask,
    positions,
    relpos_table,
    tri_norm_in,
    tri_in_weight,
    tri_in_gate,
    tri_out_gate,
    tri_norm_out,
    tri_out_weight,
    att_norm,
    att_qkv,
    att_gate,
    att_bias,
    att_out,
):
    row_count, col_count, channels = pair_in.shape
    row_first = lax.axis_index("row") * row_count
    col_first = lax.axis_index("col") * col_count
    mask_float = token_mask.astype(jnp.float32)
    row_mask = lax.dynamic_slice_in_dim(mask_float, row_first, row_count)
    col_mask = lax.dynamic_slice_in_dim(mask_float, col_first, col_count)
    row_pos = lax.dynamic_slice_in_dim(positions, row_first, row_count)
    col_pos = lax.dynamic_slice_in_dim(positions, col_first, col_count)
    bin_count = relpos_table.shape[0]
    bin_centre = bin_count // 2
    bucket = jnp.clip(row_pos[:, None] - col_pos[None, :], -bin_centre, bin_centre - 1) + bin_centre
    onehot = (bucket[:, :, None] == jnp.arange(bin_count, dtype=jnp.int32)[None, None, :]).astype(
        jnp.bfloat16
    )
    residual = pair_in.astype(jnp.float32) + jnp.einsum(
        "rjb,bc->rjc", onehot, relpos_table, preferred_element_type=jnp.float32
    )
    normed = layer_norm(residual, tri_norm_in).astype(jnp.bfloat16)
    pair_mask = row_mask[:, None] * col_mask[None, :]
    gate_in = jnp.einsum("rjc,cd->drj", normed, tri_in_gate, preferred_element_type=jnp.float32)
    proj_in = jnp.einsum("rjc,cd->drj", normed, tri_in_weight, preferred_element_type=jnp.float32)
    projected = (jax.nn.sigmoid(gate_in) * proj_in * pair_mask[None, :, :]).astype(jnp.bfloat16)
    left_ch, right_ch = (
        lax.all_to_all(projected[:channels], "row", split_axis=0, concat_axis=1, tiled=True),
        lax.all_to_all(projected[channels:], "row", split_axis=0, concat_axis=1, tiled=True),
    )
    right_rows = lax.all_to_all(right_ch, "col", split_axis=1, concat_axis=2, tiled=True)
    product_sum = jnp.einsum(
        "cik,cjk->cij",
        lax.all_gather(left_ch, "col", axis=2, tiled=True),
        right_rows,
        preferred_element_type=jnp.float32,
    )
    products = product_sum.astype(jnp.bfloat16)
    product_tile = lax.all_to_all(products, "row", split_axis=1, concat_axis=0, tiled=True)
    tri_x = jnp.transpose(product_tile, (1, 2, 0)).astype(jnp.float32)
    normed_out = layer_norm(tri_x, tri_norm_out).astype(jnp.bfloat16)
    out_gate = jax.nn.sigmoid(
        jnp.einsum("rjc,cd->rjd", normed, tri_out_gate, preferred_element_type=jnp.float32)
    )
    residual = residual + out_gate * jnp.einsum(
        "rjc,cd->rjd", normed_out, tri_out_weight, preferred_element_type=jnp.float32
    )
    normed_att = layer_norm(residual, att_norm).astype(jnp.bfloat16)
    bias_piece = jnp.einsum(
        "kic,ch->hik", normed_att, att_bias, preferred_element_type=jnp.float32
    ).astype(jnp.bfloat16)
    key_bias = (mask_float - 1.0) * 1000000000.0
    head_count = att_bias.shape[1]
    head_dim = channels // head_count
    columns = lax.all_to_all(normed_att, "row", split_axis=1, concat_axis=0, tiled=True)
    bias_half = lax.all_gather(bias_piece, "col", axis=1, tiled=True)
    bias_all = lax.all_gather(bias_half, "row", axis=2, tiled=True)
    gated = column_attention(columns, att_qkv, att_gate, bias_all, key_bias, head_count, head_dim)
    gated_tile = lax.all_to_all(gated, "row", split_axis=0, concat_axis=1, tiled=True)
    update = jnp.einsum("rjc,cd->rjd", gated_tile, att_out, preferred_element_type=jnp.float32)
    return (residual + update).astype(jnp.bfloat16)


def on_device(row_dim, col_dim, pair_in, *others):
    rows, cols, width = pair_in.shape
    tokens = row_dim * rows
    whole_bytes = tokens * tokens * width * pair_in.dtype.itemsize
    bins = others[2].shape[0]
    tiled = cols % 8 == 0 and cols % rows == 0 and width == bins == tokens * cols == 128
    if whole_bytes <= WHOLE_PAIR_BYTES and tiled and (row_dim, col_dim) == (8, 2):
        return whole_pair_on_device(row_dim, pair_in, *others)
    return split_pair_on_device(pair_in, *others)


def solution(mesh):
    return jax.shard_map(
        functools.partial(on_device, mesh.shape["row"], mesh.shape["col"]),
        mesh=mesh,
        in_specs=(P(("groups", "row"), "col", None), P("groups"), P("groups")) + (P(),) * 12,
        out_specs=P(("groups", "row"), "col", None),
        check_vma=False,
    )
```

```python
import functools
import math

import jax
import jax.numpy as jnp
from jax import lax
from jax.experimental import pallas as pl
from jax.experimental.pallas import tpu as pltpu
from jax.sharding import PartitionSpec as P

epsilon = 1e-05

WHOLE_PAIR_BYTES = 256 * 1024
SPARE_ROWS = 16
STAGE_FLOPS = 10**9


def layer_norm(values, gain):
    mean_val = jnp.mean(values, axis=-1, keepdims=True)
    centred = values - mean_val
    var_val = jnp.mean(centred * centred, axis=-1, keepdims=True)
    return centred * lax.rsqrt(var_val + epsilon) * gain


def sigmoid(values):
    return 0.5 * jnp.tanh(0.5 * values) + 0.5


def dot(left, right):
    return jnp.dot(left, right, preferred_element_type=jnp.float32)


def dot_t(left, right):
    return lax.dot_general(
        left, right, (((1,), (1,)), ((), ())), preferred_element_type=jnp.float32
    )


def round_bf16(values):
    return values.astype(jnp.bfloat16).astype(jnp.float32)


def column_kernel(other_columns_ref):
    sub = lax.broadcasted_iota(jnp.int32, other_columns_ref.shape, 0)
    lane = lax.broadcasted_iota(jnp.int32, other_columns_ref.shape, 1)
    other_columns_ref[...] = jnp.where(lane % other_columns_ref.shape[0] == sub, 0.0, -jnp.inf)


def token_rows(chips, rows):
    return [(lax.axis_index("row") ^ chip) * rows + r for chip in chips for r in range(rows)]


def stage_kernel(
    chips,
    rows,
    pair_ref,
    mask_ref,
    pos_ref,
    table_ref,
    norm_in_ref,
    norm_out_ref,
    att_norm_ref,
    att_bias_ref,
    other_columns_ref,
    chip_ref,
    rel_ref,
    pair_mask_ref,
    gains_ref,
    bias_ref,
    key_bias_ref,
    pos_rows_ref,
    mask_rows_ref,
):
    chip_ref[0] = pair_ref[...]
    gains_ref[0:1] = norm_in_ref[...]
    gains_ref[1:2] = norm_out_ref[...]
    gains_ref[2:3] = att_norm_ref[...]
    bias_ref[...] = att_bias_ref[...]
    tokens, (cols, lanes) = pos_ref.shape[1], key_bias_ref.shape
    bins, width = table_ref.shape
    f32 = jnp.float32

    def by_row(ref):
        sub = lax.broadcasted_iota(jnp.int32, (tokens, tokens), 0)
        lane = lax.broadcasted_iota(jnp.int32, (tokens, tokens), 1)
        spread = jnp.where(sub == lane, jnp.broadcast_to(ref[...].astype(f32), (tokens, tokens)), 0.0)
        return jnp.broadcast_to(jnp.sum(spread, axis=1, keepdims=True), (tokens, bins))

    pos_rows_ref[...] = by_row(pos_ref)
    mask_rows_ref[...] = by_row(mask_ref)
    own_half = lax.axis_index("col")
    halves = [pl.ds(pl.multiple_of((own_half ^ half) * cols, cols), cols) for half in range(tokens // cols)]
    lane = lax.broadcasted_iota(jnp.int32, (cols, bins), 1).astype(f32)
    key_of = lax.broadcasted_iota(jnp.int32, (1, lanes), 1) // cols
    key_mask = jnp.zeros((1, lanes), f32)
    centre = float(bins // 2)
    hot = []
    for at, token in enumerate(token_rows(chips, rows)):
        pos, mask = pos_rows_ref[pl.ds(token, 1), :], mask_rows_ref[pl.ds(token, 1), :]
        for half in halves:
            bucket = jnp.clip(pos - pos_rows_ref[half, :], -centre, centre - 1.0) + centre
            first = len(hot) * cols
            pair_mask_ref[first : first + cols, :] = mask_rows_ref[half, :] * mask
            hot.append((bucket == lane).astype(f32))
        key_mask = jnp.where(key_of == at, mask, key_mask)
    rel_ref[...] = dot(jnp.concatenate(hot, axis=0).astype(jnp.bfloat16), table_ref[...])
    key_bias_ref[...] = (key_mask - 1.0) * 1000000000.0 + other_columns_ref[...]


def edge_operands(pieces, orders, rows, rel, pair_mask, gain, in_gate, in_weight):
    width = rel.shape[1]
    blocks = {
        place: piece[at].astype(jnp.float32) for piece, order in zip(pieces, orders) for at, place in enumerate(order)
    }
    tiles = [blocks[2 * chip + half][r] for chip in chips_of(orders) for r in range(rows) for half in range(2)]
    base = jnp.concatenate(tiles, axis=0) + rel
    normed = layer_norm(base, gain).astype(jnp.bfloat16)
    projected = sigmoid(dot(normed, in_gate)) * dot(normed, in_weight)
    left = round_bf16(projected[:, :width] * pair_mask)
    right = round_bf16(projected[:, width:] * pair_mask)
    return left, right, base, normed.astype(jnp.float32)


def chips_of(orders):
    return list(dict.fromkeys(place // 2 for order in orders for place in order))


def early_kernel(orders, *refs):
    piece_refs = refs[: len(orders)]
    rel_ref, pair_mask_ref, gains_ref, in_weight_ref, in_gate_ref = refs[len(orders) : len(orders) + 5]
    here = refs[-1].shape[0] - SPARE_ROWS
    found = edge_operands(
        piece_refs,
        orders,
        piece_refs[0].shape[1],
        rel_ref[:here],
        pair_mask_ref[:here],
        gains_ref[0:1],
        in_gate_ref[...],
        in_weight_ref[...],
    )
    for ref, values in zip(refs[-4:], found):
        ref[:here] = values


def whole_pair_kernel(row_dim, heads, early, late, *refs):
    whole_pair_steps(row_dim, heads, early, late, refs[: len(late)], *refs[len(late) :])


def whole_pair_steps(
    row_dim,
    heads,
    early,
    late,
    piece_refs,
    early_left_ref,
    early_right_ref,
    early_base_ref,
    early_normed_ref,
    rel_ref,
    pair_mask_ref,
    gains_ref,
    att_bias_ref,
    key_bias_ref,
    in_weight_ref,
    in_gate_ref,
    out_gate_ref,
    out_weight_ref,
    qkv_ref,
    att_gate_ref,
    att_out_ref,
    out_ref,
    late_left_ref,
    late_base_ref,
    late_normed_ref,
    right_ref,
    products_ref,
):
    rows, cols, width = piece_refs[0].shape[1:]
    tokens = row_dim * rows
    head_dim = width // heads
    row, col = lax.axis_index("row"), lax.axis_index("col")
    f32, bf16 = jnp.float32, jnp.bfloat16

    here = early_left_ref.shape[0] - SPARE_ROWS
    left, right, base, normed = edge_operands(
        piece_refs, late, rows, rel_ref[here:], pair_mask_ref[here:], gains_ref[0:1], in_gate_ref[...], in_weight_ref[...]
    )
    late_left_ref[:here] = left
    late_base_ref[:here] = base
    late_normed_ref[:here] = normed
    lefts = (early_left_ref, late_left_ref)

    for at, token in enumerate(token_rows(chips_of(early + late), rows)):
        place = pl.ds(pl.multiple_of(token * tokens, tokens), tokens)
        first = at * tokens
        if first < here:
            right_ref[place, :] = early_right_ref[first : first + tokens]
        else:
            right_ref[place, :] = right[first - here : first - here + tokens]

    right_at = [right_ref[pl.ds(col * cols * tokens + m, cols, stride=tokens), :] for m in range(tokens)]
    together = 4
    for at, ref in enumerate(lefts):

        def some_tokens(step, carry, at=at, ref=ref):
            for i in range(together):
                i = step * together + i
                first = pl.multiple_of(i * tokens, tokens)
                total = ref[pl.ds(first, 1), :] * right_at[0]
                for m in range(1, tokens):
                    total = total + ref[pl.ds(first + m, 1), :] * right_at[m]
                place = pl.multiple_of((at * here // tokens + i) * cols, cols)
                products_ref[pl.ds(place, cols), :] = total
            return carry

        lax.fori_loop(0, here // tokens // together, some_tokens, 0)
    extra = [None] * rows
    for m in range(tokens):
        left_at = jnp.concatenate([ref[pl.ds(m, here // tokens, stride=tokens), :] for ref in lefts], axis=0)
        for r in range(rows):
            term = left_at * early_right_ref[r * tokens + m : r * tokens + m + 1]
            extra[r] = term if m == 0 else extra[r] + term
    products = round_bf16(jnp.concatenate([products_ref[...]] + extra, axis=0))

    own_token = row * rows
    own_column = ((own_token // cols) ^ col) * cols + own_token % cols

    def chosen(early_ref, late_ref):
        pair = (early_ref, late_ref)
        own = [pair[i * tokens // here][i * tokens % here : i * tokens % here + cols] for i in range(tokens)]
        for r in range(rows):
            own += [ref[pl.ds(own_column + r, here // tokens, stride=tokens), :] for ref in pair]
        return jnp.concatenate(own, axis=0)

    normed_out = layer_norm(products, gains_ref[1:2]).astype(bf16)
    out_gate = sigmoid(dot(chosen(early_normed_ref, late_normed_ref).astype(bf16), out_gate_ref[...]))
    updated = chosen(early_base_ref, late_base_ref) + out_gate * dot(normed_out, out_weight_ref[...])
    normed_att = layer_norm(updated, gains_ref[2:3]).astype(bf16)
    own_pairs = rows * cols
    column_pairs = tokens * cols

    own = normed_att[:own_pairs]
    column = normed_att[:column_pairs]
    queries = dot(own, qkv_ref[:, :width])
    keys = dot(column, qkv_ref[:, width : 2 * width]).astype(bf16)
    values = dot(column, qkv_ref[:, 2 * width :]).astype(bf16)
    own_gate = sigmoid(dot(own, att_gate_ref[...]))

    bias = dot_t(att_bias_ref[...], normed_att[column_pairs:]).astype(bf16)
    shape = (rows * tokens, rows * column_pairs)
    source = lax.broadcasted_iota(jnp.int32, shape, 0)
    repeated = source == lax.broadcasted_iota(jnp.int32, shape, 1) // cols
    bias = dot(bias, repeated.astype(f32).astype(bf16))

    head_of = lax.broadcasted_iota(jnp.int32, (own_pairs, width), 1) // head_dim
    queries = round_bf16(queries)
    by_head = jnp.concatenate(
        [jnp.where(head_of == h, queries, 0.0) for h in range(heads)], axis=0
    ).astype(bf16)
    scores = dot_t(by_head, keys) * (1.0 / math.sqrt(head_dim))
    biases = jnp.concatenate(
        [
            jnp.broadcast_to(bias[h : h + 1, r * column_pairs : (r + 1) * column_pairs], (cols, column_pairs))
            for h in range(heads)
            for r in range(rows)
        ],
        axis=0,
    )
    key_bias = jnp.concatenate([key_bias_ref[...]] * (heads * rows), axis=0)
    scores = scores + biases + key_bias
    expo = jnp.exp(scores - jnp.max(scores, axis=-1, keepdims=True))
    shares = 1.0 / jnp.sum(expo, axis=-1, keepdims=True)
    mixed = dot(expo.astype(bf16), values) * shares
    attended = jnp.zeros((own_pairs, width), f32)
    for h in range(heads):
        attended = jnp.where(head_of == h, mixed[h * own_pairs : (h + 1) * own_pairs], attended)

    gated = (own_gate * attended).astype(bf16)
    result = updated[:own_pairs] + dot(gated, att_out_ref[...])
    out_ref[...] = result.reshape(rows, cols, width).astype(bf16)


def whole_pair_on_device(
    row_dim,
    pair_in,
    token_mask,
    positions,
    relpos_table,
    tri_norm_in,
    tri_in_weight,
    tri_in_gate,
    tri_out_gate,
    tri_norm_out,
    tri_out_weight,
    att_norm,
    att_qkv,
    att_gate,
    att_bias,
    att_out,
):
    rows, cols, width = pair_in.shape
    vmem = pl.BlockSpec(memory_space=pltpu.VMEM)
    params = pltpu.CompilerParams(vmem_limit_bytes=16 * 1024 * 1024)
    tokens, heads = row_dim * rows, att_bias.shape[1]

    blocks = 2 * row_dim

    def moved(order, step):
        return tuple(place ^ step for place in order)

    def move(values, step):
        return lax.ppermute(values, ("row", "col"), [(device, device ^ step) for device in range(blocks)])

    own_order = (0, 1)
    early = [own_order] + [moved(own_order, step) for step in (9, 15, 7)]
    late = [moved(own_order + early[1], step) for step in (3, 5)]

    beside = pl.CostEstimate(flops=STAGE_FLOPS, bytes_accessed=2**20, transcendentals=0)
    wide_out = jax.ShapeDtypeStruct((tokens * tokens, width), jnp.float32)
    key_shape = jax.ShapeDtypeStruct((cols, tokens * cols), jnp.float32)
    other_columns = pl.pallas_call(
        column_kernel,
        out_shape=key_shape,
        out_specs=vmem,
        compiler_params=params,
        cost_estimate=beside,
    )()
    chip, *staged = pl.pallas_call(
        functools.partial(stage_kernel, chips_of(early + late), rows),
        out_shape=[
            jax.ShapeDtypeStruct((2,) + pair_in.shape, pair_in.dtype),
            wide_out,
            wide_out,
            jax.ShapeDtypeStruct((3, width), jnp.float32),
            jax.ShapeDtypeStruct((heads, width), att_bias.dtype),
            key_shape,
        ],
        in_specs=[vmem] * 9,
        out_specs=[vmem] * 6,
        scratch_shapes=[pltpu.VMEM((tokens, relpos_table.shape[0]), jnp.float32)] * 2,
        compiler_params=params,
        cost_estimate=beside,
    )(
        pair_in,
        token_mask.reshape(1, tokens),
        positions.reshape(1, tokens),
        relpos_table,
        tri_norm_in.reshape(1, width),
        tri_norm_out.reshape(1, width),
        att_norm.reshape(1, width),
        att_bias.T,
        other_columns,
    )

    chip = chip.at[1].set(move(pair_in, 1))
    first = move(chip, 9)
    pieces = [chip, first, move(chip, 15), move(chip, 7)]
    both = jnp.concatenate([chip, first], axis=0)
    last = [move(both, 3), move(both, 5)]
    weights = (tri_in_weight, tri_in_gate, tri_out_gate, tri_out_weight, att_qkv, att_gate, att_out)
    rel, pair_mask, gains, *_ = staged
    half = jax.ShapeDtypeStruct((tokens * tokens // 2 + SPARE_ROWS, width), jnp.float32)
    halves = pl.pallas_call(
        functools.partial(early_kernel, early),
        out_shape=[half] * 4,
        in_specs=[vmem] * (7 + len(weights)),
        out_specs=[vmem] * 4,
        compiler_params=params,
        cost_estimate=beside,
    )(*pieces, rel, pair_mask, gains, *weights)
    return pl.pallas_call(
        functools.partial(whole_pair_kernel, row_dim, heads, early, late),
        out_shape=jax.ShapeDtypeStruct(pair_in.shape, pair_in.dtype),
        in_specs=[vmem] * (len(last) + 9 + len(weights)),
        out_specs=vmem,
        scratch_shapes=[pltpu.VMEM(half.shape, half.dtype)] * 3 + [pltpu.VMEM((count, width), jnp.float32) for count in (tokens * tokens + SPARE_ROWS, tokens * cols)],
        compiler_params=params,
    )(*last, *halves, *staged, *weights)


def attend_column(query_col, key_col, value_col, bias_all, key_bias, block_rows):
    tok_total = query_col.shape[0]
    scale = 1.0 / math.sqrt(query_col.shape[2])

    def one_block(block_idx):
        scores = (
            jnp.einsum("ihe,khe->hik", query_col, key_col, preferred_element_type=jnp.float32)
            * scale
        )
        scores = scores + bias_all.astype(jnp.float32) + key_bias[None, None, :]
        row_max = jnp.max(scores, axis=-1, keepdims=True)
        expo_f = jnp.exp(scores - row_max)
        totals = jnp.sum(expo_f, axis=-1)
        weights = expo_f.astype(jnp.bfloat16)
        result = jnp.einsum("hik,khe->ihe", weights, value_col, preferred_element_type=jnp.float32)
        return result / jnp.transpose(totals)[:, :, None]

    blocks = lax.map(one_block, jnp.arange(tok_total // block_rows))
    return blocks.reshape(tok_total, query_col.shape[1], query_col.shape[2])


def column_attention(columns, att_qkv, att_gate, bias_all, key_bias, head_local, head_dim):
    tok_total, col_count, channels = columns.shape
    local_width = head_local * head_dim
    weight_three = att_qkv.reshape(channels, 3, channels)
    qkv_all = jnp.einsum(
        "kmc,ctd->tmkd", columns, weight_three, preferred_element_type=jnp.float32
    ).astype(jnp.bfloat16)
    qkv_all = qkv_all.reshape(3, col_count, tok_total, head_local, head_dim)
    gate_val = jax.nn.sigmoid(
        jnp.einsum("kmc,cd->kmd", columns, att_gate, preferred_element_type=jnp.float32)
    )
    block_rows = min(1024, tok_total)

    def one_column(triple):
        return attend_column(triple[0], triple[1], triple[2], bias_all, key_bias, block_rows)

    attended = lax.map(one_column, (qkv_all[0], qkv_all[1], qkv_all[2]))
    attended = jnp.transpose(attended, (1, 0, 2, 3)).reshape(tok_total, col_count, local_width)
    return (gate_val * attended).astype(jnp.bfloat16)


def split_pair_on_device(
    pair_in,
    token_mask,
    positions,
    relpos_table,
    tri_norm_in,
    tri_in_weight,
    tri_in_gate,
    tri_out_gate,
    tri_norm_out,
    tri_out_weight,
    att_norm,
    att_qkv,
    att_gate,
    att_bias,
    att_out,
):
    row_count, col_count, channels = pair_in.shape
    row_first = lax.axis_index("row") * row_count
    col_first = lax.axis_index("col") * col_count
    mask_float = token_mask.astype(jnp.float32)
    row_mask = lax.dynamic_slice_in_dim(mask_float, row_first, row_count)
    col_mask = lax.dynamic_slice_in_dim(mask_float, col_first, col_count)
    row_pos = lax.dynamic_slice_in_dim(positions, row_first, row_count)
    col_pos = lax.dynamic_slice_in_dim(positions, col_first, col_count)
    bin_count = relpos_table.shape[0]
    bin_centre = bin_count // 2
    bucket = jnp.clip(row_pos[:, None] - col_pos[None, :], -bin_centre, bin_centre - 1) + bin_centre
    onehot = (bucket[:, :, None] == jnp.arange(bin_count, dtype=jnp.int32)[None, None, :]).astype(
        jnp.bfloat16
    )
    residual = pair_in.astype(jnp.float32) + jnp.einsum(
        "rjb,bc->rjc", onehot, relpos_table, preferred_element_type=jnp.float32
    )
    normed = layer_norm(residual, tri_norm_in).astype(jnp.bfloat16)
    pair_mask = row_mask[:, None] * col_mask[None, :]
    gate_in = jnp.einsum("rjc,cd->drj", normed, tri_in_gate, preferred_element_type=jnp.float32)
    proj_in = jnp.einsum("rjc,cd->drj", normed, tri_in_weight, preferred_element_type=jnp.float32)
    projected = (jax.nn.sigmoid(gate_in) * proj_in * pair_mask[None, :, :]).astype(jnp.bfloat16)
    left_ch, right_ch = (
        lax.all_to_all(projected[:channels], "row", split_axis=0, concat_axis=1, tiled=True),
        lax.all_to_all(projected[channels:], "row", split_axis=0, concat_axis=1, tiled=True),
    )
    right_rows = lax.all_to_all(right_ch, "col", split_axis=1, concat_axis=2, tiled=True)
    product_sum = jnp.einsum(
        "cik,cjk->cij",
        lax.all_gather(left_ch, "col", axis=2, tiled=True),
        right_rows,
        preferred_element_type=jnp.float32,
    )
    products = product_sum.astype(jnp.bfloat16)
    product_tile = lax.all_to_all(products, "row", split_axis=1, concat_axis=0, tiled=True)
    tri_x = jnp.transpose(product_tile, (1, 2, 0)).astype(jnp.float32)
    normed_out = layer_norm(tri_x, tri_norm_out).astype(jnp.bfloat16)
    out_gate = jax.nn.sigmoid(
        jnp.einsum("rjc,cd->rjd", normed, tri_out_gate, preferred_element_type=jnp.float32)
    )
    residual = residual + out_gate * jnp.einsum(
        "rjc,cd->rjd", normed_out, tri_out_weight, preferred_element_type=jnp.float32
    )
    normed_att = layer_norm(residual, att_norm).astype(jnp.bfloat16)
    bias_piece = jnp.einsum(
        "kic,ch->hik", normed_att, att_bias, preferred_element_type=jnp.float32
    ).astype(jnp.bfloat16)
    key_bias = (mask_float - 1.0) * 1000000000.0
    head_count = att_bias.shape[1]
    head_dim = channels // head_count
    columns = lax.all_to_all(normed_att, "row", split_axis=1, concat_axis=0, tiled=True)
    bias_half = lax.all_gather(bias_piece, "col", axis=1, tiled=True)
    bias_all = lax.all_gather(bias_half, "row", axis=2, tiled=True)
    gated = column_attention(columns, att_qkv, att_gate, bias_all, key_bias, head_count, head_dim)
    gated_tile = lax.all_to_all(gated, "row", split_axis=0, concat_axis=1, tiled=True)
    update = jnp.einsum("rjc,cd->rjd", gated_tile, att_out, preferred_element_type=jnp.float32)
    return (residual + update).astype(jnp.bfloat16)


def on_device(row_dim, col_dim, pair_in, *others):
    rows, cols, width = pair_in.shape
    tokens = row_dim * rows
    whole_bytes = tokens * tokens * width * pair_in.dtype.itemsize
    bins = others[2].shape[0]
    tiled = cols % 8 == 0 and cols % rows == 0 and width == bins == tokens * cols == 128
    if whole_bytes <= WHOLE_PAIR_BYTES and tiled and (row_dim, col_dim) == (8, 2):
        return whole_pair_on_device(row_dim, pair_in, *others)
    return split_pair_on_device(pair_in, *others)


def solution(mesh):
    return jax.shard_map(
        functools.partial(on_device, mesh.shape["row"], mesh.shape["col"]),
        mesh=mesh,
        in_specs=(P(("groups", "row"), "col", None), P("groups"), P("groups")) + (P(),) * 12,
        out_specs=P(("groups", "row"), "col", None),
        check_vma=False,
    )
```

```python
import functools
import math

import jax
import jax.numpy as jnp
from jax import lax
from jax.experimental import pallas as pl
from jax.experimental.pallas import tpu as pltpu
from jax.sharding import PartitionSpec as P

epsilon = 1e-05

WHOLE_PAIR_BYTES = 256 * 1024
SPARE_ROWS = 16
STAGE_FLOPS = 10**9


def layer_norm(values, gain):
    mean_val = jnp.mean(values, axis=-1, keepdims=True)
    centred = values - mean_val
    var_val = jnp.mean(centred * centred, axis=-1, keepdims=True)
    return centred * lax.rsqrt(var_val + epsilon) * gain


def sigmoid(values):
    return 0.5 * jnp.tanh(0.5 * values) + 0.5


def dot(left, right):
    return jnp.dot(left, right, preferred_element_type=jnp.float32)


def dot_t(left, right):
    return lax.dot_general(
        left, right, (((1,), (1,)), ((), ())), preferred_element_type=jnp.float32
    )


def round_bf16(values):
    return values.astype(jnp.bfloat16).astype(jnp.float32)


def column_kernel(other_columns_ref):
    sub = lax.broadcasted_iota(jnp.int32, other_columns_ref.shape, 0)
    lane = lax.broadcasted_iota(jnp.int32, other_columns_ref.shape, 1)
    other_columns_ref[...] = jnp.where(lane % other_columns_ref.shape[0] == sub, 0.0, -jnp.inf)


def token_rows(chips, rows):
    return [(lax.axis_index("row") ^ chip) * rows + r for chip in chips for r in range(rows)]


def stage_kernel(
    chips,
    rows,
    pair_ref,
    mask_ref,
    pos_ref,
    table_ref,
    norm_in_ref,
    norm_out_ref,
    att_norm_ref,
    att_bias_ref,
    other_columns_ref,
    chip_ref,
    rel_ref,
    pair_mask_ref,
    gains_ref,
    bias_ref,
    key_bias_ref,
    pos_rows_ref,
    mask_rows_ref,
):
    chip_ref[0] = pair_ref[...]
    gains_ref[0:1] = norm_in_ref[...]
    gains_ref[1:2] = norm_out_ref[...]
    gains_ref[2:3] = att_norm_ref[...]
    bias_ref[...] = att_bias_ref[...]
    tokens, (cols, lanes) = pos_ref.shape[1], key_bias_ref.shape
    bins, width = table_ref.shape
    f32 = jnp.float32

    def by_row(ref):
        sub = lax.broadcasted_iota(jnp.int32, (tokens, tokens), 0)
        lane = lax.broadcasted_iota(jnp.int32, (tokens, tokens), 1)
        spread = jnp.where(sub == lane, jnp.broadcast_to(ref[...].astype(f32), (tokens, tokens)), 0.0)
        return jnp.broadcast_to(jnp.sum(spread, axis=1, keepdims=True), (tokens, bins))

    pos_rows_ref[...] = by_row(pos_ref)
    mask_rows_ref[...] = by_row(mask_ref)
    own_half = lax.axis_index("col")
    halves = [pl.ds(pl.multiple_of((own_half ^ half) * cols, cols), cols) for half in range(tokens // cols)]
    lane = lax.broadcasted_iota(jnp.int32, (cols, bins), 1).astype(f32)
    key_of = lax.broadcasted_iota(jnp.int32, (1, lanes), 1) // cols
    key_mask = jnp.zeros((1, lanes), f32)
    centre = float(bins // 2)
    hot = []
    for at, token in enumerate(token_rows(chips, rows)):
        pos, mask = pos_rows_ref[pl.ds(token, 1), :], mask_rows_ref[pl.ds(token, 1), :]
        for half in halves:
            bucket = jnp.clip(pos - pos_rows_ref[half, :], -centre, centre - 1.0) + centre
            first = len(hot) * cols
            pair_mask_ref[first : first + cols, :] = mask_rows_ref[half, :] * mask
            hot.append((bucket == lane).astype(f32))
        key_mask = jnp.where(key_of == at, mask, key_mask)
    rel_ref[...] = dot(jnp.concatenate(hot, axis=0).astype(jnp.bfloat16), table_ref[...])
    key_bias_ref[...] = (key_mask - 1.0) * 1000000000.0 + other_columns_ref[...]


def edge_operands(pieces, orders, rows, rel, pair_mask, gain, in_gate, in_weight):
    width = rel.shape[1]
    blocks = {
        place: piece[at].astype(jnp.float32) for piece, order in zip(pieces, orders) for at, place in enumerate(order)
    }
    tiles = [blocks[2 * chip + half][r] for chip in chips_of(orders) for r in range(rows) for half in range(2)]
    base = jnp.concatenate(tiles, axis=0) + rel
    normed = layer_norm(base, gain).astype(jnp.bfloat16)
    projected = sigmoid(dot(normed, in_gate)) * dot(normed, in_weight)
    left = round_bf16(projected[:, :width] * pair_mask)
    right = round_bf16(projected[:, width:] * pair_mask)
    return left, right, base, normed.astype(jnp.float32)


def chips_of(orders):
    return list(dict.fromkeys(place // 2 for order in orders for place in order))


def early_kernel(orders, *refs):
    piece_refs = refs[: len(orders)]
    rel_ref, pair_mask_ref, gains_ref, in_weight_ref, in_gate_ref = refs[len(orders) : len(orders) + 5]
    here = refs[-1].shape[0] - SPARE_ROWS
    found = edge_operands(
        piece_refs,
        orders,
        piece_refs[0].shape[1],
        rel_ref[:here],
        pair_mask_ref[:here],
        gains_ref[0:1],
        in_gate_ref[...],
        in_weight_ref[...],
    )
    for ref, values in zip(refs[-4:], found):
        ref[:here] = values


def whole_pair_kernel(row_dim, heads, early, late, *refs):
    whole_pair_steps(row_dim, heads, early, late, refs[: len(late)], *refs[len(late) :])


def whole_pair_steps(
    row_dim,
    heads,
    early,
    late,
    piece_refs,
    early_left_ref,
    early_right_ref,
    early_base_ref,
    early_normed_ref,
    rel_ref,
    pair_mask_ref,
    gains_ref,
    att_bias_ref,
    key_bias_ref,
    in_weight_ref,
    in_gate_ref,
    out_gate_ref,
    out_weight_ref,
    qkv_ref,
    att_gate_ref,
    att_out_ref,
    out_ref,
    late_left_ref,
    late_base_ref,
    late_normed_ref,
    right_ref,
):
    rows, cols, width = piece_refs[0].shape[1:]
    tokens = row_dim * rows
    head_dim = width // heads
    row, col = lax.axis_index("row"), lax.axis_index("col")
    f32, bf16 = jnp.float32, jnp.bfloat16

    here = early_left_ref.shape[0] - SPARE_ROWS
    left, right, base, normed = edge_operands(
        piece_refs, late, rows, rel_ref[here:], pair_mask_ref[here:], gains_ref[0:1], in_gate_ref[...], in_weight_ref[...]
    )
    late_left_ref[:here] = left
    late_base_ref[:here] = base
    late_normed_ref[:here] = normed
    lefts = (early_left_ref, late_left_ref)

    for at, token in enumerate(token_rows(chips_of(early + late), rows)):
        place = pl.ds(pl.multiple_of(token * tokens, tokens), tokens)
        first = at * tokens
        if first < here:
            right_ref[place, :] = early_right_ref[first : first + tokens]
        else:
            right_ref[place, :] = right[first - here : first - here + tokens]

    right_at = [right_ref[pl.ds(col * cols * tokens + m, cols, stride=tokens), :] for m in range(tokens)]
    products = []
    for i in range(tokens):
        ref, first = lefts[i * tokens // here], i * tokens % here
        total = ref[first : first + 1] * right_at[0]
        for m in range(1, tokens):
            total = total + ref[first + m : first + m + 1] * right_at[m]
        products.append(total)
    extra = [None] * rows
    for m in range(tokens):
        left_at = jnp.concatenate([ref[pl.ds(m, here // tokens, stride=tokens), :] for ref in lefts], axis=0)
        for r in range(rows):
            term = left_at * early_right_ref[r * tokens + m : r * tokens + m + 1]
            extra[r] = term if m == 0 else extra[r] + term

    own_token = row * rows
    own_column = ((own_token // cols) ^ col) * cols + own_token % cols

    def own_columns(early_ref, late_ref):
        pair = (early_ref, late_ref)
        return jnp.concatenate(
            [pair[i * tokens // here][i * tokens % here : i * tokens % here + cols] for i in range(tokens)], axis=0
        )

    def own_tokens(early_ref, late_ref):
        return jnp.concatenate(
            [
                ref[pl.ds(own_column + r, here // tokens, stride=tokens), :]
                for r in range(rows)
                for ref in (early_ref, late_ref)
            ],
            axis=0,
        )

    def attention_input(products, chosen):
        normed_out = layer_norm(round_bf16(jnp.concatenate(products, axis=0)), gains_ref[1:2]).astype(bf16)
        out_gate = sigmoid(dot(chosen(early_normed_ref, late_normed_ref).astype(bf16), out_gate_ref[...]))
        updated = chosen(early_base_ref, late_base_ref) + out_gate * dot(normed_out, out_weight_ref[...])
        return updated, layer_norm(updated, gains_ref[2:3]).astype(bf16)

    updated, column = attention_input(products, own_columns)
    _, of_tokens = attention_input(extra, own_tokens)
    own_pairs = rows * cols
    column_pairs = tokens * cols

    own = column[:own_pairs]
    queries = dot(own, qkv_ref[:, :width])
    keys = dot(column, qkv_ref[:, width : 2 * width]).astype(bf16)
    values = dot(column, qkv_ref[:, 2 * width :]).astype(bf16)
    own_gate = sigmoid(dot(own, att_gate_ref[...]))

    bias = dot_t(att_bias_ref[...], of_tokens).astype(bf16)
    shape = (rows * tokens, rows * column_pairs)
    source = lax.broadcasted_iota(jnp.int32, shape, 0)
    repeated = source == lax.broadcasted_iota(jnp.int32, shape, 1) // cols
    bias = dot(bias, repeated.astype(f32).astype(bf16))

    head_of = lax.broadcasted_iota(jnp.int32, (own_pairs, width), 1) // head_dim
    queries = round_bf16(queries)
    by_head = jnp.concatenate(
        [jnp.where(head_of == h, queries, 0.0) for h in range(heads)], axis=0
    ).astype(bf16)
    scores = dot_t(by_head, keys) * (1.0 / math.sqrt(head_dim))
    biases = jnp.concatenate(
        [
            jnp.broadcast_to(bias[h : h + 1, r * column_pairs : (r + 1) * column_pairs], (cols, column_pairs))
            for h in range(heads)
            for r in range(rows)
        ],
        axis=0,
    )
    key_bias = jnp.concatenate([key_bias_ref[...]] * (heads * rows), axis=0)
    scores = scores + biases + key_bias
    expo = jnp.exp(scores - jnp.max(scores, axis=-1, keepdims=True))
    shares = 1.0 / jnp.sum(expo, axis=-1, keepdims=True)
    mixed = dot(expo.astype(bf16), values) * shares
    attended = jnp.zeros((own_pairs, width), f32)
    for h in range(heads):
        attended = jnp.where(head_of == h, mixed[h * own_pairs : (h + 1) * own_pairs], attended)

    gated = (own_gate * attended).astype(bf16)
    result = updated[:own_pairs] + dot(gated, att_out_ref[...])
    out_ref[...] = result.reshape(rows, cols, width).astype(bf16)


def whole_pair_on_device(
    row_dim,
    pair_in,
    token_mask,
    positions,
    relpos_table,
    tri_norm_in,
    tri_in_weight,
    tri_in_gate,
    tri_out_gate,
    tri_norm_out,
    tri_out_weight,
    att_norm,
    att_qkv,
    att_gate,
    att_bias,
    att_out,
):
    rows, cols, width = pair_in.shape
    vmem = pl.BlockSpec(memory_space=pltpu.VMEM)
    params = pltpu.CompilerParams(vmem_limit_bytes=16 * 1024 * 1024)
    tokens, heads = row_dim * rows, att_bias.shape[1]

    blocks = 2 * row_dim

    def moved(order, step):
        return tuple(place ^ step for place in order)

    def move(values, step):
        return lax.ppermute(values, ("row", "col"), [(device, device ^ step) for device in range(blocks)])

    own_order = (0, 1)
    early = [own_order] + [moved(own_order, step) for step in (9, 15, 7)]
    late = [moved(own_order + early[1], step) for step in (3, 5)]

    beside = pl.CostEstimate(flops=STAGE_FLOPS, bytes_accessed=2**20, transcendentals=0)
    wide_out = jax.ShapeDtypeStruct((tokens * tokens, width), jnp.float32)
    key_shape = jax.ShapeDtypeStruct((cols, tokens * cols), jnp.float32)
    other_columns = pl.pallas_call(
        column_kernel,
        out_shape=key_shape,
        out_specs=vmem,
        compiler_params=params,
        cost_estimate=beside,
    )()
    chip, *staged = pl.pallas_call(
        functools.partial(stage_kernel, chips_of(early + late), rows),
        out_shape=[
            jax.ShapeDtypeStruct((2,) + pair_in.shape, pair_in.dtype),
            wide_out,
            wide_out,
            jax.ShapeDtypeStruct((3, width), jnp.float32),
            jax.ShapeDtypeStruct((heads, width), att_bias.dtype),
            key_shape,
        ],
        in_specs=[vmem] * 9,
        out_specs=[vmem] * 6,
        scratch_shapes=[pltpu.VMEM((tokens, relpos_table.shape[0]), jnp.float32)] * 2,
        compiler_params=params,
        cost_estimate=beside,
    )(
        pair_in,
        token_mask.reshape(1, tokens),
        positions.reshape(1, tokens),
        relpos_table,
        tri_norm_in.reshape(1, width),
        tri_norm_out.reshape(1, width),
        att_norm.reshape(1, width),
        att_bias.T,
        other_columns,
    )

    chip = chip.at[1].set(move(pair_in, 1))
    first = move(chip, 9)
    pieces = [chip, first, move(chip, 15), move(chip, 7)]
    both = jnp.concatenate([chip, first], axis=0)
    last = [move(both, 3), move(both, 5)]
    weights = (tri_in_weight, tri_in_gate, tri_out_gate, tri_out_weight, att_qkv, att_gate, att_out)
    rel, pair_mask, gains, *_ = staged
    half = jax.ShapeDtypeStruct((tokens * tokens // 2 + SPARE_ROWS, width), jnp.float32)
    halves = pl.pallas_call(
        functools.partial(early_kernel, early),
        out_shape=[half] * 4,
        in_specs=[vmem] * (7 + len(weights)),
        out_specs=[vmem] * 4,
        compiler_params=params,
        cost_estimate=beside,
    )(*pieces, rel, pair_mask, gains, *weights)
    return pl.pallas_call(
        functools.partial(whole_pair_kernel, row_dim, heads, early, late),
        out_shape=jax.ShapeDtypeStruct(pair_in.shape, pair_in.dtype),
        in_specs=[vmem] * (len(last) + 9 + len(weights)),
        out_specs=vmem,
        scratch_shapes=[pltpu.VMEM(half.shape, half.dtype)] * 3 + [pltpu.VMEM((tokens * tokens + SPARE_ROWS, width), jnp.float32)],
        compiler_params=params,
    )(*last, *halves, *staged, *weights)


def attend_column(query_col, key_col, value_col, bias_all, key_bias, block_rows):
    tok_total = query_col.shape[0]
    scale = 1.0 / math.sqrt(query_col.shape[2])

    def one_block(block_idx):
        scores = (
            jnp.einsum("ihe,khe->hik", query_col, key_col, preferred_element_type=jnp.float32)
            * scale
        )
        scores = scores + bias_all.astype(jnp.float32) + key_bias[None, None, :]
        row_max = jnp.max(scores, axis=-1, keepdims=True)
        expo_f = jnp.exp(scores - row_max)
        totals = jnp.sum(expo_f, axis=-1)
        weights = expo_f.astype(jnp.bfloat16)
        result = jnp.einsum("hik,khe->ihe", weights, value_col, preferred_element_type=jnp.float32)
        return result / jnp.transpose(totals)[:, :, None]

    blocks = lax.map(one_block, jnp.arange(tok_total // block_rows))
    return blocks.reshape(tok_total, query_col.shape[1], query_col.shape[2])


def column_attention(columns, att_qkv, att_gate, bias_all, key_bias, head_local, head_dim):
    tok_total, col_count, channels = columns.shape
    local_width = head_local * head_dim
    weight_three = att_qkv.reshape(channels, 3, channels)
    qkv_all = jnp.einsum(
        "kmc,ctd->tmkd", columns, weight_three, preferred_element_type=jnp.float32
    ).astype(jnp.bfloat16)
    qkv_all = qkv_all.reshape(3, col_count, tok_total, head_local, head_dim)
    gate_val = jax.nn.sigmoid(
        jnp.einsum("kmc,cd->kmd", columns, att_gate, preferred_element_type=jnp.float32)
    )
    block_rows = min(1024, tok_total)

    def one_column(triple):
        return attend_column(triple[0], triple[1], triple[2], bias_all, key_bias, block_rows)

    attended = lax.map(one_column, (qkv_all[0], qkv_all[1], qkv_all[2]))
    attended = jnp.transpose(attended, (1, 0, 2, 3)).reshape(tok_total, col_count, local_width)
    return (gate_val * attended).astype(jnp.bfloat16)


def split_pair_on_device(
    pair_in,
    token_mask,
    positions,
    relpos_table,
    tri_norm_in,
    tri_in_weight,
    tri_in_gate,
    tri_out_gate,
    tri_norm_out,
    tri_out_weight,
    att_norm,
    att_qkv,
    att_gate,
    att_bias,
    att_out,
):
    row_count, col_count, channels = pair_in.shape
    row_first = lax.axis_index("row") * row_count
    col_first = lax.axis_index("col") * col_count
    mask_float = token_mask.astype(jnp.float32)
    row_mask = lax.dynamic_slice_in_dim(mask_float, row_first, row_count)
    col_mask = lax.dynamic_slice_in_dim(mask_float, col_first, col_count)
    row_pos = lax.dynamic_slice_in_dim(positions, row_first, row_count)
    col_pos = lax.dynamic_slice_in_dim(positions, col_first, col_count)
    bin_count = relpos_table.shape[0]
    bin_centre = bin_count // 2
    bucket = jnp.clip(row_pos[:, None] - col_pos[None, :], -bin_centre, bin_centre - 1) + bin_centre
    onehot = (bucket[:, :, None] == jnp.arange(bin_count, dtype=jnp.int32)[None, None, :]).astype(
        jnp.bfloat16
    )
    residual = pair_in.astype(jnp.float32) + jnp.einsum(
        "rjb,bc->rjc", onehot, relpos_table, preferred_element_type=jnp.float32
    )
    normed = layer_norm(residual, tri_norm_in).astype(jnp.bfloat16)
    pair_mask = row_mask[:, None] * col_mask[None, :]
    gate_in = jnp.einsum("rjc,cd->drj", normed, tri_in_gate, preferred_element_type=jnp.float32)
    proj_in = jnp.einsum("rjc,cd->drj", normed, tri_in_weight, preferred_element_type=jnp.float32)
    projected = (jax.nn.sigmoid(gate_in) * proj_in * pair_mask[None, :, :]).astype(jnp.bfloat16)
    left_ch, right_ch = (
        lax.all_to_all(projected[:channels], "row", split_axis=0, concat_axis=1, tiled=True),
        lax.all_to_all(projected[channels:], "row", split_axis=0, concat_axis=1, tiled=True),
    )
    right_rows = lax.all_to_all(right_ch, "col", split_axis=1, concat_axis=2, tiled=True)
    product_sum = jnp.einsum(
        "cik,cjk->cij",
        lax.all_gather(left_ch, "col", axis=2, tiled=True),
        right_rows,
        preferred_element_type=jnp.float32,
    )
    products = product_sum.astype(jnp.bfloat16)
    product_tile = lax.all_to_all(products, "row", split_axis=1, concat_axis=0, tiled=True)
    tri_x = jnp.transpose(product_tile, (1, 2, 0)).astype(jnp.float32)
    normed_out = layer_norm(tri_x, tri_norm_out).astype(jnp.bfloat16)
    out_gate = jax.nn.sigmoid(
        jnp.einsum("rjc,cd->rjd", normed, tri_out_gate, preferred_element_type=jnp.float32)
    )
    residual = residual + out_gate * jnp.einsum(
        "rjc,cd->rjd", normed_out, tri_out_weight, preferred_element_type=jnp.float32
    )
    normed_att = layer_norm(residual, att_norm).astype(jnp.bfloat16)
    bias_piece = jnp.einsum(
        "kic,ch->hik", normed_att, att_bias, preferred_element_type=jnp.float32
    ).astype(jnp.bfloat16)
    key_bias = (mask_float - 1.0) * 1000000000.0
    head_count = att_bias.shape[1]
    head_dim = channels // head_count
    columns = lax.all_to_all(normed_att, "row", split_axis=1, concat_axis=0, tiled=True)
    bias_half = lax.all_gather(bias_piece, "col", axis=1, tiled=True)
    bias_all = lax.all_gather(bias_half, "row", axis=2, tiled=True)
    gated = column_attention(columns, att_qkv, att_gate, bias_all, key_bias, head_count, head_dim)
    gated_tile = lax.all_to_all(gated, "row", split_axis=0, concat_axis=1, tiled=True)
    update = jnp.einsum("rjc,cd->rjd", gated_tile, att_out, preferred_element_type=jnp.float32)
    return (residual + update).astype(jnp.bfloat16)


def on_device(row_dim, col_dim, pair_in, *others):
    rows, cols, width = pair_in.shape
    tokens = row_dim * rows
    whole_bytes = tokens * tokens * width * pair_in.dtype.itemsize
    bins = others[2].shape[0]
    tiled = cols % 8 == 0 and cols % rows == 0 and width == bins == tokens * cols == 128
    if whole_bytes <= WHOLE_PAIR_BYTES and tiled and (row_dim, col_dim) == (8, 2):
        return whole_pair_on_device(row_dim, pair_in, *others)
    return split_pair_on_device(pair_in, *others)


def solution(mesh):
    return jax.shard_map(
        functools.partial(on_device, mesh.shape["row"], mesh.shape["col"]),
        mesh=mesh,
        in_specs=(P(("groups", "row"), "col", None), P("groups"), P("groups")) + (P(),) * 12,
        out_specs=P(("groups", "row"), "col", None),
        check_vma=False,
    )
```

```python
import functools
import math

import jax
import jax.numpy as jnp
from jax import lax
from jax.experimental import pallas as pl
from jax.experimental.pallas import tpu as pltpu
from jax.sharding import PartitionSpec as P

epsilon = 1e-05

WHOLE_PAIR_BYTES = 256 * 1024
SPARE_ROWS = 16
STAGE_FLOPS = 10**9


def layer_norm(values, gain):
    mean_val = jnp.mean(values, axis=-1, keepdims=True)
    centred = values - mean_val
    var_val = jnp.mean(centred * centred, axis=-1, keepdims=True)
    return centred * lax.rsqrt(var_val + epsilon) * gain


def sigmoid(values):
    return 0.5 * jnp.tanh(0.5 * values) + 0.5


def dot(left, right):
    return jnp.dot(left, right, preferred_element_type=jnp.float32)


def dot_t(left, right):
    return lax.dot_general(
        left, right, (((1,), (1,)), ((), ())), preferred_element_type=jnp.float32
    )


def round_bf16(values):
    return values.astype(jnp.bfloat16).astype(jnp.float32)


def column_kernel(other_columns_ref):
    sub = lax.broadcasted_iota(jnp.int32, other_columns_ref.shape, 0)
    lane = lax.broadcasted_iota(jnp.int32, other_columns_ref.shape, 1)
    other_columns_ref[...] = jnp.where(lane % other_columns_ref.shape[0] == sub, 0.0, -jnp.inf)


def token_rows(chips, rows):
    return [(lax.axis_index("row") ^ chip) * rows + r for chip in chips for r in range(rows)]


def stage_kernel(
    chips,
    rows,
    pair_ref,
    mask_ref,
    pos_ref,
    table_ref,
    norm_in_ref,
    norm_out_ref,
    att_norm_ref,
    att_bias_ref,
    other_columns_ref,
    chip_ref,
    rel_ref,
    pair_mask_ref,
    gains_ref,
    bias_ref,
    key_bias_ref,
    pos_rows_ref,
    mask_rows_ref,
):
    chip_ref[0] = pair_ref[...]
    gains_ref[0:1] = norm_in_ref[...]
    gains_ref[1:2] = norm_out_ref[...]
    gains_ref[2:3] = att_norm_ref[...]
    bias_ref[...] = att_bias_ref[...]
    tokens, (cols, lanes) = pos_ref.shape[1], key_bias_ref.shape
    bins, width = table_ref.shape
    f32 = jnp.float32

    def by_row(ref):
        sub = lax.broadcasted_iota(jnp.int32, (tokens, tokens), 0)
        lane = lax.broadcasted_iota(jnp.int32, (tokens, tokens), 1)
        spread = jnp.where(sub == lane, jnp.broadcast_to(ref[...].astype(f32), (tokens, tokens)), 0.0)
        return jnp.broadcast_to(jnp.sum(spread, axis=1, keepdims=True), (tokens, bins))

    pos_rows_ref[...] = by_row(pos_ref)
    mask_rows_ref[...] = by_row(mask_ref)
    own_half = lax.axis_index("col")
    halves = [pl.ds(pl.multiple_of((own_half ^ half) * cols, cols), cols) for half in range(tokens // cols)]
    lane = lax.broadcasted_iota(jnp.int32, (cols, bins), 1).astype(f32)
    key_of = lax.broadcasted_iota(jnp.int32, (1, lanes), 1) // cols
    key_mask = jnp.zeros((1, lanes), f32)
    centre = float(bins // 2)
    hot = []
    for at, token in enumerate(token_rows(chips, rows)):
        pos, mask = pos_rows_ref[pl.ds(token, 1), :], mask_rows_ref[pl.ds(token, 1), :]
        for half in halves:
            bucket = jnp.clip(pos - pos_rows_ref[half, :], -centre, centre - 1.0) + centre
            first = len(hot) * cols
            pair_mask_ref[first : first + cols, :] = mask_rows_ref[half, :] * mask
            hot.append((bucket == lane).astype(f32))
        key_mask = jnp.where(key_of == at, mask, key_mask)
    rel_ref[...] = dot(jnp.concatenate(hot, axis=0).astype(jnp.bfloat16), table_ref[...])
    key_bias_ref[...] = (key_mask - 1.0) * 1000000000.0 + other_columns_ref[...]


def edge_operands(pieces, orders, rows, rel, pair_mask, gain, in_gate, in_weight, for_right=lambda values: values):
    width = rel.shape[1]
    blocks = {
        place: piece[at].astype(jnp.float32) for piece, order in zip(pieces, orders) for at, place in enumerate(order)
    }
    tiles = [blocks[2 * chip + half][r] for chip in chips_of(orders) for r in range(rows) for half in range(2)]
    base = jnp.concatenate(tiles, axis=0) + rel
    normed_f = layer_norm(base, gain).astype(jnp.bfloat16).astype(jnp.float32)

    def operand(values, mask, columns):
        values = values.astype(jnp.bfloat16)
        return round_bf16(sigmoid(dot(values, in_gate[:, columns])) * dot(values, in_weight[:, columns]) * mask)

    left = operand(normed_f, pair_mask, slice(0, width))
    right = operand(for_right(normed_f), for_right(pair_mask), slice(width, 2 * width))
    return left, right, base, normed_f


def chips_of(orders):
    return list(dict.fromkeys(place // 2 for order in orders for place in order))


def early_kernel(orders, *refs):
    piece_refs = refs[: len(orders)]
    rel_ref, pair_mask_ref, gains_ref, in_weight_ref, in_gate_ref = refs[len(orders) : len(orders) + 5]
    here = refs[-1].shape[0] - SPARE_ROWS
    found = edge_operands(
        piece_refs,
        orders,
        piece_refs[0].shape[1],
        rel_ref[:here],
        pair_mask_ref[:here],
        gains_ref[0:1],
        in_gate_ref[...],
        in_weight_ref[...],
    )
    for ref, values in zip(refs[-4:], found):
        ref[:here] = values


def whole_pair_kernel(row_dim, heads, early, late, *refs):
    whole_pair_steps(row_dim, heads, early, late, refs[: len(late)], *refs[len(late) :])


def whole_pair_steps(
    row_dim,
    heads,
    early,
    late,
    piece_refs,
    early_left_ref,
    early_right_ref,
    early_base_ref,
    early_normed_ref,
    rel_ref,
    pair_mask_ref,
    gains_ref,
    att_bias_ref,
    key_bias_ref,
    in_weight_ref,
    in_gate_ref,
    out_gate_ref,
    out_weight_ref,
    qkv_ref,
    att_gate_ref,
    att_out_ref,
    out_ref,
    late_left_ref,
    late_base_ref,
    late_normed_ref,
    right_ref,
):
    rows, cols, width = piece_refs[0].shape[1:]
    tokens = row_dim * rows
    head_dim = width // heads
    row, col = lax.axis_index("row"), lax.axis_index("col")
    f32, bf16 = jnp.float32, jnp.bfloat16

    here = early_left_ref.shape[0] - SPARE_ROWS
    late_chips = chips_of(late)
    near = [chip for chip in late_chips if chip < row_dim // 2]
    far = [chip for chip in late_chips if chip >= row_dim // 2]
    near_is_own = row // (row_dim // 2) == col

    def for_right(values):
        count = rows * tokens
        rows_of = {chip: values[at * count : (at + 1) * count] for at, chip in enumerate(late_chips)}
        return jnp.concatenate([jnp.where(near_is_own, rows_of[n], rows_of[f]) for n, f in zip(near, far)], axis=0)

    left, right, base, normed = edge_operands(
        piece_refs,
        late,
        rows,
        rel_ref[here:],
        pair_mask_ref[here:],
        gains_ref[0:1],
        in_gate_ref[...],
        in_weight_ref[...],
        for_right,
    )
    late_left_ref[:here] = left
    late_base_ref[:here] = base
    late_normed_ref[:here] = normed
    lefts = (early_left_ref, late_left_ref)

    own_half = [jnp.where(near_is_own, n, f) for n, f in zip(near, far)]
    for tokens_of, values in (
        (token_rows(chips_of(early), rows), early_right_ref),
        (token_rows(own_half, rows), right),
    ):
        for at, token in enumerate(tokens_of):
            place = pl.ds(pl.multiple_of(token * tokens, tokens), tokens)
            right_ref[place, :] = values[at * tokens : (at + 1) * tokens]

    right_at = [right_ref[pl.ds(col * cols * tokens + m, cols, stride=tokens), :] for m in range(tokens)]
    products = []
    for i in range(tokens):
        ref, first = lefts[i * tokens // here], i * tokens % here
        total = ref[first : first + 1] * right_at[0]
        for m in range(1, tokens):
            total = total + ref[first + m : first + m + 1] * right_at[m]
        products.append(total)
    extra = [None] * rows
    for m in range(tokens):
        left_at = jnp.concatenate([ref[pl.ds(m, here // tokens, stride=tokens), :] for ref in lefts], axis=0)
        for r in range(rows):
            term = left_at * early_right_ref[r * tokens + m : r * tokens + m + 1]
            extra[r] = term if m == 0 else extra[r] + term

    own_token = row * rows
    own_column = ((own_token // cols) ^ col) * cols + own_token % cols

    def own_columns(early_ref, late_ref):
        pair = (early_ref, late_ref)
        return jnp.concatenate(
            [pair[i * tokens // here][i * tokens % here : i * tokens % here + cols] for i in range(tokens)], axis=0
        )

    def own_tokens(early_ref, late_ref):
        return jnp.concatenate(
            [
                ref[pl.ds(own_column + r, here // tokens, stride=tokens), :]
                for r in range(rows)
                for ref in (early_ref, late_ref)
            ],
            axis=0,
        )

    def attention_input(products, chosen):
        normed_out = layer_norm(round_bf16(jnp.concatenate(products, axis=0)), gains_ref[1:2]).astype(bf16)
        out_gate = sigmoid(dot(chosen(early_normed_ref, late_normed_ref).astype(bf16), out_gate_ref[...]))
        updated = chosen(early_base_ref, late_base_ref) + out_gate * dot(normed_out, out_weight_ref[...])
        return updated, layer_norm(updated, gains_ref[2:3]).astype(bf16)

    updated, column = attention_input(products, own_columns)
    _, of_tokens = attention_input(extra, own_tokens)
    own_pairs = rows * cols
    column_pairs = tokens * cols

    own = column[:own_pairs]
    queries = dot(own, qkv_ref[:, :width])
    keys = dot(column, qkv_ref[:, width : 2 * width]).astype(bf16)
    values = dot(column, qkv_ref[:, 2 * width :]).astype(bf16)
    own_gate = sigmoid(dot(own, att_gate_ref[...]))

    bias = dot_t(att_bias_ref[...], of_tokens).astype(bf16)
    shape = (rows * tokens, rows * column_pairs)
    source = lax.broadcasted_iota(jnp.int32, shape, 0)
    repeated = source == lax.broadcasted_iota(jnp.int32, shape, 1) // cols
    bias = dot(bias, repeated.astype(f32).astype(bf16))

    head_of = lax.broadcasted_iota(jnp.int32, (own_pairs, width), 1) // head_dim
    queries = round_bf16(queries)
    by_head = jnp.concatenate(
        [jnp.where(head_of == h, queries, 0.0) for h in range(heads)], axis=0
    ).astype(bf16)
    scores = dot_t(by_head, keys) * (1.0 / math.sqrt(head_dim))
    biases = jnp.concatenate(
        [
            jnp.broadcast_to(bias[h : h + 1, r * column_pairs : (r + 1) * column_pairs], (cols, column_pairs))
            for h in range(heads)
            for r in range(rows)
        ],
        axis=0,
    )
    key_bias = jnp.concatenate([key_bias_ref[...]] * (heads * rows), axis=0)
    scores = scores + biases + key_bias
    expo = jnp.exp(scores - jnp.max(scores, axis=-1, keepdims=True))
    shares = 1.0 / jnp.sum(expo, axis=-1, keepdims=True)
    mixed = dot(expo.astype(bf16), values) * shares
    attended = jnp.zeros((own_pairs, width), f32)
    for h in range(heads):
        attended = jnp.where(head_of == h, mixed[h * own_pairs : (h + 1) * own_pairs], attended)

    gated = (own_gate * attended).astype(bf16)
    result = updated[:own_pairs] + dot(gated, att_out_ref[...])
    out_ref[...] = result.reshape(rows, cols, width).astype(bf16)


def whole_pair_on_device(
    row_dim,
    pair_in,
    token_mask,
    positions,
    relpos_table,
    tri_norm_in,
    tri_in_weight,
    tri_in_gate,
    tri_out_gate,
    tri_norm_out,
    tri_out_weight,
    att_norm,
    att_qkv,
    att_gate,
    att_bias,
    att_out,
):
    rows, cols, width = pair_in.shape
    vmem = pl.BlockSpec(memory_space=pltpu.VMEM)
    params = pltpu.CompilerParams(vmem_limit_bytes=16 * 1024 * 1024)
    tokens, heads = row_dim * rows, att_bias.shape[1]

    blocks = 2 * row_dim

    def moved(order, step):
        return tuple(place ^ step for place in order)

    def move(values, step):
        return lax.ppermute(values, ("row", "col"), [(device, device ^ step) for device in range(blocks)])

    own_order = (0, 1)
    early = [own_order] + [moved(own_order, step) for step in (9, 15, 7)]
    late = [moved(own_order + early[1], step) for step in (3, 5)]

    beside = pl.CostEstimate(flops=STAGE_FLOPS, bytes_accessed=2**20, transcendentals=0)
    wide_out = jax.ShapeDtypeStruct((tokens * tokens, width), jnp.float32)
    key_shape = jax.ShapeDtypeStruct((cols, tokens * cols), jnp.float32)
    other_columns = pl.pallas_call(
        column_kernel,
        out_shape=key_shape,
        out_specs=vmem,
        compiler_params=params,
        cost_estimate=beside,
    )()
    chip, *staged = pl.pallas_call(
        functools.partial(stage_kernel, chips_of(early + late), rows),
        out_shape=[
            jax.ShapeDtypeStruct((2,) + pair_in.shape, pair_in.dtype),
            wide_out,
            wide_out,
            jax.ShapeDtypeStruct((3, width), jnp.float32),
            jax.ShapeDtypeStruct((heads, width), att_bias.dtype),
            key_shape,
        ],
        in_specs=[vmem] * 9,
        out_specs=[vmem] * 6,
        scratch_shapes=[pltpu.VMEM((tokens, relpos_table.shape[0]), jnp.float32)] * 2,
        compiler_params=params,
        cost_estimate=beside,
    )(
        pair_in,
        token_mask.reshape(1, tokens),
        positions.reshape(1, tokens),
        relpos_table,
        tri_norm_in.reshape(1, width),
        tri_norm_out.reshape(1, width),
        att_norm.reshape(1, width),
        att_bias.T,
        other_columns,
    )

    chip = chip.at[1].set(move(pair_in, 1))
    first = move(chip, 9)
    pieces = [chip, first, move(chip, 15), move(chip, 7)]
    both = jnp.concatenate([chip, first], axis=0)
    last = [move(both, 3), move(both, 5)]
    weights = (tri_in_weight, tri_in_gate, tri_out_gate, tri_out_weight, att_qkv, att_gate, att_out)
    rel, pair_mask, gains, *_ = staged
    half = jax.ShapeDtypeStruct((tokens * tokens // 2 + SPARE_ROWS, width), jnp.float32)
    halves = pl.pallas_call(
        functools.partial(early_kernel, early),
        out_shape=[half] * 4,
        in_specs=[vmem] * (7 + len(weights)),
        out_specs=[vmem] * 4,
        compiler_params=params,
        cost_estimate=beside,
    )(*pieces, rel, pair_mask, gains, *weights)
    return pl.pallas_call(
        functools.partial(whole_pair_kernel, row_dim, heads, early, late),
        out_shape=jax.ShapeDtypeStruct(pair_in.shape, pair_in.dtype),
        in_specs=[vmem] * (len(last) + 9 + len(weights)),
        out_specs=vmem,
        scratch_shapes=[pltpu.VMEM(half.shape, half.dtype)] * 3 + [pltpu.VMEM((tokens * tokens + SPARE_ROWS, width), jnp.float32)],
        compiler_params=params,
    )(*last, *halves, *staged, *weights)


def attend_column(query_col, key_col, value_col, bias_all, key_bias, block_rows):
    tok_total = query_col.shape[0]
    scale = 1.0 / math.sqrt(query_col.shape[2])

    def one_block(block_idx):
        scores = (
            jnp.einsum("ihe,khe->hik", query_col, key_col, preferred_element_type=jnp.float32)
            * scale
        )
        scores = scores + bias_all.astype(jnp.float32) + key_bias[None, None, :]
        row_max = jnp.max(scores, axis=-1, keepdims=True)
        expo_f = jnp.exp(scores - row_max)
        totals = jnp.sum(expo_f, axis=-1)
        weights = expo_f.astype(jnp.bfloat16)
        result = jnp.einsum("hik,khe->ihe", weights, value_col, preferred_element_type=jnp.float32)
        return result / jnp.transpose(totals)[:, :, None]

    blocks = lax.map(one_block, jnp.arange(tok_total // block_rows))
    return blocks.reshape(tok_total, query_col.shape[1], query_col.shape[2])


def column_attention(columns, att_qkv, att_gate, bias_all, key_bias, head_local, head_dim):
    tok_total, col_count, channels = columns.shape
    local_width = head_local * head_dim
    weight_three = att_qkv.reshape(channels, 3, channels)
    qkv_all = jnp.einsum(
        "kmc,ctd->tmkd", columns, weight_three, preferred_element_type=jnp.float32
    ).astype(jnp.bfloat16)
    qkv_all = qkv_all.reshape(3, col_count, tok_total, head_local, head_dim)
    gate_val = jax.nn.sigmoid(
        jnp.einsum("kmc,cd->kmd", columns, att_gate, preferred_element_type=jnp.float32)
    )
    block_rows = min(1024, tok_total)

    def one_column(triple):
        return attend_column(triple[0], triple[1], triple[2], bias_all, key_bias, block_rows)

    attended = lax.map(one_column, (qkv_all[0], qkv_all[1], qkv_all[2]))
    attended = jnp.transpose(attended, (1, 0, 2, 3)).reshape(tok_total, col_count, local_width)
    return (gate_val * attended).astype(jnp.bfloat16)


def split_pair_on_device(
    pair_in,
    token_mask,
    positions,
    relpos_table,
    tri_norm_in,
    tri_in_weight,
    tri_in_gate,
    tri_out_gate,
    tri_norm_out,
    tri_out_weight,
    att_norm,
    att_qkv,
    att_gate,
    att_bias,
    att_out,
):
    row_count, col_count, channels = pair_in.shape
    row_first = lax.axis_index("row") * row_count
    col_first = lax.axis_index("col") * col_count
    mask_float = token_mask.astype(jnp.float32)
    row_mask = lax.dynamic_slice_in_dim(mask_float, row_first, row_count)
    col_mask = lax.dynamic_slice_in_dim(mask_float, col_first, col_count)
    row_pos = lax.dynamic_slice_in_dim(positions, row_first, row_count)
    col_pos = lax.dynamic_slice_in_dim(positions, col_first, col_count)
    bin_count = relpos_table.shape[0]
    bin_centre = bin_count // 2
    bucket = jnp.clip(row_pos[:, None] - col_pos[None, :], -bin_centre, bin_centre - 1) + bin_centre
    onehot = (bucket[:, :, None] == jnp.arange(bin_count, dtype=jnp.int32)[None, None, :]).astype(
        jnp.bfloat16
    )
    residual = pair_in.astype(jnp.float32) + jnp.einsum(
        "rjb,bc->rjc", onehot, relpos_table, preferred_element_type=jnp.float32
    )
    normed = layer_norm(residual, tri_norm_in).astype(jnp.bfloat16)
    pair_mask = row_mask[:, None] * col_mask[None, :]
    gate_in = jnp.einsum("rjc,cd->drj", normed, tri_in_gate, preferred_element_type=jnp.float32)
    proj_in = jnp.einsum("rjc,cd->drj", normed, tri_in_weight, preferred_element_type=jnp.float32)
    projected = (jax.nn.sigmoid(gate_in) * proj_in * pair_mask[None, :, :]).astype(jnp.bfloat16)
    left_ch, right_ch = (
        lax.all_to_all(projected[:channels], "row", split_axis=0, concat_axis=1, tiled=True),
        lax.all_to_all(projected[channels:], "row", split_axis=0, concat_axis=1, tiled=True),
    )
    right_rows = lax.all_to_all(right_ch, "col", split_axis=1, concat_axis=2, tiled=True)
    product_sum = jnp.einsum(
        "cik,cjk->cij",
        lax.all_gather(left_ch, "col", axis=2, tiled=True),
        right_rows,
        preferred_element_type=jnp.float32,
    )
    products = product_sum.astype(jnp.bfloat16)
    product_tile = lax.all_to_all(products, "row", split_axis=1, concat_axis=0, tiled=True)
    tri_x = jnp.transpose(product_tile, (1, 2, 0)).astype(jnp.float32)
    normed_out = layer_norm(tri_x, tri_norm_out).astype(jnp.bfloat16)
    out_gate = jax.nn.sigmoid(
        jnp.einsum("rjc,cd->rjd", normed, tri_out_gate, preferred_element_type=jnp.float32)
    )
    residual = residual + out_gate * jnp.einsum(
        "rjc,cd->rjd", normed_out, tri_out_weight, preferred_element_type=jnp.float32
    )
    normed_att = layer_norm(residual, att_norm).astype(jnp.bfloat16)
    bias_piece = jnp.einsum(
        "kic,ch->hik", normed_att, att_bias, preferred_element_type=jnp.float32
    ).astype(jnp.bfloat16)
    key_bias = (mask_float - 1.0) * 1000000000.0
    head_count = att_bias.shape[1]
    head_dim = channels // head_count
    columns = lax.all_to_all(normed_att, "row", split_axis=1, concat_axis=0, tiled=True)
    bias_half = lax.all_gather(bias_piece, "col", axis=1, tiled=True)
    bias_all = lax.all_gather(bias_half, "row", axis=2, tiled=True)
    gated = column_attention(columns, att_qkv, att_gate, bias_all, key_bias, head_count, head_dim)
    gated_tile = lax.all_to_all(gated, "row", split_axis=0, concat_axis=1, tiled=True)
    update = jnp.einsum("rjc,cd->rjd", gated_tile, att_out, preferred_element_type=jnp.float32)
    return (residual + update).astype(jnp.bfloat16)


def on_device(row_dim, col_dim, pair_in, *others):
    rows, cols, width = pair_in.shape
    tokens = row_dim * rows
    whole_bytes = tokens * tokens * width * pair_in.dtype.itemsize
    bins = others[2].shape[0]
    tiled = cols % 8 == 0 and cols % rows == 0 and width == bins == tokens * cols == 128
    if whole_bytes <= WHOLE_PAIR_BYTES and tiled and (row_dim, col_dim) == (8, 2):
        return whole_pair_on_device(row_dim, pair_in, *others)
    return split_pair_on_device(pair_in, *others)


def solution(mesh):
    return jax.shard_map(
        functools.partial(on_device, mesh.shape["row"], mesh.shape["col"]),
        mesh=mesh,
        in_specs=(P(("groups", "row"), "col", None), P("groups"), P("groups")) + (P(),) * 12,
        out_specs=P(("groups", "row"), "col", None),
        check_vma=False,
    )
```

```python
import functools
import math

import jax
import jax.numpy as jnp
from jax import lax
from jax.experimental import pallas as pl
from jax.experimental.pallas import tpu as pltpu
from jax.sharding import PartitionSpec as P

epsilon = 1e-05

WHOLE_PAIR_BYTES = 256 * 1024
SPARE_ROWS = 16
STAGE_FLOPS = 10**9


def layer_norm(values, gain):
    mean_val = jnp.mean(values, axis=-1, keepdims=True)
    centred = values - mean_val
    var_val = jnp.mean(centred * centred, axis=-1, keepdims=True)
    return centred * lax.rsqrt(var_val + epsilon) * gain


def sigmoid(values):
    return 0.5 * jnp.tanh(0.5 * values) + 0.5


def dot(left, right):
    return jnp.dot(left, right, preferred_element_type=jnp.float32)


def dot_t(left, right):
    return lax.dot_general(
        left, right, (((1,), (1,)), ((), ())), preferred_element_type=jnp.float32
    )


def round_bf16(values):
    return values.astype(jnp.bfloat16).astype(jnp.float32)


def column_kernel(other_columns_ref):
    sub = lax.broadcasted_iota(jnp.int32, other_columns_ref.shape, 0)
    lane = lax.broadcasted_iota(jnp.int32, other_columns_ref.shape, 1)
    other_columns_ref[...] = jnp.where(lane % other_columns_ref.shape[0] == sub, 0.0, -jnp.inf)


def token_rows(chips, rows):
    return [(lax.axis_index("row") ^ chip) * rows + r for chip in chips for r in range(rows)]


def stage_kernel(
    chips,
    rows,
    pair_ref,
    mask_ref,
    pos_ref,
    table_ref,
    norm_in_ref,
    norm_out_ref,
    att_norm_ref,
    att_bias_ref,
    other_columns_ref,
    chip_ref,
    rel_ref,
    pair_mask_ref,
    gains_ref,
    bias_ref,
    key_bias_ref,
    pos_rows_ref,
    mask_rows_ref,
):
    chip_ref[0] = pair_ref[...]
    gains_ref[0:1] = norm_in_ref[...]
    gains_ref[1:2] = norm_out_ref[...]
    gains_ref[2:3] = att_norm_ref[...]
    bias_ref[...] = att_bias_ref[...]
    tokens, (cols, lanes) = pos_ref.shape[1], key_bias_ref.shape
    bins, width = table_ref.shape
    f32 = jnp.float32

    def by_row(ref):
        sub = lax.broadcasted_iota(jnp.int32, (tokens, tokens), 0)
        lane = lax.broadcasted_iota(jnp.int32, (tokens, tokens), 1)
        spread = jnp.where(sub == lane, jnp.broadcast_to(ref[...].astype(f32), (tokens, tokens)), 0.0)
        return jnp.broadcast_to(jnp.sum(spread, axis=1, keepdims=True), (tokens, bins))

    pos_rows_ref[...] = by_row(pos_ref)
    mask_rows_ref[...] = by_row(mask_ref)
    own_half = lax.axis_index("col")
    halves = [pl.ds(pl.multiple_of((own_half ^ half) * cols, cols), cols) for half in range(tokens // cols)]
    lane = lax.broadcasted_iota(jnp.int32, (cols, bins), 1).astype(f32)
    key_of = lax.broadcasted_iota(jnp.int32, (1, lanes), 1) // cols
    key_mask = jnp.zeros((1, lanes), f32)
    centre = float(bins // 2)
    hot = []
    for at, token in enumerate(token_rows(chips, rows)):
        pos, mask = pos_rows_ref[pl.ds(token, 1), :], mask_rows_ref[pl.ds(token, 1), :]
        for half in halves:
            bucket = jnp.clip(pos - pos_rows_ref[half, :], -centre, centre - 1.0) + centre
            first = len(hot) * cols
            pair_mask_ref[first : first + cols, :] = mask_rows_ref[half, :] * mask
            hot.append((bucket == lane).astype(f32))
        key_mask = jnp.where(key_of == at, mask, key_mask)
    rel_ref[...] = dot(jnp.concatenate(hot, axis=0).astype(jnp.bfloat16), table_ref[...])
    key_bias_ref[...] = (key_mask - 1.0) * 1000000000.0 + other_columns_ref[...]


def edge_operands(
    pieces, orders, rows, rel, pair_mask, gain, in_gate, in_weight, out_gate, for_right=lambda values: values
):
    width = rel.shape[1]
    blocks = {
        place: piece[at].astype(jnp.float32) for piece, order in zip(pieces, orders) for at, place in enumerate(order)
    }
    tiles = [blocks[2 * chip + half][r] for chip in chips_of(orders) for r in range(rows) for half in range(2)]
    base = jnp.concatenate(tiles, axis=0) + rel
    normed_f = layer_norm(base, gain).astype(jnp.bfloat16).astype(jnp.float32)

    def operand(values, mask, columns):
        values = values.astype(jnp.bfloat16)
        return round_bf16(sigmoid(dot(values, in_gate[:, columns])) * dot(values, in_weight[:, columns]) * mask)

    left = operand(normed_f, pair_mask, slice(0, width))
    right = operand(for_right(normed_f), for_right(pair_mask), slice(width, 2 * width))
    return left, right, base, sigmoid(dot(normed_f.astype(jnp.bfloat16), out_gate))


def chips_of(orders):
    return list(dict.fromkeys(place // 2 for order in orders for place in order))


def early_kernel(orders, *refs):
    piece_refs = refs[: len(orders)]
    rel_ref, pair_mask_ref, gains_ref, in_weight_ref, in_gate_ref, out_gate_ref = refs[len(orders) : len(orders) + 6]
    here = refs[-1].shape[0] - SPARE_ROWS
    found = edge_operands(
        piece_refs,
        orders,
        piece_refs[0].shape[1],
        rel_ref[:here],
        pair_mask_ref[:here],
        gains_ref[0:1],
        in_gate_ref[...],
        in_weight_ref[...],
        out_gate_ref[...],
    )
    for ref, values in zip(refs[-4:], found):
        ref[:here] = values


def whole_pair_kernel(row_dim, heads, early, late, *refs):
    whole_pair_steps(row_dim, heads, early, late, refs[: len(late)], *refs[len(late) :])


def whole_pair_steps(
    row_dim,
    heads,
    early,
    late,
    piece_refs,
    early_left_ref,
    early_right_ref,
    early_base_ref,
    early_gate_ref,
    rel_ref,
    pair_mask_ref,
    gains_ref,
    att_bias_ref,
    key_bias_ref,
    in_weight_ref,
    in_gate_ref,
    out_gate_ref,
    out_weight_ref,
    qkv_ref,
    att_gate_ref,
    att_out_ref,
    out_ref,
    late_left_ref,
    late_base_ref,
    late_gate_ref,
    right_ref,
):
    rows, cols, width = piece_refs[0].shape[1:]
    tokens = row_dim * rows
    head_dim = width // heads
    row, col = lax.axis_index("row"), lax.axis_index("col")
    f32, bf16 = jnp.float32, jnp.bfloat16

    here = early_left_ref.shape[0] - SPARE_ROWS
    late_chips = chips_of(late)
    near = [chip for chip in late_chips if chip < row_dim // 2]
    far = [chip for chip in late_chips if chip >= row_dim // 2]
    near_is_own = row // (row_dim // 2) == col

    def for_right(values):
        count = rows * tokens
        rows_of = {chip: values[at * count : (at + 1) * count] for at, chip in enumerate(late_chips)}
        return jnp.concatenate([jnp.where(near_is_own, rows_of[n], rows_of[f]) for n, f in zip(near, far)], axis=0)

    left, right, base, gate = edge_operands(
        piece_refs,
        late,
        rows,
        rel_ref[here:],
        pair_mask_ref[here:],
        gains_ref[0:1],
        in_gate_ref[...],
        in_weight_ref[...],
        out_gate_ref[...],
        for_right,
    )
    late_left_ref[:here] = left
    late_base_ref[:here] = base
    late_gate_ref[:here] = gate
    lefts = (early_left_ref, late_left_ref)

    own_half = [jnp.where(near_is_own, n, f) for n, f in zip(near, far)]
    for tokens_of, values in (
        (token_rows(chips_of(early), rows), early_right_ref),
        (token_rows(own_half, rows), right),
    ):
        for at, token in enumerate(tokens_of):
            place = pl.ds(pl.multiple_of(token * tokens, tokens), tokens)
            right_ref[place, :] = values[at * tokens : (at + 1) * tokens]

    right_at = [right_ref[pl.ds(col * cols * tokens + m, cols, stride=tokens), :] for m in range(tokens)]
    products = []
    for i in range(tokens):
        ref, first = lefts[i * tokens // here], i * tokens % here
        total = ref[first : first + 1] * right_at[0]
        for m in range(1, tokens):
            total = total + ref[first + m : first + m + 1] * right_at[m]
        products.append(total)
    extra = [None] * rows
    for m in range(tokens):
        left_at = jnp.concatenate([ref[pl.ds(m, here // tokens, stride=tokens), :] for ref in lefts], axis=0)
        for r in range(rows):
            term = left_at * early_right_ref[r * tokens + m : r * tokens + m + 1]
            extra[r] = term if m == 0 else extra[r] + term

    own_token = row * rows
    own_column = ((own_token // cols) ^ col) * cols + own_token % cols

    def own_columns(early_ref, late_ref):
        pair = (early_ref, late_ref)
        return jnp.concatenate(
            [pair[i * tokens // here][i * tokens % here : i * tokens % here + cols] for i in range(tokens)], axis=0
        )

    def own_tokens(early_ref, late_ref):
        return jnp.concatenate(
            [
                ref[pl.ds(own_column + r, here // tokens, stride=tokens), :]
                for r in range(rows)
                for ref in (early_ref, late_ref)
            ],
            axis=0,
        )

    def attention_input(products, chosen):
        normed_out = layer_norm(round_bf16(jnp.concatenate(products, axis=0)), gains_ref[1:2]).astype(bf16)
        update = chosen(early_gate_ref, late_gate_ref) * dot(normed_out, out_weight_ref[...])
        updated = chosen(early_base_ref, late_base_ref) + update
        return updated, layer_norm(updated, gains_ref[2:3]).astype(bf16)

    updated, column = attention_input(products, own_columns)
    _, of_tokens = attention_input(extra, own_tokens)
    own_pairs = rows * cols
    column_pairs = tokens * cols

    own = column[:own_pairs]
    queries = dot(own, qkv_ref[:, :width])
    keys = dot(column, qkv_ref[:, width : 2 * width]).astype(bf16)
    values = dot(column, qkv_ref[:, 2 * width :]).astype(bf16)
    own_gate = sigmoid(dot(own, att_gate_ref[...]))

    bias = dot_t(att_bias_ref[...], of_tokens).astype(bf16)
    shape = (rows * tokens, rows * column_pairs)
    source = lax.broadcasted_iota(jnp.int32, shape, 0)
    repeated = source == lax.broadcasted_iota(jnp.int32, shape, 1) // cols
    bias = dot(bias, repeated.astype(f32).astype(bf16))

    head_of = lax.broadcasted_iota(jnp.int32, (own_pairs, width), 1) // head_dim
    queries = round_bf16(queries)
    by_head = jnp.concatenate(
        [jnp.where(head_of == h, queries, 0.0) for h in range(heads)], axis=0
    ).astype(bf16)
    scores = dot_t(by_head, keys) * (1.0 / math.sqrt(head_dim))
    biases = jnp.concatenate(
        [
            jnp.broadcast_to(bias[h : h + 1, r * column_pairs : (r + 1) * column_pairs], (cols, column_pairs))
            for h in range(heads)
            for r in range(rows)
        ],
        axis=0,
    )
    key_bias = jnp.concatenate([key_bias_ref[...]] * (heads * rows), axis=0)
    scores = scores + biases + key_bias
    expo = jnp.exp(scores - jnp.max(scores, axis=-1, keepdims=True))
    shares = 1.0 / jnp.sum(expo, axis=-1, keepdims=True)
    mixed = dot(expo.astype(bf16), values) * shares
    attended = jnp.zeros((own_pairs, width), f32)
    for h in range(heads):
        attended = jnp.where(head_of == h, mixed[h * own_pairs : (h + 1) * own_pairs], attended)

    gated = (own_gate * attended).astype(bf16)
    result = updated[:own_pairs] + dot(gated, att_out_ref[...])
    out_ref[...] = result.reshape(rows, cols, width).astype(bf16)


def whole_pair_on_device(
    row_dim,
    pair_in,
    token_mask,
    positions,
    relpos_table,
    tri_norm_in,
    tri_in_weight,
    tri_in_gate,
    tri_out_gate,
    tri_norm_out,
    tri_out_weight,
    att_norm,
    att_qkv,
    att_gate,
    att_bias,
    att_out,
):
    rows, cols, width = pair_in.shape
    vmem = pl.BlockSpec(memory_space=pltpu.VMEM)
    params = pltpu.CompilerParams(vmem_limit_bytes=16 * 1024 * 1024)
    tokens, heads = row_dim * rows, att_bias.shape[1]

    blocks = 2 * row_dim

    def moved(order, step):
        return tuple(place ^ step for place in order)

    def move(values, step):
        return lax.ppermute(values, ("row", "col"), [(device, device ^ step) for device in range(blocks)])

    own_order = (0, 1)
    early = [own_order] + [moved(own_order, step) for step in (9, 15, 7)]
    late = [moved(own_order + early[1], step) for step in (3, 5)]

    beside = pl.CostEstimate(flops=STAGE_FLOPS, bytes_accessed=2**20, transcendentals=0)
    wide_out = jax.ShapeDtypeStruct((tokens * tokens, width), jnp.float32)
    key_shape = jax.ShapeDtypeStruct((cols, tokens * cols), jnp.float32)
    other_columns = pl.pallas_call(
        column_kernel,
        out_shape=key_shape,
        out_specs=vmem,
        compiler_params=params,
        cost_estimate=beside,
    )()
    chip, *staged = pl.pallas_call(
        functools.partial(stage_kernel, chips_of(early + late), rows),
        out_shape=[
            jax.ShapeDtypeStruct((2,) + pair_in.shape, pair_in.dtype),
            wide_out,
            wide_out,
            jax.ShapeDtypeStruct((3, width), jnp.float32),
            jax.ShapeDtypeStruct((heads, width), att_bias.dtype),
            key_shape,
        ],
        in_specs=[vmem] * 9,
        out_specs=[vmem] * 6,
        scratch_shapes=[pltpu.VMEM((tokens, relpos_table.shape[0]), jnp.float32)] * 2,
        compiler_params=params,
        cost_estimate=beside,
    )(
        pair_in,
        token_mask.reshape(1, tokens),
        positions.reshape(1, tokens),
        relpos_table,
        tri_norm_in.reshape(1, width),
        tri_norm_out.reshape(1, width),
        att_norm.reshape(1, width),
        att_bias.T,
        other_columns,
    )

    chip = chip.at[1].set(move(pair_in, 1))
    first = move(chip, 9)
    pieces = [chip, first, move(chip, 15), move(chip, 7)]
    both = jnp.concatenate([chip, first], axis=0)
    last = [move(both, 3), move(both, 5)]
    weights = (tri_in_weight, tri_in_gate, tri_out_gate, tri_out_weight, att_qkv, att_gate, att_out)
    rel, pair_mask, gains, *_ = staged
    half = jax.ShapeDtypeStruct((tokens * tokens // 2 + SPARE_ROWS, width), jnp.float32)
    halves = pl.pallas_call(
        functools.partial(early_kernel, early),
        out_shape=[half] * 4,
        in_specs=[vmem] * (7 + len(weights)),
        out_specs=[vmem] * 4,
        compiler_params=params,
        cost_estimate=beside,
    )(*pieces, rel, pair_mask, gains, *weights)
    return pl.pallas_call(
        functools.partial(whole_pair_kernel, row_dim, heads, early, late),
        out_shape=jax.ShapeDtypeStruct(pair_in.shape, pair_in.dtype),
        in_specs=[vmem] * (len(last) + 9 + len(weights)),
        out_specs=vmem,
        scratch_shapes=[pltpu.VMEM(half.shape, half.dtype)] * 3 + [pltpu.VMEM((tokens * tokens + SPARE_ROWS, width), jnp.float32)],
        compiler_params=params,
    )(*last, *halves, *staged, *weights)


def attend_column(query_col, key_col, value_col, bias_all, key_bias, block_rows):
    tok_total = query_col.shape[0]
    scale = 1.0 / math.sqrt(query_col.shape[2])

    def one_block(block_idx):
        scores = (
            jnp.einsum("ihe,khe->hik", query_col, key_col, preferred_element_type=jnp.float32)
            * scale
        )
        scores = scores + bias_all.astype(jnp.float32) + key_bias[None, None, :]
        row_max = jnp.max(scores, axis=-1, keepdims=True)
        expo_f = jnp.exp(scores - row_max)
        totals = jnp.sum(expo_f, axis=-1)
        weights = expo_f.astype(jnp.bfloat16)
        result = jnp.einsum("hik,khe->ihe", weights, value_col, preferred_element_type=jnp.float32)
        return result / jnp.transpose(totals)[:, :, None]

    blocks = lax.map(one_block, jnp.arange(tok_total // block_rows))
    return blocks.reshape(tok_total, query_col.shape[1], query_col.shape[2])


def column_attention(columns, att_qkv, att_gate, bias_all, key_bias, head_local, head_dim):
    tok_total, col_count, channels = columns.shape
    local_width = head_local * head_dim
    weight_three = att_qkv.reshape(channels, 3, channels)
    qkv_all = jnp.einsum(
        "kmc,ctd->tmkd", columns, weight_three, preferred_element_type=jnp.float32
    ).astype(jnp.bfloat16)
    qkv_all = qkv_all.reshape(3, col_count, tok_total, head_local, head_dim)
    gate_val = jax.nn.sigmoid(
        jnp.einsum("kmc,cd->kmd", columns, att_gate, preferred_element_type=jnp.float32)
    )
    block_rows = min(1024, tok_total)

    def one_column(triple):
        return attend_column(triple[0], triple[1], triple[2], bias_all, key_bias, block_rows)

    attended = lax.map(one_column, (qkv_all[0], qkv_all[1], qkv_all[2]))
    attended = jnp.transpose(attended, (1, 0, 2, 3)).reshape(tok_total, col_count, local_width)
    return (gate_val * attended).astype(jnp.bfloat16)


def split_pair_on_device(
    pair_in,
    token_mask,
    positions,
    relpos_table,
    tri_norm_in,
    tri_in_weight,
    tri_in_gate,
    tri_out_gate,
    tri_norm_out,
    tri_out_weight,
    att_norm,
    att_qkv,
    att_gate,
    att_bias,
    att_out,
):
    row_count, col_count, channels = pair_in.shape
    row_first = lax.axis_index("row") * row_count
    col_first = lax.axis_index("col") * col_count
    mask_float = token_mask.astype(jnp.float32)
    row_mask = lax.dynamic_slice_in_dim(mask_float, row_first, row_count)
    col_mask = lax.dynamic_slice_in_dim(mask_float, col_first, col_count)
    row_pos = lax.dynamic_slice_in_dim(positions, row_first, row_count)
    col_pos = lax.dynamic_slice_in_dim(positions, col_first, col_count)
    bin_count = relpos_table.shape[0]
    bin_centre = bin_count // 2
    bucket = jnp.clip(row_pos[:, None] - col_pos[None, :], -bin_centre, bin_centre - 1) + bin_centre
    onehot = (bucket[:, :, None] == jnp.arange(bin_count, dtype=jnp.int32)[None, None, :]).astype(
        jnp.bfloat16
    )
    residual = pair_in.astype(jnp.float32) + jnp.einsum(
        "rjb,bc->rjc", onehot, relpos_table, preferred_element_type=jnp.float32
    )
    normed = layer_norm(residual, tri_norm_in).astype(jnp.bfloat16)
    pair_mask = row_mask[:, None] * col_mask[None, :]
    gate_in = jnp.einsum("rjc,cd->drj", normed, tri_in_gate, preferred_element_type=jnp.float32)
    proj_in = jnp.einsum("rjc,cd->drj", normed, tri_in_weight, preferred_element_type=jnp.float32)
    projected = (jax.nn.sigmoid(gate_in) * proj_in * pair_mask[None, :, :]).astype(jnp.bfloat16)
    left_ch, right_ch = (
        lax.all_to_all(projected[:channels], "row", split_axis=0, concat_axis=1, tiled=True),
        lax.all_to_all(projected[channels:], "row", split_axis=0, concat_axis=1, tiled=True),
    )
    right_rows = lax.all_to_all(right_ch, "col", split_axis=1, concat_axis=2, tiled=True)
    product_sum = jnp.einsum(
        "cik,cjk->cij",
        lax.all_gather(left_ch, "col", axis=2, tiled=True),
        right_rows,
        preferred_element_type=jnp.float32,
    )
    products = product_sum.astype(jnp.bfloat16)
    product_tile = lax.all_to_all(products, "row", split_axis=1, concat_axis=0, tiled=True)
    tri_x = jnp.transpose(product_tile, (1, 2, 0)).astype(jnp.float32)
    normed_out = layer_norm(tri_x, tri_norm_out).astype(jnp.bfloat16)
    out_gate = jax.nn.sigmoid(
        jnp.einsum("rjc,cd->rjd", normed, tri_out_gate, preferred_element_type=jnp.float32)
    )
    residual = residual + out_gate * jnp.einsum(
        "rjc,cd->rjd", normed_out, tri_out_weight, preferred_element_type=jnp.float32
    )
    normed_att = layer_norm(residual, att_norm).astype(jnp.bfloat16)
    bias_piece = jnp.einsum(
        "kic,ch->hik", normed_att, att_bias, preferred_element_type=jnp.float32
    ).astype(jnp.bfloat16)
    key_bias = (mask_float - 1.0) * 1000000000.0
    head_count = att_bias.shape[1]
    head_dim = channels // head_count
    columns = lax.all_to_all(normed_att, "row", split_axis=1, concat_axis=0, tiled=True)
    bias_half = lax.all_gather(bias_piece, "col", axis=1, tiled=True)
    bias_all = lax.all_gather(bias_half, "row", axis=2, tiled=True)
    gated = column_attention(columns, att_qkv, att_gate, bias_all, key_bias, head_count, head_dim)
    gated_tile = lax.all_to_all(gated, "row", split_axis=0, concat_axis=1, tiled=True)
    update = jnp.einsum("rjc,cd->rjd", gated_tile, att_out, preferred_element_type=jnp.float32)
    return (residual + update).astype(jnp.bfloat16)


def on_device(row_dim, col_dim, pair_in, *others):
    rows, cols, width = pair_in.shape
    tokens = row_dim * rows
    whole_bytes = tokens * tokens * width * pair_in.dtype.itemsize
    bins = others[2].shape[0]
    tiled = cols % 8 == 0 and cols % rows == 0 and width == bins == tokens * cols == 128
    if whole_bytes <= WHOLE_PAIR_BYTES and tiled and (row_dim, col_dim) == (8, 2):
        return whole_pair_on_device(row_dim, pair_in, *others)
    return split_pair_on_device(pair_in, *others)


def solution(mesh):
    return jax.shard_map(
        functools.partial(on_device, mesh.shape["row"], mesh.shape["col"]),
        mesh=mesh,
        in_specs=(P(("groups", "row"), "col", None), P("groups"), P("groups")) + (P(),) * 12,
        out_specs=P(("groups", "row"), "col", None),
        check_vma=False,
    )
```

```python
import functools
import math

import jax
import jax.numpy as jnp
from jax import lax
from jax.experimental import pallas as pl
from jax.experimental.pallas import tpu as pltpu
from jax.sharding import PartitionSpec as P

epsilon = 1e-05

WHOLE_PAIR_BYTES = 256 * 1024
SPARE_ROWS = 16
STAGE_FLOPS = 10**9


def layer_norm(values, gain):
    mean_val = jnp.mean(values, axis=-1, keepdims=True)
    centred = values - mean_val
    var_val = jnp.mean(centred * centred, axis=-1, keepdims=True)
    return centred * lax.rsqrt(var_val + epsilon) * gain


def sigmoid(values):
    return 0.5 * jnp.tanh(0.5 * values) + 0.5


def dot(left, right):
    return jnp.dot(left, right, preferred_element_type=jnp.float32)


def dot_t(left, right):
    return lax.dot_general(
        left, right, (((1,), (1,)), ((), ())), preferred_element_type=jnp.float32
    )


def two_dots(left, first, second):
    both = dot(left, jnp.concatenate([first, second], axis=1))
    return both[:, : first.shape[1]], both[:, first.shape[1] :]


def round_bf16(values):
    return values.astype(jnp.bfloat16).astype(jnp.float32)


def column_kernel(other_columns_ref):
    sub = lax.broadcasted_iota(jnp.int32, other_columns_ref.shape, 0)
    lane = lax.broadcasted_iota(jnp.int32, other_columns_ref.shape, 1)
    other_columns_ref[...] = jnp.where(lane % other_columns_ref.shape[0] == sub, 0.0, -jnp.inf)


def token_rows(chips, rows):
    return [(lax.axis_index("row") ^ chip) * rows + r for chip in chips for r in range(rows)]


def stage_kernel(
    chips,
    rows,
    pair_ref,
    mask_ref,
    pos_ref,
    table_ref,
    norm_in_ref,
    norm_out_ref,
    att_norm_ref,
    att_bias_ref,
    other_columns_ref,
    chip_ref,
    rel_ref,
    pair_mask_ref,
    gains_ref,
    bias_ref,
    key_bias_ref,
    pos_rows_ref,
    mask_rows_ref,
):
    chip_ref[0] = pair_ref[...]
    gains_ref[0:1] = norm_in_ref[...]
    gains_ref[1:2] = norm_out_ref[...]
    gains_ref[2:3] = att_norm_ref[...]
    bias_ref[...] = att_bias_ref[...]
    tokens, (cols, lanes) = pos_ref.shape[1], key_bias_ref.shape
    bins, width = table_ref.shape
    f32 = jnp.float32

    def by_row(ref):
        sub = lax.broadcasted_iota(jnp.int32, (tokens, tokens), 0)
        lane = lax.broadcasted_iota(jnp.int32, (tokens, tokens), 1)
        spread = jnp.where(sub == lane, jnp.broadcast_to(ref[...].astype(f32), (tokens, tokens)), 0.0)
        return jnp.broadcast_to(jnp.sum(spread, axis=1, keepdims=True), (tokens, bins))

    pos_rows_ref[...] = by_row(pos_ref)
    mask_rows_ref[...] = by_row(mask_ref)
    own_half = lax.axis_index("col")
    halves = [pl.ds(pl.multiple_of((own_half ^ half) * cols, cols), cols) for half in range(tokens // cols)]
    lane = lax.broadcasted_iota(jnp.int32, (cols, bins), 1).astype(f32)
    key_of = lax.broadcasted_iota(jnp.int32, (1, lanes), 1) // cols
    key_mask = jnp.zeros((1, lanes), f32)
    centre = float(bins // 2)
    hot = []
    for at, token in enumerate(token_rows(chips, rows)):
        pos, mask = pos_rows_ref[pl.ds(token, 1), :], mask_rows_ref[pl.ds(token, 1), :]
        for half in halves:
            bucket = jnp.clip(pos - pos_rows_ref[half, :], -centre, centre - 1.0) + centre
            first = len(hot) * cols
            pair_mask_ref[first : first + cols, :] = mask_rows_ref[half, :] * mask
            hot.append((bucket == lane).astype(f32))
        key_mask = jnp.where(key_of == at, mask, key_mask)
    rel_ref[...] = dot(jnp.concatenate(hot, axis=0).astype(jnp.bfloat16), table_ref[...])
    key_bias_ref[...] = (key_mask - 1.0) * 1000000000.0 + other_columns_ref[...]


def edge_operands(pieces, orders, rows, rel, pair_mask, gain, in_gate, in_weight, for_right=lambda values: values):
    width = rel.shape[1]
    blocks = {
        place: piece[at].astype(jnp.float32) for piece, order in zip(pieces, orders) for at, place in enumerate(order)
    }
    tiles = [blocks[2 * chip + half][r] for chip in chips_of(orders) for r in range(rows) for half in range(2)]
    base = jnp.concatenate(tiles, axis=0) + rel
    normed_f = layer_norm(base, gain).astype(jnp.bfloat16).astype(jnp.float32)

    def operand(values, mask, columns):
        values = values.astype(jnp.bfloat16)
        gate, value = two_dots(values, in_gate[:, columns], in_weight[:, columns])
        return round_bf16(sigmoid(gate) * value * mask)

    left = operand(normed_f, pair_mask, slice(0, width))
    right = operand(for_right(normed_f), for_right(pair_mask), slice(width, 2 * width))
    return left, right, base, normed_f


def chips_of(orders):
    return list(dict.fromkeys(place // 2 for order in orders for place in order))


def early_kernel(orders, *refs):
    piece_refs = refs[: len(orders)]
    rel_ref, pair_mask_ref, gains_ref, in_weight_ref, in_gate_ref = refs[len(orders) : len(orders) + 5]
    here = refs[-1].shape[0] - SPARE_ROWS
    found = edge_operands(
        piece_refs,
        orders,
        piece_refs[0].shape[1],
        rel_ref[:here],
        pair_mask_ref[:here],
        gains_ref[0:1],
        in_gate_ref[...],
        in_weight_ref[...],
    )
    for ref, values in zip(refs[-4:], found):
        ref[:here] = values


def whole_pair_kernel(row_dim, heads, early, late, *refs):
    whole_pair_steps(row_dim, heads, early, late, refs[: len(late)], *refs[len(late) :])


def whole_pair_steps(
    row_dim,
    heads,
    early,
    late,
    piece_refs,
    early_left_ref,
    early_right_ref,
    early_base_ref,
    early_normed_ref,
    rel_ref,
    pair_mask_ref,
    gains_ref,
    att_bias_ref,
    key_bias_ref,
    in_weight_ref,
    in_gate_ref,
    out_gate_ref,
    out_weight_ref,
    qkv_ref,
    att_gate_ref,
    att_out_ref,
    out_ref,
    late_left_ref,
    late_base_ref,
    late_normed_ref,
    right_ref,
):
    rows, cols, width = piece_refs[0].shape[1:]
    tokens = row_dim * rows
    head_dim = width // heads
    row, col = lax.axis_index("row"), lax.axis_index("col")
    f32, bf16 = jnp.float32, jnp.bfloat16

    here = early_left_ref.shape[0] - SPARE_ROWS
    late_chips = chips_of(late)
    near = [chip for chip in late_chips if chip < row_dim // 2]
    far = [chip for chip in late_chips if chip >= row_dim // 2]
    near_is_own = row // (row_dim // 2) == col

    def for_right(values):
        count = rows * tokens
        rows_of = {chip: values[at * count : (at + 1) * count] for at, chip in enumerate(late_chips)}
        return jnp.concatenate([jnp.where(near_is_own, rows_of[n], rows_of[f]) for n, f in zip(near, far)], axis=0)

    left, right, base, normed = edge_operands(
        piece_refs,
        late,
        rows,
        rel_ref[here:],
        pair_mask_ref[here:],
        gains_ref[0:1],
        in_gate_ref[...],
        in_weight_ref[...],
        for_right,
    )
    late_left_ref[:here] = left
    late_base_ref[:here] = base
    late_normed_ref[:here] = normed
    lefts = (early_left_ref, late_left_ref)

    own_half = [jnp.where(near_is_own, n, f) for n, f in zip(near, far)]
    for tokens_of, values in (
        (token_rows(chips_of(early), rows), early_right_ref),
        (token_rows(own_half, rows), right),
    ):
        for at, token in enumerate(tokens_of):
            place = pl.ds(pl.multiple_of(token * tokens, tokens), tokens)
            right_ref[place, :] = values[at * tokens : (at + 1) * tokens]

    right_at = [right_ref[pl.ds(col * cols * tokens + m, cols, stride=tokens), :] for m in range(tokens)]
    products = []
    for i in range(tokens):
        ref, first = lefts[i * tokens // here], i * tokens % here
        total = ref[first : first + 1] * right_at[0]
        for m in range(1, tokens):
            total = total + ref[first + m : first + m + 1] * right_at[m]
        products.append(total)
    extra = [None] * rows
    for m in range(tokens):
        left_at = jnp.concatenate([ref[pl.ds(m, here // tokens, stride=tokens), :] for ref in lefts], axis=0)
        for r in range(rows):
            term = left_at * early_right_ref[r * tokens + m : r * tokens + m + 1]
            extra[r] = term if m == 0 else extra[r] + term

    own_token = row * rows
    own_column = ((own_token // cols) ^ col) * cols + own_token % cols

    def own_columns(early_ref, late_ref):
        pair = (early_ref, late_ref)
        return jnp.concatenate(
            [pair[i * tokens // here][i * tokens % here : i * tokens % here + cols] for i in range(tokens)], axis=0
        )

    def own_tokens(early_ref, late_ref):
        return jnp.concatenate(
            [
                ref[pl.ds(own_column + r, here // tokens, stride=tokens), :]
                for r in range(rows)
                for ref in (early_ref, late_ref)
            ],
            axis=0,
        )

    def attention_input(products, chosen):
        normed_out = layer_norm(round_bf16(jnp.concatenate(products, axis=0)), gains_ref[1:2]).astype(bf16)
        out_gate = sigmoid(dot(chosen(early_normed_ref, late_normed_ref).astype(bf16), out_gate_ref[...]))
        updated = chosen(early_base_ref, late_base_ref) + out_gate * dot(normed_out, out_weight_ref[...])
        return updated, layer_norm(updated, gains_ref[2:3]).astype(bf16)

    updated, column = attention_input(products, own_columns)
    _, of_tokens = attention_input(extra, own_tokens)
    own_pairs = rows * cols
    column_pairs = tokens * cols

    own = column[:own_pairs]
    queries, own_gate = two_dots(own, qkv_ref[:, :width], att_gate_ref[...])
    own_gate = sigmoid(own_gate)
    both = dot(column, qkv_ref[:, width:]).astype(bf16)
    keys, values = both[:, :width], both[:, width:]

    bias = dot_t(att_bias_ref[...], of_tokens).astype(bf16)
    shape = (rows * tokens, rows * column_pairs)
    source = lax.broadcasted_iota(jnp.int32, shape, 0)
    repeated = source == lax.broadcasted_iota(jnp.int32, shape, 1) // cols
    bias = dot(bias, repeated.astype(f32).astype(bf16))

    head_of = lax.broadcasted_iota(jnp.int32, (own_pairs, width), 1) // head_dim
    queries = round_bf16(queries)
    by_head = jnp.concatenate(
        [jnp.where(head_of == h, queries, 0.0) for h in range(heads)], axis=0
    ).astype(bf16)
    scores = dot_t(by_head, keys) * (1.0 / math.sqrt(head_dim))
    biases = jnp.concatenate(
        [
            jnp.broadcast_to(bias[h : h + 1, r * column_pairs : (r + 1) * column_pairs], (cols, column_pairs))
            for h in range(heads)
            for r in range(rows)
        ],
        axis=0,
    )
    key_bias = jnp.concatenate([key_bias_ref[...]] * (heads * rows), axis=0)
    scores = scores + biases + key_bias
    expo = jnp.exp(scores - jnp.max(scores, axis=-1, keepdims=True))
    shares = 1.0 / jnp.sum(expo, axis=-1, keepdims=True)
    mixed = dot(expo.astype(bf16), values) * shares
    attended = jnp.zeros((own_pairs, width), f32)
    for h in range(heads):
        attended = jnp.where(head_of == h, mixed[h * own_pairs : (h + 1) * own_pairs], attended)

    gated = (own_gate * attended).astype(bf16)
    result = updated[:own_pairs] + dot(gated, att_out_ref[...])
    out_ref[...] = result.reshape(rows, cols, width).astype(bf16)


def whole_pair_on_device(
    row_dim,
    pair_in,
    token_mask,
    positions,
    relpos_table,
    tri_norm_in,
    tri_in_weight,
    tri_in_gate,
    tri_out_gate,
    tri_norm_out,
    tri_out_weight,
    att_norm,
    att_qkv,
    att_gate,
    att_bias,
    att_out,
):
    rows, cols, width = pair_in.shape
    vmem = pl.BlockSpec(memory_space=pltpu.VMEM)
    params = pltpu.CompilerParams(vmem_limit_bytes=16 * 1024 * 1024)
    tokens, heads = row_dim * rows, att_bias.shape[1]

    blocks = 2 * row_dim

    def moved(order, step):
        return tuple(place ^ step for place in order)

    def move(values, step):
        return lax.ppermute(values, ("row", "col"), [(device, device ^ step) for device in range(blocks)])

    own_order = (0, 1)
    early = [own_order] + [moved(own_order, step) for step in (9, 15, 7)]
    late = [moved(own_order + early[1], step) for step in (3, 5)]

    beside = pl.CostEstimate(flops=STAGE_FLOPS, bytes_accessed=2**20, transcendentals=0)
    wide_out = jax.ShapeDtypeStruct((tokens * tokens, width), jnp.float32)
    key_shape = jax.ShapeDtypeStruct((cols, tokens * cols), jnp.float32)
    other_columns = pl.pallas_call(
        column_kernel,
        out_shape=key_shape,
        out_specs=vmem,
        compiler_params=params,
        cost_estimate=beside,
    )()
    chip, *staged = pl.pallas_call(
        functools.partial(stage_kernel, chips_of(early + late), rows),
        out_shape=[
            jax.ShapeDtypeStruct((2,) + pair_in.shape, pair_in.dtype),
            wide_out,
            wide_out,
            jax.ShapeDtypeStruct((3, width), jnp.float32),
            jax.ShapeDtypeStruct((heads, width), att_bias.dtype),
            key_shape,
        ],
        in_specs=[vmem] * 9,
        out_specs=[vmem] * 6,
        scratch_shapes=[pltpu.VMEM((tokens, relpos_table.shape[0]), jnp.float32)] * 2,
        compiler_params=params,
        cost_estimate=beside,
    )(
        pair_in,
        token_mask.reshape(1, tokens),
        positions.reshape(1, tokens),
        relpos_table,
        tri_norm_in.reshape(1, width),
        tri_norm_out.reshape(1, width),
        att_norm.reshape(1, width),
        att_bias.T,
        other_columns,
    )

    chip = chip.at[1].set(move(pair_in, 1))
    first = move(chip, 9)
    pieces = [chip, first, move(chip, 15), move(chip, 7)]
    both = jnp.concatenate([chip, first], axis=0)
    last = [move(both, 3), move(both, 5)]
    weights = (tri_in_weight, tri_in_gate, tri_out_gate, tri_out_weight, att_qkv, att_gate, att_out)
    rel, pair_mask, gains, *_ = staged
    half = jax.ShapeDtypeStruct((tokens * tokens // 2 + SPARE_ROWS, width), jnp.float32)
    halves = pl.pallas_call(
        functools.partial(early_kernel, early),
        out_shape=[half] * 4,
        in_specs=[vmem] * (7 + len(weights)),
        out_specs=[vmem] * 4,
        compiler_params=params,
        cost_estimate=beside,
    )(*pieces, rel, pair_mask, gains, *weights)
    return pl.pallas_call(
        functools.partial(whole_pair_kernel, row_dim, heads, early, late),
        out_shape=jax.ShapeDtypeStruct(pair_in.shape, pair_in.dtype),
        in_specs=[vmem] * (len(last) + 9 + len(weights)),
        out_specs=vmem,
        scratch_shapes=[pltpu.VMEM(half.shape, half.dtype)] * 3 + [pltpu.VMEM((tokens * tokens + SPARE_ROWS, width), jnp.float32)],
        compiler_params=params,
    )(*last, *halves, *staged, *weights)


def attend_column(query_col, key_col, value_col, bias_all, key_bias, block_rows):
    tok_total = query_col.shape[0]
    scale = 1.0 / math.sqrt(query_col.shape[2])

    def one_block(block_idx):
        scores = (
            jnp.einsum("ihe,khe->hik", query_col, key_col, preferred_element_type=jnp.float32)
            * scale
        )
        scores = scores + bias_all.astype(jnp.float32) + key_bias[None, None, :]
        row_max = jnp.max(scores, axis=-1, keepdims=True)
        expo_f = jnp.exp(scores - row_max)
        totals = jnp.sum(expo_f, axis=-1)
        weights = expo_f.astype(jnp.bfloat16)
        result = jnp.einsum("hik,khe->ihe", weights, value_col, preferred_element_type=jnp.float32)
        return result / jnp.transpose(totals)[:, :, None]

    blocks = lax.map(one_block, jnp.arange(tok_total // block_rows))
    return blocks.reshape(tok_total, query_col.shape[1], query_col.shape[2])


def column_attention(columns, att_qkv, att_gate, bias_all, key_bias, head_local, head_dim):
    tok_total, col_count, channels = columns.shape
    local_width = head_local * head_dim
    weight_three = att_qkv.reshape(channels, 3, channels)
    qkv_all = jnp.einsum(
        "kmc,ctd->tmkd", columns, weight_three, preferred_element_type=jnp.float32
    ).astype(jnp.bfloat16)
    qkv_all = qkv_all.reshape(3, col_count, tok_total, head_local, head_dim)
    gate_val = jax.nn.sigmoid(
        jnp.einsum("kmc,cd->kmd", columns, att_gate, preferred_element_type=jnp.float32)
    )
    block_rows = min(1024, tok_total)

    def one_column(triple):
        return attend_column(triple[0], triple[1], triple[2], bias_all, key_bias, block_rows)

    attended = lax.map(one_column, (qkv_all[0], qkv_all[1], qkv_all[2]))
    attended = jnp.transpose(attended, (1, 0, 2, 3)).reshape(tok_total, col_count, local_width)
    return (gate_val * attended).astype(jnp.bfloat16)


def split_pair_on_device(
    pair_in,
    token_mask,
    positions,
    relpos_table,
    tri_norm_in,
    tri_in_weight,
    tri_in_gate,
    tri_out_gate,
    tri_norm_out,
    tri_out_weight,
    att_norm,
    att_qkv,
    att_gate,
    att_bias,
    att_out,
):
    row_count, col_count, channels = pair_in.shape
    row_first = lax.axis_index("row") * row_count
    col_first = lax.axis_index("col") * col_count
    mask_float = token_mask.astype(jnp.float32)
    row_mask = lax.dynamic_slice_in_dim(mask_float, row_first, row_count)
    col_mask = lax.dynamic_slice_in_dim(mask_float, col_first, col_count)
    row_pos = lax.dynamic_slice_in_dim(positions, row_first, row_count)
    col_pos = lax.dynamic_slice_in_dim(positions, col_first, col_count)
    bin_count = relpos_table.shape[0]
    bin_centre = bin_count // 2
    bucket = jnp.clip(row_pos[:, None] - col_pos[None, :], -bin_centre, bin_centre - 1) + bin_centre
    onehot = (bucket[:, :, None] == jnp.arange(bin_count, dtype=jnp.int32)[None, None, :]).astype(
        jnp.bfloat16
    )
    residual = pair_in.astype(jnp.float32) + jnp.einsum(
        "rjb,bc->rjc", onehot, relpos_table, preferred_element_type=jnp.float32
    )
    normed = layer_norm(residual, tri_norm_in).astype(jnp.bfloat16)
    pair_mask = row_mask[:, None] * col_mask[None, :]
    gate_in = jnp.einsum("rjc,cd->drj", normed, tri_in_gate, preferred_element_type=jnp.float32)
    proj_in = jnp.einsum("rjc,cd->drj", normed, tri_in_weight, preferred_element_type=jnp.float32)
    projected = (jax.nn.sigmoid(gate_in) * proj_in * pair_mask[None, :, :]).astype(jnp.bfloat16)
    left_ch, right_ch = (
        lax.all_to_all(projected[:channels], "row", split_axis=0, concat_axis=1, tiled=True),
        lax.all_to_all(projected[channels:], "row", split_axis=0, concat_axis=1, tiled=True),
    )
    right_rows = lax.all_to_all(right_ch, "col", split_axis=1, concat_axis=2, tiled=True)
    product_sum = jnp.einsum(
        "cik,cjk->cij",
        lax.all_gather(left_ch, "col", axis=2, tiled=True),
        right_rows,
        preferred_element_type=jnp.float32,
    )
    products = product_sum.astype(jnp.bfloat16)
    product_tile = lax.all_to_all(products, "row", split_axis=1, concat_axis=0, tiled=True)
    tri_x = jnp.transpose(product_tile, (1, 2, 0)).astype(jnp.float32)
    normed_out = layer_norm(tri_x, tri_norm_out).astype(jnp.bfloat16)
    out_gate = jax.nn.sigmoid(
        jnp.einsum("rjc,cd->rjd", normed, tri_out_gate, preferred_element_type=jnp.float32)
    )
    residual = residual + out_gate * jnp.einsum(
        "rjc,cd->rjd", normed_out, tri_out_weight, preferred_element_type=jnp.float32
    )
    normed_att = layer_norm(residual, att_norm).astype(jnp.bfloat16)
    bias_piece = jnp.einsum(
        "kic,ch->hik", normed_att, att_bias, preferred_element_type=jnp.float32
    ).astype(jnp.bfloat16)
    key_bias = (mask_float - 1.0) * 1000000000.0
    head_count = att_bias.shape[1]
    head_dim = channels // head_count
    columns = lax.all_to_all(normed_att, "row", split_axis=1, concat_axis=0, tiled=True)
    bias_half = lax.all_gather(bias_piece, "col", axis=1, tiled=True)
    bias_all = lax.all_gather(bias_half, "row", axis=2, tiled=True)
    gated = column_attention(columns, att_qkv, att_gate, bias_all, key_bias, head_count, head_dim)
    gated_tile = lax.all_to_all(gated, "row", split_axis=0, concat_axis=1, tiled=True)
    update = jnp.einsum("rjc,cd->rjd", gated_tile, att_out, preferred_element_type=jnp.float32)
    return (residual + update).astype(jnp.bfloat16)


def on_device(row_dim, col_dim, pair_in, *others):
    rows, cols, width = pair_in.shape
    tokens = row_dim * rows
    whole_bytes = tokens * tokens * width * pair_in.dtype.itemsize
    bins = others[2].shape[0]
    tiled = cols % 8 == 0 and cols % rows == 0 and width == bins == tokens * cols == 128
    if whole_bytes <= WHOLE_PAIR_BYTES and tiled and (row_dim, col_dim) == (8, 2):
        return whole_pair_on_device(row_dim, pair_in, *others)
    return split_pair_on_device(pair_in, *others)


def solution(mesh):
    return jax.shard_map(
        functools.partial(on_device, mesh.shape["row"], mesh.shape["col"]),
        mesh=mesh,
        in_specs=(P(("groups", "row"), "col", None), P("groups"), P("groups")) + (P(),) * 12,
        out_specs=P(("groups", "row"), "col", None),
        check_vma=False,
    )
```

```python
import functools
import math

import jax
import jax.numpy as jnp
from jax import lax
from jax.experimental import pallas as pl
from jax.experimental.pallas import tpu as pltpu
from jax.sharding import PartitionSpec as P

epsilon = 1e-05

WHOLE_PAIR_BYTES = 256 * 1024
SPARE_ROWS = 16
STAGE_FLOPS = 10**9


def layer_norm(values, gain):
    mean_val = jnp.mean(values, axis=-1, keepdims=True)
    centred = values - mean_val
    var_val = jnp.mean(centred * centred, axis=-1, keepdims=True)
    return centred * lax.rsqrt(var_val + epsilon) * gain


def sigmoid(values):
    return 0.5 * jnp.tanh(0.5 * values) + 0.5


def dot(left, right):
    return jnp.dot(left, right, preferred_element_type=jnp.float32)


def dot_t(left, right):
    return lax.dot_general(
        left, right, (((1,), (1,)), ((), ())), preferred_element_type=jnp.float32
    )


def round_bf16(values):
    return values.astype(jnp.bfloat16).astype(jnp.float32)


def column_kernel(other_columns_ref):
    sub = lax.broadcasted_iota(jnp.int32, other_columns_ref.shape, 0)
    lane = lax.broadcasted_iota(jnp.int32, other_columns_ref.shape, 1)
    other_columns_ref[...] = jnp.where(lane % other_columns_ref.shape[0] == sub, 0.0, -jnp.inf)


def token_rows(chips, rows):
    return [(lax.axis_index("row") ^ chip) * rows + r for chip in chips for r in range(rows)]


def stage_kernel(
    chips,
    rows,
    pair_ref,
    mask_ref,
    pos_ref,
    table_ref,
    norm_in_ref,
    norm_out_ref,
    att_norm_ref,
    att_bias_ref,
    other_columns_ref,
    chip_ref,
    rel_ref,
    pair_mask_ref,
    gains_ref,
    bias_ref,
    key_bias_ref,
    pos_rows_ref,
    mask_rows_ref,
):
    chip_ref[0] = pair_ref[...]
    gains_ref[0:1] = norm_in_ref[...]
    gains_ref[1:2] = norm_out_ref[...]
    gains_ref[2:3] = att_norm_ref[...]
    bias_ref[...] = att_bias_ref[...]
    tokens, (cols, lanes) = pos_ref.shape[1], key_bias_ref.shape
    bins, width = table_ref.shape
    f32 = jnp.float32

    def by_row(ref):
        sub = lax.broadcasted_iota(jnp.int32, (tokens, tokens), 0)
        lane = lax.broadcasted_iota(jnp.int32, (tokens, tokens), 1)
        spread = jnp.where(sub == lane, jnp.broadcast_to(ref[...].astype(f32), (tokens, tokens)), 0.0)
        return jnp.broadcast_to(jnp.sum(spread, axis=1, keepdims=True), (tokens, bins))

    pos_rows_ref[...] = by_row(pos_ref)
    mask_rows_ref[...] = by_row(mask_ref)
    own_half = lax.axis_index("col")
    halves = [pl.ds(pl.multiple_of((own_half ^ half) * cols, cols), cols) for half in range(tokens // cols)]
    lane = lax.broadcasted_iota(jnp.int32, (cols, bins), 1).astype(f32)
    key_of = lax.broadcasted_iota(jnp.int32, (1, lanes), 1) // cols
    key_mask = jnp.zeros((1, lanes), f32)
    centre = float(bins // 2)
    hot = []
    for at, token in enumerate(token_rows(chips, rows)):
        pos, mask = pos_rows_ref[pl.ds(token, 1), :], mask_rows_ref[pl.ds(token, 1), :]
        for half in halves:
            bucket = jnp.clip(pos - pos_rows_ref[half, :], -centre, centre - 1.0) + centre
            first = len(hot) * cols
            pair_mask_ref[first : first + cols, :] = mask_rows_ref[half, :] * mask
            hot.append((bucket == lane).astype(f32))
        key_mask = jnp.where(key_of == at, mask, key_mask)
    rel_ref[...] = dot(jnp.concatenate(hot, axis=0).astype(jnp.bfloat16), table_ref[...])
    key_bias_ref[...] = (key_mask - 1.0) * 1000000000.0 + other_columns_ref[...]


def edge_operands(pieces, orders, rows, rel, pair_mask, gain, in_gate, in_weight, for_right=lambda values: values):
    width = rel.shape[1]
    blocks = {
        place: piece[at].astype(jnp.float32) for piece, order in zip(pieces, orders) for at, place in enumerate(order)
    }
    tiles = [blocks[2 * chip + half][r] for chip in chips_of(orders) for r in range(rows) for half in range(2)]
    base = jnp.concatenate(tiles, axis=0) + rel
    normed_f = layer_norm(base, gain).astype(jnp.bfloat16).astype(jnp.float32)

    def operand(values, mask, columns):
        values = values.astype(jnp.bfloat16)
        return round_bf16(sigmoid(dot(values, in_gate[:, columns])) * dot(values, in_weight[:, columns]) * mask)

    left = operand(normed_f, pair_mask, slice(0, width))
    right = operand(for_right(normed_f), for_right(pair_mask), slice(width, 2 * width))
    return left, right, base, normed_f


def chips_of(orders):
    return list(dict.fromkeys(place // 2 for order in orders for place in order))


def early_kernel(orders, *refs):
    piece_refs = refs[: len(orders)]
    rel_ref, pair_mask_ref, gains_ref, in_weight_ref, in_gate_ref = refs[len(orders) : len(orders) + 5]
    here = refs[-1].shape[0] - SPARE_ROWS
    found = edge_operands(
        piece_refs,
        orders,
        piece_refs[0].shape[1],
        rel_ref[:here],
        pair_mask_ref[:here],
        gains_ref[0:1],
        in_gate_ref[...],
        in_weight_ref[...],
    )
    for ref, values in zip(refs[-4:], found):
        ref[:here] = values


def whole_pair_kernel(row_dim, heads, early, late, *refs):
    whole_pair_steps(row_dim, heads, early, late, refs[: len(late)], *refs[len(late) :])


def whole_pair_steps(
    row_dim,
    heads,
    early,
    late,
    piece_refs,
    early_left_ref,
    early_right_ref,
    early_base_ref,
    early_normed_ref,
    rel_ref,
    pair_mask_ref,
    gains_ref,
    att_bias_ref,
    key_bias_ref,
    in_weight_ref,
    in_gate_ref,
    out_gate_ref,
    out_weight_ref,
    qkv_ref,
    att_gate_ref,
    att_out_ref,
    out_ref,
    late_left_ref,
    late_base_ref,
    late_normed_ref,
    right_ref,
):
    rows, cols, width = piece_refs[0].shape[1:]
    tokens = row_dim * rows
    head_dim = width // heads
    row, col = lax.axis_index("row"), lax.axis_index("col")
    f32, bf16 = jnp.float32, jnp.bfloat16

    here = early_left_ref.shape[0] - SPARE_ROWS
    late_chips = chips_of(late)
    near = [chip for chip in late_chips if chip < row_dim // 2]
    far = [chip for chip in late_chips if chip >= row_dim // 2]
    near_is_own = row // (row_dim // 2) == col

    def for_right(values):
        count = rows * tokens
        rows_of = {chip: values[at * count : (at + 1) * count] for at, chip in enumerate(late_chips)}
        return jnp.concatenate([jnp.where(near_is_own, rows_of[n], rows_of[f]) for n, f in zip(near, far)], axis=0)

    left, right, base, normed = edge_operands(
        piece_refs,
        late,
        rows,
        rel_ref[here:],
        pair_mask_ref[here:],
        gains_ref[0:1],
        in_gate_ref[...],
        in_weight_ref[...],
        for_right,
    )
    late_left_ref[:here] = left
    late_base_ref[:here] = base
    late_normed_ref[:here] = normed
    lefts = (early_left_ref, late_left_ref)

    own_half = [jnp.where(near_is_own, n, f) for n, f in zip(near, far)]
    for tokens_of, values in (
        (token_rows(chips_of(early), rows), early_right_ref),
        (token_rows(own_half, rows), right),
    ):
        for at, token in enumerate(tokens_of):
            place = pl.ds(pl.multiple_of(token * tokens, tokens), tokens)
            right_ref[place, :] = values[at * tokens : (at + 1) * tokens]

    right_at = [right_ref[pl.ds(col * cols * tokens + m, cols, stride=tokens), :] for m in range(tokens)]
    products = []
    for i in range(tokens):
        ref, first = lefts[i * tokens // here], i * tokens % here
        total = ref[first : first + 1] * right_at[0]
        for m in range(1, tokens):
            total = total + ref[first + m : first + m + 1] * right_at[m]
        products.append(total)
    extra = [None] * rows
    for m in range(tokens):
        left_at = jnp.concatenate([ref[pl.ds(m, here // tokens, stride=tokens), :] for ref in lefts], axis=0)
        for r in range(rows):
            term = left_at * early_right_ref[r * tokens + m : r * tokens + m + 1]
            extra[r] = term if m == 0 else extra[r] + term

    own_token = row * rows
    own_column = ((own_token // cols) ^ col) * cols + own_token % cols

    def own_columns(early_ref, late_ref):
        pair = (early_ref, late_ref)
        return jnp.concatenate(
            [pair[i * tokens // here][i * tokens % here : i * tokens % here + cols] for i in range(tokens)], axis=0
        )

    def own_tokens(early_ref, late_ref):
        return jnp.concatenate(
            [
                ref[pl.ds(own_column + r, here // tokens, stride=tokens), :]
                for r in range(rows)
                for ref in (early_ref, late_ref)
            ],
            axis=0,
        )

    def attention_input(products, chosen):
        normed_out = layer_norm(round_bf16(jnp.concatenate(products, axis=0)), gains_ref[1:2]).astype(bf16)
        out_gate = sigmoid(dot(chosen(early_normed_ref, late_normed_ref).astype(bf16), out_gate_ref[...]))
        updated = chosen(early_base_ref, late_base_ref) + out_gate * dot(normed_out, out_weight_ref[...])
        return updated, layer_norm(updated, gains_ref[2:3]).astype(bf16)

    updated, column = attention_input(products, own_columns)
    _, of_tokens = attention_input(extra, own_tokens)
    own_pairs = rows * cols
    column_pairs = tokens * cols

    own = column[:own_pairs]
    queries = dot(own, qkv_ref[:, :width])
    keys = dot(column, qkv_ref[:, width : 2 * width]).astype(bf16)
    values = dot(column, qkv_ref[:, 2 * width :]).astype(bf16)
    own_gate = sigmoid(dot(own, att_gate_ref[...]))

    bias = dot_t(att_bias_ref[...], of_tokens).astype(bf16)
    shape = (rows * tokens, rows * column_pairs)
    source = lax.broadcasted_iota(jnp.int32, shape, 0)
    repeated = source == lax.broadcasted_iota(jnp.int32, shape, 1) // cols
    bias = dot(bias, repeated.astype(f32).astype(bf16))

    head_of = lax.broadcasted_iota(jnp.int32, (own_pairs, width), 1) // head_dim
    queries = round_bf16(queries)
    by_head = jnp.concatenate(
        [jnp.where(head_of == h, queries, 0.0) for h in range(heads)], axis=0
    ).astype(bf16)
    scores = dot_t(by_head, keys) * (1.0 / math.sqrt(head_dim))
    biases = jnp.concatenate(
        [
            jnp.broadcast_to(bias[h : h + 1, r * column_pairs : (r + 1) * column_pairs], (cols, column_pairs))
            for h in range(heads)
            for r in range(rows)
        ],
        axis=0,
    )
    key_bias = jnp.concatenate([key_bias_ref[...]] * (heads * rows), axis=0)
    scores = scores + biases + key_bias
    expo = jnp.exp(scores - jnp.max(scores, axis=-1, keepdims=True))
    shares = 1.0 / jnp.sum(expo, axis=-1, keepdims=True)
    gates = jnp.concatenate([jnp.where(head_of == h, own_gate, 0.0) for h in range(heads)], axis=0)
    mixed = dot(expo.astype(bf16), values) * (gates * shares)

    gated = sum(mixed[h * own_pairs : (h + 1) * own_pairs] for h in range(heads)).astype(bf16)
    result = updated[:own_pairs] + dot(gated, att_out_ref[...])
    out_ref[...] = result.reshape(rows, cols, width).astype(bf16)


def whole_pair_on_device(
    row_dim,
    pair_in,
    token_mask,
    positions,
    relpos_table,
    tri_norm_in,
    tri_in_weight,
    tri_in_gate,
    tri_out_gate,
    tri_norm_out,
    tri_out_weight,
    att_norm,
    att_qkv,
    att_gate,
    att_bias,
    att_out,
):
    rows, cols, width = pair_in.shape
    vmem = pl.BlockSpec(memory_space=pltpu.VMEM)
    params = pltpu.CompilerParams(vmem_limit_bytes=16 * 1024 * 1024)
    tokens, heads = row_dim * rows, att_bias.shape[1]

    blocks = 2 * row_dim

    def moved(order, step):
        return tuple(place ^ step for place in order)

    def move(values, step):
        return lax.ppermute(values, ("row", "col"), [(device, device ^ step) for device in range(blocks)])

    own_order = (0, 1)
    early = [own_order] + [moved(own_order, step) for step in (9, 15, 7)]
    late = [moved(own_order + early[1], step) for step in (3, 5)]

    beside = pl.CostEstimate(flops=STAGE_FLOPS, bytes_accessed=2**20, transcendentals=0)
    wide_out = jax.ShapeDtypeStruct((tokens * tokens, width), jnp.float32)
    key_shape = jax.ShapeDtypeStruct((cols, tokens * cols), jnp.float32)
    other_columns = pl.pallas_call(
        column_kernel,
        out_shape=key_shape,
        out_specs=vmem,
        compiler_params=params,
        cost_estimate=beside,
    )()
    chip, *staged = pl.pallas_call(
        functools.partial(stage_kernel, chips_of(early + late), rows),
        out_shape=[
            jax.ShapeDtypeStruct((2,) + pair_in.shape, pair_in.dtype),
            wide_out,
            wide_out,
            jax.ShapeDtypeStruct((3, width), jnp.float32),
            jax.ShapeDtypeStruct((heads, width), att_bias.dtype),
            key_shape,
        ],
        in_specs=[vmem] * 9,
        out_specs=[vmem] * 6,
        scratch_shapes=[pltpu.VMEM((tokens, relpos_table.shape[0]), jnp.float32)] * 2,
        compiler_params=params,
        cost_estimate=beside,
    )(
        pair_in,
        token_mask.reshape(1, tokens),
        positions.reshape(1, tokens),
        relpos_table,
        tri_norm_in.reshape(1, width),
        tri_norm_out.reshape(1, width),
        att_norm.reshape(1, width),
        att_bias.T,
        other_columns,
    )

    chip = chip.at[1].set(move(pair_in, 1))
    first = move(chip, 9)
    pieces = [chip, first, move(chip, 15), move(chip, 7)]
    both = jnp.concatenate([chip, first], axis=0)
    last = [move(both, 3), move(both, 5)]
    weights = (tri_in_weight, tri_in_gate, tri_out_gate, tri_out_weight, att_qkv, att_gate, att_out)
    rel, pair_mask, gains, *_ = staged
    half = jax.ShapeDtypeStruct((tokens * tokens // 2 + SPARE_ROWS, width), jnp.float32)
    halves = pl.pallas_call(
        functools.partial(early_kernel, early),
        out_shape=[half] * 4,
        in_specs=[vmem] * (7 + len(weights)),
        out_specs=[vmem] * 4,
        compiler_params=params,
        cost_estimate=beside,
    )(*pieces, rel, pair_mask, gains, *weights)
    return pl.pallas_call(
        functools.partial(whole_pair_kernel, row_dim, heads, early, late),
        out_shape=jax.ShapeDtypeStruct(pair_in.shape, pair_in.dtype),
        in_specs=[vmem] * (len(last) + 9 + len(weights)),
        out_specs=vmem,
        scratch_shapes=[pltpu.VMEM(half.shape, half.dtype)] * 3 + [pltpu.VMEM((tokens * tokens + SPARE_ROWS, width), jnp.float32)],
        compiler_params=params,
    )(*last, *halves, *staged, *weights)


def attend_column(query_col, key_col, value_col, bias_all, key_bias, block_rows):
    tok_total = query_col.shape[0]
    scale = 1.0 / math.sqrt(query_col.shape[2])

    def one_block(block_idx):
        scores = (
            jnp.einsum("ihe,khe->hik", query_col, key_col, preferred_element_type=jnp.float32)
            * scale
        )
        scores = scores + bias_all.astype(jnp.float32) + key_bias[None, None, :]
        row_max = jnp.max(scores, axis=-1, keepdims=True)
        expo_f = jnp.exp(scores - row_max)
        totals = jnp.sum(expo_f, axis=-1)
        weights = expo_f.astype(jnp.bfloat16)
        result = jnp.einsum("hik,khe->ihe", weights, value_col, preferred_element_type=jnp.float32)
        return result / jnp.transpose(totals)[:, :, None]

    blocks = lax.map(one_block, jnp.arange(tok_total // block_rows))
    return blocks.reshape(tok_total, query_col.shape[1], query_col.shape[2])


def column_attention(columns, att_qkv, att_gate, bias_all, key_bias, head_local, head_dim):
    tok_total, col_count, channels = columns.shape
    local_width = head_local * head_dim
    weight_three = att_qkv.reshape(channels, 3, channels)
    qkv_all = jnp.einsum(
        "kmc,ctd->tmkd", columns, weight_three, preferred_element_type=jnp.float32
    ).astype(jnp.bfloat16)
    qkv_all = qkv_all.reshape(3, col_count, tok_total, head_local, head_dim)
    gate_val = jax.nn.sigmoid(
        jnp.einsum("kmc,cd->kmd", columns, att_gate, preferred_element_type=jnp.float32)
    )
    block_rows = min(1024, tok_total)

    def one_column(triple):
        return attend_column(triple[0], triple[1], triple[2], bias_all, key_bias, block_rows)

    attended = lax.map(one_column, (qkv_all[0], qkv_all[1], qkv_all[2]))
    attended = jnp.transpose(attended, (1, 0, 2, 3)).reshape(tok_total, col_count, local_width)
    return (gate_val * attended).astype(jnp.bfloat16)


def split_pair_on_device(
    pair_in,
    token_mask,
    positions,
    relpos_table,
    tri_norm_in,
    tri_in_weight,
    tri_in_gate,
    tri_out_gate,
    tri_norm_out,
    tri_out_weight,
    att_norm,
    att_qkv,
    att_gate,
    att_bias,
    att_out,
):
    row_count, col_count, channels = pair_in.shape
    row_first = lax.axis_index("row") * row_count
    col_first = lax.axis_index("col") * col_count
    mask_float = token_mask.astype(jnp.float32)
    row_mask = lax.dynamic_slice_in_dim(mask_float, row_first, row_count)
    col_mask = lax.dynamic_slice_in_dim(mask_float, col_first, col_count)
    row_pos = lax.dynamic_slice_in_dim(positions, row_first, row_count)
    col_pos = lax.dynamic_slice_in_dim(positions, col_first, col_count)
    bin_count = relpos_table.shape[0]
    bin_centre = bin_count // 2
    bucket = jnp.clip(row_pos[:, None] - col_pos[None, :], -bin_centre, bin_centre - 1) + bin_centre
    onehot = (bucket[:, :, None] == jnp.arange(bin_count, dtype=jnp.int32)[None, None, :]).astype(
        jnp.bfloat16
    )
    residual = pair_in.astype(jnp.float32) + jnp.einsum(
        "rjb,bc->rjc", onehot, relpos_table, preferred_element_type=jnp.float32
    )
    normed = layer_norm(residual, tri_norm_in).astype(jnp.bfloat16)
    pair_mask = row_mask[:, None] * col_mask[None, :]
    gate_in = jnp.einsum("rjc,cd->drj", normed, tri_in_gate, preferred_element_type=jnp.float32)
    proj_in = jnp.einsum("rjc,cd->drj", normed, tri_in_weight, preferred_element_type=jnp.float32)
    projected = (jax.nn.sigmoid(gate_in) * proj_in * pair_mask[None, :, :]).astype(jnp.bfloat16)
    left_ch, right_ch = (
        lax.all_to_all(projected[:channels], "row", split_axis=0, concat_axis=1, tiled=True),
        lax.all_to_all(projected[channels:], "row", split_axis=0, concat_axis=1, tiled=True),
    )
    right_rows = lax.all_to_all(right_ch, "col", split_axis=1, concat_axis=2, tiled=True)
    product_sum = jnp.einsum(
        "cik,cjk->cij",
        lax.all_gather(left_ch, "col", axis=2, tiled=True),
        right_rows,
        preferred_element_type=jnp.float32,
    )
    products = product_sum.astype(jnp.bfloat16)
    product_tile = lax.all_to_all(products, "row", split_axis=1, concat_axis=0, tiled=True)
    tri_x = jnp.transpose(product_tile, (1, 2, 0)).astype(jnp.float32)
    normed_out = layer_norm(tri_x, tri_norm_out).astype(jnp.bfloat16)
    out_gate = jax.nn.sigmoid(
        jnp.einsum("rjc,cd->rjd", normed, tri_out_gate, preferred_element_type=jnp.float32)
    )
    residual = residual + out_gate * jnp.einsum(
        "rjc,cd->rjd", normed_out, tri_out_weight, preferred_element_type=jnp.float32
    )
    normed_att = layer_norm(residual, att_norm).astype(jnp.bfloat16)
    bias_piece = jnp.einsum(
        "kic,ch->hik", normed_att, att_bias, preferred_element_type=jnp.float32
    ).astype(jnp.bfloat16)
    key_bias = (mask_float - 1.0) * 1000000000.0
    head_count = att_bias.shape[1]
    head_dim = channels // head_count
    columns = lax.all_to_all(normed_att, "row", split_axis=1, concat_axis=0, tiled=True)
    bias_half = lax.all_gather(bias_piece, "col", axis=1, tiled=True)
    bias_all = lax.all_gather(bias_half, "row", axis=2, tiled=True)
    gated = column_attention(columns, att_qkv, att_gate, bias_all, key_bias, head_count, head_dim)
    gated_tile = lax.all_to_all(gated, "row", split_axis=0, concat_axis=1, tiled=True)
    update = jnp.einsum("rjc,cd->rjd", gated_tile, att_out, preferred_element_type=jnp.float32)
    return (residual + update).astype(jnp.bfloat16)


def on_device(row_dim, col_dim, pair_in, *others):
    rows, cols, width = pair_in.shape
    tokens = row_dim * rows
    whole_bytes = tokens * tokens * width * pair_in.dtype.itemsize
    bins = others[2].shape[0]
    tiled = cols % 8 == 0 and cols % rows == 0 and width == bins == tokens * cols == 128
    if whole_bytes <= WHOLE_PAIR_BYTES and tiled and (row_dim, col_dim) == (8, 2):
        return whole_pair_on_device(row_dim, pair_in, *others)
    return split_pair_on_device(pair_in, *others)


def solution(mesh):
    return jax.shard_map(
        functools.partial(on_device, mesh.shape["row"], mesh.shape["col"]),
        mesh=mesh,
        in_specs=(P(("groups", "row"), "col", None), P("groups"), P("groups")) + (P(),) * 12,
        out_specs=P(("groups", "row"), "col", None),
        check_vma=False,
    )
```

```python
import functools
import math

import jax
import jax.numpy as jnp
from jax import lax
from jax.experimental import pallas as pl
from jax.experimental.pallas import tpu as pltpu
from jax.sharding import PartitionSpec as P

epsilon = 1e-05

WHOLE_PAIR_BYTES = 256 * 1024
SPARE_ROWS = 16
STAGE_FLOPS = 10**9


def layer_norm(values, gain):
    mean_val = jnp.mean(values, axis=-1, keepdims=True)
    centred = values - mean_val
    var_val = jnp.mean(centred * centred, axis=-1, keepdims=True)
    return centred * lax.rsqrt(var_val + epsilon) * gain


def sigmoid(values):
    return 0.5 * jnp.tanh(0.5 * values) + 0.5


def dot(left, right):
    return jnp.dot(left, right, preferred_element_type=jnp.float32)


def dot_t(left, right):
    return lax.dot_general(
        left, right, (((1,), (1,)), ((), ())), preferred_element_type=jnp.float32
    )


def round_bf16(values):
    return values.astype(jnp.bfloat16).astype(jnp.float32)


def column_kernel(other_columns_ref):
    sub = lax.broadcasted_iota(jnp.int32, other_columns_ref.shape, 0)
    lane = lax.broadcasted_iota(jnp.int32, other_columns_ref.shape, 1)
    other_columns_ref[...] = jnp.where(lane % other_columns_ref.shape[0] == sub, 0.0, -jnp.inf)


def token_rows(chips, rows):
    return [(lax.axis_index("row") ^ chip) * rows + r for chip in chips for r in range(rows)]


def stage_kernel(
    chips,
    rows,
    pair_ref,
    mask_ref,
    pos_ref,
    table_ref,
    norm_in_ref,
    norm_out_ref,
    att_norm_ref,
    att_bias_ref,
    other_columns_ref,
    chip_ref,
    rel_ref,
    pair_mask_ref,
    gains_ref,
    bias_ref,
    key_bias_ref,
    pos_rows_ref,
    mask_rows_ref,
):
    chip_ref[0] = pair_ref[...]
    gains_ref[0:1] = norm_in_ref[...]
    gains_ref[1:2] = norm_out_ref[...]
    gains_ref[2:3] = att_norm_ref[...]
    bias_ref[...] = att_bias_ref[...]
    tokens, (cols, lanes) = pos_ref.shape[1], key_bias_ref.shape
    bins, width = table_ref.shape
    f32 = jnp.float32

    def by_row(ref):
        sub = lax.broadcasted_iota(jnp.int32, (tokens, tokens), 0)
        lane = lax.broadcasted_iota(jnp.int32, (tokens, tokens), 1)
        spread = jnp.where(sub == lane, jnp.broadcast_to(ref[...].astype(f32), (tokens, tokens)), 0.0)
        return jnp.broadcast_to(jnp.sum(spread, axis=1, keepdims=True), (tokens, bins))

    pos_rows_ref[...] = by_row(pos_ref)
    mask_rows_ref[...] = by_row(mask_ref)
    own_half = lax.axis_index("col")
    halves = [pl.ds(pl.multiple_of((own_half ^ half) * cols, cols), cols) for half in range(tokens // cols)]
    lane = lax.broadcasted_iota(jnp.int32, (cols, bins), 1).astype(f32)
    key_of = lax.broadcasted_iota(jnp.int32, (1, lanes), 1) // cols
    key_mask = jnp.zeros((1, lanes), f32)
    centre = float(bins // 2)
    hot = []
    for at, token in enumerate(token_rows(chips, rows)):
        pos, mask = pos_rows_ref[pl.ds(token, 1), :], mask_rows_ref[pl.ds(token, 1), :]
        for half in halves:
            bucket = jnp.clip(pos - pos_rows_ref[half, :], -centre, centre - 1.0) + centre
            first = len(hot) * cols
            pair_mask_ref[first : first + cols, :] = mask_rows_ref[half, :] * (0.5 * mask)
            hot.append((bucket == lane).astype(f32))
        key_mask = jnp.where(key_of == at, mask, key_mask)
    rel_ref[...] = dot(jnp.concatenate(hot, axis=0).astype(jnp.bfloat16), table_ref[...])
    key_bias_ref[...] = (key_mask - 1.0) * 1000000000.0 + other_columns_ref[...]


def edge_operands(pieces, orders, rows, rel, pair_mask, gain, in_gate, in_weight, for_right=lambda values: values):
    width = rel.shape[1]
    blocks = {
        place: piece[at].astype(jnp.float32) for piece, order in zip(pieces, orders) for at, place in enumerate(order)
    }
    tiles = [blocks[2 * chip + half][r] for chip in chips_of(orders) for r in range(rows) for half in range(2)]
    base = jnp.concatenate(tiles, axis=0) + rel
    normed_f = layer_norm(base, gain).astype(jnp.bfloat16).astype(jnp.float32)

    def operand(values, mask, columns):
        values = values.astype(jnp.bfloat16)
        gate = jnp.tanh(0.5 * dot(values, in_gate[:, columns])) + 1.0
        return round_bf16(gate * (dot(values, in_weight[:, columns]) * mask))

    left = operand(normed_f, pair_mask, slice(0, width))
    right = operand(for_right(normed_f), for_right(pair_mask), slice(width, 2 * width))
    return left, right, base, normed_f


def chips_of(orders):
    return list(dict.fromkeys(place // 2 for order in orders for place in order))


def early_kernel(orders, *refs):
    piece_refs = refs[: len(orders)]
    rel_ref, pair_mask_ref, gains_ref, in_weight_ref, in_gate_ref = refs[len(orders) : len(orders) + 5]
    here = refs[-1].shape[0] - SPARE_ROWS
    found = edge_operands(
        piece_refs,
        orders,
        piece_refs[0].shape[1],
        rel_ref[:here],
        pair_mask_ref[:here],
        gains_ref[0:1],
        in_gate_ref[...],
        in_weight_ref[...],
    )
    for ref, values in zip(refs[-4:], found):
        ref[:here] = values


def whole_pair_kernel(row_dim, heads, early, late, *refs):
    whole_pair_steps(row_dim, heads, early, late, refs[: len(late)], *refs[len(late) :])


def whole_pair_steps(
    row_dim,
    heads,
    early,
    late,
    piece_refs,
    early_left_ref,
    early_right_ref,
    early_base_ref,
    early_normed_ref,
    rel_ref,
    pair_mask_ref,
    gains_ref,
    att_bias_ref,
    key_bias_ref,
    in_weight_ref,
    in_gate_ref,
    out_gate_ref,
    out_weight_ref,
    qkv_ref,
    att_gate_ref,
    att_out_ref,
    out_ref,
    late_left_ref,
    late_base_ref,
    late_normed_ref,
    right_ref,
):
    rows, cols, width = piece_refs[0].shape[1:]
    tokens = row_dim * rows
    head_dim = width // heads
    row, col = lax.axis_index("row"), lax.axis_index("col")
    f32, bf16 = jnp.float32, jnp.bfloat16

    here = early_left_ref.shape[0] - SPARE_ROWS
    late_chips = chips_of(late)
    near = [chip for chip in late_chips if chip < row_dim // 2]
    far = [chip for chip in late_chips if chip >= row_dim // 2]
    near_is_own = row // (row_dim // 2) == col

    def for_right(values):
        count = rows * tokens
        rows_of = {chip: values[at * count : (at + 1) * count] for at, chip in enumerate(late_chips)}
        return jnp.concatenate([jnp.where(near_is_own, rows_of[n], rows_of[f]) for n, f in zip(near, far)], axis=0)

    left, right, base, normed = edge_operands(
        piece_refs,
        late,
        rows,
        rel_ref[here:],
        pair_mask_ref[here:],
        gains_ref[0:1],
        in_gate_ref[...],
        in_weight_ref[...],
        for_right,
    )
    late_left_ref[:here] = left
    late_base_ref[:here] = base
    late_normed_ref[:here] = normed
    lefts = (early_left_ref, late_left_ref)

    own_half = [jnp.where(near_is_own, n, f) for n, f in zip(near, far)]
    for tokens_of, values in (
        (token_rows(chips_of(early), rows), early_right_ref),
        (token_rows(own_half, rows), right),
    ):
        for at, token in enumerate(tokens_of):
            place = pl.ds(pl.multiple_of(token * tokens, tokens), tokens)
            right_ref[place, :] = values[at * tokens : (at + 1) * tokens]

    right_at = [right_ref[pl.ds(col * cols * tokens + m, cols, stride=tokens), :] for m in range(tokens)]
    products = []
    for i in range(tokens):
        ref, first = lefts[i * tokens // here], i * tokens % here
        total = ref[first : first + 1] * right_at[0]
        for m in range(1, tokens):
            total = total + ref[first + m : first + m + 1] * right_at[m]
        products.append(total)
    extra = [None] * rows
    for m in range(tokens):
        left_at = jnp.concatenate([ref[pl.ds(m, here // tokens, stride=tokens), :] for ref in lefts], axis=0)
        for r in range(rows):
            term = left_at * early_right_ref[r * tokens + m : r * tokens + m + 1]
            extra[r] = term if m == 0 else extra[r] + term

    own_token = row * rows
    own_column = ((own_token // cols) ^ col) * cols + own_token % cols

    def own_columns(early_ref, late_ref):
        pair = (early_ref, late_ref)
        return jnp.concatenate(
            [pair[i * tokens // here][i * tokens % here : i * tokens % here + cols] for i in range(tokens)], axis=0
        )

    def own_tokens(early_ref, late_ref):
        return jnp.concatenate(
            [
                ref[pl.ds(own_column + r, here // tokens, stride=tokens), :]
                for r in range(rows)
                for ref in (early_ref, late_ref)
            ],
            axis=0,
        )

    def attention_input(products, chosen):
        normed_out = layer_norm(round_bf16(jnp.concatenate(products, axis=0)), gains_ref[1:2]).astype(bf16)
        out_gate = sigmoid(dot(chosen(early_normed_ref, late_normed_ref).astype(bf16), out_gate_ref[...]))
        updated = chosen(early_base_ref, late_base_ref) + out_gate * dot(normed_out, out_weight_ref[...])
        return updated, layer_norm(updated, gains_ref[2:3]).astype(bf16)

    updated, column = attention_input(products, own_columns)
    _, of_tokens = attention_input(extra, own_tokens)
    own_pairs = rows * cols
    column_pairs = tokens * cols

    own = column[:own_pairs]
    queries = dot(own, qkv_ref[:, :width])
    keys = dot(column, qkv_ref[:, width : 2 * width]).astype(bf16)
    values = dot(column, qkv_ref[:, 2 * width :]).astype(bf16)
    own_gate = sigmoid(dot(own, att_gate_ref[...]))

    bias = dot_t(att_bias_ref[...], of_tokens).astype(bf16)
    shape = (rows * tokens, rows * column_pairs)
    source = lax.broadcasted_iota(jnp.int32, shape, 0)
    repeated = source == lax.broadcasted_iota(jnp.int32, shape, 1) // cols
    bias = dot(bias, repeated.astype(f32).astype(bf16))

    head_of = lax.broadcasted_iota(jnp.int32, (own_pairs, width), 1) // head_dim
    queries = round_bf16(queries)
    by_head = jnp.concatenate(
        [jnp.where(head_of == h, queries, 0.0) for h in range(heads)], axis=0
    ).astype(bf16)
    scores = dot_t(by_head, keys) * (1.0 / math.sqrt(head_dim))
    biases = jnp.concatenate(
        [
            jnp.broadcast_to(bias[h : h + 1, r * column_pairs : (r + 1) * column_pairs], (cols, column_pairs))
            for h in range(heads)
            for r in range(rows)
        ],
        axis=0,
    )
    key_bias = jnp.concatenate([key_bias_ref[...]] * (heads * rows), axis=0)
    scores = scores + biases + key_bias
    expo = jnp.exp(scores - jnp.max(scores, axis=-1, keepdims=True))
    shares = 1.0 / jnp.sum(expo, axis=-1, keepdims=True)
    gates = jnp.concatenate([jnp.where(head_of == h, own_gate, 0.0) for h in range(heads)], axis=0)
    mixed = dot(expo.astype(bf16), values) * (gates * shares)

    gated = sum(mixed[h * own_pairs : (h + 1) * own_pairs] for h in range(heads)).astype(bf16)
    result = updated[:own_pairs] + dot(gated, att_out_ref[...])
    out_ref[...] = result.reshape(rows, cols, width).astype(bf16)


def whole_pair_on_device(
    row_dim,
    pair_in,
    token_mask,
    positions,
    relpos_table,
    tri_norm_in,
    tri_in_weight,
    tri_in_gate,
    tri_out_gate,
    tri_norm_out,
    tri_out_weight,
    att_norm,
    att_qkv,
    att_gate,
    att_bias,
    att_out,
):
    rows, cols, width = pair_in.shape
    vmem = pl.BlockSpec(memory_space=pltpu.VMEM)
    params = pltpu.CompilerParams(vmem_limit_bytes=16 * 1024 * 1024)
    tokens, heads = row_dim * rows, att_bias.shape[1]

    blocks = 2 * row_dim

    def moved(order, step):
        return tuple(place ^ step for place in order)

    def move(values, step):
        return lax.ppermute(values, ("row", "col"), [(device, device ^ step) for device in range(blocks)])

    own_order = (0, 1)
    early = [own_order] + [moved(own_order, step) for step in (9, 15, 7)]
    late = [moved(own_order + early[1], step) for step in (3, 5)]

    beside = pl.CostEstimate(flops=STAGE_FLOPS, bytes_accessed=2**20, transcendentals=0)
    wide_out = jax.ShapeDtypeStruct((tokens * tokens, width), jnp.float32)
    key_shape = jax.ShapeDtypeStruct((cols, tokens * cols), jnp.float32)
    other_columns = pl.pallas_call(
        column_kernel,
        out_shape=key_shape,
        out_specs=vmem,
        compiler_params=params,
        cost_estimate=beside,
    )()
    chip, *staged = pl.pallas_call(
        functools.partial(stage_kernel, chips_of(early + late), rows),
        out_shape=[
            jax.ShapeDtypeStruct((2,) + pair_in.shape, pair_in.dtype),
            wide_out,
            wide_out,
            jax.ShapeDtypeStruct((3, width), jnp.float32),
            jax.ShapeDtypeStruct((heads, width), att_bias.dtype),
            key_shape,
        ],
        in_specs=[vmem] * 9,
        out_specs=[vmem] * 6,
        scratch_shapes=[pltpu.VMEM((tokens, relpos_table.shape[0]), jnp.float32)] * 2,
        compiler_params=params,
        cost_estimate=beside,
    )(
        pair_in,
        token_mask.reshape(1, tokens),
        positions.reshape(1, tokens),
        relpos_table,
        tri_norm_in.reshape(1, width),
        tri_norm_out.reshape(1, width),
        att_norm.reshape(1, width),
        att_bias.T,
        other_columns,
    )

    chip = chip.at[1].set(move(pair_in, 1))
    first = move(chip, 9)
    pieces = [chip, first, move(chip, 15), move(chip, 7)]
    both = jnp.concatenate([chip, first], axis=0)
    last = [move(both, 3), move(both, 5)]
    weights = (tri_in_weight, tri_in_gate, tri_out_gate, tri_out_weight, att_qkv, att_gate, att_out)
    rel, pair_mask, gains, *_ = staged
    half = jax.ShapeDtypeStruct((tokens * tokens // 2 + SPARE_ROWS, width), jnp.float32)
    halves = pl.pallas_call(
        functools.partial(early_kernel, early),
        out_shape=[half] * 4,
        in_specs=[vmem] * (7 + len(weights)),
        out_specs=[vmem] * 4,
        compiler_params=params,
        cost_estimate=beside,
    )(*pieces, rel, pair_mask, gains, *weights)
    return pl.pallas_call(
        functools.partial(whole_pair_kernel, row_dim, heads, early, late),
        out_shape=jax.ShapeDtypeStruct(pair_in.shape, pair_in.dtype),
        in_specs=[vmem] * (len(last) + 9 + len(weights)),
        out_specs=vmem,
        scratch_shapes=[pltpu.VMEM(half.shape, half.dtype)] * 3 + [pltpu.VMEM((tokens * tokens + SPARE_ROWS, width), jnp.float32)],
        compiler_params=params,
    )(*last, *halves, *staged, *weights)


def attend_column(query_col, key_col, value_col, bias_all, key_bias, block_rows):
    tok_total = query_col.shape[0]
    scale = 1.0 / math.sqrt(query_col.shape[2])

    def one_block(block_idx):
        scores = (
            jnp.einsum("ihe,khe->hik", query_col, key_col, preferred_element_type=jnp.float32)
            * scale
        )
        scores = scores + bias_all.astype(jnp.float32) + key_bias[None, None, :]
        row_max = jnp.max(scores, axis=-1, keepdims=True)
        expo_f = jnp.exp(scores - row_max)
        totals = jnp.sum(expo_f, axis=-1)
        weights = expo_f.astype(jnp.bfloat16)
        result = jnp.einsum("hik,khe->ihe", weights, value_col, preferred_element_type=jnp.float32)
        return result / jnp.transpose(totals)[:, :, None]

    blocks = lax.map(one_block, jnp.arange(tok_total // block_rows))
    return blocks.reshape(tok_total, query_col.shape[1], query_col.shape[2])


def column_attention(columns, att_qkv, att_gate, bias_all, key_bias, head_local, head_dim):
    tok_total, col_count, channels = columns.shape
    local_width = head_local * head_dim
    weight_three = att_qkv.reshape(channels, 3, channels)
    qkv_all = jnp.einsum(
        "kmc,ctd->tmkd", columns, weight_three, preferred_element_type=jnp.float32
    ).astype(jnp.bfloat16)
    qkv_all = qkv_all.reshape(3, col_count, tok_total, head_local, head_dim)
    gate_val = jax.nn.sigmoid(
        jnp.einsum("kmc,cd->kmd", columns, att_gate, preferred_element_type=jnp.float32)
    )
    block_rows = min(1024, tok_total)

    def one_column(triple):
        return attend_column(triple[0], triple[1], triple[2], bias_all, key_bias, block_rows)

    attended = lax.map(one_column, (qkv_all[0], qkv_all[1], qkv_all[2]))
    attended = jnp.transpose(attended, (1, 0, 2, 3)).reshape(tok_total, col_count, local_width)
    return (gate_val * attended).astype(jnp.bfloat16)


def split_pair_on_device(
    pair_in,
    token_mask,
    positions,
    relpos_table,
    tri_norm_in,
    tri_in_weight,
    tri_in_gate,
    tri_out_gate,
    tri_norm_out,
    tri_out_weight,
    att_norm,
    att_qkv,
    att_gate,
    att_bias,
    att_out,
):
    row_count, col_count, channels = pair_in.shape
    row_first = lax.axis_index("row") * row_count
    col_first = lax.axis_index("col") * col_count
    mask_float = token_mask.astype(jnp.float32)
    row_mask = lax.dynamic_slice_in_dim(mask_float, row_first, row_count)
    col_mask = lax.dynamic_slice_in_dim(mask_float, col_first, col_count)
    row_pos = lax.dynamic_slice_in_dim(positions, row_first, row_count)
    col_pos = lax.dynamic_slice_in_dim(positions, col_first, col_count)
    bin_count = relpos_table.shape[0]
    bin_centre = bin_count // 2
    bucket = jnp.clip(row_pos[:, None] - col_pos[None, :], -bin_centre, bin_centre - 1) + bin_centre
    onehot = (bucket[:, :, None] == jnp.arange(bin_count, dtype=jnp.int32)[None, None, :]).astype(
        jnp.bfloat16
    )
    residual = pair_in.astype(jnp.float32) + jnp.einsum(
        "rjb,bc->rjc", onehot, relpos_table, preferred_element_type=jnp.float32
    )
    normed = layer_norm(residual, tri_norm_in).astype(jnp.bfloat16)
    pair_mask = row_mask[:, None] * col_mask[None, :]
    gate_in = jnp.einsum("rjc,cd->drj", normed, tri_in_gate, preferred_element_type=jnp.float32)
    proj_in = jnp.einsum("rjc,cd->drj", normed, tri_in_weight, preferred_element_type=jnp.float32)
    projected = (jax.nn.sigmoid(gate_in) * proj_in * pair_mask[None, :, :]).astype(jnp.bfloat16)
    left_ch, right_ch = (
        lax.all_to_all(projected[:channels], "row", split_axis=0, concat_axis=1, tiled=True),
        lax.all_to_all(projected[channels:], "row", split_axis=0, concat_axis=1, tiled=True),
    )
    right_rows = lax.all_to_all(right_ch, "col", split_axis=1, concat_axis=2, tiled=True)
    product_sum = jnp.einsum(
        "cik,cjk->cij",
        lax.all_gather(left_ch, "col", axis=2, tiled=True),
        right_rows,
        preferred_element_type=jnp.float32,
    )
    products = product_sum.astype(jnp.bfloat16)
    product_tile = lax.all_to_all(products, "row", split_axis=1, concat_axis=0, tiled=True)
    tri_x = jnp.transpose(product_tile, (1, 2, 0)).astype(jnp.float32)
    normed_out = layer_norm(tri_x, tri_norm_out).astype(jnp.bfloat16)
    out_gate = jax.nn.sigmoid(
        jnp.einsum("rjc,cd->rjd", normed, tri_out_gate, preferred_element_type=jnp.float32)
    )
    residual = residual + out_gate * jnp.einsum(
        "rjc,cd->rjd", normed_out, tri_out_weight, preferred_element_type=jnp.float32
    )
    normed_att = layer_norm(residual, att_norm).astype(jnp.bfloat16)
    bias_piece = jnp.einsum(
        "kic,ch->hik", normed_att, att_bias, preferred_element_type=jnp.float32
    ).astype(jnp.bfloat16)
    key_bias = (mask_float - 1.0) * 1000000000.0
    head_count = att_bias.shape[1]
    head_dim = channels // head_count
    columns = lax.all_to_all(normed_att, "row", split_axis=1, concat_axis=0, tiled=True)
    bias_half = lax.all_gather(bias_piece, "col", axis=1, tiled=True)
    bias_all = lax.all_gather(bias_half, "row", axis=2, tiled=True)
    gated = column_attention(columns, att_qkv, att_gate, bias_all, key_bias, head_count, head_dim)
    gated_tile = lax.all_to_all(gated, "row", split_axis=0, concat_axis=1, tiled=True)
    update = jnp.einsum("rjc,cd->rjd", gated_tile, att_out, preferred_element_type=jnp.float32)
    return (residual + update).astype(jnp.bfloat16)


def on_device(row_dim, col_dim, pair_in, *others):
    rows, cols, width = pair_in.shape
    tokens = row_dim * rows
    whole_bytes = tokens * tokens * width * pair_in.dtype.itemsize
    bins = others[2].shape[0]
    tiled = cols % 8 == 0 and cols % rows == 0 and width == bins == tokens * cols == 128
    if whole_bytes <= WHOLE_PAIR_BYTES and tiled and (row_dim, col_dim) == (8, 2):
        return whole_pair_on_device(row_dim, pair_in, *others)
    return split_pair_on_device(pair_in, *others)


def solution(mesh):
    return jax.shard_map(
        functools.partial(on_device, mesh.shape["row"], mesh.shape["col"]),
        mesh=mesh,
        in_specs=(P(("groups", "row"), "col", None), P("groups"), P("groups")) + (P(),) * 12,
        out_specs=P(("groups", "row"), "col", None),
        check_vma=False,
    )
```
